32 devices in a mesh: segment: 2 (over core), row: 4 (over y, x), col: 4 (over z).
Axes of the slice: x: 2, y: 2, z: 4, core: 2. Of those that a mesh axis runs over, the one named last changes fastest.
Arguments:
- activations: bfloat16 [2, 96, 96, 128], P('segment', 'row', 'col'), may hold values from -6 to 6
- cotangent: bfloat16 [2, 96, 96, 128], P('segment', 'row', 'col'), may hold values from -6 to 6
- conv_weight: bfloat16 [2, 9, 128, 64], P('segment'), may hold values from -0.1875 to 0.1875
- conv_bias: bfloat16 [2, 64], P('segment'), may hold values from -3 to 3
- out_weight: bfloat16 [2, 64, 128], P('segment'), may hold values from -0.75 to 0.75
Outputs:
- input_gradient: bfloat16 [2, 96, 96, 128], P('segment', 'row', 'col')
- conv_gradient: float32 [2, 9, 128, 64], P('segment')
- bias_gradient: float32 [2, 64], P('segment')
- output_weight_gradient: float32 [2, 64, 128], P('segment')
The draws below stay inside these ranges and needn't reach their ends.
All inputs are finite; a program needn't handle non-finite values.
Results may differ from the reference program's by a relative error of at most 0.022.
The reference program's roundings to bfloat16 on the way (of `hidden`, `bottle`, `branch_sum`, `sym`, `grad_branch` and `grad_pre`) count: a program that leaves them out, or rounds other values in their place, can miss the bound.
Values may be sent and summed in bfloat16 or wider, within the bound.
No kernel may reach another device: no remote copies, remote signals or barrier semaphores. Data moves between devices by JAX's collectives and lax.ppermute only.
A program may use at most 64 MiB of HBM per device.

```python
import jax
import jax.numpy as jnp
from jax import lax

C = 128
K = 64
FIRST_DILATION = 2
SECOND_DILATION = 8
MB = 2
NB = 96


def with_spikes(drawn, own_key, source, target, blocks, factor):
    def block_of(position):
        return (jnp.arange(drawn.shape[position]) // (drawn.shape[position] // blocks)).reshape((-1,) + (1,) * (drawn.ndim - 1 - position))

    one_side = jax.random.permutation(own_key, blocks)[block_of(target)]
    second = (block_of(target) + blocks // 2) % blocks
    return jnp.where((block_of(source) == one_side) | (block_of(source) == second), factor * drawn, drawn)


def steps_of(own_key, extent, shards, low, high):
    level = 1.0
    for axis_at, shards_of in shards:
        heights = jax.random.uniform(jax.random.fold_in(jax.random.fold_in(own_key, 6), axis_at), (shards_of,), jnp.float32, low / len(shards), high / len(shards))
        level = level * jnp.repeat(jnp.exp(heights), extent[axis_at] // shards_of).reshape((-1,) + (1,) * (len(extent) - 1 - axis_at))
    return level


def centred(rng, shape, width, reach, pieces=(), dtype=jnp.bfloat16):
    factor_of = steps_of(rng, shape, pieces, -0.22, 0.18) if pieces else 1.0
    drawn = jax.random.normal(rng, shape, jnp.float32) * width * factor_of
    return jnp.minimum(jnp.maximum(drawn, -reach), reach).astype(dtype)


def noise_with(stream_key, dims, width, most, shards, heavy, kind=jnp.bfloat16):
    entries = width * jax.random.normal(stream_key, dims, jnp.float32)
    if shards:
        entries = entries * steps_of(stream_key, dims, shards, -0.22, 0.18)
    return jnp.clip(with_spikes(entries, jax.random.fold_in(stream_key, 3), *heavy), -most, most).astype(kind)


def setup_inputs(seed: int = 0) -> dict:
    keys = jax.random.split(jax.random.key(seed), 6)
    activations = centred(keys[0], (MB, NB, NB, C), 1.0, 6.0, ((0, 2), (1, 4), (2, 4)))
    cotangent = noise_with(keys[1], (MB, NB, NB, C), 1.0, 6.0, ((0, 2), (1, 4), (2, 4)), (1, 3, 4, 2.0))
    conv_weight = centred(keys[2], (2, 9, C, K), (9 * C) ** -0.5, 0.1875, ((0, 2),))
    conv_bias = centred(keys[3], (2, K), 0.5, 3.0, ((0, 2),))
    out_weight = centred(keys[4], (2, K, C), K ** -0.5, 0.75, ((0, 2),))
    return {"activations": activations, "cotangent": cotangent, "conv_weight": conv_weight, "conv_bias": conv_bias, "out_weight": out_weight}


def tap_window(padded, dilation, row_offset_tap, col_tap, side):
    row_start = dilation * (1 + row_offset_tap)
    col_start = dilation * (1 + col_tap)
    return padded[row_start:row_start + side, col_start:col_start + side]

def forward_section(inputs, conv, bias, projection, dilation):
    side = inputs.shape[0]
    channels = inputs.shape[2]
    hidden = jnp.maximum(inputs, 0)
    padded = jnp.pad(hidden, ((dilation, dilation), (dilation, dilation), (0, 0)))
    summed = jnp.zeros((side * side, conv.shape[2]), jnp.float32)
    for tap_index in range(9):
        window = tap_window(padded, dilation, tap_index // 3 - 1, tap_index % 3 - 1, side)
        summed = summed + jnp.dot(window.reshape(-1, channels), conv[tap_index], preferred_element_type=jnp.float32)
    pre_act = summed + bias.astype(jnp.float32)
    bottle = jnp.maximum(pre_act, 0.0).astype(jnp.bfloat16)
    branch_sum = (inputs.reshape(-1, channels).astype(jnp.float32) + jnp.dot(bottle, projection, preferred_element_type=jnp.float32)).astype(jnp.bfloat16).reshape(side, side, channels)
    sym = ((branch_sum.astype(jnp.float32) + jnp.swapaxes(branch_sum, 0, 1).astype(jnp.float32)) * 0.5).astype(jnp.bfloat16)
    return (sym, (inputs, padded, pre_act, bottle))

def backward_section(upstream, stored, conv, projection, dilation):
    inputs, padded, pre_act, bottle = stored
    side = inputs.shape[0]
    channels = inputs.shape[2]
    grad_branch = ((upstream.astype(jnp.float32) + jnp.swapaxes(upstream, 0, 1).astype(jnp.float32)) * 0.5).astype(jnp.bfloat16).reshape(-1, channels)
    grad_bottle = lax.dot_general(grad_branch, projection, (((1,), (1,)), ((), ())), preferred_element_type=jnp.float32)
    grad_pre = jnp.where(pre_act > 0, grad_bottle, 0.0).astype(jnp.bfloat16)
    grad_proj = lax.dot_general(bottle, grad_branch, (((0,), (0,)), ((), ())), preferred_element_type=jnp.float32)
    grad_bias = lax.optimization_barrier(jnp.sum(grad_pre.astype(jnp.float32), axis=0))
    conv_terms = []
    for tap_index in range(9):
        window = tap_window(padded, dilation, tap_index // 3 - 1, tap_index % 3 - 1, side)
        conv_terms.append(lax.dot_general(window.reshape(-1, channels), grad_pre, (((0,), (0,)), ((), ())), preferred_element_type=jnp.float32))
    grad_conv = jnp.stack(conv_terms)
    grad_square = grad_pre.reshape(side, side, -1)
    grad_padded = jnp.pad(grad_square, ((dilation, dilation), (dilation, dilation), (0, 0)))
    summed = jnp.zeros((side * side, channels), jnp.float32)
    for tap_index in range(9):
        window = tap_window(grad_padded, dilation, 1 - tap_index // 3, 1 - tap_index % 3, side)
        summed = summed + lax.dot_general(window.reshape(-1, window.shape[2]), conv[tap_index], (((1,), (1,)), ((), ())), preferred_element_type=jnp.float32)
    masked = jnp.where(inputs.reshape(-1, channels) > 0, summed, 0.0)
    grad_inputs = (grad_branch.astype(jnp.float32) + masked).astype(jnp.bfloat16).reshape(side, side, channels)
    return (grad_inputs, (grad_conv, grad_bias, grad_proj))

def reference(activations, cotangent, conv_weight, conv_bias, out_weight):
    dilation_list = (FIRST_DILATION, SECOND_DILATION)
    conv_total = jnp.zeros(conv_weight.shape, jnp.float32)
    bias_total = jnp.zeros(conv_bias.shape, jnp.float32)
    proj_total = jnp.zeros(out_weight.shape, jnp.float32)
    results = []
    for batch_index in range(activations.shape[0]):
        current = activations[batch_index]
        stored_list = []
        for section in range(2):
            current, stored = forward_section(current, conv_weight[section], conv_bias[section], out_weight[section], dilation_list[section])
            stored_list.append(stored)
        upstream = cotangent[batch_index]
        for section in (1, 0):
            upstream, section_grads = backward_section(upstream, stored_list[section], conv_weight[section], out_weight[section], dilation_list[section])
            conv_total = conv_total.at[section].add(section_grads[0])
            bias_total = bias_total.at[section].add(section_grads[1])
            proj_total = proj_total.at[section].add(section_grads[2])
        results.append(upstream)
    factor = 1.0 / jnp.sqrt(jnp.float32(activations.shape[0] * activations.shape[1] * activations.shape[2]))
    return (jnp.stack(results), conv_total * factor, bias_total * factor, proj_total * factor)
```

```python
import jax
import jax.numpy as jnp
from jax import lax
from jax.sharding import PartitionSpec as P

FIRST_DILATION = 2
SECOND_DILATION = 8
HALO = FIRST_DILATION + SECOND_DILATION
GATHER_LIMIT = 16
GRID = ("row", "col")


def mirror_pairs():
    number = lax.axis_size("row")
    return [(r * number + c, c * number + r) for r in range(number) for c in range(number)]


def extended(x, width):
    for axis, dim in (("row", 0), ("col", 1)):
        count, length = (lax.axis_size(axis), x.shape[dim])
        up = [(i, i + 1) for i in range(count - 1)]
        down = [(j, i) for i, j in up]
        last = lax.slice_in_dim(x, length - width, length, axis=dim)
        first = lax.slice_in_dim(x, 0, width, axis=dim)
        before = lax.ppermute(last, axis, up)
        after = lax.ppermute(first, axis, down)
        x = jnp.concatenate([before, x, after], axis=dim)
    return x


def both_regions(tile, width):
    number, side, channels = lax.axis_size("row"), tile.shape[0], tile.shape[2]
    if number * number > GATHER_LIMIT:
        mirrored = jnp.swapaxes(lax.ppermute(tile, GRID, mirror_pairs()), 0, 1)
        return extended(jnp.concatenate([tile, mirrored], axis=2), width)
    tiles = lax.all_gather(tile, GRID)
    whole = tiles.reshape(number, number, side, side, channels).transpose(0, 2, 1, 3, 4)
    whole = whole.reshape(number * side, number * side, channels)
    whole = jnp.pad(whole, ((width, width), (width, width), (0, 0)))
    at_row, at_col = lax.axis_index("row") * side, lax.axis_index("col") * side
    size = (side + 2 * width, side + 2 * width, channels)
    own = lax.dynamic_slice(whole, (at_row, at_col, 0), size)
    other = lax.dynamic_slice(whole, (at_col, at_row, 0), size)
    return jnp.concatenate([own, jnp.swapaxes(other, 0, 1)], axis=2)


def inside(side, width):
    number = lax.axis_size("row") * side
    index = jnp.arange(side + 2 * width) - width
    rows = index + lax.axis_index("row") * side
    cols = index + lax.axis_index("col") * side
    rows = (rows >= 0) & (rows < number)
    cols = (cols >= 0) & (cols < number)
    return (rows[:, None] & cols[None, :])[:, :, None]


def middle(x, width):
    return x[width : x.shape[0] - width, width : x.shape[1] - width]


def window(x, dilation, a, b):
    rows, cols = x.shape[0] - 2 * dilation, x.shape[1] - 2 * dilation
    top, left = dilation * (1 + a), dilation * (1 + b)
    return x[top : top + rows, left : left + cols].reshape(rows * cols, x.shape[2])


TAPS = [(a, b) for a in (-1, 0, 1) for b in (-1, 0, 1)]


def tap(a, b):
    return 3 * (a + 1) + (b + 1)


def dot(x, y, dims=((1,), (0,))):
    return lax.dot_general(x, y, (dims, ((), ())), preferred_element_type=jnp.float32)


def diagonal(x, y):
    return jnp.block([[x, jnp.zeros((x.shape[0], y.shape[1]), x.dtype)], [jnp.zeros((y.shape[0], x.shape[1]), x.dtype), y]])


def half_sum(x, y):
    return ((x.astype(jnp.float32) + y.astype(jnp.float32)) * 0.5).astype(jnp.bfloat16)


def weight_grads(hidden, dilation, grad_pre, bottle, grad_branch):
    rows = [dot(grad_pre, window(hidden, dilation, a, b), ((0,), (0,))) for a, b in TAPS]
    rows.append(dot(bottle, grad_branch, ((0,), (0,))))
    return jnp.concatenate(rows), jnp.sum(grad_pre.astype(jnp.float32), axis=0)


def local(activations, cotangent, conv_weight, conv_bias, out_weight):
    side, channels, inner = activations.shape[1], activations.shape[3], conv_weight.shape[3]
    number = lax.axis_size("row")
    first, second = FIRST_DILATION, SECOND_DILATION

    bias_rows = jnp.pad(conv_bias, ((0, 7), (0, channels - inner)))
    packed = jnp.concatenate(
        [jnp.swapaxes(conv_weight[0], 1, 2).reshape(9 * inner, channels), out_weight[0], bias_rows]
    )
    packed = lax.all_gather(packed, "segment")
    conv = packed[:, : 9 * inner].reshape(2, 9, inner, channels)
    proj = packed[:, 9 * inner : 10 * inner]
    bias = packed[:, 10 * inner, :inner].astype(jnp.float32)

    tile = jnp.concatenate([activations[0], cotangent[0]], axis=2)
    mirrored = jnp.swapaxes(lax.ppermute(tile, GRID, mirror_pairs()), 0, 1)
    grad_branch = half_sum(tile[..., channels:], mirrored[..., channels:])
    stacked = extended(jnp.concatenate([tile[..., :channels], mirrored[..., :channels], grad_branch], axis=2), HALO)
    grad_branch = middle(stacked[..., 2 * channels :], second)
    both = stacked[..., : 2 * channels]

    hidden = jnp.maximum(both, 0)
    span = side + 2 * second
    pre_first = jnp.tile(bias[0], 2)
    for a, b in TAPS:
        weight = diagonal(conv[0, tap(a, b)].T, conv[0, tap(b, a)].T)
        pre_first = pre_first + dot(window(hidden, first, a, b), weight)
    bottle_first = jnp.maximum(pre_first, 0).astype(jnp.bfloat16)
    branch = dot(bottle_first, diagonal(proj[0], proj[0])).reshape(span, span, 2 * channels)
    branch = (middle(both, first).astype(jnp.float32) + branch).astype(jnp.bfloat16)
    current = jnp.where(inside(side, second), half_sum(branch[..., :channels], branch[..., channels:]), 0)
    pre_first = pre_first[:, :inner].reshape(span, span, inner)
    bottle_first = bottle_first[:, :inner].reshape(span, span, inner)

    hidden_second = jnp.maximum(current, 0)
    pre_second = bias[1]
    for a, b in TAPS:
        pre_second = pre_second + dot(window(hidden_second, second, a, b), conv[1, tap(a, b)], ((1,), (1,)))
    bottle_second = jnp.maximum(pre_second, 0).astype(jnp.bfloat16)
    grad_tile = middle(grad_branch, first).reshape(side * side, channels)
    grad_pre = jnp.where(pre_second > 0, dot(grad_tile, proj[1], ((1,), (1,))), 0).astype(jnp.bfloat16)
    around = both_regions(grad_pre.reshape(side, side, inner), HALO)
    second_sums = weight_grads(hidden_second, second, grad_pre, bottle_second, grad_tile)

    near = side + 2 * first
    summed = 0
    for a, b in TAPS:
        weight = diagonal(conv[1, tap(a, b)], conv[1, tap(b, a)])
        summed = summed + dot(window(around, second, -a, -b), weight)
    summed = summed.reshape(near, near, 2 * channels)
    positive = middle(current, second - first) > 0
    up_own, up_other = (
        (grad_branch.astype(jnp.float32) + jnp.where(positive, part, 0)).astype(jnp.bfloat16)
        for part in (summed[..., :channels], summed[..., channels:])
    )
    grad_branch = half_sum(up_own, up_other)

    alive = (middle(pre_first, second - first) > 0) & inside(side, first)
    grad_pre = dot(grad_branch.reshape(near * near, channels), proj[0], ((1,), (1,))).reshape(near, near, inner)
    grad_pre = jnp.where(alive, grad_pre, 0).astype(jnp.bfloat16)
    grad_tile = middle(grad_branch, first).reshape(side * side, channels)
    first_sums = weight_grads(
        middle(hidden[..., :channels], second),
        first,
        middle(grad_pre, first).reshape(side * side, inner),
        middle(bottle_first, second).reshape(side * side, inner),
        grad_tile,
    )

    devices = number * number
    share = -(-10 * inner // (8 * devices)) * 8
    parts = []
    for rows, ends in (first_sums, second_sums):
        rows = jnp.pad(rows, ((0, share * devices - 10 * inner), (0, 0))).reshape(devices, share, channels)
        ends = jnp.pad(ends[None], ((0, 7), (0, channels - inner)))
        parts.append(jnp.concatenate([rows, jnp.broadcast_to(ends, (devices, 8, channels))], axis=1))
    parts = jnp.concatenate(parts).astype(jnp.bfloat16)
    parts = lax.all_to_all(parts, ("segment",) + GRID, 0, 0, tiled=True)

    summed = 0
    for a, b in TAPS:
        summed = summed + dot(window(grad_pre, first, -a, -b), conv[0, tap(a, b)])
    masked = jnp.where(activations[0].reshape(side * side, channels) > 0, summed, 0)
    input_gradient = (grad_tile.astype(jnp.float32) + masked).astype(jnp.bfloat16).reshape(1, side, side, channels)

    cells = lax.axis_size("segment") * (side * number) * (side * number)
    total = jnp.sum(parts.astype(jnp.float32), axis=0) * (1.0 / jnp.sqrt(jnp.float32(cells)))
    rows = lax.all_gather(total[:share], GRID, tiled=True)
    conv_gradient = jnp.swapaxes(rows[: 9 * inner].reshape(1, 9, inner, channels), 2, 3)
    return (input_gradient, conv_gradient, total[share : share + 1, :inner], rows[None, 9 * inner : 10 * inner])


def solution(mesh):
    in_specs = (
        P("segment", "row", "col", None),
        P("segment", "row", "col", None),
        P("segment", None, None, None),
        P("segment", None),
        P("segment", None, None),
    )
    out_specs = (
        P("segment", "row", "col", None),
        P("segment", None, None, None),
        P("segment", None),
        P("segment", None, None),
    )
    return jax.shard_map(local, mesh=mesh, in_specs=in_specs, out_specs=out_specs, check_vma=False)
```

```python
import jax
import jax.numpy as jnp
from jax import lax
from jax.sharding import PartitionSpec as P

FIRST_DILATION = 2
SECOND_DILATION = 8
HALO = FIRST_DILATION + SECOND_DILATION
GRID = ("row", "col")


def mirror_pairs():
    number = lax.axis_size("row")
    return [(r * number + c, c * number + r) for r in range(number) for c in range(number)]


def neighbours(strip_first, strip_last, axis):
    count = lax.axis_size(axis)
    up = [(i, i + 1) for i in range(count - 1)]
    down = [(j, i) for i, j in up]
    return lax.ppermute(strip_last, axis, up), lax.ppermute(strip_first, axis, down)


def extended(x, width):
    length = x.shape[0]
    before, after = neighbours(x[:width], x[length - width :], "row")
    x = jnp.concatenate([before, x, after])
    length = x.shape[1]
    before, after = neighbours(jnp.swapaxes(x[:, :width], 0, 1), jnp.swapaxes(x[:, length - width :], 0, 1), "col")
    return jnp.concatenate([jnp.swapaxes(before, 0, 1), x, jnp.swapaxes(after, 0, 1)], axis=1)


def extended_pair(x, y, width, narrow):
    side, channels = x.shape[0], x.shape[2]
    strips = neighbours(
        jnp.concatenate([x[:width], y[:narrow]]), jnp.concatenate([x[side - width :], y[side - narrow :]]), "row"
    )
    x = jnp.concatenate([strips[0][:width], x, strips[1][:width]])
    y = jnp.concatenate([strips[0][width:], y, strips[1][width:]])
    gap = ((0, 0), (width - narrow, width - narrow), (0, 0))

    def strip(at, to, low, high):
        first = jnp.swapaxes(x[:, at:to], 0, 1)
        second = jnp.swapaxes(y[:, low:high], 0, 1)
        return jnp.concatenate([first, jnp.pad(second, gap)])

    strips = neighbours(strip(0, width, 0, narrow), strip(side - width, side, side - narrow, side), "col")
    before, after = (jnp.swapaxes(part, 0, 1) for part in strips)
    inner = slice(width - narrow, before.shape[0] - width + narrow)
    x = jnp.concatenate([before[:, :width], x, after[:, :width]], axis=1)
    y = jnp.concatenate([before[inner, width:], y, after[inner, width:]], axis=1)
    return x, y


def inside(side, width):
    number = lax.axis_size("row") * side
    index = jnp.arange(side + 2 * width) - width
    rows = index + lax.axis_index("row") * side
    cols = index + lax.axis_index("col") * side
    rows = (rows >= 0) & (rows < number)
    cols = (cols >= 0) & (cols < number)
    return (rows[:, None] & cols[None, :])[:, :, None]


def middle(x, width):
    return x[width : x.shape[0] - width, width : x.shape[1] - width]


def window(x, dilation, a, b):
    rows, cols = x.shape[0] - 2 * dilation, x.shape[1] - 2 * dilation
    top, left = dilation * (1 + a), dilation * (1 + b)
    return x[top : top + rows, left : left + cols].reshape(rows * cols, x.shape[2])


TAPS = [(a, b) for a in (-1, 0, 1) for b in (-1, 0, 1)]


def tap(a, b):
    return 3 * (a + 1) + (b + 1)


def dot(x, y, dims=((1,), (0,))):
    return lax.dot_general(x, y, (dims, ((), ())), preferred_element_type=jnp.float32)


def diagonal(x, y):
    return jnp.block([[x, jnp.zeros((x.shape[0], y.shape[1]), x.dtype)], [jnp.zeros((y.shape[0], x.shape[1]), x.dtype), y]])


def half_sum(x, y):
    return ((x.astype(jnp.float32) + y.astype(jnp.float32)) * 0.5).astype(jnp.bfloat16)


def weight_grads(hidden, dilation, grad_pre, bottle, grad_branch):
    rows = [dot(grad_pre, window(hidden, dilation, a, b), ((0,), (0,))) for a, b in TAPS]
    rows.append(dot(bottle, grad_branch, ((0,), (0,))))
    return jnp.concatenate(rows), jnp.sum(grad_pre.astype(jnp.float32), axis=0)


def local(activations, cotangent, conv_weight, conv_bias, out_weight):
    side, channels, inner = activations.shape[1], activations.shape[3], conv_weight.shape[3]
    number = lax.axis_size("row")
    first, second = FIRST_DILATION, SECOND_DILATION

    bias_rows = jnp.pad(conv_bias, ((0, 7), (0, channels - inner)))
    packed = jnp.concatenate(
        [jnp.swapaxes(conv_weight[0], 1, 2).reshape(9 * inner, channels), out_weight[0], bias_rows]
    )
    packed = lax.all_gather(packed, "segment")
    conv = packed[:, : 9 * inner].reshape(2, 9, inner, channels)
    proj = packed[:, 9 * inner : 10 * inner]
    bias = packed[:, 10 * inner, :inner].astype(jnp.float32)

    tile = activations[0]
    mirrored = jnp.swapaxes(lax.ppermute(tile, GRID, mirror_pairs()), 0, 1)
    stacked = jnp.concatenate([tile, mirrored], axis=2)
    before, after = neighbours(stacked[:HALO], stacked[side - HALO :], "row")
    before, after, late = lax.optimization_barrier((before, after, cotangent[0]))
    stacked = jnp.concatenate([before, stacked, after])
    left, right = neighbours(
        jnp.swapaxes(stacked[:, :HALO], 0, 1), jnp.swapaxes(stacked[:, side - HALO :], 0, 1), "col"
    )
    mirrored = jnp.swapaxes(lax.ppermute(late, GRID, mirror_pairs()), 0, 1)
    grad_branch = half_sum(late, mirrored)
    both = jnp.concatenate([jnp.swapaxes(left, 0, 1), stacked, jnp.swapaxes(right, 0, 1)], axis=1)

    hidden = jnp.maximum(both, 0)
    span = side + 2 * second
    pre_first = jnp.tile(bias[0], 2)
    for a, b in TAPS:
        weight = diagonal(conv[0, tap(a, b)].T, conv[0, tap(b, a)].T)
        pre_first = pre_first + dot(window(hidden, first, a, b), weight)
    bottle_first = jnp.maximum(pre_first, 0).astype(jnp.bfloat16)
    branch = dot(bottle_first, diagonal(proj[0], proj[0])).reshape(span, span, 2 * channels)
    branch = (middle(both, first).astype(jnp.float32) + branch).astype(jnp.bfloat16)
    current = jnp.where(inside(side, second), half_sum(branch[..., :channels], branch[..., channels:]), 0)
    pre_first = pre_first[:, :inner].reshape(span, span, inner)
    bottle_first = bottle_first[:, :inner].reshape(span, span, inner)

    hidden_second = jnp.maximum(current, 0)
    pre_second = bias[1]
    for a, b in TAPS:
        pre_second = pre_second + dot(window(hidden_second, second, a, b), conv[1, tap(a, b)], ((1,), (1,)))
    bottle_second = jnp.maximum(pre_second, 0).astype(jnp.bfloat16)
    grad_tile = grad_branch.reshape(side * side, channels)
    grad_pre = jnp.where(pre_second > 0, dot(grad_tile, proj[1], ((1,), (1,))), 0).astype(jnp.bfloat16)
    square = grad_pre.reshape(side, side, inner)
    half = side // 2
    sent = jnp.concatenate([square[:half], square[half:]], axis=2)
    sent = lax.ppermute(sent, GRID, mirror_pairs())
    mirrored = jnp.concatenate([sent[..., :inner], sent[..., inner:]])
    around = jnp.concatenate([square, jnp.swapaxes(mirrored, 0, 1)], axis=2)
    around, grad_branch = extended_pair(around, grad_branch, HALO, first)
    second_sums = weight_grads(hidden_second, second, grad_pre, bottle_second, grad_tile)

    near = side + 2 * first
    summed = 0
    for a, b in TAPS:
        weight = diagonal(conv[1, tap(a, b)], conv[1, tap(b, a)])
        summed = summed + dot(window(around, second, -a, -b), weight)
    summed = summed.reshape(near, near, 2 * channels)
    positive = middle(current, second - first) > 0
    up_own, up_other = (
        (grad_branch.astype(jnp.float32) + jnp.where(positive, part, 0)).astype(jnp.bfloat16)
        for part in (summed[..., :channels], summed[..., channels:])
    )
    grad_branch = half_sum(up_own, up_other)

    alive = (middle(pre_first, second - first) > 0) & inside(side, first)
    grad_pre = dot(grad_branch.reshape(near * near, channels), proj[0], ((1,), (1,))).reshape(near, near, inner)
    grad_pre = jnp.where(alive, grad_pre, 0).astype(jnp.bfloat16)
    grad_tile = middle(grad_branch, first).reshape(side * side, channels)
    first_sums = weight_grads(
        middle(hidden[..., :channels], second),
        first,
        middle(grad_pre, first).reshape(side * side, inner),
        middle(bottle_first, second).reshape(side * side, inner),
        grad_tile,
    )

    devices = number * number
    share = -(-10 * inner // (8 * devices)) * 8
    parts = []
    for rows, ends in (first_sums, second_sums):
        rows = jnp.pad(rows, ((0, share * devices - 10 * inner), (0, 0))).reshape(devices, share, channels)
        ends = jnp.pad(ends[None], ((0, 7), (0, channels - inner)))
        parts.append(jnp.concatenate([rows, jnp.broadcast_to(ends, (devices, 8, channels))], axis=1))
    parts = jnp.concatenate(parts).astype(jnp.bfloat16)
    parts = lax.all_to_all(parts, ("segment",) + GRID, 0, 0, tiled=True)

    summed = 0
    for a, b in TAPS:
        summed = summed + dot(window(grad_pre, first, -a, -b), conv[0, tap(a, b)])
    masked = jnp.where(activations[0].reshape(side * side, channels) > 0, summed, 0)
    input_gradient = (grad_tile.astype(jnp.float32) + masked).astype(jnp.bfloat16).reshape(1, side, side, channels)

    cells = lax.axis_size("segment") * (side * number) * (side * number)
    total = jnp.sum(parts.astype(jnp.float32), axis=0) * (1.0 / jnp.sqrt(jnp.float32(cells)))
    rows = jnp.broadcast_to(total[None, :share], (devices, share, channels))
    rows = lax.all_to_all(rows, GRID, 0, 0, tiled=True).reshape(devices * share, channels)
    conv_gradient = jnp.swapaxes(rows[: 9 * inner].reshape(1, 9, inner, channels), 2, 3)
    return (input_gradient, conv_gradient, total[share : share + 1, :inner], rows[None, 9 * inner : 10 * inner])


def solution(mesh):
    in_specs = (
        P("segment", "row", "col", None),
        P("segment", "row", "col", None),
        P("segment", None, None, None),
        P("segment", None),
        P("segment", None, None),
    )
    out_specs = (
        P("segment", "row", "col", None),
        P("segment", None, None, None),
        P("segment", None),
        P("segment", None, None),
    )
    return jax.shard_map(local, mesh=mesh, in_specs=in_specs, out_specs=out_specs, check_vma=False)
```

```python
import functools

import jax
import jax.numpy as jnp
from jax import lax
from jax.experimental import pallas as pl
from jax.experimental.pallas import tpu as pltpu
from jax.sharding import PartitionSpec as P

FIRST_DILATION = 2
SECOND_DILATION = 8
HALO = FIRST_DILATION + SECOND_DILATION
GRID = ("row", "col")
TAPS = [(a, b) for a in (-1, 0, 1) for b in (-1, 0, 1)]
LEAD = 16
F32, BF16 = jnp.float32, jnp.bfloat16


def tap(a, b):
    return 3 * (a + 1) + (b + 1)


def dot(x, y):
    return jnp.dot(x, y, preferred_element_type=F32)


def rounded(x):
    return x.astype(BF16).astype(F32)


def up16(n):
    return -(-n // 16) * 16


def send(x, to):
    number = lax.axis_size("row")
    pairs = []
    for r in range(number):
        for c in range(number):
            row, col = to(r, c)
            if 0 <= row < number and 0 <= col < number:
                pairs.append((r * number + c, row * number + col))
    return lax.ppermute(x, GRID, pairs)


def inside(shape, side, width, top):
    number = lax.axis_size("row") * side
    rows = lax.broadcasted_iota(jnp.int32, shape, 0) + top - width
    cols = lax.broadcasted_iota(jnp.int32, shape, 1) - width
    at_row = lax.axis_index("row") * side + rows
    at_col = lax.axis_index("col") * side + cols
    return (at_row >= 0) & (at_row < number) & (at_col >= 0) & (at_col < number) & (cols < side + width)


def forward_kernel(
    tile, mirrored, above, below, above_other, below_other, left, right, w_first, p_first, b_first, w_second, b_second,
    gate_first, bottle_first, near_hidden, gate_second, hidden_second, pre_second,
    area, shifted, pre, current,
):
    side, channels = tile.shape[0], tile.shape[2]
    first, second, inner = FIRST_DILATION, SECOND_DILATION, p_first.shape[0] // 2
    full, span, near = side + 2 * HALO, side + 2 * second, side + 2 * first
    wide, small = pre.shape[1], pre_second.shape[1]
    own, other = slice(0, channels), slice(channels, 2 * channels)
    middle = slice(LEAD, LEAD + side)

    area[:, :LEAD] = jnp.zeros((full, LEAD, 2 * channels), F32)
    area[:, LEAD + side :] = jnp.zeros((full, area.shape[1] - LEAD - side, 2 * channels), F32)
    area[HALO : HALO + side, middle, own] = tile[...].astype(F32)
    area[HALO : HALO + side, middle, other] = jnp.swapaxes(mirrored[...].astype(F32), 0, 1)
    area[:HALO, middle, own] = above[...].astype(F32)
    area[:HALO, middle, other] = above_other[...].astype(F32)
    area[HALO + side :, middle, own] = below[...].astype(F32)
    area[HALO + side :, middle, other] = below_other[...].astype(F32)
    area[:, LEAD - HALO : LEAD] = left[...].astype(F32)
    area[:, LEAD + side : LEAD + side + HALO] = right[...].astype(F32)

    start = LEAD - second

    def shift(step, _):
        rows = pl.ds(step * 4, 4)
        for b in (-1, 0, 1):
            at = start + first * b
            shifted[b + 1, rows] = jnp.maximum(area[rows, at : at + wide], 0).astype(BF16)
        return 0

    lax.fori_loop(0, full // 4, shift, 0)
    for b in (-1, 0, 1):
        at = LEAD + first * b
        part = area[HALO - first : HALO + side + first, at : at + small, own]
        near_hidden[b + 1] = jnp.maximum(part, 0).astype(BF16)

    def first_section(step, _):
        top = step * 8
        size = 8 * wide
        total = jnp.broadcast_to(b_first[...], (size, 2 * inner))
        for a, b in TAPS:
            window = shifted[b + 1, pl.ds(top + first * (1 + a), 8)].reshape(size, 2 * channels)
            total = total + dot(window, w_first[tap(a, b)])
        pre[pl.ds(top, 8)] = total.reshape(8, wide, 2 * inner)
        branch = dot(jnp.maximum(total, 0).astype(BF16), p_first[...])
        middle_part = area[pl.ds(top + first, 8), start : start + wide].reshape(size, 2 * channels)
        branch = rounded(middle_part + branch)
        sym = rounded((branch[:, own] + branch[:, other]) * 0.5).reshape(8, wide, channels)
        current[pl.ds(top, 8)] = jnp.where(inside(sym.shape, side, second, top), sym, 0)
        return 0

    lax.fori_loop(0, span // 8, first_section, 0)

    edge = second - first
    part = pre[edge : edge + near, edge : edge + small]
    alive = (part > 0) & inside(part.shape, side, first, 0)
    gate_first[...] = jnp.where(alive, 1.0, 0.0).astype(BF16)
    part = current[edge : edge + near, edge : edge + small]
    gate_second[...] = jnp.where(part > 0, 1.0, 0.0).astype(BF16)
    bottle_first[...] = jnp.maximum(pre[second : second + side, second : second + small], 0).astype(BF16)
    for b in (-1, 0, 1):
        at = second * (1 + b)
        hidden_second[b + 1] = jnp.maximum(current[:, at : at + small], 0).astype(BF16)

    def second_section(step, _):
        top = step * 8
        total = jnp.broadcast_to(b_second[...], (8 * small, 2 * inner))
        for a, b in TAPS:
            window = hidden_second[b + 1, pl.ds(top + second * (1 + a), 8)].reshape(8 * small, channels)
            total = total + dot(window, w_second[tap(a, b)])
        pre_second[pl.ds(top, 8)] = total.reshape(8, small, 2 * inner)
        return 0

    lax.fori_loop(0, side // 8, second_section, 0)


def turn_kernel(cotangent, mirrored, pre_second, p_second, grad_tile, grad_pre, above, below, padded):
    side, channels = cotangent.shape[0], cotangent.shape[2]
    small, first = pre_second.shape[1], FIRST_DILATION
    branch = (cotangent[...].astype(F32) + jnp.swapaxes(mirrored[...].astype(F32), 0, 1)) * 0.5
    padded[:, side:] = jnp.zeros((side, small - side, channels), F32)
    padded[:, :side] = rounded(branch)
    branch = padded[...].astype(BF16)
    grad_tile[...] = branch
    grad = dot(branch.reshape(side * small, channels), p_second[...]).reshape(side, small, channels)
    grad = jnp.where(pre_second[...] > 0, grad, 0)
    grad_pre[...] = grad.astype(BF16)
    grad, branch = grad[:, :side].astype(BF16), padded[:, :side].astype(BF16)
    above[:HALO], above[HALO:] = grad[:HALO], branch[:first]
    below[:HALO], below[HALO:] = grad[side - HALO :], branch[side - first :]


def weight_sums(rows, ends, grad_pre, hidden, dilation, bottle, grad_tile):
    side, small, lanes = grad_pre.shape
    inner = lanes // 2
    size = side * small
    flat = grad_pre.reshape(size, lanes)
    turned = flat.T[:inner].astype(BF16)
    for a, b in TAPS:
        top = dilation * (1 + a)
        window = hidden[b + 1, top : top + side].reshape(size, lanes)
        at = tap(a, b) * inner
        rows[at : at + inner] = dot(turned, window)
    turned = bottle[...].reshape(size, lanes).astype(F32).T[:inner].astype(BF16)
    rows[9 * inner : 10 * inner] = dot(turned, grad_tile.reshape(size, lanes))
    ends[...] = jnp.broadcast_to(jnp.sum(flat, axis=0, keepdims=True), ends.shape)


def second_sums_kernel(grad_pre, hidden, pre_second, grad_tile, rows, ends):
    bottle = jnp.maximum(pre_second[...], 0).astype(BF16)
    weight_sums(rows, ends, grad_pre[...].astype(F32), hidden, SECOND_DILATION, bottle, grad_tile[...])


def backward_kernel(
    grad_pre, grad_tile, above, below, left, right, left_branch, right_branch, gate_second, gate_first, near_hidden,
    bottle_first, v_second, p_first, rows_second, ends_second,
    parts, windows, grad_first,
    area, shifted, branch, grads, rows, ends,
):
    side, channels = grad_first.shape[0], grad_first.shape[2]
    first, second = FIRST_DILATION, SECOND_DILATION
    full, near = side + 2 * HALO, side + 2 * first
    small = grad_pre.shape[1]
    middle = slice(LEAD, LEAD + side)

    area[:, :LEAD] = jnp.zeros((full, LEAD, channels), F32)
    area[:, LEAD + side :] = jnp.zeros((full, area.shape[1] - LEAD - side, channels), F32)
    area[HALO : HALO + side, LEAD : LEAD + small] = grad_pre[...].astype(F32)
    area[:HALO, middle] = above[:HALO].astype(F32)
    area[HALO + side :, middle] = below[:HALO].astype(F32)
    area[:, LEAD - HALO : LEAD] = left[...].astype(F32)
    area[:, LEAD + side : LEAD + side + HALO] = right[...].astype(F32)
    branch[...] = jnp.zeros(branch.shape, F32)
    branch[first : first + side, first : first + side] = grad_tile[:, :side].astype(F32)
    branch[:first, first : first + side] = above[HALO:].astype(F32)
    branch[first + side :, first : first + side] = below[HALO:].astype(F32)
    branch[:, :first] = left_branch[...].astype(F32)
    branch[:, first + side : near] = right_branch[...].astype(F32)
    for b in (-1, 0, 1):
        at = LEAD - HALO + second * (1 - b)
        shifted[b + 1] = area[:, at : at + small].astype(BF16)
    grads[:, small:] = jnp.zeros((near, grads.shape[1] - small, channels), F32)

    def sections(step, _):
        top = step * 7
        size = 7 * small
        total = jnp.zeros((size, 2 * channels), F32)
        for a, b in TAPS:
            window = shifted[b + 1, pl.ds(top + second * (1 - a), 7)].reshape(size, channels)
            total = total + dot(window, v_second[tap(a, b)])
        here = pl.ds(top, 7)
        grad = branch[here, :small].reshape(size, channels)
        gate = gate_second[here].astype(F32).reshape(size, channels) > 0
        own = rounded(grad + jnp.where(gate, total[:, :channels], 0))
        other = rounded(grad + jnp.where(gate, total[:, channels:], 0))
        grad = ((own + other) * 0.5).astype(BF16)
        branch[here, :small] = grad.astype(F32).reshape(7, small, channels)
        gate = gate_first[here].astype(F32).reshape(size, channels) > 0
        grad = rounded(jnp.where(gate, dot(grad, p_first[...]), 0))
        grads[here, :small] = grad.reshape(7, small, channels)
        return 0

    lax.fori_loop(0, near // 7, sections, 0)
    for b in (-1, 0, 1):
        at = first * (1 - b)
        windows[b + 1] = grads[:, at : at + small].astype(BF16)
    part = branch[first : first + side, first : first + small]
    grad_first[...] = part[:, :side].astype(BF16)
    keep = lax.broadcasted_iota(jnp.int32, part.shape, 1) < side
    part = jnp.where(keep, part, 0).astype(BF16)
    grad = jnp.where(keep, grads[first : first + side, first : first + small], 0)
    weight_sums(rows, ends, grad, near_hidden, first, bottle_first, part)

    devices, share = parts.shape[0] // 2, parts.shape[1] - 8
    count = rows.shape[0]
    for section, (table, end) in enumerate(((rows, ends), (rows_second, ends_second))):
        for j in range(devices):
            at = section * devices + j
            low, high = min(j * share, count), min((j + 1) * share, count)
            pieces = [table[low:high]] if low < high else []
            if high - low < share:
                pieces.append(jnp.zeros((share - (high - low), channels), F32))
            parts[at] = jnp.concatenate(pieces + [end[...]]).astype(BF16)


def input_kernel(windows, grad_first, tile, v_first, out):
    side, channels = tile.shape[0], tile.shape[2]
    small = windows.shape[2]
    first = FIRST_DILATION

    def rows(step, _):
        top = step * 8
        total = jnp.zeros((8 * small, channels), F32)
        for a, b in TAPS:
            window = windows[b + 1, pl.ds(top + first * (1 - a), 8)].reshape(8 * small, channels)
            total = total + dot(window, v_first[tap(a, b)])
        here = pl.ds(top, 8)
        total = total.reshape(8, small, channels)[:, :side]
        total = jnp.where(tile[here].astype(F32) > 0, total, 0)
        out[here] = (grad_first[here].astype(F32) + total).astype(BF16)
        return 0

    lax.fori_loop(0, side // 8, rows, 0)


def total_kernel(scale, parts, rows, ends):
    share = rows.shape[1]
    total = jnp.sum(parts[...].astype(F32), axis=0) * scale
    rows[...] = jnp.broadcast_to(total[:share].astype(BF16)[None], rows.shape)
    ends[...] = total[share:]


def call(kernel, name, outs, scratch, flops, *operands):
    outs = [jax.ShapeDtypeStruct(shape, dtype) for shape, dtype in outs]
    moved = sum(x.size * x.dtype.itemsize for x in list(operands) + outs)
    return pl.pallas_call(
        kernel,
        name=name,
        out_shape=outs,
        scratch_shapes=[pltpu.VMEM(shape, dtype) for shape, dtype in scratch],
        cost_estimate=pl.CostEstimate(flops=flops, bytes_accessed=moved, transcendentals=0),
        compiler_params=pltpu.CompilerParams(vmem_limit_bytes=40 * 1024 * 1024),
    )(*operands)


def beside(x, y, axis):
    if axis is not None:
        return jnp.concatenate([x, y], axis=axis)
    zero = jnp.zeros_like(x)
    return jnp.concatenate([jnp.concatenate([x, zero], axis=-1), jnp.concatenate([zero, y], axis=-1)], axis=-2)


def local(activations, cotangent, conv_weight, conv_bias, out_weight):
    side, channels, inner = activations.shape[1], activations.shape[3], conv_weight.shape[3]
    number = lax.axis_size("row")
    first, second = FIRST_DILATION, SECOND_DILATION
    full, span, near = side + 2 * HALO, side + 2 * second, side + 2 * first
    wide, small = up16(span), up16(near)
    tile = activations[0]

    mirrored = send(tile, lambda r, c: (c, r))
    above = send(tile[side - HALO :], lambda r, c: (r + 1, c))
    below = send(tile[:HALO], lambda r, c: (r - 1, c))
    above_other = send(jnp.swapaxes(tile[:, side - HALO :], 0, 1), lambda r, c: (c + 1, r))
    below_other = send(jnp.swapaxes(tile[:, :HALO], 0, 1), lambda r, c: (c - 1, r))

    bias_rows = jnp.pad(conv_bias, ((0, 7), (0, channels - inner)))
    packed = jnp.concatenate(
        [jnp.swapaxes(conv_weight[0], 1, 2).reshape(9 * inner, channels), out_weight[0], bias_rows]
    )
    packed = lax.all_gather(packed, "segment")
    conv = packed[:, : 9 * inner].reshape(2, 9, inner, channels)
    swapped = jnp.stack([conv[:, tap(b, a)] for a, b in TAPS], axis=1)
    proj = packed[:, 9 * inner : 10 * inner]
    bias = jnp.tile(packed[:, 10 * inner, :inner].astype(F32), (1, 2))[:, None]
    w_first = beside(jnp.swapaxes(conv[0], 1, 2), jnp.swapaxes(swapped[0], 1, 2), None)
    w_second = beside(jnp.swapaxes(conv[1], 1, 2), jnp.swapaxes(swapped[1], 1, 2), 2)
    v_second = beside(conv[1], swapped[1], None)
    v_first = jnp.pad(conv[0], ((0, 0), (0, inner), (0, 0)))
    p_first = beside(proj[0], proj[0], None)
    p_second = beside(proj[1].T, proj[1].T, 1)
    p_back = jnp.pad(proj[0].T, ((0, 0), (0, inner)))

    other = jnp.swapaxes(mirrored, 0, 1)

    def columns(low, high):
        own = jnp.concatenate([above[:, low:high], tile[:, low:high], below[:, low:high]])
        turned = jnp.concatenate([above_other[:, low:high], other[:, low:high], below_other[:, low:high]])
        return jnp.swapaxes(jnp.concatenate([own, turned], axis=2), 0, 1)

    left = send(columns(side - HALO, side), lambda r, c: (r, c + 1))
    right = send(columns(0, HALO), lambda r, c: (r, c - 1))
    left, right, late = lax.optimization_barrier((left, right, cotangent[0]))
    late_mirrored = send(late, lambda r, c: (c, r))

    gate_first, bottle_first, near_hidden, gate_second, hidden_second, pre_second = call(
        forward_kernel,
        "forward",
        [
            ((near, small, channels), BF16),
            ((side, small, channels), BF16),
            ((3, near, small, channels), BF16),
            ((near, small, channels), BF16),
            ((3, span, small, channels), BF16),
            ((side, small, 2 * inner), F32),
        ],
        [
            ((full, LEAD + up16(side + LEAD + second + first), 2 * channels), F32),
            ((3, full, wide, 2 * channels), BF16),
            ((span, wide, 2 * inner), F32),
            ((span, wide, channels), F32),
        ],
        span * wide * 2 * channels * 2 * inner * 20,
        *(tile, mirrored, above, below, above_other, below_other),
        *(jnp.swapaxes(left, 0, 1), jnp.swapaxes(right, 0, 1)),
        *(w_first, p_first, bias[0], w_second, bias[1]),
    )

    grad_tile, grad_pre, strip_above, strip_below = call(
        turn_kernel,
        "turn",
        [
            ((side, small, channels), BF16),
            ((side, small, 2 * inner), BF16),
            ((HALO + first, side, channels), BF16),
            ((HALO + first, side, channels), BF16),
        ],
        [((side, small, channels), F32)],
        2 * side * small * channels * 2 * inner,
        *(late, late_mirrored, pre_second, p_second),
    )

    above = send(strip_below, lambda r, c: (r + 1, c))
    below = send(strip_above, lambda r, c: (r - 1, c))
    rows_second, ends_second = call(
        second_sums_kernel,
        "second_sums",
        [((10 * inner, channels), F32), ((8, channels), F32)],
        [],
        20 * side * small * channels * inner,
        *(grad_pre, hidden_second, pre_second, grad_tile),
    )

    def columns(low, high, low_branch, high_branch):
        grads = jnp.concatenate([above[:HALO, low:high], grad_pre[:, low:high], below[:HALO, low:high]])
        here = slice(low_branch, high_branch)
        branches = jnp.concatenate([above[HALO:, here], grad_tile[:, here], below[HALO:, here]])
        branches = jnp.pad(branches, ((second, second), (0, 0), (0, 0)))
        return jnp.swapaxes(jnp.concatenate([grads, branches], axis=1), 0, 1)

    left = send(columns(side - HALO, side, side - first, side), lambda r, c: (r, c + 1))
    right = send(columns(0, HALO, 0, first), lambda r, c: (r, c - 1))
    left, right = jnp.swapaxes(left, 0, 1), jnp.swapaxes(right, 0, 1)

    devices = number * number
    share = -(-10 * inner // (8 * devices)) * 8
    parts, windows, grad_first = call(
        backward_kernel,
        "backward",
        [
            ((2 * devices, share + 8, channels), BF16),
            ((3, near, small, channels), BF16),
            ((side, side, channels), BF16),
        ],
        [
            ((full, LEAD + up16(side + HALO + first), channels), F32),
            ((3, full, small, channels), BF16),
            ((near, small + 16, channels), F32),
            ((near, small + 16, channels), F32),
            ((10 * inner, channels), F32),
            ((8, channels), F32),
        ],
        36 * near * small * channels * channels,
        *(grad_pre, grad_tile, above, below, left[:, :HALO], right[:, :HALO]),
        *(left[second : second + near, HALO:], right[second : second + near, HALO:]),
        *(gate_second, gate_first, near_hidden, bottle_first, v_second, p_back, rows_second, ends_second),
    )

    parts = lax.all_to_all(parts, ("segment",) + GRID, 0, 0, tiled=True)
    (input_gradient,) = call(
        input_kernel,
        "input",
        [((side, side, channels), BF16)],
        [],
        18 * side * small * channels * channels,
        *(windows, grad_first, tile, v_first),
    )
    cells = lax.axis_size("segment") * (side * number) * (side * number)
    rows, ends = call(
        functools.partial(total_kernel, float(cells) ** -0.5),
        "total",
        [((devices, share, channels), BF16), ((8, channels), F32)],
        [],
        parts.size,
        parts,
    )
    rows = lax.all_to_all(rows, GRID, 0, 0, tiled=True).reshape(devices * share, channels).astype(F32)
    conv_gradient = jnp.swapaxes(rows[: 9 * inner].reshape(1, 9, inner, channels), 2, 3)
    return (input_gradient[None], conv_gradient, ends[:1, :inner], rows[None, 9 * inner : 10 * inner])


def solution(mesh):
    in_specs = (
        P("segment", "row", "col", None),
        P("segment", "row", "col", None),
        P("segment", None, None, None),
        P("segment", None),
        P("segment", None, None),
    )
    out_specs = (
        P("segment", "row", "col", None),
        P("segment", None, None, None),
        P("segment", None),
        P("segment", None, None),
    )
    return jax.shard_map(local, mesh=mesh, in_specs=in_specs, out_specs=out_specs, check_vma=False)
```

```python
import functools

import jax
import jax.numpy as jnp
from jax import lax
from jax.experimental import pallas as pl
from jax.experimental.pallas import tpu as pltpu
from jax.sharding import PartitionSpec as P

FIRST_DILATION = 2
SECOND_DILATION = 8
HALO = FIRST_DILATION + SECOND_DILATION
GRID = ("row", "col")
TAPS = [(a, b) for a in (-1, 0, 1) for b in (-1, 0, 1)]
LEAD = 16
F32, BF16 = jnp.float32, jnp.bfloat16


ORDER = [0, 1, 3, 4, 6, 7, 2, 5, 8]


def dot(x, y):
    return jnp.dot(x, y, preferred_element_type=F32)


def rounded(x):
    return x.astype(BF16).astype(F32)


def up16(n):
    return -(-n // 16) * 16


def send(x, to):
    number = lax.axis_size("row")
    pairs = []
    for r in range(number):
        for c in range(number):
            row, col = to(r, c)
            if 0 <= row < number and 0 <= col < number:
                pairs.append((r * number + c, row * number + col))
    return lax.ppermute(x, GRID, pairs)


def inside(shape, side, width, top):
    number = lax.axis_size("row") * side
    rows = lax.broadcasted_iota(jnp.int32, shape, 0) + top - width
    cols = lax.broadcasted_iota(jnp.int32, shape, 1) - width
    at_row = lax.axis_index("row") * side + rows
    at_col = lax.axis_index("col") * side + cols
    return (at_row >= 0) & (at_row < number) & (at_col >= 0) & (at_col < number) & (cols < side + width)


def paired(source, starts, width, dilation, pairs, last, change):
    lanes = source.shape[2]
    low, high = slice(0, lanes), slice(lanes, 2 * lanes)

    def step(k, _):
        rows, lower = pl.ds(4 * k, 4), pl.ds(4 * k + dilation, 4)
        window = [change(source[rows, at : at + width]).astype(BF16) for at in starts]
        pairs[rows, :, low] = window[0]
        pairs[rows, :, high] = window[1]
        last[lower, :, low] = window[2]
        last[rows, :, high] = window[2]
        return 0

    lax.fori_loop(0, source.shape[0] // 4, step, 0)


def taps_sum(pairs, last, top, rows, dilation, weights):
    width, lanes = pairs.shape[1], pairs.shape[2] // 2
    size = rows * width
    total = None
    for k in range(5):
        if k < 3:
            window = pairs[pl.ds(top + dilation * k, rows)]
        elif k == 3:
            window = last[pl.ds(top + dilation, rows)]
        else:
            window = last[pl.ds(top + 3 * dilation, rows), :, :lanes]
        weight = weights[2 * lanes * k : min(2 * lanes * (k + 1), 9 * lanes)]
        term = dot(window.reshape(size, window.shape[2]), weight)
        total = term if total is None else total + term
    return total


def positive(x):
    return jnp.maximum(x, 0)


def assemble(area, tile, above, below, left, right):
    side = tile.shape[0]
    full, wide, channels = area.shape
    middle = slice(LEAD, LEAD + side)
    area[:, :LEAD] = jnp.zeros((full, LEAD, channels), F32)
    area[:, LEAD + side :] = jnp.zeros((full, wide - LEAD - side, channels), F32)
    area[HALO : HALO + side, middle] = tile
    area[:HALO, middle] = above[:HALO].astype(F32)
    area[HALO + side :, middle] = below[:HALO].astype(F32)
    area[:, LEAD - HALO : LEAD] = left[...].astype(F32)
    area[:, LEAD + side : LEAD + side + HALO] = right[...].astype(F32)


def first_branch(area, pairs, last, weights, bias, proj, store):
    full, wide = pairs.shape[:2]
    start = LEAD - SECOND_DILATION
    starts = [start + FIRST_DILATION * b for b in (-1, 0, 1)]
    paired(area, starts, wide, FIRST_DILATION, pairs, last, positive)

    def rows(step, _):
        top = step * 8
        pre = taps_sum(pairs, last, top, 8, FIRST_DILATION, weights) + bias[...]
        branch = dot(positive(pre).astype(BF16), proj[...])
        inputs = area[pl.ds(top + FIRST_DILATION, 8), start : start + wide]
        branch = rounded(inputs + branch.reshape(inputs.shape))
        store(top, pre.reshape(8, wide, pre.shape[1]), branch)
        return 0

    lax.fori_loop(0, (full - 2 * FIRST_DILATION) // 8, rows, 0)


def own_kernel(
    tile, above, below, left, right, weights, bias, proj,
    branch_own, gate_first, bottle_first, near_hidden,
    area, pairs, last, pre,
):
    side, first, second = tile.shape[0], FIRST_DILATION, SECOND_DILATION
    near, small = gate_first.shape[:2]
    assemble(area, tile[...].astype(F32), above, below, left, right)

    def store(top, pre_act, branch):
        pre[pl.ds(top, 8)] = pre_act
        branch_own[pl.ds(top, 8)] = branch

    first_branch(area, pairs, last, weights, bias, proj, store)
    for b in (-1, 0, 1):
        at = LEAD + first * b
        near_hidden[b + 1] = positive(area[HALO - first : HALO + side + first, at : at + small]).astype(BF16)
    edge = second - first
    part = pre[edge : edge + near, edge : edge + small]
    alive = (part > 0) & inside(part.shape, side, first, 0)
    gate_first[...] = jnp.where(alive, 1.0, 0.0).astype(BF16)
    bottle_first[...] = positive(pre[second : second + side, second : second + small]).astype(BF16)


def other_kernel(
    tile, above, below, left, right, weights, bias, proj, branch_own, w_second, b_second,
    gate_second, hidden_pairs, hidden_last, pre_second,
    area, pairs, last, current,
):
    side, first, second = tile.shape[0], FIRST_DILATION, SECOND_DILATION
    near, small = gate_second.shape[:2]
    assemble(area, tile[...].astype(F32), above, below, left, right)

    def store(top, pre_act, branch):
        here = pl.ds(top, 8)
        sym = rounded((branch_own[here] + branch) * 0.5)
        current[here] = jnp.where(inside(sym.shape, side, second, top), sym, 0)

    first_branch(area, pairs, last, weights, bias, proj, store)
    edge = second - first
    part = current[edge : edge + near, edge : edge + small]
    gate_second[...] = jnp.where(part > 0, 1.0, 0.0).astype(BF16)
    paired(current, [0, second, 2 * second], small, second, hidden_pairs, hidden_last, positive)

    def rows(step, _):
        top = step * 8
        total = taps_sum(hidden_pairs, hidden_last, top, 8, second, w_second) + b_second[...]
        pre_second[pl.ds(top, 8)] = total.reshape(8, small, total.shape[1])
        return 0

    lax.fori_loop(0, side // 8, rows, 0)


def turn_kernel(cotangent, mirrored, pre_second, p_second, grad_tile, grad_pre, above, below, padded):
    side, channels = cotangent.shape[0], cotangent.shape[2]
    small, first = pre_second.shape[1], FIRST_DILATION
    branch = (cotangent[...].astype(F32) + jnp.swapaxes(mirrored[...].astype(F32), 0, 1)) * 0.5
    padded[:, side:] = jnp.zeros((side, small - side, channels), F32)
    padded[:, :side] = rounded(branch)
    branch = padded[...].astype(BF16)
    grad_tile[...] = branch
    grad = dot(branch.reshape(side * small, channels), p_second[...]).reshape(side, small, channels)
    grad = jnp.where(pre_second[...] > 0, grad, 0)
    grad_pre[...] = grad.astype(BF16)
    grad, branch = grad[:, :side].astype(BF16), padded[:, :side].astype(BF16)
    above[:HALO], above[HALO:] = grad[:HALO], branch[:first]
    below[:HALO], below[HALO:] = grad[side - HALO :], branch[side - first :]


def weight_sums(rows, ends, grad_pre, hidden, bottle, grad_tile):
    side, small, lanes = grad_pre.shape
    inner = bottle.shape[2]
    size = side * small
    flat = grad_pre.reshape(size, lanes)
    turned = flat.T[:inner].astype(BF16)
    for a in range(3):
        b = 0
        while b < 3:
            window = hidden(a, b)
            grads = dot(turned, window.reshape(size, window.shape[2]))
            for at in range(0, window.shape[2], grad_tile.shape[2]):
                rows[(3 * a + b) * inner : (3 * a + b + 1) * inner] = grads[:, at : at + grad_tile.shape[2]]
                b += 1
    turned = bottle[...].reshape(size, inner).astype(F32).T.astype(BF16)
    rows[9 * inner : 10 * inner] = dot(turned, grad_tile.reshape(size, grad_tile.shape[2]))
    ends[...] = jnp.zeros(ends.shape, F32)
    ends[:, :lanes] = jnp.broadcast_to(jnp.sum(flat, axis=0, keepdims=True), (ends.shape[0], lanes))


def second_sums_kernel(grad_pre, pairs, last, pre_second, grad_tile, rows, ends):
    side, inner = grad_pre.shape[0], grad_pre.shape[2] // 2
    channels = grad_tile.shape[2]

    def hidden(a, b):
        top = SECOND_DILATION * a
        if b == 0:
            return pairs[top : top + side]
        return last[top + SECOND_DILATION : top + SECOND_DILATION + side, :, :channels]

    bottle = positive(pre_second[:, :, :inner]).astype(BF16)
    weight_sums(rows, ends, grad_pre[...].astype(F32), hidden, bottle, grad_tile[...])


def backward_kernel(
    grad_pre, grad_tile, above, below, left, right, left_branch, right_branch, gate_second, gate_first, near_hidden,
    bottle_first, v_second, p_first, rows_second, ends_second,
    parts, windows, windows_last, grad_first,
    area, pairs, last, branch, grads, rows, ends,
):
    side, channels, inner = grad_first.shape[0], grad_first.shape[2], bottle_first.shape[2]
    first, second = FIRST_DILATION, SECOND_DILATION
    near, small = gate_first.shape[:2]
    assemble(area, grad_pre[:, :side].astype(F32), above, below, left, right)
    branch[...] = jnp.zeros(branch.shape, F32)
    branch[first : first + side, first : first + side] = grad_tile[:, :side].astype(F32)
    branch[:first, first : first + side] = above[HALO:].astype(F32)
    branch[first + side :, first : first + side] = below[HALO:].astype(F32)
    branch[:, :first] = left_branch[...].astype(F32)
    branch[:, first + side : near] = right_branch[...].astype(F32)
    starts = [LEAD - HALO + second * (1 + b) for b in (-1, 0, 1)]
    paired(area, starts, small, second, pairs, last, lambda x: x)
    grads[:, small:] = jnp.zeros((near, grads.shape[1] - small, inner), F32)

    def sections(step, _):
        top = step * 7
        size = 7 * small
        total = taps_sum(pairs, last, top, 7, second, v_second)
        here = pl.ds(top, 7)
        grad = branch[here, :small].reshape(size, channels)
        gate = gate_second[here].astype(F32).reshape(size, channels) > 0
        own = rounded(grad + jnp.where(gate, total[:, :channels], 0))
        other = rounded(grad + jnp.where(gate, total[:, channels:], 0))
        grad = ((own + other) * 0.5).astype(BF16)
        branch[here, :small] = grad.astype(F32).reshape(7, small, channels)
        gate = gate_first[here].astype(F32).reshape(size, inner) > 0
        grad = rounded(jnp.where(gate, dot(grad, p_first[...]), 0))
        grads[here, :small] = grad.reshape(7, small, inner)
        return 0

    lax.fori_loop(0, near // 7, sections, 0)
    paired(grads, [0, first, 2 * first], small, first, windows, windows_last, lambda x: x)
    part = branch[first : first + side, first : first + small]
    grad_first[...] = part[:, :side].astype(BF16)
    def kept(x):
        return jnp.where(lax.broadcasted_iota(jnp.int32, x.shape, 1) < side, x, 0)

    part = kept(part).astype(BF16)
    grad = kept(grads[first : first + side, first : first + small])

    def hidden(a, b):
        return near_hidden[b, first * a : first * a + side]

    weight_sums(rows, ends, grad, hidden, bottle_first, part)

    devices, share = parts.shape[0] // 2, parts.shape[1] - 8
    count = rows.shape[0]
    for section, (table, end) in enumerate(((rows, ends), (rows_second, ends_second))):
        for j in range(devices):
            at = section * devices + j
            low, high = min(j * share, count), min((j + 1) * share, count)
            pieces = [table[low:high]] if low < high else []
            if high - low < share:
                pieces.append(jnp.zeros((share - (high - low), channels), F32))
            parts[at] = jnp.concatenate(pieces + [end[...]]).astype(BF16)


def input_kernel(windows, windows_last, grad_first, tile, v_first, out):
    side, channels = tile.shape[0], tile.shape[2]
    small = windows.shape[1]

    def rows(step, _):
        top = step * 8
        total = taps_sum(windows, windows_last, top, 8, FIRST_DILATION, v_first)
        here = pl.ds(top, 8)
        total = total.reshape(8, small, channels)[:, :side]
        total = jnp.where(tile[here].astype(F32) > 0, total, 0)
        out[here] = (grad_first[here].astype(F32) + total).astype(BF16)
        return 0

    lax.fori_loop(0, side // 8, rows, 0)


def total_kernel(scale, parts, rows, ends):
    share = rows.shape[1]
    total = jnp.sum(parts[...].astype(F32), axis=0) * scale
    rows[...] = jnp.broadcast_to(total[:share].astype(BF16)[None], rows.shape)
    ends[...] = total[share:]


def call(kernel, name, outs, scratch, flops, *operands):
    outs = [jax.ShapeDtypeStruct(shape, dtype) for shape, dtype in outs]
    moved = sum(x.size * x.dtype.itemsize for x in list(operands) + outs)
    return pl.pallas_call(
        kernel,
        name=name,
        out_shape=outs,
        scratch_shapes=[pltpu.VMEM(shape, dtype) for shape, dtype in scratch],
        cost_estimate=pl.CostEstimate(flops=flops, bytes_accessed=moved, transcendentals=0),
        compiler_params=pltpu.CompilerParams(vmem_limit_bytes=40 * 1024 * 1024),
    )(*operands)


def diagonal(x, y):
    zero = jnp.zeros_like(x)
    return jnp.concatenate([jnp.concatenate([x, zero], axis=-1), jnp.concatenate([zero, y], axis=-1)], axis=-2)


def local(activations, cotangent, conv_weight, conv_bias, out_weight):
    side, channels, inner = activations.shape[1], activations.shape[3], conv_weight.shape[3]
    number = lax.axis_size("row")
    first, second = FIRST_DILATION, SECOND_DILATION
    full, span, near = side + 2 * HALO, side + 2 * second, side + 2 * first
    wide, small = up16(span), up16(near)
    tile = activations[0]

    def row_strips(x):
        return send(x[side - HALO :], lambda r, c: (r + 1, c)), send(x[:HALO], lambda r, c: (r - 1, c))

    def column_strips(x, above, below):
        whole = jnp.concatenate([above, x, below])
        left = send(jnp.swapaxes(whole[:, side - HALO :], 0, 1), lambda r, c: (r, c + 1))
        right = send(jnp.swapaxes(whole[:, :HALO], 0, 1), lambda r, c: (r, c - 1))
        return jnp.swapaxes(left, 0, 1), jnp.swapaxes(right, 0, 1)

    mirrored = send(tile, lambda r, c: (c, r))
    above, below = row_strips(tile)
    left, right = column_strips(tile, above, below)
    own = (tile, above, below, left, right)
    other = jnp.swapaxes(mirrored, 0, 1)
    above, below = row_strips(other)
    left, right = column_strips(other, above, below)
    other = (other, above, below, left, right)

    bias_rows = jnp.pad(conv_bias, ((0, 7), (0, channels - inner)))
    packed = jnp.concatenate(
        [jnp.swapaxes(conv_weight[0], 1, 2).reshape(9 * inner, channels), out_weight[0], bias_rows]
    )
    packed = lax.all_gather(packed, "segment")
    conv = packed[:, : 9 * inner].reshape(2, 9, inner, channels)
    swapped = conv.reshape(2, 3, 3, inner, channels).swapaxes(1, 2).reshape(conv.shape)
    proj = packed[:, 9 * inner : 10 * inner]
    bias = packed[:, 10 * inner, :inner].astype(F32)[:, None]

    def ordered(x):
        return jnp.concatenate([x[k] for k in ORDER])

    w_own = ordered(jnp.swapaxes(conv[0], 1, 2))
    w_other = ordered(jnp.swapaxes(swapped[0], 1, 2))
    w_second = ordered(jnp.swapaxes(jnp.concatenate([conv[1], swapped[1]], axis=1), 1, 2))
    v_second = ordered(diagonal(conv[1, ::-1], swapped[1, ::-1]))
    v_first = ordered(conv[0, ::-1])
    p_second = jnp.concatenate([proj[1].T, proj[1].T], axis=1)
    p_back = proj[0].T

    late, _ = lax.optimization_barrier((cotangent[0], own[3]))
    late_mirrored = send(late, lambda r, c: (c, r))

    area = ((full, LEAD + up16(side + LEAD), channels), F32)
    pairs = ((full, wide, 2 * channels), BF16)
    last = ((full + first, wide, 2 * channels), BF16)
    branch_own, gate_first, bottle_first, near_hidden = call(
        own_kernel,
        "own_branch",
        [
            ((span, wide, channels), F32),
            ((near, small, inner), BF16),
            ((side, small, inner), BF16),
            ((3, near, small, channels), BF16),
        ],
        [area, pairs, last, ((span, wide, inner), F32)],
        span * wide * channels * inner * 20,
        *own,
        *(w_own, bias[0], proj[0]),
    )
    gate_second, hidden_pairs, hidden_last, pre_second = call(
        other_kernel,
        "other_branch",
        [
            ((near, small, channels), BF16),
            ((span, small, 2 * channels), BF16),
            ((span + second, small, 2 * channels), BF16),
            ((side, small, 2 * inner), F32),
        ],
        [area, pairs, last, ((span, wide, channels), F32)],
        span * wide * channels * inner * 30,
        *other,
        *(w_other, bias[0], proj[0], branch_own, w_second, jnp.tile(bias[1], (1, 2))),
    )

    grad_tile, grad_pre, strip_above, strip_below = call(
        turn_kernel,
        "turn",
        [
            ((side, small, channels), BF16),
            ((side, small, 2 * inner), BF16),
            ((HALO + first, side, channels), BF16),
            ((HALO + first, side, channels), BF16),
        ],
        [((side, small, channels), F32)],
        2 * side * small * channels * 2 * inner,
        *(late, late_mirrored, pre_second, p_second),
    )

    above = send(strip_below, lambda r, c: (r + 1, c))
    below = send(strip_above, lambda r, c: (r - 1, c))
    rows_second, ends_second = call(
        second_sums_kernel,
        "second_sums",
        [((10 * inner, channels), F32), ((8, channels), F32)],
        [],
        20 * side * small * channels * inner,
        *(grad_pre, hidden_pairs, hidden_last, pre_second, grad_tile),
    )

    def columns(low, high, low_branch, high_branch):
        grads = jnp.concatenate([above[:HALO, low:high], grad_pre[:, low:high], below[:HALO, low:high]])
        here = slice(low_branch, high_branch)
        branches = jnp.concatenate([above[HALO:, here], grad_tile[:, here], below[HALO:, here]])
        branches = jnp.pad(branches, ((second, second), (0, 0), (0, 0)))
        return jnp.swapaxes(jnp.concatenate([grads, branches], axis=1), 0, 1)

    left = send(columns(side - HALO, side, side - first, side), lambda r, c: (r, c + 1))
    right = send(columns(0, HALO, 0, first), lambda r, c: (r, c - 1))
    left, right = jnp.swapaxes(left, 0, 1), jnp.swapaxes(right, 0, 1)

    devices = number * number
    share = -(-10 * inner // (8 * devices)) * 8
    parts, windows, windows_last, grad_first = call(
        backward_kernel,
        "backward",
        [
            ((2 * devices, share + 8, channels), BF16),
            ((near, small, 2 * inner), BF16),
            ((near + first, small, 2 * inner), BF16),
            ((side, side, channels), BF16),
        ],
        [
            area,
            ((full, small, 2 * channels), BF16),
            ((full + second, small, 2 * channels), BF16),
            ((near, small + 16, channels), F32),
            ((near, small + 16, inner), F32),
            ((10 * inner, channels), F32),
            ((8, channels), F32),
        ],
        36 * near * small * channels * channels,
        *(grad_pre, grad_tile, above, below, left[:, :HALO], right[:, :HALO]),
        *(left[second : second + near, HALO:], right[second : second + near, HALO:]),
        *(gate_second, gate_first, near_hidden, bottle_first, v_second, p_back, rows_second, ends_second),
    )

    parts = lax.all_to_all(parts, ("segment",) + GRID, 0, 0, tiled=True)
    (input_gradient,) = call(
        input_kernel,
        "input",
        [((side, side, channels), BF16)],
        [],
        18 * side * small * channels * channels,
        *(windows, windows_last, grad_first, tile, v_first),
    )
    cells = lax.axis_size("segment") * (side * number) * (side * number)
    rows, ends = call(
        functools.partial(total_kernel, float(cells) ** -0.5),
        "total",
        [((devices, share, channels), BF16), ((8, channels), F32)],
        [],
        parts.size,
        parts,
    )
    rows = lax.all_to_all(rows, GRID, 0, 0, tiled=True).reshape(devices * share, channels).astype(F32)
    conv_gradient = jnp.swapaxes(rows[: 9 * inner].reshape(1, 9, inner, channels), 2, 3)
    return (input_gradient[None], conv_gradient, ends[:1, :inner], rows[None, 9 * inner : 10 * inner])


def solution(mesh):
    in_specs = (
        P("segment", "row", "col", None),
        P("segment", "row", "col", None),
        P("segment", None, None, None),
        P("segment", None),
        P("segment", None, None),
    )
    out_specs = (
        P("segment", "row", "col", None),
        P("segment", None, None, None),
        P("segment", None),
        P("segment", None, None),
    )
    return jax.shard_map(local, mesh=mesh, in_specs=in_specs, out_specs=out_specs, check_vma=False)
```

```python
import functools

import jax
import jax.numpy as jnp
from jax import lax
from jax.experimental import pallas as pl
from jax.experimental.pallas import tpu as pltpu
from jax.sharding import PartitionSpec as P

FIRST_DILATION = 2
SECOND_DILATION = 8
HALO = FIRST_DILATION + SECOND_DILATION
GRID = ("row", "col")
TAPS = [(a, b) for a in (-1, 0, 1) for b in (-1, 0, 1)]
LEAD = 16
F32, BF16 = jnp.float32, jnp.bfloat16


def tap(a, b):
    return 3 * (a + 1) + (b + 1)


def dot(x, y):
    return jnp.dot(x, y, preferred_element_type=F32)


def rounded(x):
    return x.astype(BF16).astype(F32)


def up16(n):
    return -(-n // 16) * 16


def send(x, to):
    number = lax.axis_size("row")
    pairs = []
    for r in range(number):
        for c in range(number):
            row, col = to(r, c)
            if 0 <= row < number and 0 <= col < number:
                pairs.append((r * number + c, row * number + col))
    return lax.ppermute(x, GRID, pairs)


def inside(shape, side, width, top):
    number = lax.axis_size("row") * side
    rows = lax.broadcasted_iota(jnp.int32, shape, 0) + top - width
    cols = lax.broadcasted_iota(jnp.int32, shape, 1) - width
    at_row = lax.axis_index("row") * side + rows
    at_col = lax.axis_index("col") * side + cols
    return (at_row >= 0) & (at_row < number) & (at_col >= 0) & (at_col < number) & (cols < side + width)


def forward_kernel(
    stacked, above, below, left, right, w_first, p_first, b_first, w_second, b_second,
    gate_first, bottle_first, near_hidden, gate_second, hidden_second, pre_second,
    area, shifted, pre, current,
):
    side, channels = stacked.shape[0], stacked.shape[2] // 2
    first, second, inner = FIRST_DILATION, SECOND_DILATION, p_first.shape[0] // 2
    full, span, near = side + 2 * HALO, side + 2 * second, side + 2 * first
    wide, small = pre.shape[1], pre_second.shape[1]
    own, other = slice(0, channels), slice(channels, 2 * channels)
    middle = slice(LEAD, LEAD + side)

    area[:, :LEAD] = jnp.zeros((full, LEAD, 2 * channels), F32)
    area[:, LEAD + side :] = jnp.zeros((full, area.shape[1] - LEAD - side, 2 * channels), F32)
    area[HALO : HALO + side, middle] = stacked[...].astype(F32)
    area[:HALO, middle] = above[...].astype(F32)
    area[HALO + side :, middle] = below[...].astype(F32)
    area[:, LEAD - HALO : LEAD] = left[...].astype(F32)
    area[:, LEAD + side : LEAD + side + HALO] = right[...].astype(F32)

    start = LEAD - second

    def shift(step, _):
        rows = pl.ds(step * 4, 4)
        for b in (-1, 0, 1):
            at = start + first * b
            shifted[b + 1, rows] = jnp.maximum(area[rows, at : at + wide], 0).astype(BF16)
        return 0

    lax.fori_loop(0, full // 4, shift, 0)
    for b in (-1, 0, 1):
        at = LEAD + first * b
        part = area[HALO - first : HALO + side + first, at : at + small, own]
        near_hidden[b + 1] = jnp.maximum(part, 0).astype(BF16)

    def first_section(step, _):
        top = step * 8
        size = 8 * wide
        total = jnp.broadcast_to(b_first[...], (size, 2 * inner))
        for a, b in TAPS:
            window = shifted[b + 1, pl.ds(top + first * (1 + a), 8)].reshape(size, 2 * channels)
            total = total + dot(window, w_first[tap(a, b)])
        pre[pl.ds(top, 8)] = total.reshape(8, wide, 2 * inner)
        branch = dot(jnp.maximum(total, 0).astype(BF16), p_first[...])
        middle_part = area[pl.ds(top + first, 8), start : start + wide].reshape(size, 2 * channels)
        branch = rounded(middle_part + branch)
        sym = rounded((branch[:, own] + branch[:, other]) * 0.5).reshape(8, wide, channels)
        current[pl.ds(top, 8)] = jnp.where(inside(sym.shape, side, second, top), sym, 0)
        return 0

    lax.fori_loop(0, span // 8, first_section, 0)

    edge = second - first
    part = pre[edge : edge + near, edge : edge + small]
    alive = (part > 0) & inside(part.shape, side, first, 0)
    gate_first[...] = jnp.where(alive, 1.0, 0.0).astype(BF16)
    part = current[edge : edge + near, edge : edge + small]
    gate_second[...] = jnp.where(part > 0, 1.0, 0.0).astype(BF16)
    bottle_first[...] = jnp.maximum(pre[second : second + side, second : second + small], 0).astype(BF16)
    for b in (-1, 0, 1):
        at = second * (1 + b)
        hidden_second[b + 1] = jnp.maximum(current[:, at : at + small], 0).astype(BF16)

    def second_section(step, _):
        top = step * 8
        total = jnp.broadcast_to(b_second[...], (8 * small, 2 * inner))
        for a, b in TAPS:
            window = hidden_second[b + 1, pl.ds(top + second * (1 + a), 8)].reshape(8 * small, channels)
            total = total + dot(window, w_second[tap(a, b)])
        pre_second[pl.ds(top, 8)] = total.reshape(8, small, 2 * inner)
        return 0

    lax.fori_loop(0, side // 8, second_section, 0)


def turn_kernel(cotangent, mirrored, pre_second, p_second, grad_tile, grad_pre, above, below, padded):
    side, channels = cotangent.shape[0], cotangent.shape[2]
    small, first = pre_second.shape[1], FIRST_DILATION
    branch = (cotangent[...].astype(F32) + jnp.swapaxes(mirrored[...].astype(F32), 0, 1)) * 0.5
    padded[:, side:] = jnp.zeros((side, small - side, channels), F32)
    padded[:, :side] = rounded(branch)
    branch = padded[...].astype(BF16)
    grad_tile[...] = branch
    grad = dot(branch.reshape(side * small, channels), p_second[...]).reshape(side, small, channels)
    grad = jnp.where(pre_second[...] > 0, grad, 0)
    grad_pre[...] = grad.astype(BF16)
    grad, branch = grad[:, :side].astype(BF16), padded[:, :side].astype(BF16)
    above[:HALO], above[HALO:] = grad[:HALO], branch[:first]
    below[:HALO], below[HALO:] = grad[side - HALO :], branch[side - first :]


def weight_sums(rows, ends, grad_pre, hidden, dilation, bottle, grad_tile):
    side, small, lanes = grad_pre.shape
    inner = lanes // 2
    size = side * small
    flat = grad_pre.reshape(size, lanes)
    turned = flat.T[:inner].astype(BF16)
    for a, b in TAPS:
        top = dilation * (1 + a)
        window = hidden[b + 1, top : top + side].reshape(size, lanes)
        at = tap(a, b) * inner
        rows[at : at + inner] = dot(turned, window)
    turned = bottle[...].reshape(size, lanes).astype(F32).T[:inner].astype(BF16)
    rows[9 * inner : 10 * inner] = dot(turned, grad_tile.reshape(size, lanes))
    ends[...] = jnp.broadcast_to(jnp.sum(flat, axis=0, keepdims=True), ends.shape)


def second_sums_kernel(grad_pre, hidden, pre_second, grad_tile, rows, ends):
    bottle = jnp.maximum(pre_second[...], 0).astype(BF16)
    weight_sums(rows, ends, grad_pre[...].astype(F32), hidden, SECOND_DILATION, bottle, grad_tile[...])


def backward_kernel(
    grad_pre, grad_tile, above, below, left, right, left_branch, right_branch, gate_second, gate_first, near_hidden,
    bottle_first, v_second, p_first, rows_second, ends_second,
    parts, windows, grad_first,
    area, shifted, branch, grads, rows, ends,
):
    side, channels = grad_first.shape[0], grad_first.shape[2]
    first, second = FIRST_DILATION, SECOND_DILATION
    full, near = side + 2 * HALO, side + 2 * first
    small = grad_pre.shape[1]
    middle = slice(LEAD, LEAD + side)

    area[:, :LEAD] = jnp.zeros((full, LEAD, channels), F32)
    area[:, LEAD + side :] = jnp.zeros((full, area.shape[1] - LEAD - side, channels), F32)
    area[HALO : HALO + side, LEAD : LEAD + small] = grad_pre[...].astype(F32)
    area[:HALO, middle] = above[:HALO].astype(F32)
    area[HALO + side :, middle] = below[:HALO].astype(F32)
    area[:, LEAD - HALO : LEAD] = left[...].astype(F32)
    area[:, LEAD + side : LEAD + side + HALO] = right[...].astype(F32)
    branch[...] = jnp.zeros(branch.shape, F32)
    branch[first : first + side, first : first + side] = grad_tile[:, :side].astype(F32)
    branch[:first, first : first + side] = above[HALO:].astype(F32)
    branch[first + side :, first : first + side] = below[HALO:].astype(F32)
    branch[:, :first] = left_branch[...].astype(F32)
    branch[:, first + side : near] = right_branch[...].astype(F32)
    for b in (-1, 0, 1):
        at = LEAD - HALO + second * (1 - b)
        shifted[b + 1] = area[:, at : at + small].astype(BF16)
    grads[:, small:] = jnp.zeros((near, grads.shape[1] - small, channels), F32)

    def sections(step, _):
        top = step * 7
        size = 7 * small
        total = jnp.zeros((size, 2 * channels), F32)
        for a, b in TAPS:
            window = shifted[b + 1, pl.ds(top + second * (1 - a), 7)].reshape(size, channels)
            total = total + dot(window, v_second[tap(a, b)])
        here = pl.ds(top, 7)
        grad = branch[here, :small].reshape(size, channels)
        gate = gate_second[here].astype(F32).reshape(size, channels) > 0
        own = rounded(grad + jnp.where(gate, total[:, :channels], 0))
        other = rounded(grad + jnp.where(gate, total[:, channels:], 0))
        grad = ((own + other) * 0.5).astype(BF16)
        branch[here, :small] = grad.astype(F32).reshape(7, small, channels)
        gate = gate_first[here].astype(F32).reshape(size, channels) > 0
        grad = rounded(jnp.where(gate, dot(grad, p_first[...]), 0))
        grads[here, :small] = grad.reshape(7, small, channels)
        return 0

    lax.fori_loop(0, near // 7, sections, 0)
    for b in (-1, 0, 1):
        at = first * (1 - b)
        windows[b + 1] = grads[:, at : at + small].astype(BF16)
    part = branch[first : first + side, first : first + small]
    grad_first[...] = part[:, :side].astype(BF16)
    keep = lax.broadcasted_iota(jnp.int32, part.shape, 1) < side
    part = jnp.where(keep, part, 0).astype(BF16)
    grad = jnp.where(keep, grads[first : first + side, first : first + small], 0)
    weight_sums(rows, ends, grad, near_hidden, first, bottle_first, part)

    devices, share = parts.shape[0] // 2, parts.shape[1] - 8
    count = rows.shape[0]
    for section, (table, end) in enumerate(((rows, ends), (rows_second, ends_second))):
        for j in range(devices):
            at = section * devices + j
            low, high = min(j * share, count), min((j + 1) * share, count)
            pieces = [table[low:high]] if low < high else []
            if high - low < share:
                pieces.append(jnp.zeros((share - (high - low), channels), F32))
            parts[at] = jnp.concatenate(pieces + [end[...]]).astype(BF16)


def input_kernel(windows, grad_first, tile, v_first, out):
    side, channels = tile.shape[0], tile.shape[2]
    small = windows.shape[2]
    first = FIRST_DILATION

    def rows(step, _):
        top = step * 8
        total = jnp.zeros((8 * small, channels), F32)
        for a, b in TAPS:
            window = windows[b + 1, pl.ds(top + first * (1 - a), 8)].reshape(8 * small, channels)
            total = total + dot(window, v_first[tap(a, b)])
        here = pl.ds(top, 8)
        total = total.reshape(8, small, channels)[:, :side]
        total = jnp.where(tile[here].astype(F32) > 0, total, 0)
        out[here] = (grad_first[here].astype(F32) + total).astype(BF16)
        return 0

    lax.fori_loop(0, side // 8, rows, 0)


def total_kernel(scale, parts, rows, ends):
    share = rows.shape[1]
    total = jnp.sum(parts[...].astype(F32), axis=0) * scale
    rows[...] = jnp.broadcast_to(total[:share].astype(BF16)[None], rows.shape)
    ends[...] = total[share:]


def outputs_kernel(rows, ends, conv_gradient, bias_gradient, out_gradient):
    count, inner = conv_gradient.shape[0], out_gradient.shape[0]
    conv_gradient[...] = rows[:count].astype(F32)
    out_gradient[...] = rows[count : count + inner].astype(F32)
    bias_gradient[...] = ends[:1, :inner]


def call(kernel, name, outs, scratch, flops, *operands):
    outs = [jax.ShapeDtypeStruct(shape, dtype) for shape, dtype in outs]
    moved = sum(x.size * x.dtype.itemsize for x in list(operands) + outs)
    return pl.pallas_call(
        kernel,
        name=name,
        out_shape=outs,
        scratch_shapes=[pltpu.VMEM(shape, dtype) for shape, dtype in scratch],
        cost_estimate=pl.CostEstimate(flops=flops, bytes_accessed=moved, transcendentals=0),
        compiler_params=pltpu.CompilerParams(vmem_limit_bytes=40 * 1024 * 1024),
    )(*operands)


def beside(x, y, axis):
    if axis is not None:
        return jnp.concatenate([x, y], axis=axis)
    zero = jnp.zeros_like(x)
    return jnp.concatenate([jnp.concatenate([x, zero], axis=-1), jnp.concatenate([zero, y], axis=-1)], axis=-2)


def local(activations, cotangent, conv_weight, conv_bias, out_weight):
    side, channels, inner = activations.shape[1], activations.shape[3], conv_weight.shape[3]
    number = lax.axis_size("row")
    first, second = FIRST_DILATION, SECOND_DILATION
    full, span, near = side + 2 * HALO, side + 2 * second, side + 2 * first
    wide, small = up16(span), up16(near)
    tile = activations[0]

    mirrored = send(tile, lambda r, c: (c, r))
    stacked = jnp.concatenate([tile, jnp.swapaxes(mirrored, 0, 1)], axis=2)
    above = send(stacked[side - HALO :], lambda r, c: (r + 1, c))
    below = send(stacked[:HALO], lambda r, c: (r - 1, c))

    def columns(low, high):
        strip = jnp.concatenate([above[:, low:high], stacked[:, low:high], below[:, low:high]])
        return jnp.swapaxes(strip, 0, 1)

    left = send(columns(side - HALO, side), lambda r, c: (r, c + 1))
    right = send(columns(0, HALO), lambda r, c: (r, c - 1))
    left, late = lax.optimization_barrier((left, cotangent[0]))
    late_mirrored = send(late, lambda r, c: (c, r))

    bias_rows = jnp.pad(conv_bias, ((0, 7), (0, channels - inner)))
    packed = jnp.concatenate(
        [jnp.swapaxes(conv_weight[0], 1, 2).reshape(9 * inner, channels), out_weight[0], bias_rows]
    )
    packed = lax.all_gather(packed, "segment")
    conv = packed[:, : 9 * inner].reshape(2, 9, inner, channels)
    swapped = jnp.stack([conv[:, tap(b, a)] for a, b in TAPS], axis=1)
    proj = packed[:, 9 * inner : 10 * inner]
    bias = jnp.tile(packed[:, 10 * inner, :inner].astype(F32), (1, 2))[:, None]
    w_first = beside(jnp.swapaxes(conv[0], 1, 2), jnp.swapaxes(swapped[0], 1, 2), None)
    w_second = beside(jnp.swapaxes(conv[1], 1, 2), jnp.swapaxes(swapped[1], 1, 2), 2)
    v_second = beside(conv[1], swapped[1], None)
    v_first = jnp.pad(conv[0], ((0, 0), (0, inner), (0, 0)))
    p_first = beside(proj[0], proj[0], None)
    p_second = beside(proj[1].T, proj[1].T, 1)
    p_back = jnp.pad(proj[0].T, ((0, 0), (0, inner)))

    gate_first, bottle_first, near_hidden, gate_second, hidden_second, pre_second = call(
        forward_kernel,
        "forward",
        [
            ((near, small, channels), BF16),
            ((side, small, channels), BF16),
            ((3, near, small, channels), BF16),
            ((near, small, channels), BF16),
            ((3, span, small, channels), BF16),
            ((side, small, 2 * inner), F32),
        ],
        [
            ((full, LEAD + up16(side + LEAD), 2 * channels), F32),
            ((3, full, wide, 2 * channels), BF16),
            ((span, wide, 2 * inner), F32),
            ((span, wide, channels), F32),
        ],
        span * wide * 2 * channels * 2 * inner * 20,
        *(stacked, above, below),
        *(jnp.swapaxes(left, 0, 1), jnp.swapaxes(right, 0, 1)),
        *(w_first, p_first, bias[0], w_second, bias[1]),
    )

    grad_tile, grad_pre, strip_above, strip_below = call(
        turn_kernel,
        "turn",
        [
            ((side, small, channels), BF16),
            ((side, small, 2 * inner), BF16),
            ((HALO + first, side, channels), BF16),
            ((HALO + first, side, channels), BF16),
        ],
        [((side, small, channels), F32)],
        2 * side * small * channels * 2 * inner,
        *(late, late_mirrored, pre_second, p_second),
    )

    above = send(strip_below, lambda r, c: (r + 1, c))
    below = send(strip_above, lambda r, c: (r - 1, c))
    rows_second, ends_second = call(
        second_sums_kernel,
        "second_sums",
        [((10 * inner, channels), F32), ((8, channels), F32)],
        [],
        20 * side * small * channels * inner,
        *(grad_pre, hidden_second, pre_second, grad_tile),
    )

    def columns(low, high, low_branch, high_branch):
        grads = jnp.concatenate([above[:HALO, low:high], grad_pre[:, low:high], below[:HALO, low:high]])
        here = slice(low_branch, high_branch)
        branches = jnp.concatenate([above[HALO:, here], grad_tile[:, here], below[HALO:, here]])
        branches = jnp.pad(branches, ((second, second), (0, 0), (0, 0)))
        return jnp.swapaxes(jnp.concatenate([grads, branches], axis=1), 0, 1)

    left = send(columns(side - HALO, side, side - first, side), lambda r, c: (r, c + 1))
    right = send(columns(0, HALO, 0, first), lambda r, c: (r, c - 1))
    left, right = jnp.swapaxes(left, 0, 1), jnp.swapaxes(right, 0, 1)

    devices = number * number
    share = -(-10 * inner // (8 * devices)) * 8
    parts, windows, grad_first = call(
        backward_kernel,
        "backward",
        [
            ((2 * devices, share + 8, channels), BF16),
            ((3, near, small, channels), BF16),
            ((side, side, channels), BF16),
        ],
        [
            ((full, LEAD + up16(side + HALO + first), channels), F32),
            ((3, full, small, channels), BF16),
            ((near, small + 16, channels), F32),
            ((near, small + 16, channels), F32),
            ((10 * inner, channels), F32),
            ((8, channels), F32),
        ],
        36 * near * small * channels * channels,
        *(grad_pre, grad_tile, above, below, left[:, :HALO], right[:, :HALO]),
        *(left[second : second + near, HALO:], right[second : second + near, HALO:]),
        *(gate_second, gate_first, near_hidden, bottle_first, v_second, p_back, rows_second, ends_second),
    )

    parts = lax.all_to_all(parts, ("segment",) + GRID, 0, 0, tiled=True)
    (input_gradient,) = call(
        input_kernel,
        "input",
        [((side, side, channels), BF16)],
        [],
        18 * side * small * channels * channels,
        *(windows, grad_first, tile, v_first),
    )
    cells = lax.axis_size("segment") * (side * number) * (side * number)
    rows, ends = call(
        functools.partial(total_kernel, float(cells) ** -0.5),
        "total",
        [((devices, share, channels), BF16), ((8, channels), F32)],
        [],
        parts.size,
        parts,
    )
    rows = lax.all_to_all(rows, GRID, 0, 0, tiled=True).reshape(devices * share, channels)
    conv_gradient, bias_gradient, out_gradient = call(
        outputs_kernel,
        "outputs",
        [((9 * inner, channels), F32), ((1, inner), F32), ((inner, channels), F32)],
        [],
        rows.size,
        *(rows, ends),
    )
    conv_gradient = jnp.swapaxes(conv_gradient.reshape(1, 9, inner, channels), 2, 3)
    return (input_gradient[None], conv_gradient, bias_gradient, out_gradient[None])


def solution(mesh):
    in_specs = (
        P("segment", "row", "col", None),
        P("segment", "row", "col", None),
        P("segment", None, None, None),
        P("segment", None),
        P("segment", None, None),
    )
    out_specs = (
        P("segment", "row", "col", None),
        P("segment", None, None, None),
        P("segment", None),
        P("segment", None, None),
    )
    return jax.shard_map(local, mesh=mesh, in_specs=in_specs, out_specs=out_specs, check_vma=False)
```

```python
import functools

import jax
import jax.numpy as jnp
from jax import lax
from jax.experimental import pallas as pl
from jax.experimental.pallas import tpu as pltpu
from jax.sharding import PartitionSpec as P

FIRST_DILATION = 2
SECOND_DILATION = 8
HALO = FIRST_DILATION + SECOND_DILATION
GRID = ("row", "col")
TAPS = [(a, b) for a in (-1, 0, 1) for b in (-1, 0, 1)]
LEAD = 16
F32, BF16 = jnp.float32, jnp.bfloat16


def tap(a, b):
    return 3 * (a + 1) + (b + 1)


def dot(x, y):
    return jnp.dot(x, y, preferred_element_type=F32)


def rounded(x):
    return x.astype(BF16).astype(F32)


def up16(n):
    return -(-n // 16) * 16


def send(x, to):
    number = lax.axis_size("row")
    pairs = []
    for r in range(number):
        for c in range(number):
            row, col = to(r, c)
            if 0 <= row < number and 0 <= col < number:
                pairs.append((r * number + c, row * number + col))
    return lax.ppermute(x, GRID, pairs)


def inside(shape, side, width, top):
    number = lax.axis_size("row") * side
    rows = lax.broadcasted_iota(jnp.int32, shape, 0) + top - width
    cols = lax.broadcasted_iota(jnp.int32, shape, 1) - width
    at_row = lax.axis_index("row") * side + rows
    at_col = lax.axis_index("col") * side + cols
    return (at_row >= 0) & (at_row < number) & (at_col >= 0) & (at_col < number) & (cols < side + width)


def forward_kernel(
    stacked, above, below, left, right, w_first, p_first, b_first, w_second, b_second,
    gate_first, bottle_first, near_hidden, gate_second, hidden_second, pre_second,
    area, shifted, pre, current,
):
    side, channels = stacked.shape[0], stacked.shape[2] // 2
    first, second, inner = FIRST_DILATION, SECOND_DILATION, p_first.shape[0] // 2
    full, span, near = side + 2 * HALO, side + 2 * second, side + 2 * first
    wide, small = pre.shape[1], pre_second.shape[1]
    own, other = slice(0, channels), slice(channels, 2 * channels)
    middle = slice(LEAD, LEAD + side)

    area[:, :LEAD] = jnp.zeros((full, LEAD, 2 * channels), F32)
    area[:, LEAD + side :] = jnp.zeros((full, area.shape[1] - LEAD - side, 2 * channels), F32)
    area[HALO : HALO + side, middle] = stacked[...].astype(F32)
    area[:HALO, middle] = above[...].astype(F32)
    area[HALO + side :, middle] = below[...].astype(F32)
    area[:, LEAD - HALO : LEAD] = left[...].astype(F32)
    area[:, LEAD + side : LEAD + side + HALO] = right[...].astype(F32)

    start = LEAD - second

    def shift(step, _):
        rows = pl.ds(step * 4, 4)
        for b in (-1, 0, 1):
            at = start + first * b
            shifted[b + 1, rows] = jnp.maximum(area[rows, at : at + wide], 0).astype(BF16)
        return 0

    lax.fori_loop(0, full // 4, shift, 0)
    for b in (-1, 0, 1):
        at = LEAD + first * b
        part = area[HALO - first : HALO + side + first, at : at + small, own]
        near_hidden[b + 1] = jnp.maximum(part, 0).astype(BF16)

    def first_section(step, _):
        top = step * 8
        size = 8 * wide
        total = jnp.broadcast_to(b_first[...], (size, 2 * inner))
        for a, b in TAPS:
            window = shifted[b + 1, pl.ds(top + first * (1 + a), 8)].reshape(size, 2 * channels)
            total = total + dot(window, w_first[tap(a, b)])
        pre[pl.ds(top, 8)] = total.reshape(8, wide, 2 * inner)
        branch = dot(jnp.maximum(total, 0).astype(BF16), p_first[...])
        middle_part = area[pl.ds(top + first, 8), start : start + wide].reshape(size, 2 * channels)
        branch = rounded(middle_part + branch)
        sym = rounded((branch[:, own] + branch[:, other]) * 0.5).reshape(8, wide, channels)
        current[pl.ds(top, 8)] = jnp.where(inside(sym.shape, side, second, top), sym, 0)
        return 0

    lax.fori_loop(0, span // 8, first_section, 0)

    edge = second - first
    part = pre[edge : edge + near, edge : edge + small]
    alive = (part > 0) & inside(part.shape, side, first, 0)
    gate_first[...] = jnp.where(alive, 1.0, 0.0).astype(BF16)
    part = current[edge : edge + near, edge : edge + small]
    gate_second[...] = jnp.where(part > 0, 1.0, 0.0).astype(BF16)
    bottle_first[...] = jnp.maximum(pre[second : second + side, second : second + small], 0).astype(BF16)
    for b in (-1, 0, 1):
        at = second * (1 + b)
        hidden_second[b + 1] = jnp.maximum(current[:, at : at + small], 0).astype(BF16)

    def second_section(step, _):
        top = step * 8
        total = jnp.broadcast_to(b_second[...], (8 * small, 2 * inner))
        for a, b in TAPS:
            window = hidden_second[b + 1, pl.ds(top + second * (1 + a), 8)].reshape(8 * small, channels)
            total = total + dot(window, w_second[tap(a, b)])
        pre_second[pl.ds(top, 8)] = total.reshape(8, small, 2 * inner)
        return 0

    lax.fori_loop(0, side // 8, second_section, 0)


def turn_kernel(cotangent, mirrored, pre_second, p_second, grad_tile, grad_pre, above, below, padded):
    side, channels = cotangent.shape[0], cotangent.shape[2]
    small, first = pre_second.shape[1], FIRST_DILATION
    branch = (cotangent[...].astype(F32) + jnp.swapaxes(mirrored[...].astype(F32), 0, 1)) * 0.5
    padded[:, side:] = jnp.zeros((side, small - side, channels), F32)
    padded[:, :side] = rounded(branch)
    branch = padded[...].astype(BF16)
    grad_tile[...] = branch
    grad = dot(branch.reshape(side * small, channels), p_second[...]).reshape(side, small, channels)
    grad = jnp.where(pre_second[...] > 0, grad, 0)
    grad_pre[...] = grad.astype(BF16)
    grad, branch = grad[:, :side].astype(BF16), padded[:, :side].astype(BF16)
    above[:HALO], above[HALO:] = grad[:HALO], branch[:first]
    below[:HALO], below[HALO:] = grad[side - HALO :], branch[side - first :]


def weight_sums(rows, ends, grad_pre, hidden, dilation, bottle, grad_tile):
    side, small, lanes = grad_pre.shape
    inner = lanes // 2
    size = side * small
    flat = grad_pre.reshape(size, lanes)
    turned = flat.T[:inner].astype(BF16)
    for a, b in TAPS:
        top = dilation * (1 + a)
        window = hidden[b + 1, top : top + side].reshape(size, lanes)
        at = tap(a, b) * inner
        rows[at : at + inner] = dot(turned, window)
    turned = bottle[...].reshape(size, lanes).astype(F32).T[:inner].astype(BF16)
    rows[9 * inner : 10 * inner] = dot(turned, grad_tile.reshape(size, lanes))
    ends[...] = jnp.broadcast_to(jnp.sum(flat, axis=0, keepdims=True), ends.shape)


def second_sums_kernel(grad_pre, hidden, pre_second, grad_tile, rows, ends):
    bottle = jnp.maximum(pre_second[...], 0).astype(BF16)
    weight_sums(rows, ends, grad_pre[...].astype(F32), hidden, SECOND_DILATION, bottle, grad_tile[...])


def backward_kernel(
    grad_pre, grad_tile, above, below, left, right, left_branch, right_branch, gate_second, gate_first, near_hidden,
    bottle_first, v_second, p_first, rows_second, ends_second,
    parts, windows, grad_first,
    area, shifted, branch, grads, rows, ends,
):
    side, channels = grad_first.shape[0], grad_first.shape[2]
    first, second = FIRST_DILATION, SECOND_DILATION
    full, near = side + 2 * HALO, side + 2 * first
    small = grad_pre.shape[1]
    middle = slice(LEAD, LEAD + side)

    area[:, :LEAD] = jnp.zeros((full, LEAD, channels), F32)
    area[:, LEAD + side :] = jnp.zeros((full, area.shape[1] - LEAD - side, channels), F32)
    area[HALO : HALO + side, LEAD : LEAD + small] = grad_pre[...].astype(F32)
    area[:HALO, middle] = above[:HALO].astype(F32)
    area[HALO + side :, middle] = below[:HALO].astype(F32)
    area[:, LEAD - HALO : LEAD] = left[...].astype(F32)
    area[:, LEAD + side : LEAD + side + HALO] = right[...].astype(F32)
    branch[...] = jnp.zeros(branch.shape, F32)
    branch[first : first + side, first : first + side] = grad_tile[:, :side].astype(F32)
    branch[:first, first : first + side] = above[HALO:].astype(F32)
    branch[first + side :, first : first + side] = below[HALO:].astype(F32)
    branch[:, :first] = left_branch[...].astype(F32)
    branch[:, first + side : near] = right_branch[...].astype(F32)
    for b in (-1, 0, 1):
        at = LEAD - HALO + second * (1 - b)
        shifted[b + 1] = area[:, at : at + small].astype(BF16)
    grads[:, small:] = jnp.zeros((near, grads.shape[1] - small, channels), F32)

    def sections(step, _):
        top = step * 7
        size = 7 * small
        total = jnp.zeros((size, 2 * channels), F32)
        for a, b in TAPS:
            window = shifted[b + 1, pl.ds(top + second * (1 - a), 7)].reshape(size, channels)
            total = total + dot(window, v_second[tap(a, b)])
        here = pl.ds(top, 7)
        grad = branch[here, :small].reshape(size, channels)
        gate = gate_second[here].astype(F32).reshape(size, channels) > 0
        own = rounded(grad + jnp.where(gate, total[:, :channels], 0))
        other = rounded(grad + jnp.where(gate, total[:, channels:], 0))
        grad = ((own + other) * 0.5).astype(BF16)
        branch[here, :small] = grad.astype(F32).reshape(7, small, channels)
        gate = gate_first[here].astype(F32).reshape(size, channels) > 0
        grad = rounded(jnp.where(gate, dot(grad, p_first[...]), 0))
        grads[here, :small] = grad.reshape(7, small, channels)
        return 0

    lax.fori_loop(0, near // 7, sections, 0)
    for b in (-1, 0, 1):
        at = first * (1 - b)
        windows[b + 1] = grads[:, at : at + small].astype(BF16)
    part = branch[first : first + side, first : first + small]
    grad_first[...] = part[:, :side].astype(BF16)
    keep = lax.broadcasted_iota(jnp.int32, part.shape, 1) < side
    part = jnp.where(keep, part, 0).astype(BF16)
    grad = jnp.where(keep, grads[first : first + side, first : first + small], 0)
    weight_sums(rows, ends, grad, near_hidden, first, bottle_first, part)

    devices, share = parts.shape[0] // 2, parts.shape[1] - 8
    count = rows.shape[0]
    for section, (table, end) in enumerate(((rows, ends), (rows_second, ends_second))):
        for j in range(devices):
            at = section * devices + j
            low, high = min(j * share, count), min((j + 1) * share, count)
            pieces = [table[low:high]] if low < high else []
            if high - low < share:
                pieces.append(jnp.zeros((share - (high - low), channels), F32))
            parts[at] = jnp.concatenate(pieces + [end[...]]).astype(BF16)


def input_kernel(windows, grad_first, tile, v_first, out):
    side, channels = tile.shape[0], tile.shape[2]
    small = windows.shape[2]
    first = FIRST_DILATION

    def rows(step, _):
        top = step * 8
        total = jnp.zeros((8 * small, channels), F32)
        for a, b in TAPS:
            window = windows[b + 1, pl.ds(top + first * (1 - a), 8)].reshape(8 * small, channels)
            total = total + dot(window, v_first[tap(a, b)])
        here = pl.ds(top, 8)
        total = total.reshape(8, small, channels)[:, :side]
        total = jnp.where(tile[here].astype(F32) > 0, total, 0)
        out[here] = (grad_first[here].astype(F32) + total).astype(BF16)
        return 0

    lax.fori_loop(0, side // 8, rows, 0)


def total_kernel(scale, parts, rows, ends):
    share = rows.shape[1]
    total = jnp.sum(parts[...].astype(F32), axis=0) * scale
    rows[...] = jnp.broadcast_to(total[:share].astype(BF16)[None], rows.shape)
    ends[...] = total[share:]


def outputs_kernel(rows, ends, conv_gradient, bias_gradient, out_gradient):
    count, inner = conv_gradient.shape[0], out_gradient.shape[0]
    conv_gradient[...] = rows[:count].astype(F32)
    out_gradient[...] = rows[count : count + inner].astype(F32)
    bias_gradient[...] = ends[:1, :inner]


def call(kernel, name, outs, scratch, flops, *operands):
    outs = [jax.ShapeDtypeStruct(shape, dtype) for shape, dtype in outs]
    moved = sum(x.size * x.dtype.itemsize for x in list(operands) + outs)
    return pl.pallas_call(
        kernel,
        name=name,
        out_shape=outs,
        scratch_shapes=[pltpu.VMEM(shape, dtype) for shape, dtype in scratch],
        cost_estimate=pl.CostEstimate(flops=flops, bytes_accessed=moved, transcendentals=0),
        compiler_params=pltpu.CompilerParams(vmem_limit_bytes=40 * 1024 * 1024),
    )(*operands)


def beside(x, y, axis):
    if axis is not None:
        return jnp.concatenate([x, y], axis=axis)
    zero = jnp.zeros_like(x)
    return jnp.concatenate([jnp.concatenate([x, zero], axis=-1), jnp.concatenate([zero, y], axis=-1)], axis=-2)


def local(activations, cotangent, conv_weight, conv_bias, out_weight):
    side, channels, inner = activations.shape[1], activations.shape[3], conv_weight.shape[3]
    number = lax.axis_size("row")
    first, second = FIRST_DILATION, SECOND_DILATION
    full, span, near = side + 2 * HALO, side + 2 * second, side + 2 * first
    wide, small = up16(span), up16(near)
    tile = activations[0]

    def row_strips(x):
        return send(x[side - HALO :], lambda r, c: (r + 1, c)), send(x[:HALO], lambda r, c: (r - 1, c))

    mirrored = send(tile, lambda r, c: (c, r))
    above, below = row_strips(tile)
    other = jnp.swapaxes(mirrored, 0, 1)
    above_other, below_other = row_strips(other)
    above_other, late = lax.optimization_barrier((above_other, cotangent[0]))
    late_mirrored = send(late, lambda r, c: (c, r))
    stacked = jnp.concatenate([tile, other], axis=2)
    above = jnp.concatenate([above, above_other], axis=2)
    below = jnp.concatenate([below, below_other], axis=2)

    def columns(low, high):
        strip = jnp.concatenate([above[:, low:high], stacked[:, low:high], below[:, low:high]])
        return jnp.swapaxes(strip, 0, 1)

    left = send(columns(side - HALO, side), lambda r, c: (r, c + 1))
    right = send(columns(0, HALO), lambda r, c: (r, c - 1))

    bias_rows = jnp.pad(conv_bias, ((0, 7), (0, channels - inner)))
    packed = jnp.concatenate(
        [jnp.swapaxes(conv_weight[0], 1, 2).reshape(9 * inner, channels), out_weight[0], bias_rows]
    )
    packed = lax.all_gather(packed, "segment")
    conv = packed[:, : 9 * inner].reshape(2, 9, inner, channels)
    swapped = jnp.stack([conv[:, tap(b, a)] for a, b in TAPS], axis=1)
    proj = packed[:, 9 * inner : 10 * inner]
    bias = jnp.tile(packed[:, 10 * inner, :inner].astype(F32), (1, 2))[:, None]
    w_first = beside(jnp.swapaxes(conv[0], 1, 2), jnp.swapaxes(swapped[0], 1, 2), None)
    w_second = beside(jnp.swapaxes(conv[1], 1, 2), jnp.swapaxes(swapped[1], 1, 2), 2)
    v_second = beside(conv[1], swapped[1], None)
    v_first = jnp.pad(conv[0], ((0, 0), (0, inner), (0, 0)))
    p_first = beside(proj[0], proj[0], None)
    p_second = beside(proj[1].T, proj[1].T, 1)
    p_back = jnp.pad(proj[0].T, ((0, 0), (0, inner)))

    gate_first, bottle_first, near_hidden, gate_second, hidden_second, pre_second = call(
        forward_kernel,
        "forward",
        [
            ((near, small, channels), BF16),
            ((side, small, channels), BF16),
            ((3, near, small, channels), BF16),
            ((near, small, channels), BF16),
            ((3, span, small, channels), BF16),
            ((side, small, 2 * inner), F32),
        ],
        [
            ((full, LEAD + up16(side + LEAD), 2 * channels), F32),
            ((3, full, wide, 2 * channels), BF16),
            ((span, wide, 2 * inner), F32),
            ((span, wide, channels), F32),
        ],
        span * wide * 2 * channels * 2 * inner * 20,
        *(stacked, above, below),
        *(jnp.swapaxes(left, 0, 1), jnp.swapaxes(right, 0, 1)),
        *(w_first, p_first, bias[0], w_second, bias[1]),
    )

    grad_tile, grad_pre, strip_above, strip_below = call(
        turn_kernel,
        "turn",
        [
            ((side, small, channels), BF16),
            ((side, small, 2 * inner), BF16),
            ((HALO + first, side, channels), BF16),
            ((HALO + first, side, channels), BF16),
        ],
        [((side, small, channels), F32)],
        2 * side * small * channels * 2 * inner,
        *(late, late_mirrored, pre_second, p_second),
    )

    above = send(strip_below, lambda r, c: (r + 1, c))
    below = send(strip_above, lambda r, c: (r - 1, c))
    rows_second, ends_second = call(
        second_sums_kernel,
        "second_sums",
        [((10 * inner, channels), F32), ((8, channels), F32)],
        [],
        20 * side * small * channels * inner,
        *(grad_pre, hidden_second, pre_second, grad_tile),
    )

    def columns(low, high, low_branch, high_branch):
        grads = jnp.concatenate([above[:HALO, low:high], grad_pre[:, low:high], below[:HALO, low:high]])
        here = slice(low_branch, high_branch)
        branches = jnp.concatenate([above[HALO:, here], grad_tile[:, here], below[HALO:, here]])
        branches = jnp.pad(branches, ((second, second), (0, 0), (0, 0)))
        return jnp.swapaxes(jnp.concatenate([grads, branches], axis=1), 0, 1)

    left = send(columns(side - HALO, side, side - first, side), lambda r, c: (r, c + 1))
    right = send(columns(0, HALO, 0, first), lambda r, c: (r, c - 1))
    left, right = jnp.swapaxes(left, 0, 1), jnp.swapaxes(right, 0, 1)

    devices = number * number
    share = -(-10 * inner // (8 * devices)) * 8
    parts, windows, grad_first = call(
        backward_kernel,
        "backward",
        [
            ((2 * devices, share + 8, channels), BF16),
            ((3, near, small, channels), BF16),
            ((side, side, channels), BF16),
        ],
        [
            ((full, LEAD + up16(side + HALO + first), channels), F32),
            ((3, full, small, channels), BF16),
            ((near, small + 16, channels), F32),
            ((near, small + 16, channels), F32),
            ((10 * inner, channels), F32),
            ((8, channels), F32),
        ],
        36 * near * small * channels * channels,
        *(grad_pre, grad_tile, above, below, left[:, :HALO], right[:, :HALO]),
        *(left[second : second + near, HALO:], right[second : second + near, HALO:]),
        *(gate_second, gate_first, near_hidden, bottle_first, v_second, p_back, rows_second, ends_second),
    )

    parts = lax.all_to_all(parts, ("segment",) + GRID, 0, 0, tiled=True)
    (input_gradient,) = call(
        input_kernel,
        "input",
        [((side, side, channels), BF16)],
        [],
        18 * side * small * channels * channels,
        *(windows, grad_first, tile, v_first),
    )
    cells = lax.axis_size("segment") * (side * number) * (side * number)
    rows, ends = call(
        functools.partial(total_kernel, float(cells) ** -0.5),
        "total",
        [((devices, share, channels), BF16), ((8, channels), F32)],
        [],
        parts.size,
        parts,
    )
    rows = lax.all_to_all(rows, GRID, 0, 0, tiled=True).reshape(devices * share, channels)
    conv_gradient, bias_gradient, out_gradient = call(
        outputs_kernel,
        "outputs",
        [((9 * inner, channels), F32), ((1, inner), F32), ((inner, channels), F32)],
        [],
        rows.size,
        *(rows, ends),
    )
    conv_gradient = jnp.swapaxes(conv_gradient.reshape(1, 9, inner, channels), 2, 3)
    return (input_gradient[None], conv_gradient, bias_gradient, out_gradient[None])


def solution(mesh):
    in_specs = (
        P("segment", "row", "col", None),
        P("segment", "row", "col", None),
        P("segment", None, None, None),
        P("segment", None),
        P("segment", None, None),
    )
    out_specs = (
        P("segment", "row", "col", None),
        P("segment", None, None, None),
        P("segment", None),
        P("segment", None, None),
    )
    return jax.shard_map(local, mesh=mesh, in_specs=in_specs, out_specs=out_specs, check_vma=False)
```

```python
import functools

import jax
import jax.numpy as jnp
from jax import lax
from jax.experimental import pallas as pl
from jax.experimental.pallas import tpu as pltpu
from jax.sharding import PartitionSpec as P

FIRST_DILATION = 2
SECOND_DILATION = 8
HALO = FIRST_DILATION + SECOND_DILATION
GRID = ("row", "col")
ALL = ("segment",) + GRID
TAPS = [(a, b) for a in (-1, 0, 1) for b in (-1, 0, 1)]
LEAD = 16
F32, BF16 = jnp.float32, jnp.bfloat16


def tap(a, b):
    return 3 * (a + 1) + (b + 1)


def dot(x, y):
    return jnp.dot(x, y, preferred_element_type=F32)


def rounded(x):
    return x.astype(BF16).astype(F32)


def up16(n):
    return -(-n // 16) * 16


def home(batch, r, c):
    number = lax.axis_size("row")
    core, row, col = (batch, r, c) if r == c else (int(r > c), r, c)
    if r != c and (r < c) == (batch == 1):
        row, col = c, r
    return (core * number + row) * number + col


def place():
    row, col = lax.axis_index("row"), lax.axis_index("col")
    low, high = jnp.minimum(row, col), jnp.maximum(row, col)
    upper = lax.axis_index("segment") == 0
    return jnp.where(upper, low, high), jnp.where(upper, high, low)


def permute(x, pair):
    number = lax.axis_size("row")
    tiles = [(m, r, c) for m in range(lax.axis_size("segment")) for r in range(number) for c in range(number)]
    pairs = [pair(*tile) for tile in tiles]
    return lax.ppermute(x, ALL, [found for found in pairs if found is not None])


def stored(batch, r, c):
    number = lax.axis_size("row")
    return (batch * number + r) * number + c


def bring(x):
    return permute(x, lambda m, r, c: (stored(m, r, c), home(m, r, c)))


def take_back(x):
    return permute(x, lambda m, r, c: (home(m, r, c), stored(m, r, c)))


def send(x, to):
    number = lax.axis_size("row")

    def pair(batch, r, c):
        row, col = to(r, c)
        if 0 <= row < number and 0 <= col < number:
            return home(batch, r, c), home(batch, row, col)

    return permute(x, pair)


def inside(shape, side, width, top):
    number = lax.axis_size("row") * side
    rows = lax.broadcasted_iota(jnp.int32, shape, 0) + top - width
    cols = lax.broadcasted_iota(jnp.int32, shape, 1) - width
    row, col = place()
    at_row = row * side + rows
    at_col = col * side + cols
    return (at_row >= 0) & (at_row < number) & (at_col >= 0) & (at_col < number) & (cols < side + width)


def forward_kernel(
    stacked, above, below, left, right, w_first, p_first, b_first, w_second, b_second,
    gate_first, bottle_first, near_hidden, gate_second, hidden_second, pre_second,
    area, shifted, pre, current,
):
    side, channels = stacked.shape[0], stacked.shape[2] // 2
    first, second, inner = FIRST_DILATION, SECOND_DILATION, p_first.shape[0] // 2
    full, span, near = side + 2 * HALO, side + 2 * second, side + 2 * first
    wide, small = pre.shape[1], pre_second.shape[1]
    own, other = slice(0, channels), slice(channels, 2 * channels)
    middle = slice(LEAD, LEAD + side)

    area[:, :LEAD] = jnp.zeros((full, LEAD, 2 * channels), F32)
    area[:, LEAD + side :] = jnp.zeros((full, area.shape[1] - LEAD - side, 2 * channels), F32)
    area[HALO : HALO + side, middle] = stacked[...].astype(F32)
    area[:HALO, middle] = above[...].astype(F32)
    area[HALO + side :, middle] = below[...].astype(F32)
    area[:, LEAD - HALO : LEAD] = left[...].astype(F32)
    area[:, LEAD + side : LEAD + side + HALO] = right[...].astype(F32)

    start = LEAD - second

    def shift(step, _):
        rows = pl.ds(step * 4, 4)
        for b in (-1, 0, 1):
            at = start + first * b
            shifted[b + 1, rows] = jnp.maximum(area[rows, at : at + wide], 0).astype(BF16)
        return 0

    lax.fori_loop(0, full // 4, shift, 0)
    for b in (-1, 0, 1):
        at = LEAD + first * b
        part = area[HALO - first : HALO + side + first, at : at + small, own]
        near_hidden[b + 1] = jnp.maximum(part, 0).astype(BF16)

    def first_section(step, _):
        top = step * 8
        size = 8 * wide
        total = jnp.broadcast_to(b_first[...], (size, 2 * inner))
        for a, b in TAPS:
            window = shifted[b + 1, pl.ds(top + first * (1 + a), 8)].reshape(size, 2 * channels)
            total = total + dot(window, w_first[tap(a, b)])
        pre[pl.ds(top, 8)] = total.reshape(8, wide, 2 * inner)
        branch = dot(jnp.maximum(total, 0).astype(BF16), p_first[...])
        middle_part = area[pl.ds(top + first, 8), start : start + wide].reshape(size, 2 * channels)
        branch = rounded(middle_part + branch)
        sym = rounded((branch[:, own] + branch[:, other]) * 0.5).reshape(8, wide, channels)
        current[pl.ds(top, 8)] = jnp.where(inside(sym.shape, side, second, top), sym, 0)
        return 0

    lax.fori_loop(0, span // 8, first_section, 0)

    edge = second - first
    part = pre[edge : edge + near, edge : edge + small]
    alive = (part > 0) & inside(part.shape, side, first, 0)
    gate_first[...] = jnp.where(alive, 1.0, 0.0).astype(BF16)
    part = current[edge : edge + near, edge : edge + small]
    gate_second[...] = jnp.where(part > 0, 1.0, 0.0).astype(BF16)
    bottle_first[...] = jnp.maximum(pre[second : second + side, second : second + small], 0).astype(BF16)
    for b in (-1, 0, 1):
        at = second * (1 + b)
        hidden_second[b + 1] = jnp.maximum(current[:, at : at + small], 0).astype(BF16)

    def second_section(step, _):
        top = step * 8
        total = jnp.broadcast_to(b_second[...], (8 * small, 2 * inner))
        for a, b in TAPS:
            window = hidden_second[b + 1, pl.ds(top + second * (1 + a), 8)].reshape(8 * small, channels)
            total = total + dot(window, w_second[tap(a, b)])
        pre_second[pl.ds(top, 8)] = total.reshape(8, small, 2 * inner)
        return 0

    lax.fori_loop(0, side // 8, second_section, 0)


def turn_kernel(cotangent, mirrored, pre_second, p_second, grad_tile, grad_pre, above, below, padded):
    side, channels = cotangent.shape[0], cotangent.shape[2]
    small, first = pre_second.shape[1], FIRST_DILATION
    branch = (cotangent[...].astype(F32) + jnp.swapaxes(mirrored[...].astype(F32), 0, 1)) * 0.5
    padded[:, side:] = jnp.zeros((side, small - side, channels), F32)
    padded[:, :side] = rounded(branch)
    branch = padded[...].astype(BF16)
    grad_tile[...] = branch
    grad = dot(branch.reshape(side * small, channels), p_second[...]).reshape(side, small, channels)
    grad = jnp.where(pre_second[...] > 0, grad, 0)
    grad_pre[...] = grad.astype(BF16)
    grad, branch = grad[:, :side].astype(BF16), padded[:, :side].astype(BF16)
    above[:HALO], above[HALO:] = grad[:HALO], branch[:first]
    below[:HALO], below[HALO:] = grad[side - HALO :], branch[side - first :]


def weight_sums(rows, ends, grad_pre, hidden, dilation, bottle, grad_tile):
    side, small, lanes = grad_pre.shape
    inner = lanes // 2
    size = side * small
    flat = grad_pre.reshape(size, lanes)
    turned = flat.T[:inner].astype(BF16)
    for a, b in TAPS:
        top = dilation * (1 + a)
        window = hidden[b + 1, top : top + side].reshape(size, lanes)
        at = tap(a, b) * inner
        rows[at : at + inner] = dot(turned, window)
    turned = bottle[...].reshape(size, lanes).astype(F32).T[:inner].astype(BF16)
    rows[9 * inner : 10 * inner] = dot(turned, grad_tile.reshape(size, lanes))
    ends[...] = jnp.broadcast_to(jnp.sum(flat, axis=0, keepdims=True), ends.shape)


def second_sums_kernel(grad_pre, hidden, pre_second, grad_tile, rows, ends):
    bottle = jnp.maximum(pre_second[...], 0).astype(BF16)
    weight_sums(rows, ends, grad_pre[...].astype(F32), hidden, SECOND_DILATION, bottle, grad_tile[...])


def backward_kernel(
    grad_pre, grad_tile, above, below, left, right, left_branch, right_branch, gate_second, gate_first, near_hidden,
    bottle_first, v_second, p_first, rows_second, ends_second,
    parts, windows, grad_first,
    area, shifted, branch, grads, rows, ends,
):
    side, channels = grad_first.shape[0], grad_first.shape[2]
    first, second = FIRST_DILATION, SECOND_DILATION
    full, near = side + 2 * HALO, side + 2 * first
    small = grad_pre.shape[1]
    middle = slice(LEAD, LEAD + side)

    area[:, :LEAD] = jnp.zeros((full, LEAD, channels), F32)
    area[:, LEAD + side :] = jnp.zeros((full, area.shape[1] - LEAD - side, channels), F32)
    area[HALO : HALO + side, LEAD : LEAD + small] = grad_pre[...].astype(F32)
    area[:HALO, middle] = above[:HALO].astype(F32)
    area[HALO + side :, middle] = below[:HALO].astype(F32)
    area[:, LEAD - HALO : LEAD] = left[...].astype(F32)
    area[:, LEAD + side : LEAD + side + HALO] = right[...].astype(F32)
    branch[...] = jnp.zeros(branch.shape, F32)
    branch[first : first + side, first : first + side] = grad_tile[:, :side].astype(F32)
    branch[:first, first : first + side] = above[HALO:].astype(F32)
    branch[first + side :, first : first + side] = below[HALO:].astype(F32)
    branch[:, :first] = left_branch[...].astype(F32)
    branch[:, first + side : near] = right_branch[...].astype(F32)
    for b in (-1, 0, 1):
        at = LEAD - HALO + second * (1 - b)
        shifted[b + 1] = area[:, at : at + small].astype(BF16)
    grads[:, small:] = jnp.zeros((near, grads.shape[1] - small, channels), F32)

    def sections(step, _):
        top = step * 7
        size = 7 * small
        total = jnp.zeros((size, 2 * channels), F32)
        for a, b in TAPS:
            window = shifted[b + 1, pl.ds(top + second * (1 - a), 7)].reshape(size, channels)
            total = total + dot(window, v_second[tap(a, b)])
        here = pl.ds(top, 7)
        grad = branch[here, :small].reshape(size, channels)
        gate = gate_second[here].astype(F32).reshape(size, channels) > 0
        own = rounded(grad + jnp.where(gate, total[:, :channels], 0))
        other = rounded(grad + jnp.where(gate, total[:, channels:], 0))
        grad = ((own + other) * 0.5).astype(BF16)
        branch[here, :small] = grad.astype(F32).reshape(7, small, channels)
        gate = gate_first[here].astype(F32).reshape(size, channels) > 0
        grad = rounded(jnp.where(gate, dot(grad, p_first[...]), 0))
        grads[here, :small] = grad.reshape(7, small, channels)
        return 0

    lax.fori_loop(0, near // 7, sections, 0)
    for b in (-1, 0, 1):
        at = first * (1 - b)
        windows[b + 1] = grads[:, at : at + small].astype(BF16)
    part = branch[first : first + side, first : first + small]
    grad_first[...] = part[:, :side].astype(BF16)
    keep = lax.broadcasted_iota(jnp.int32, part.shape, 1) < side
    part = jnp.where(keep, part, 0).astype(BF16)
    grad = jnp.where(keep, grads[first : first + side, first : first + small], 0)
    weight_sums(rows, ends, grad, near_hidden, first, bottle_first, part)

    devices, share = parts.shape[0] // 2, parts.shape[1] - 8
    count = rows.shape[0]
    for section, (table, end) in enumerate(((rows, ends), (rows_second, ends_second))):
        for j in range(devices):
            at = section * devices + j
            low, high = min(j * share, count), min((j + 1) * share, count)
            pieces = [table[low:high]] if low < high else []
            if high - low < share:
                pieces.append(jnp.zeros((share - (high - low), channels), F32))
            parts[at] = jnp.concatenate(pieces + [end[...]]).astype(BF16)


def input_kernel(windows, grad_first, tile, v_first, out):
    side, channels = tile.shape[0], tile.shape[2]
    small = windows.shape[2]
    first = FIRST_DILATION

    def rows(step, _):
        top = step * 8
        total = jnp.zeros((8 * small, channels), F32)
        for a, b in TAPS:
            window = windows[b + 1, pl.ds(top + first * (1 - a), 8)].reshape(8 * small, channels)
            total = total + dot(window, v_first[tap(a, b)])
        here = pl.ds(top, 8)
        total = total.reshape(8, small, channels)[:, :side]
        total = jnp.where(tile[here].astype(F32) > 0, total, 0)
        out[here] = (grad_first[here].astype(F32) + total).astype(BF16)
        return 0

    lax.fori_loop(0, side // 8, rows, 0)


def total_kernel(scale, parts, rows, ends):
    share = rows.shape[1]
    total = jnp.sum(parts[...].astype(F32), axis=0) * scale
    rows[...] = jnp.broadcast_to(total[:share].astype(BF16)[None], rows.shape)
    ends[...] = total[share:]


def outputs_kernel(rows, ends, conv_gradient, bias_gradient, out_gradient):
    count, inner = conv_gradient.shape[0], out_gradient.shape[0]
    conv_gradient[...] = rows[:count].astype(F32)
    out_gradient[...] = rows[count : count + inner].astype(F32)
    bias_gradient[...] = ends[:1, :inner]


def call(kernel, name, outs, scratch, flops, *operands):
    outs = [jax.ShapeDtypeStruct(shape, dtype) for shape, dtype in outs]
    moved = sum(x.size * x.dtype.itemsize for x in list(operands) + outs)
    return pl.pallas_call(
        kernel,
        name=name,
        out_shape=outs,
        scratch_shapes=[pltpu.VMEM(shape, dtype) for shape, dtype in scratch],
        cost_estimate=pl.CostEstimate(flops=flops, bytes_accessed=moved, transcendentals=0),
        compiler_params=pltpu.CompilerParams(vmem_limit_bytes=40 * 1024 * 1024),
    )(*operands)


def beside(x, y, axis):
    if axis is not None:
        return jnp.concatenate([x, y], axis=axis)
    zero = jnp.zeros_like(x)
    return jnp.concatenate([jnp.concatenate([x, zero], axis=-1), jnp.concatenate([zero, y], axis=-1)], axis=-2)


def local(activations, cotangent, conv_weight, conv_bias, out_weight):
    side, channels, inner = activations.shape[1], activations.shape[3], conv_weight.shape[3]
    number = lax.axis_size("row")
    first, second = FIRST_DILATION, SECOND_DILATION
    full, span, near = side + 2 * HALO, side + 2 * second, side + 2 * first
    wide, small = up16(span), up16(near)
    tile = bring(activations[0])

    mirrored = send(tile, lambda r, c: (c, r))
    stacked = jnp.concatenate([tile, jnp.swapaxes(mirrored, 0, 1)], axis=2)
    above = send(stacked[side - HALO :], lambda r, c: (r + 1, c))
    below = send(stacked[:HALO], lambda r, c: (r - 1, c))

    def columns(low, high):
        strip = jnp.concatenate([above[:, low:high], stacked[:, low:high], below[:, low:high]])
        return jnp.swapaxes(strip, 0, 1)

    left = send(columns(side - HALO, side), lambda r, c: (r, c + 1))
    right = send(columns(0, HALO), lambda r, c: (r, c - 1))
    _, late = lax.optimization_barrier((tile, cotangent[0]))
    _, late = lax.optimization_barrier((above, bring(late)))
    late_mirrored = send(late, lambda r, c: (c, r))

    bias_rows = jnp.pad(conv_bias, ((0, 7), (0, channels - inner)))
    packed = jnp.concatenate(
        [jnp.swapaxes(conv_weight[0], 1, 2).reshape(9 * inner, channels), out_weight[0], bias_rows]
    )
    packed = lax.all_gather(packed, "segment")
    conv = packed[:, : 9 * inner].reshape(2, 9, inner, channels)
    swapped = jnp.stack([conv[:, tap(b, a)] for a, b in TAPS], axis=1)
    proj = packed[:, 9 * inner : 10 * inner]
    bias = jnp.tile(packed[:, 10 * inner, :inner].astype(F32), (1, 2))[:, None]
    w_first = beside(jnp.swapaxes(conv[0], 1, 2), jnp.swapaxes(swapped[0], 1, 2), None)
    w_second = beside(jnp.swapaxes(conv[1], 1, 2), jnp.swapaxes(swapped[1], 1, 2), 2)
    v_second = beside(conv[1], swapped[1], None)
    v_first = jnp.pad(conv[0], ((0, 0), (0, inner), (0, 0)))
    p_first = beside(proj[0], proj[0], None)
    p_second = beside(proj[1].T, proj[1].T, 1)
    p_back = jnp.pad(proj[0].T, ((0, 0), (0, inner)))

    gate_first, bottle_first, near_hidden, gate_second, hidden_second, pre_second = call(
        forward_kernel,
        "forward",
        [
            ((near, small, channels), BF16),
            ((side, small, channels), BF16),
            ((3, near, small, channels), BF16),
            ((near, small, channels), BF16),
            ((3, span, small, channels), BF16),
            ((side, small, 2 * inner), F32),
        ],
        [
            ((full, LEAD + up16(side + LEAD), 2 * channels), F32),
            ((3, full, wide, 2 * channels), BF16),
            ((span, wide, 2 * inner), F32),
            ((span, wide, channels), F32),
        ],
        span * wide * 2 * channels * 2 * inner * 20,
        *(stacked, above, below),
        *(jnp.swapaxes(left, 0, 1), jnp.swapaxes(right, 0, 1)),
        *(w_first, p_first, bias[0], w_second, bias[1]),
    )

    grad_tile, grad_pre, strip_above, strip_below = call(
        turn_kernel,
        "turn",
        [
            ((side, small, channels), BF16),
            ((side, small, 2 * inner), BF16),
            ((HALO + first, side, channels), BF16),
            ((HALO + first, side, channels), BF16),
        ],
        [((side, small, channels), F32)],
        2 * side * small * channels * 2 * inner,
        *(late, late_mirrored, pre_second, p_second),
    )

    above = send(strip_below, lambda r, c: (r + 1, c))
    below = send(strip_above, lambda r, c: (r - 1, c))
    rows_second, ends_second = call(
        second_sums_kernel,
        "second_sums",
        [((10 * inner, channels), F32), ((8, channels), F32)],
        [],
        20 * side * small * channels * inner,
        *(grad_pre, hidden_second, pre_second, grad_tile),
    )

    def columns(low, high, low_branch, high_branch):
        grads = jnp.concatenate([above[:HALO, low:high], grad_pre[:, low:high], below[:HALO, low:high]])
        here = slice(low_branch, high_branch)
        branches = jnp.concatenate([above[HALO:, here], grad_tile[:, here], below[HALO:, here]])
        branches = jnp.pad(branches, ((second, second), (0, 0), (0, 0)))
        return jnp.swapaxes(jnp.concatenate([grads, branches], axis=1), 0, 1)

    left = send(columns(side - HALO, side, side - first, side), lambda r, c: (r, c + 1))
    right = send(columns(0, HALO, 0, first), lambda r, c: (r, c - 1))
    left, right = jnp.swapaxes(left, 0, 1), jnp.swapaxes(right, 0, 1)

    devices = number * number
    share = -(-10 * inner // (8 * devices)) * 8
    parts, windows, grad_first = call(
        backward_kernel,
        "backward",
        [
            ((2 * devices, share + 8, channels), BF16),
            ((3, near, small, channels), BF16),
            ((side, side, channels), BF16),
        ],
        [
            ((full, LEAD + up16(side + HALO + first), channels), F32),
            ((3, full, small, channels), BF16),
            ((near, small + 16, channels), F32),
            ((near, small + 16, channels), F32),
            ((10 * inner, channels), F32),
            ((8, channels), F32),
        ],
        36 * near * small * channels * channels,
        *(grad_pre, grad_tile, above, below, left[:, :HALO], right[:, :HALO]),
        *(left[second : second + near, HALO:], right[second : second + near, HALO:]),
        *(gate_second, gate_first, near_hidden, bottle_first, v_second, p_back, rows_second, ends_second),
    )

    parts = lax.all_to_all(parts, ALL, 0, 0, tiled=True)
    (input_gradient,) = call(
        input_kernel,
        "input",
        [((side, side, channels), BF16)],
        [],
        18 * side * small * channels * channels,
        *(windows, grad_first, tile, v_first),
    )
    cells = lax.axis_size("segment") * (side * number) * (side * number)
    rows, ends = call(
        functools.partial(total_kernel, float(cells) ** -0.5),
        "total",
        [((devices, share, channels), BF16), ((8, channels), F32)],
        [],
        parts.size,
        parts,
    )
    rows = lax.all_to_all(rows, GRID, 0, 0, tiled=True).reshape(devices * share, channels)
    conv_gradient, bias_gradient, out_gradient = call(
        outputs_kernel,
        "outputs",
        [((9 * inner, channels), F32), ((1, inner), F32), ((inner, channels), F32)],
        [],
        rows.size,
        *(rows, ends),
    )
    conv_gradient = jnp.swapaxes(conv_gradient.reshape(1, 9, inner, channels), 2, 3)
    return (take_back(input_gradient)[None], conv_gradient, bias_gradient, out_gradient[None])


def solution(mesh):
    in_specs = (
        P("segment", "row", "col", None),
        P("segment", "row", "col", None),
        P("segment", None, None, None),
        P("segment", None),
        P("segment", None, None),
    )
    out_specs = (
        P("segment", "row", "col", None),
        P("segment", None, None, None),
        P("segment", None),
        P("segment", None, None),
    )
    return jax.shard_map(local, mesh=mesh, in_specs=in_specs, out_specs=out_specs, check_vma=False)
```

```python
import functools

import jax
import jax.numpy as jnp
from jax import lax
from jax.experimental import pallas as pl
from jax.experimental.pallas import tpu as pltpu
from jax.sharding import PartitionSpec as P

FIRST_DILATION = 2
SECOND_DILATION = 8
HALO = FIRST_DILATION + SECOND_DILATION
GRID = ("row", "col")
ALL = ("segment",) + GRID
ORDER = [0, 1, 3, 4, 6, 7, 2, 5, 8]
TAPS = [(a, b) for a in (-1, 0, 1) for b in (-1, 0, 1)]
LEAD = 16
F32, BF16 = jnp.float32, jnp.bfloat16


def tap(a, b):
    return 3 * (a + 1) + (b + 1)


def dot(x, y):
    return jnp.dot(x, y, preferred_element_type=F32)


def rounded(x):
    return x.astype(BF16).astype(F32)


def up16(n):
    return -(-n // 16) * 16


def home(batch, r, c):
    number = lax.axis_size("row")
    core, row, col = (batch, r, c) if r == c else (int(r > c), r, c)
    if r != c and (r < c) == (batch == 1):
        row, col = c, r
    return (core * number + row) * number + col


def place():
    row, col = lax.axis_index("row"), lax.axis_index("col")
    low, high = jnp.minimum(row, col), jnp.maximum(row, col)
    upper = lax.axis_index("segment") == 0
    return jnp.where(upper, low, high), jnp.where(upper, high, low)


def permute(x, pair):
    number = lax.axis_size("row")
    tiles = [(m, r, c) for m in range(lax.axis_size("segment")) for r in range(number) for c in range(number)]
    pairs = [pair(*tile) for tile in tiles]
    return lax.ppermute(x, ALL, [found for found in pairs if found is not None])


def stored(batch, r, c):
    number = lax.axis_size("row")
    return (batch * number + r) * number + c


def bring(x):
    return permute(x, lambda m, r, c: (stored(m, r, c), home(m, r, c)))


def take_back(x):
    return permute(x, lambda m, r, c: (home(m, r, c), stored(m, r, c)))


def send(x, to):
    number = lax.axis_size("row")

    def pair(batch, r, c):
        row, col = to(r, c)
        if 0 <= row < number and 0 <= col < number:
            return home(batch, r, c), home(batch, row, col)

    return permute(x, pair)


def inside(shape, side, width, top):
    number = lax.axis_size("row") * side
    rows = lax.broadcasted_iota(jnp.int32, shape, 0) + top - width
    cols = lax.broadcasted_iota(jnp.int32, shape, 1) - width
    row, col = place()
    at_row = row * side + rows
    at_col = col * side + cols
    return (at_row >= 0) & (at_row < number) & (at_col >= 0) & (at_col < number) & (cols < side + width)


def paired(source, starts, width, dilation, pairs, last, change):
    lanes = source.shape[2]
    low, high = slice(0, lanes), slice(lanes, 2 * lanes)

    def step(k, _):
        rows, lower = pl.ds(4 * k, 4), pl.ds(4 * k + dilation, 4)
        window = [change(source[rows, at : at + width]).astype(BF16) for at in starts]
        pairs[rows, :, low] = window[0]
        pairs[rows, :, high] = window[1]
        last[lower, :, low] = window[2]
        last[rows, :, high] = window[2]
        return 0

    lax.fori_loop(0, source.shape[0] // 4, step, 0)


def taps_sum(pairs, last, top, rows, dilation, weights):
    width, lanes = pairs.shape[1], pairs.shape[2] // 2
    size = rows * width
    total = None
    for k in range(5):
        if k < 3:
            window = pairs[pl.ds(top + dilation * k, rows)]
        elif k == 3:
            window = last[pl.ds(top + dilation, rows)]
        else:
            window = last[pl.ds(top + 3 * dilation, rows), :, :lanes]
        weight = weights[2 * lanes * k : min(2 * lanes * (k + 1), 9 * lanes)]
        term = dot(window.reshape(size, window.shape[2]), weight)
        total = term if total is None else total + term
    return total


def positive(x):
    return jnp.maximum(x, 0)


def assemble(area, tile, above, below, left, right):
    side = tile.shape[0]
    full, wide, channels = area.shape
    middle = slice(LEAD, LEAD + side)
    area[:, :LEAD] = jnp.zeros((full, LEAD, channels), F32)
    area[:, LEAD + side :] = jnp.zeros((full, wide - LEAD - side, channels), F32)
    area[HALO : HALO + side, middle] = tile
    area[:HALO, middle] = above[:HALO].astype(F32)
    area[HALO + side :, middle] = below[:HALO].astype(F32)
    area[:, LEAD - HALO : LEAD] = left[...].astype(F32)
    area[:, LEAD + side : LEAD + side + HALO] = right[...].astype(F32)


def first_branch(area, pairs, last, weights, bias, proj, store):
    full, wide = pairs.shape[:2]
    start = LEAD - SECOND_DILATION
    starts = [start + FIRST_DILATION * b for b in (-1, 0, 1)]
    paired(area, starts, wide, FIRST_DILATION, pairs, last, positive)

    def rows(step, _):
        top = step * 8
        pre = taps_sum(pairs, last, top, 8, FIRST_DILATION, weights) + bias[...]
        branch = dot(positive(pre).astype(BF16), proj[...])
        inputs = area[pl.ds(top + FIRST_DILATION, 8), start : start + wide]
        branch = rounded(inputs + branch.reshape(inputs.shape))
        store(top, pre.reshape(8, wide, pre.shape[1]), branch)
        return 0

    lax.fori_loop(0, (full - 2 * FIRST_DILATION) // 8, rows, 0)


def own_kernel(
    tile, above, below, left, right, late, weights, bias, proj,
    swapped, gate_first, bottle_first, near_hidden,
    area, pairs, last, pre,
):
    side, first, second, inner = tile.shape[0], FIRST_DILATION, SECOND_DILATION, bias.shape[1]
    near, small = gate_first.shape[:2]
    span = side + 2 * second
    assemble(area, tile[...].astype(F32), above, below, left, right)

    def store(top, pre_act, branch):
        pre[pl.ds(top, 8)] = pre_act
        swapped[pl.ds(top, 8)] = branch[:, :span].astype(BF16)

    first_branch(area, pairs, last, weights, bias, proj, store)
    swapped[span:, :side] = late[...]
    for b in (-1, 0, 1):
        at = LEAD + first * b
        near_hidden[b + 1] = positive(area[HALO - first : HALO + side + first, at : at + small]).astype(BF16)
    edge = second - first
    part = pre[edge : edge + near, edge : edge + small]
    alive = (part > 0) & inside(part.shape, side, first, 0)
    gate_first[:, :, :inner] = jnp.where(alive, 1.0, 0.0).astype(BF16)
    gate_first[:, :, inner:] = jnp.zeros((near, small, gate_first.shape[2] - inner), BF16)
    bottle_first[...] = positive(pre[second : second + side, second : second + small]).astype(BF16)


def middle_kernel(
    kept, other, w_second, b_second, p_second,
    gate_second, hidden_pairs, hidden_last, bottle_second, grad_tile, grad_pre, above, below,
    current, padded, pre_second,
):
    side, channels, span = above.shape[1], kept.shape[2], kept.shape[1]
    first, second, inner = FIRST_DILATION, SECOND_DILATION, bottle_second.shape[2]
    near, small = gate_second.shape[:2]
    turned = jnp.swapaxes(other[:span].astype(F32), 0, 1)
    sym = rounded((kept[:span].astype(F32) + turned) * 0.5)
    current[:, :span] = jnp.where(inside(sym.shape, side, second, 0), sym, 0)
    current[:, span:] = jnp.zeros((span, current.shape[1] - span, channels), F32)
    edge = second - first
    part = current[edge : edge + near, edge : edge + small]
    gate_second[...] = jnp.where(part > 0, 1.0, 0.0).astype(BF16)
    paired(current, [0, second, 2 * second], small, second, hidden_pairs, hidden_last, positive)

    def rows(step, _):
        top = step * 8
        total = taps_sum(hidden_pairs, hidden_last, top, 8, second, w_second) + b_second[...]
        pre_second[pl.ds(top, 8)] = total.reshape(8, small, total.shape[1])
        return 0

    lax.fori_loop(0, side // 8, rows, 0)
    bottle_second[...] = positive(pre_second[:, :, :inner]).astype(BF16)

    turned = jnp.swapaxes(other[span:, :side].astype(F32), 0, 1)
    padded[:, side:] = jnp.zeros((side, small - side, channels), F32)
    padded[:, :side] = rounded((kept[span:, :side].astype(F32) + turned) * 0.5)
    branch = padded[...].astype(BF16)
    grad_tile[...] = branch
    grad = dot(branch.reshape(side * small, channels), p_second[...]).reshape(side, small, 2 * inner)
    grad = jnp.where(pre_second[...] > 0, grad, 0)
    grad_pre[...] = grad.astype(BF16)
    grad, branch = grad[:, :side].astype(BF16), padded[:, :side].astype(BF16)
    above[:HALO], above[HALO:] = grad[:HALO], branch[:first]
    below[:HALO], below[HALO:] = grad[side - HALO :], branch[side - first :]


def weight_sums(rows, ends, grad_pre, hidden, bottle, grad_tile):
    side, small, lanes = grad_pre.shape
    inner = bottle.shape[2]
    size = side * small
    flat = grad_pre.reshape(size, lanes)
    turned = flat.T[:inner].astype(BF16)
    for a in range(3):
        b = 0
        while b < 3:
            window = hidden(a, b)
            grads = dot(turned, window.reshape(size, window.shape[2]))
            for at in range(0, window.shape[2], grad_tile.shape[2]):
                rows[(3 * a + b) * inner : (3 * a + b + 1) * inner] = grads[:, at : at + grad_tile.shape[2]]
                b += 1
    turned = bottle[...].reshape(size, inner).astype(F32).T.astype(BF16)
    rows[9 * inner : 10 * inner] = dot(turned, grad_tile.reshape(size, grad_tile.shape[2]))
    ends[...] = jnp.zeros(ends.shape, F32)
    ends[:, :lanes] = jnp.broadcast_to(jnp.sum(flat, axis=0, keepdims=True), (ends.shape[0], lanes))


def second_sums_kernel(grad_pre, pairs, last, bottle, grad_tile, rows, ends):
    side = grad_pre.shape[0]
    channels = grad_tile.shape[2]

    def hidden(a, b):
        top = SECOND_DILATION * a
        if b == 0:
            return pairs[top : top + side]
        return last[top + SECOND_DILATION : top + SECOND_DILATION + side, :, :channels]

    weight_sums(rows, ends, grad_pre[...].astype(F32), hidden, bottle, grad_tile[...])


def backward_kernel(
    grad_pre, grad_tile, above, below, left, right, left_branch, right_branch, gate_second, gate_first, near_hidden,
    bottle_first, v_second, p_first, rows_second, ends_second,
    parts, windows, grad_first,
    area, shifted, branch, grads, rows, ends,
):
    side, channels = grad_first.shape[0], grad_first.shape[2]
    first, second = FIRST_DILATION, SECOND_DILATION
    full, near = side + 2 * HALO, side + 2 * first
    small = grad_pre.shape[1]
    middle = slice(LEAD, LEAD + side)

    area[:, :LEAD] = jnp.zeros((full, LEAD, channels), F32)
    area[:, LEAD + side :] = jnp.zeros((full, area.shape[1] - LEAD - side, channels), F32)
    area[HALO : HALO + side, LEAD : LEAD + small] = grad_pre[...].astype(F32)
    area[:HALO, middle] = above[:HALO].astype(F32)
    area[HALO + side :, middle] = below[:HALO].astype(F32)
    area[:, LEAD - HALO : LEAD] = left[...].astype(F32)
    area[:, LEAD + side : LEAD + side + HALO] = right[...].astype(F32)
    branch[...] = jnp.zeros(branch.shape, F32)
    branch[first : first + side, first : first + side] = grad_tile[:, :side].astype(F32)
    branch[:first, first : first + side] = above[HALO:].astype(F32)
    branch[first + side :, first : first + side] = below[HALO:].astype(F32)
    branch[:, :first] = left_branch[...].astype(F32)
    branch[:, first + side : near] = right_branch[...].astype(F32)
    for b in (-1, 0, 1):
        at = LEAD - HALO + second * (1 - b)
        shifted[b + 1] = area[:, at : at + small].astype(BF16)
    grads[:, small:] = jnp.zeros((near, grads.shape[1] - small, channels), F32)

    def sections(step, _):
        top = step * 7
        size = 7 * small
        total = jnp.zeros((size, 2 * channels), F32)
        for a, b in TAPS:
            window = shifted[b + 1, pl.ds(top + second * (1 - a), 7)].reshape(size, channels)
            total = total + dot(window, v_second[tap(a, b)])
        here = pl.ds(top, 7)
        grad = branch[here, :small].reshape(size, channels)
        gate = gate_second[here].astype(F32).reshape(size, channels) > 0
        own = rounded(grad + jnp.where(gate, total[:, :channels], 0))
        other = rounded(grad + jnp.where(gate, total[:, channels:], 0))
        grad = ((own + other) * 0.5).astype(BF16)
        branch[here, :small] = grad.astype(F32).reshape(7, small, channels)
        gate = gate_first[here].astype(F32).reshape(size, channels) > 0
        grad = rounded(jnp.where(gate, dot(grad, p_first[...]), 0))
        grads[here, :small] = grad.reshape(7, small, channels)
        return 0

    lax.fori_loop(0, near // 7, sections, 0)
    for b in (-1, 0, 1):
        at = first * (1 - b)
        windows[b + 1] = grads[:, at : at + small].astype(BF16)
    part = branch[first : first + side, first : first + small]
    grad_first[...] = part[:, :side].astype(BF16)
    keep = lax.broadcasted_iota(jnp.int32, part.shape, 1) < side
    part = jnp.where(keep, part, 0).astype(BF16)
    grad = jnp.where(keep, grads[first : first + side, first : first + small], 0)

    def hidden(a, b):
        return near_hidden[b, first * a : first * a + side]

    weight_sums(rows, ends, grad, hidden, bottle_first, part)

    devices, share = parts.shape[0] // 2, parts.shape[1] - 8
    count = rows.shape[0]
    for section, (table, end) in enumerate(((rows, ends), (rows_second, ends_second))):
        for j in range(devices):
            at = section * devices + j
            low, high = min(j * share, count), min((j + 1) * share, count)
            pieces = [table[low:high]] if low < high else []
            if high - low < share:
                pieces.append(jnp.zeros((share - (high - low), channels), F32))
            parts[at] = jnp.concatenate(pieces + [end[...]]).astype(BF16)


def input_kernel(windows, grad_first, tile, v_first, out):
    side, channels = tile.shape[0], tile.shape[2]
    small = windows.shape[2]
    first = FIRST_DILATION

    def rows(step, _):
        top = step * 8
        total = jnp.zeros((8 * small, channels), F32)
        for a, b in TAPS:
            window = windows[b + 1, pl.ds(top + first * (1 - a), 8)].reshape(8 * small, channels)
            total = total + dot(window, v_first[tap(a, b)])
        here = pl.ds(top, 8)
        total = total.reshape(8, small, channels)[:, :side]
        total = jnp.where(tile[here].astype(F32) > 0, total, 0)
        out[here] = (grad_first[here].astype(F32) + total).astype(BF16)
        return 0

    lax.fori_loop(0, side // 8, rows, 0)


def total_kernel(scale, parts, rows, ends):
    share = rows.shape[1]
    total = jnp.sum(parts[...].astype(F32), axis=0) * scale
    rows[...] = jnp.broadcast_to(total[:share].astype(BF16)[None], rows.shape)
    ends[...] = total[share:]


def outputs_kernel(rows, ends, conv_gradient, bias_gradient, out_gradient):
    count, inner = conv_gradient.shape[0], out_gradient.shape[0]
    conv_gradient[...] = rows[:count].astype(F32)
    out_gradient[...] = rows[count : count + inner].astype(F32)
    bias_gradient[...] = ends[:1, :inner]


def call(kernel, name, outs, scratch, flops, *operands):
    outs = [jax.ShapeDtypeStruct(shape, dtype) for shape, dtype in outs]
    moved = sum(x.size * x.dtype.itemsize for x in list(operands) + outs)
    return pl.pallas_call(
        kernel,
        name=name,
        out_shape=outs,
        scratch_shapes=[pltpu.VMEM(shape, dtype) for shape, dtype in scratch],
        cost_estimate=pl.CostEstimate(flops=flops, bytes_accessed=moved, transcendentals=0),
        compiler_params=pltpu.CompilerParams(vmem_limit_bytes=40 * 1024 * 1024),
    )(*operands)


def diagonal(x, y):
    zero = jnp.zeros_like(x)
    return jnp.concatenate([jnp.concatenate([x, zero], axis=-1), jnp.concatenate([zero, y], axis=-1)], axis=-2)


def local(activations, cotangent, conv_weight, conv_bias, out_weight):
    side, channels, inner = activations.shape[1], activations.shape[3], conv_weight.shape[3]
    number = lax.axis_size("row")
    first, second = FIRST_DILATION, SECOND_DILATION
    full, span, near = side + 2 * HALO, side + 2 * second, side + 2 * first
    wide, small = up16(span), up16(near)
    tile = bring(activations[0])

    above = send(tile[side - HALO :], lambda r, c: (r + 1, c))
    below = send(tile[:HALO], lambda r, c: (r - 1, c))

    def columns(low, high):
        strip = jnp.concatenate([above[:, low:high], tile[:, low:high], below[:, low:high]])
        return jnp.swapaxes(strip, 0, 1)

    left = send(columns(side - HALO, side), lambda r, c: (r, c + 1))
    right = send(columns(0, HALO), lambda r, c: (r, c - 1))
    _, late = lax.optimization_barrier((tile, cotangent[0]))
    late = bring(late)

    bias_rows = jnp.pad(conv_bias, ((0, 7), (0, channels - inner)))
    packed = jnp.concatenate(
        [jnp.swapaxes(conv_weight[0], 1, 2).reshape(9 * inner, channels), out_weight[0], bias_rows]
    )
    packed = lax.all_gather(packed, "segment")
    conv = packed[:, : 9 * inner].reshape(2, 9, inner, channels)
    swapped = conv.reshape(2, 3, 3, inner, channels).swapaxes(1, 2).reshape(conv.shape)
    proj = packed[:, 9 * inner : 10 * inner]
    bias = packed[:, 10 * inner, :inner].astype(F32)[:, None]

    def ordered(x):
        return jnp.concatenate([x[k] for k in ORDER])

    w_first = ordered(jnp.swapaxes(conv[0], 1, 2))
    w_second = ordered(jnp.swapaxes(jnp.concatenate([conv[1], swapped[1]], axis=1), 1, 2))
    v_second = diagonal(conv[1], swapped[1])
    v_first = jnp.pad(conv[0], ((0, 0), (0, inner), (0, 0)))
    p_second = jnp.concatenate([proj[1].T, proj[1].T], axis=1)
    p_back = jnp.pad(proj[0].T, ((0, 0), (0, inner)))

    kept, gate_first, bottle_first, near_hidden = call(
        own_kernel,
        "own_branch",
        [
            ((span + side, span, channels), BF16),
            ((near, small, channels), BF16),
            ((side, small, inner), BF16),
            ((3, near, small, channels), BF16),
        ],
        [
            ((full, LEAD + up16(side + LEAD), channels), F32),
            ((full, wide, 2 * channels), BF16),
            ((full + first, wide, 2 * channels), BF16),
            ((span, wide, inner), F32),
        ],
        span * wide * channels * inner * 20,
        *(tile, above, below, jnp.swapaxes(left, 0, 1), jnp.swapaxes(right, 0, 1), late),
        *(w_first, bias[0], proj[0]),
    )
    other = send(kept, lambda r, c: (c, r))
    gate_second, hidden_pairs, hidden_last, bottle_second, grad_tile, grad_pre, strip_above, strip_below = call(
        middle_kernel,
        "middle",
        [
            ((near, small, channels), BF16),
            ((span, small, 2 * channels), BF16),
            ((span + second, small, 2 * channels), BF16),
            ((side, small, inner), BF16),
            ((side, small, channels), BF16),
            ((side, small, 2 * inner), BF16),
            ((HALO + first, side, channels), BF16),
            ((HALO + first, side, channels), BF16),
        ],
        [
            ((span, wide, channels), F32),
            ((side, small, channels), F32),
            ((side, small, 2 * inner), F32),
        ],
        24 * side * small * channels * 2 * inner,
        *(kept, other, w_second, jnp.tile(bias[1], (1, 2)), p_second),
    )

    above = send(strip_below, lambda r, c: (r + 1, c))
    below = send(strip_above, lambda r, c: (r - 1, c))
    rows_second, ends_second = call(
        second_sums_kernel,
        "second_sums",
        [((10 * inner, channels), F32), ((8, channels), F32)],
        [],
        20 * side * small * channels * inner,
        *(grad_pre, hidden_pairs, hidden_last, bottle_second, grad_tile),
    )

    def columns(low, high, low_branch, high_branch):
        grads = jnp.concatenate([above[:HALO, low:high], grad_pre[:, low:high], below[:HALO, low:high]])
        here = slice(low_branch, high_branch)
        branches = jnp.concatenate([above[HALO:, here], grad_tile[:, here], below[HALO:, here]])
        branches = jnp.pad(branches, ((second, second), (0, 0), (0, 0)))
        return jnp.swapaxes(jnp.concatenate([grads, branches], axis=1), 0, 1)

    left = send(columns(side - HALO, side, side - first, side), lambda r, c: (r, c + 1))
    right = send(columns(0, HALO, 0, first), lambda r, c: (r, c - 1))
    left, right = jnp.swapaxes(left, 0, 1), jnp.swapaxes(right, 0, 1)

    devices = number * number
    share = -(-10 * inner // (8 * devices)) * 8
    parts, windows, grad_first = call(
        backward_kernel,
        "backward",
        [
            ((2 * devices, share + 8, channels), BF16),
            ((3, near, small, channels), BF16),
            ((side, side, channels), BF16),
        ],
        [
            ((full, LEAD + up16(side + HALO + first), channels), F32),
            ((3, full, small, channels), BF16),
            ((near, small + 16, channels), F32),
            ((near, small + 16, channels), F32),
            ((10 * inner, channels), F32),
            ((8, channels), F32),
        ],
        36 * near * small * channels * channels,
        *(grad_pre, grad_tile, above, below, left[:, :HALO], right[:, :HALO]),
        *(left[second : second + near, HALO:], right[second : second + near, HALO:]),
        *(gate_second, gate_first, near_hidden, bottle_first, v_second, p_back, rows_second, ends_second),
    )

    parts = lax.all_to_all(parts, ALL, 0, 0, tiled=True)
    (input_gradient,) = call(
        input_kernel,
        "input",
        [((side, side, channels), BF16)],
        [],
        18 * side * small * channels * channels,
        *(windows, grad_first, tile, v_first),
    )
    parts, input_gradient = lax.optimization_barrier((parts, input_gradient))
    input_gradient = take_back(input_gradient)
    cells = lax.axis_size("segment") * (side * number) * (side * number)
    rows, ends = call(
        functools.partial(total_kernel, float(cells) ** -0.5),
        "total",
        [((devices, share, channels), BF16), ((8, channels), F32)],
        [],
        parts.size,
        parts,
    )
    rows = lax.all_to_all(rows, GRID, 0, 0, tiled=True).reshape(devices * share, channels)
    conv_gradient, bias_gradient, out_gradient = call(
        outputs_kernel,
        "outputs",
        [((9 * inner, channels), F32), ((1, inner), F32), ((inner, channels), F32)],
        [],
        rows.size,
        *(rows, ends),
    )
    conv_gradient = jnp.swapaxes(conv_gradient.reshape(1, 9, inner, channels), 2, 3)
    return (input_gradient[None], conv_gradient, bias_gradient, out_gradient[None])


def solution(mesh):
    in_specs = (
        P("segment", "row", "col", None),
        P("segment", "row", "col", None),
        P("segment", None, None, None),
        P("segment", None),
        P("segment", None, None),
    )
    out_specs = (
        P("segment", "row", "col", None),
        P("segment", None, None, None),
        P("segment", None),
        P("segment", None, None),
    )
    return jax.shard_map(local, mesh=mesh, in_specs=in_specs, out_specs=out_specs, check_vma=False)
```

```python
import functools

import jax
import jax.numpy as jnp
from jax import lax
from jax.experimental import pallas as pl
from jax.experimental.pallas import tpu as pltpu
from jax.sharding import PartitionSpec as P

FIRST_DILATION = 2
SECOND_DILATION = 8
HALO = FIRST_DILATION + SECOND_DILATION
GRID = ("row", "col")
ALL = ("segment",) + GRID
ORDER = [0, 1, 3, 4, 6, 7, 2, 5, 8]
TAPS = [(a, b) for a in (-1, 0, 1) for b in (-1, 0, 1)]
LEAD = 16
F32, BF16 = jnp.float32, jnp.bfloat16


def tap(a, b):
    return 3 * (a + 1) + (b + 1)


def dot(x, y):
    return jnp.dot(x, y, preferred_element_type=F32)


def rounded(x):
    return x.astype(BF16).astype(F32)


def up16(n):
    return -(-n // 16) * 16


def home(batch, r, c):
    number = lax.axis_size("row")
    core, row, col = (batch, r, c) if r == c else (int(r > c), r, c)
    if r != c and (r < c) == (batch == 1):
        row, col = c, r
    return (core * number + row) * number + col


def place():
    row, col = lax.axis_index("row"), lax.axis_index("col")
    low, high = jnp.minimum(row, col), jnp.maximum(row, col)
    upper = lax.axis_index("segment") == 0
    return jnp.where(upper, low, high), jnp.where(upper, high, low)


def permute(x, pair):
    number = lax.axis_size("row")
    tiles = [(m, r, c) for m in range(lax.axis_size("segment")) for r in range(number) for c in range(number)]
    pairs = [pair(*tile) for tile in tiles]
    return lax.ppermute(x, ALL, [found for found in pairs if found is not None])


def stored(batch, r, c):
    number = lax.axis_size("row")
    return (batch * number + r) * number + c


def bring(x):
    return permute(x, lambda m, r, c: (stored(m, r, c), home(m, r, c)))


def take_back(x):
    return permute(x, lambda m, r, c: (home(m, r, c), stored(m, r, c)))


def send(x, to):
    number = lax.axis_size("row")

    def pair(batch, r, c):
        row, col = to(r, c)
        if 0 <= row < number and 0 <= col < number:
            return home(batch, r, c), home(batch, row, col)

    return permute(x, pair)


def inside(shape, side, width, top):
    number = lax.axis_size("row") * side
    rows = lax.broadcasted_iota(jnp.int32, shape, 0) + top - width
    cols = lax.broadcasted_iota(jnp.int32, shape, 1) - width
    row, col = place()
    at_row = row * side + rows
    at_col = col * side + cols
    return (at_row >= 0) & (at_row < number) & (at_col >= 0) & (at_col < number) & (cols < side + width)


def paired(source, starts, width, dilation, pairs, last, change):
    lanes = source.shape[2]
    low, high = slice(0, lanes), slice(lanes, 2 * lanes)

    def step(k, _):
        rows, lower = pl.ds(4 * k, 4), pl.ds(4 * k + dilation, 4)
        window = [change(source[rows, at : at + width]).astype(BF16) for at in starts]
        pairs[rows, :, low] = window[0]
        pairs[rows, :, high] = window[1]
        last[lower, :, low] = window[2]
        last[rows, :, high] = window[2]
        return 0

    lax.fori_loop(0, source.shape[0] // 4, step, 0)


def taps_sum(pairs, last, top, rows, dilation, weights):
    width, lanes = pairs.shape[1], pairs.shape[2] // 2
    size = rows * width
    total = None
    for k in range(5):
        if k < 3:
            window = pairs[pl.ds(top + dilation * k, rows)]
        elif k == 3:
            window = last[pl.ds(top + dilation, rows)]
        else:
            window = last[pl.ds(top + 3 * dilation, rows), :, :lanes]
        weight = weights[2 * lanes * k : min(2 * lanes * (k + 1), 9 * lanes)]
        term = dot(window.reshape(size, window.shape[2]), weight)
        total = term if total is None else total + term
    return total


def positive(x):
    return jnp.maximum(x, 0)


def assemble(area, tile, above, below, left, right):
    side = tile.shape[0]
    full, wide, channels = area.shape
    middle = slice(LEAD, LEAD + side)
    area[:, :LEAD] = jnp.zeros((full, LEAD, channels), F32)
    area[:, LEAD + side :] = jnp.zeros((full, wide - LEAD - side, channels), F32)
    area[HALO : HALO + side, middle] = tile
    area[:HALO, middle] = above[:HALO].astype(F32)
    area[HALO + side :, middle] = below[:HALO].astype(F32)
    area[:, LEAD - HALO : LEAD] = left[...].astype(F32)
    area[:, LEAD + side : LEAD + side + HALO] = right[...].astype(F32)


def first_branch(area, pairs, last, weights, bias, proj, store):
    full, wide = pairs.shape[:2]
    start = LEAD - SECOND_DILATION
    starts = [start + FIRST_DILATION * b for b in (-1, 0, 1)]
    paired(area, starts, wide, FIRST_DILATION, pairs, last, positive)

    def rows(step, _):
        top = step * 8
        pre = taps_sum(pairs, last, top, 8, FIRST_DILATION, weights) + bias[...]
        branch = dot(positive(pre).astype(BF16), proj[...])
        inputs = area[pl.ds(top + FIRST_DILATION, 8), start : start + wide]
        branch = rounded(inputs + branch.reshape(inputs.shape))
        store(top, pre.reshape(8, wide, pre.shape[1]), branch)
        return 0

    lax.fori_loop(0, (full - 2 * FIRST_DILATION) // 8, rows, 0)


def own_kernel(
    tile, above, below, left, right, late, weights, bias, proj,
    swapped, gate_first, bottle_first, near_hidden,
    area, pairs, last, pre,
):
    side, first, second, inner = tile.shape[0], FIRST_DILATION, SECOND_DILATION, bias.shape[1]
    near, small = gate_first.shape[:2]
    span = side + 2 * second
    assemble(area, tile[...].astype(F32), above, below, left, right)

    def store(top, pre_act, branch):
        pre[pl.ds(top, 8)] = pre_act
        swapped[pl.ds(top, 8)] = branch[:, :span].astype(BF16)

    first_branch(area, pairs, last, weights, bias, proj, store)
    swapped[span:, :side] = late[...]
    for b in (-1, 0, 1):
        at = LEAD + first * b
        near_hidden[b + 1] = positive(area[HALO - first : HALO + side + first, at : at + small]).astype(BF16)
    edge = second - first
    part = pre[edge : edge + near, edge : edge + small]
    alive = (part > 0) & inside(part.shape, side, first, 0)
    gate_first[:, :, :inner] = jnp.where(alive, 1.0, 0.0).astype(BF16)
    gate_first[:, :, inner:] = jnp.zeros((near, small, gate_first.shape[2] - inner), BF16)
    bottle_first[...] = positive(pre[second : second + side, second : second + small]).astype(BF16)


def middle_kernel(
    kept, other, w_second, b_second, p_second,
    gate_second, hidden_pairs, hidden_last, bottle_second, grad_tile, grad_pre, above, below,
    current, padded, pre_second,
):
    side, channels, span = above.shape[1], kept.shape[2], kept.shape[1]
    first, second, inner = FIRST_DILATION, SECOND_DILATION, bottle_second.shape[2]
    near, small = gate_second.shape[:2]
    turned = jnp.swapaxes(other[:span].astype(F32), 0, 1)
    sym = rounded((kept[:span].astype(F32) + turned) * 0.5)
    current[:, :span] = jnp.where(inside(sym.shape, side, second, 0), sym, 0)
    current[:, span:] = jnp.zeros((span, current.shape[1] - span, channels), F32)
    edge = second - first
    part = current[edge : edge + near, edge : edge + small]
    gate_second[...] = jnp.where(part > 0, 1.0, 0.0).astype(BF16)
    paired(current, [0, second, 2 * second], small, second, hidden_pairs, hidden_last, positive)

    def rows(step, _):
        top = step * 8
        total = taps_sum(hidden_pairs, hidden_last, top, 8, second, w_second) + b_second[...]
        pre_second[pl.ds(top, 8)] = total.reshape(8, small, total.shape[1])
        return 0

    lax.fori_loop(0, side // 8, rows, 0)
    bottle_second[...] = positive(pre_second[:, :, :inner]).astype(BF16)

    turned = jnp.swapaxes(other[span:, :side].astype(F32), 0, 1)
    padded[:, side:] = jnp.zeros((side, small - side, channels), F32)
    padded[:, :side] = rounded((kept[span:, :side].astype(F32) + turned) * 0.5)
    branch = padded[...].astype(BF16)
    grad_tile[...] = branch
    grad = dot(branch.reshape(side * small, channels), p_second[...]).reshape(side, small, 2 * inner)
    grad = jnp.where(pre_second[...] > 0, grad, 0)
    grad_pre[...] = grad.astype(BF16)
    grad, branch = grad[:, :side].astype(BF16), padded[:, :side].astype(BF16)
    above[:HALO], above[HALO:] = grad[:HALO], branch[:first]
    below[:HALO], below[HALO:] = grad[side - HALO :], branch[side - first :]


def weight_sums(rows, ends, grad_pre, hidden, bottle, grad_tile):
    side, small, lanes = grad_pre.shape
    inner = bottle.shape[2]
    size = side * small
    flat = grad_pre.reshape(size, lanes)
    turned = flat.T[:inner].astype(BF16)
    for a in range(3):
        b = 0
        while b < 3:
            window = hidden(a, b)
            grads = dot(turned, window.reshape(size, window.shape[2]))
            for at in range(0, window.shape[2], grad_tile.shape[2]):
                rows[(3 * a + b) * inner : (3 * a + b + 1) * inner] = grads[:, at : at + grad_tile.shape[2]]
                b += 1
    turned = bottle[...].reshape(size, inner).astype(F32).T.astype(BF16)
    rows[9 * inner : 10 * inner] = dot(turned, grad_tile.reshape(size, grad_tile.shape[2]))
    ends[...] = jnp.zeros(ends.shape, F32)
    ends[:, :lanes] = jnp.broadcast_to(jnp.sum(flat, axis=0, keepdims=True), (ends.shape[0], lanes))


def weights_kernel(
    mine, theirs, w_first, w_second, v_second, v_first, p_first, p_second, p_back, b_first, b_second, packed
):
    inner, channels = p_first.shape
    section = lax.axis_index("segment")
    packed[section] = mine[...]
    packed[1 - section] = theirs[...]

    def conv(section, k):
        return packed[section, k * inner : (k + 1) * inner]

    def turned(x):
        return x.astype(F32).T.astype(BF16)

    zero = jnp.zeros((inner, channels), BF16)
    for at, k in enumerate(ORDER):
        here = slice(at * channels, (at + 1) * channels)
        own, other = conv(1, k), conv(1, 3 * (k % 3) + k // 3)
        w_first[here] = turned(conv(0, k))
        w_second[here] = turned(jnp.concatenate([own, other], axis=0))
        v_second[k, :inner, :channels], v_second[k, :inner, channels:] = own, zero
        v_second[k, inner:, :channels], v_second[k, inner:, channels:] = zero, other
        v_first[k, :inner], v_first[k, inner:] = conv(0, k), zero
    p_first[...] = conv(0, 9)
    p_second[...] = turned(jnp.concatenate([conv(1, 9), conv(1, 9)], axis=0))
    p_back[...] = turned(jnp.concatenate([conv(0, 9), zero], axis=0))
    b_first[...] = packed[0, 10 * inner :].astype(F32)[:1, :inner]
    bias = packed[1, 10 * inner :].astype(F32)[:1, :inner]
    b_second[...] = jnp.concatenate([bias, bias], axis=1)


def second_sums_kernel(grad_pre, pairs, last, bottle, grad_tile, rows, ends):
    side = grad_pre.shape[0]
    channels = grad_tile.shape[2]

    def hidden(a, b):
        top = SECOND_DILATION * a
        if b == 0:
            return pairs[top : top + side]
        return last[top + SECOND_DILATION : top + SECOND_DILATION + side, :, :channels]

    weight_sums(rows, ends, grad_pre[...].astype(F32), hidden, bottle, grad_tile[...])


def backward_kernel(
    grad_pre, grad_tile, above, below, left, right, left_branch, right_branch, gate_second, gate_first, near_hidden,
    bottle_first, v_second, p_first, rows_second, ends_second,
    parts, windows, grad_first,
    area, shifted, branch, grads, rows, ends,
):
    side, channels = grad_first.shape[0], grad_first.shape[2]
    first, second = FIRST_DILATION, SECOND_DILATION
    full, near = side + 2 * HALO, side + 2 * first
    small = grad_pre.shape[1]
    middle = slice(LEAD, LEAD + side)

    area[:, :LEAD] = jnp.zeros((full, LEAD, channels), F32)
    area[:, LEAD + side :] = jnp.zeros((full, area.shape[1] - LEAD - side, channels), F32)
    area[HALO : HALO + side, LEAD : LEAD + small] = grad_pre[...].astype(F32)
    area[:HALO, middle] = above[:HALO].astype(F32)
    area[HALO + side :, middle] = below[:HALO].astype(F32)
    area[:, LEAD - HALO : LEAD] = left[...].astype(F32)
    area[:, LEAD + side : LEAD + side + HALO] = right[...].astype(F32)
    branch[...] = jnp.zeros(branch.shape, F32)
    branch[first : first + side, first : first + side] = grad_tile[:, :side].astype(F32)
    branch[:first, first : first + side] = above[HALO:].astype(F32)
    branch[first + side :, first : first + side] = below[HALO:].astype(F32)
    branch[:, :first] = left_branch[...].astype(F32)
    branch[:, first + side : near] = right_branch[...].astype(F32)
    for b in (-1, 0, 1):
        at = LEAD - HALO + second * (1 - b)
        shifted[b + 1] = area[:, at : at + small].astype(BF16)
    grads[:, small:] = jnp.zeros((near, grads.shape[1] - small, channels), F32)

    def sections(step, _):
        top = step * 7
        size = 7 * small
        total = jnp.zeros((size, 2 * channels), F32)
        for a, b in TAPS:
            window = shifted[b + 1, pl.ds(top + second * (1 - a), 7)].reshape(size, channels)
            total = total + dot(window, v_second[tap(a, b)])
        here = pl.ds(top, 7)
        grad = branch[here, :small].reshape(size, channels)
        gate = gate_second[here].astype(F32).reshape(size, channels) > 0
        own = rounded(grad + jnp.where(gate, total[:, :channels], 0))
        other = rounded(grad + jnp.where(gate, total[:, channels:], 0))
        grad = ((own + other) * 0.5).astype(BF16)
        branch[here, :small] = grad.astype(F32).reshape(7, small, channels)
        gate = gate_first[here].astype(F32).reshape(size, channels) > 0
        grad = rounded(jnp.where(gate, dot(grad, p_first[...]), 0))
        grads[here, :small] = grad.reshape(7, small, channels)
        return 0

    lax.fori_loop(0, near // 7, sections, 0)
    for b in (-1, 0, 1):
        at = first * (1 - b)
        windows[b + 1] = grads[:, at : at + small].astype(BF16)
    part = branch[first : first + side, first : first + small]
    grad_first[...] = part[:, :side].astype(BF16)
    keep = lax.broadcasted_iota(jnp.int32, part.shape, 1) < side
    part = jnp.where(keep, part, 0).astype(BF16)
    grad = jnp.where(keep, grads[first : first + side, first : first + small], 0)

    def hidden(a, b):
        return near_hidden[b, first * a : first * a + side]

    weight_sums(rows, ends, grad, hidden, bottle_first, part)

    devices, share = parts.shape[0] // 2, parts.shape[1] - 8
    count = rows.shape[0]
    for section, (table, end) in enumerate(((rows, ends), (rows_second, ends_second))):
        for j in range(devices):
            at = section * devices + j
            low, high = min(j * share, count), min((j + 1) * share, count)
            pieces = [table[low:high]] if low < high else []
            if high - low < share:
                pieces.append(jnp.zeros((share - (high - low), channels), F32))
            parts[at] = jnp.concatenate(pieces + [end[...]]).astype(BF16)


def input_kernel(windows, grad_first, tile, v_first, out):
    side, channels = tile.shape[0], tile.shape[2]
    small = windows.shape[2]
    first = FIRST_DILATION

    def rows(step, _):
        top = step * 8
        total = jnp.zeros((8 * small, channels), F32)
        for a, b in TAPS:
            window = windows[b + 1, pl.ds(top + first * (1 - a), 8)].reshape(8 * small, channels)
            total = total + dot(window, v_first[tap(a, b)])
        here = pl.ds(top, 8)
        total = total.reshape(8, small, channels)[:, :side]
        total = jnp.where(tile[here].astype(F32) > 0, total, 0)
        out[here] = (grad_first[here].astype(F32) + total).astype(BF16)
        return 0

    lax.fori_loop(0, side // 8, rows, 0)


def total_kernel(scale, parts, rows, ends):
    share = rows.shape[1]
    total = jnp.sum(parts[...].astype(F32), axis=0) * scale
    rows[...] = jnp.broadcast_to(total[:share].astype(BF16)[None], rows.shape)
    ends[...] = total[share:]


def outputs_kernel(rows, ends, conv_gradient, bias_gradient, out_gradient):
    count, inner = conv_gradient.shape[0], out_gradient.shape[0]
    conv_gradient[...] = rows[:count].astype(F32)
    out_gradient[...] = rows[count : count + inner].astype(F32)
    bias_gradient[...] = ends[:1, :inner]


def call(kernel, name, outs, scratch, flops, *operands):
    outs = [jax.ShapeDtypeStruct(shape, dtype) for shape, dtype in outs]
    moved = sum(x.size * x.dtype.itemsize for x in list(operands) + outs)
    return pl.pallas_call(
        kernel,
        name=name,
        out_shape=outs,
        scratch_shapes=[pltpu.VMEM(shape, dtype) for shape, dtype in scratch],
        cost_estimate=pl.CostEstimate(flops=flops, bytes_accessed=moved, transcendentals=0),
        compiler_params=pltpu.CompilerParams(vmem_limit_bytes=40 * 1024 * 1024),
    )(*operands)


def local(activations, cotangent, conv_weight, conv_bias, out_weight):
    side, channels, inner = activations.shape[1], activations.shape[3], conv_weight.shape[3]
    number = lax.axis_size("row")
    first, second = FIRST_DILATION, SECOND_DILATION
    full, span, near = side + 2 * HALO, side + 2 * second, side + 2 * first
    wide, small = up16(span), up16(near)
    tile = bring(activations[0])

    above = send(tile[side - HALO :], lambda r, c: (r + 1, c))
    below = send(tile[:HALO], lambda r, c: (r - 1, c))

    def columns(low, high):
        strip = jnp.concatenate([above[:, low:high], tile[:, low:high], below[:, low:high]])
        return jnp.swapaxes(strip, 0, 1)

    left = send(columns(side - HALO, side), lambda r, c: (r, c + 1))
    right = send(columns(0, HALO), lambda r, c: (r, c - 1))
    late = bring(cotangent[0])

    bias_rows = jnp.pad(conv_bias, ((0, 15), (0, channels - inner)))
    packed = jnp.concatenate(
        [jnp.swapaxes(conv_weight[0], 1, 2).reshape(9 * inner, channels), out_weight[0], bias_rows]
    )
    others = lax.ppermute(packed, "segment", [(0, 1), (1, 0)])
    w_first, w_second, v_second, v_first, p_first, p_second, p_back, b_first, b_second = call(
        weights_kernel,
        "weights",
        [
            ((9 * channels, inner), BF16),
            ((9 * channels, 2 * inner), BF16),
            ((9, 2 * inner, 2 * channels), BF16),
            ((9, 2 * inner, channels), BF16),
            ((inner, channels), BF16),
            ((channels, 2 * inner), BF16),
            ((channels, 2 * inner), BF16),
            ((1, inner), F32),
            ((1, 2 * inner), F32),
        ],
        [((2,) + packed.shape, BF16)],
        packed.size,
        *(packed, others),
    )

    kept, gate_first, bottle_first, near_hidden = call(
        own_kernel,
        "own_branch",
        [
            ((span + side, span, channels), BF16),
            ((near, small, channels), BF16),
            ((side, small, inner), BF16),
            ((3, near, small, channels), BF16),
        ],
        [
            ((full, LEAD + up16(side + LEAD), channels), F32),
            ((full, wide, 2 * channels), BF16),
            ((full + first, wide, 2 * channels), BF16),
            ((span, wide, inner), F32),
        ],
        span * wide * channels * inner * 20,
        *(tile, above, below, jnp.swapaxes(left, 0, 1), jnp.swapaxes(right, 0, 1), late),
        *(w_first, b_first, p_first),
    )
    other = send(kept, lambda r, c: (c, r))
    gate_second, hidden_pairs, hidden_last, bottle_second, grad_tile, grad_pre, strip_above, strip_below = call(
        middle_kernel,
        "middle",
        [
            ((near, small, channels), BF16),
            ((span, small, 2 * channels), BF16),
            ((span + second, small, 2 * channels), BF16),
            ((side, small, inner), BF16),
            ((side, small, channels), BF16),
            ((side, small, 2 * inner), BF16),
            ((HALO + first, side, channels), BF16),
            ((HALO + first, side, channels), BF16),
        ],
        [
            ((span, wide, channels), F32),
            ((side, small, channels), F32),
            ((side, small, 2 * inner), F32),
        ],
        24 * side * small * channels * 2 * inner,
        *(kept, other, w_second, b_second, p_second),
    )

    above = send(strip_below, lambda r, c: (r + 1, c))
    below = send(strip_above, lambda r, c: (r - 1, c))
    rows_second, ends_second = call(
        second_sums_kernel,
        "second_sums",
        [((10 * inner, channels), F32), ((8, channels), F32)],
        [],
        20 * side * small * channels * inner,
        *(grad_pre, hidden_pairs, hidden_last, bottle_second, grad_tile),
    )

    def columns(low, high, low_branch, high_branch):
        grads = jnp.concatenate([above[:HALO, low:high], grad_pre[:, low:high], below[:HALO, low:high]])
        here = slice(low_branch, high_branch)
        branches = jnp.concatenate([above[HALO:, here], grad_tile[:, here], below[HALO:, here]])
        branches = jnp.pad(branches, ((second, second), (0, 0), (0, 0)))
        return jnp.swapaxes(jnp.concatenate([grads, branches], axis=1), 0, 1)

    left = send(columns(side - HALO, side, side - first, side), lambda r, c: (r, c + 1))
    right = send(columns(0, HALO, 0, first), lambda r, c: (r, c - 1))
    left, right = jnp.swapaxes(left, 0, 1), jnp.swapaxes(right, 0, 1)

    devices = number * number
    share = -(-10 * inner // (8 * devices)) * 8
    parts, windows, grad_first = call(
        backward_kernel,
        "backward",
        [
            ((2 * devices, share + 8, channels), BF16),
            ((3, near, small, channels), BF16),
            ((side, side, channels), BF16),
        ],
        [
            ((full, LEAD + up16(side + HALO + first), channels), F32),
            ((3, full, small, channels), BF16),
            ((near, small + 16, channels), F32),
            ((near, small + 16, channels), F32),
            ((10 * inner, channels), F32),
            ((8, channels), F32),
        ],
        36 * near * small * channels * channels,
        *(grad_pre, grad_tile, above, below, left[:, :HALO], right[:, :HALO]),
        *(left[second : second + near, HALO:], right[second : second + near, HALO:]),
        *(gate_second, gate_first, near_hidden, bottle_first, v_second, p_back, rows_second, ends_second),
    )

    parts = lax.all_to_all(parts, ALL, 0, 0, tiled=True)
    (input_gradient,) = call(
        input_kernel,
        "input",
        [((side, side, channels), BF16)],
        [],
        18 * side * small * channels * channels,
        *(windows, grad_first, tile, v_first),
    )
    parts, input_gradient = lax.optimization_barrier((parts, take_back(input_gradient)))
    cells = lax.axis_size("segment") * (side * number) * (side * number)
    rows, ends = call(
        functools.partial(total_kernel, float(cells) ** -0.5),
        "total",
        [((devices, share, channels), BF16), ((8, channels), F32)],
        [],
        parts.size,
        parts,
    )
    rows = lax.all_to_all(rows, GRID, 0, 0, tiled=True).reshape(devices * share, channels)
    conv_gradient, bias_gradient, out_gradient = call(
        outputs_kernel,
        "outputs",
        [((9 * inner, channels), F32), ((1, inner), F32), ((inner, channels), F32)],
        [],
        rows.size,
        *(rows, ends),
    )
    conv_gradient = jnp.swapaxes(conv_gradient.reshape(1, 9, inner, channels), 2, 3)
    return (input_gradient[None], conv_gradient, bias_gradient, out_gradient[None])


def solution(mesh):
    in_specs = (
        P("segment", "row", "col", None),
        P("segment", "row", "col", None),
        P("segment", None, None, None),
        P("segment", None),
        P("segment", None, None),
    )
    out_specs = (
        P("segment", "row", "col", None),
        P("segment", None, None, None),
        P("segment", None),
        P("segment", None, None),
    )
    return jax.shard_map(local, mesh=mesh, in_specs=in_specs, out_specs=out_specs, check_vma=False)
```

```python
import functools

import jax
import jax.numpy as jnp
from jax import lax
from jax.experimental import pallas as pl
from jax.experimental.pallas import tpu as pltpu
from jax.sharding import PartitionSpec as P

FIRST_DILATION = 2
SECOND_DILATION = 8
HALO = FIRST_DILATION + SECOND_DILATION
GRID = ("row", "col")
ALL = ("segment",) + GRID
ORDER = [0, 1, 3, 4, 6, 7, 2, 5, 8]
TAPS = [(a, b) for a in (-1, 0, 1) for b in (-1, 0, 1)]
LEAD = 16
F32, BF16 = jnp.float32, jnp.bfloat16


def tap(a, b):
    return 3 * (a + 1) + (b + 1)


def dot(x, y):
    return jnp.dot(x, y, preferred_element_type=F32)


def rounded(x):
    return x.astype(BF16).astype(F32)


def up16(n):
    return -(-n // 16) * 16


def home(batch, r, c):
    number = lax.axis_size("row")
    core, row, col = (batch, r, c) if r == c else (int(r > c), r, c)
    if r != c and (r < c) == (batch == 1):
        row, col = c, r
    return (core * number + row) * number + col


def place():
    row, col = lax.axis_index("row"), lax.axis_index("col")
    low, high = jnp.minimum(row, col), jnp.maximum(row, col)
    upper = lax.axis_index("segment") == 0
    return jnp.where(upper, low, high), jnp.where(upper, high, low)


def permute(x, pair):
    number = lax.axis_size("row")
    tiles = [(m, r, c) for m in range(lax.axis_size("segment")) for r in range(number) for c in range(number)]
    pairs = [pair(*tile) for tile in tiles]
    return lax.ppermute(x, ALL, [found for found in pairs if found is not None])


def stored(batch, r, c):
    number = lax.axis_size("row")
    return (batch * number + r) * number + c


def bring(x, down=0):
    number = lax.axis_size("row")

    def pair(batch, r, c):
        if 0 <= r + down < number:
            return stored(batch, r, c), home(batch, r + down, c)

    return permute(x, pair)


def take_back(x):
    return permute(x, lambda m, r, c: (home(m, r, c), stored(m, r, c)))


def send(x, to):
    number = lax.axis_size("row")

    def pair(batch, r, c):
        row, col = to(r, c)
        if 0 <= row < number and 0 <= col < number:
            return home(batch, r, c), home(batch, row, col)

    return permute(x, pair)


def inside(shape, side, width, top):
    number = lax.axis_size("row") * side
    rows = lax.broadcasted_iota(jnp.int32, shape, 0) + top - width
    cols = lax.broadcasted_iota(jnp.int32, shape, 1) - width
    row, col = place()
    at_row = row * side + rows
    at_col = col * side + cols
    return (at_row >= 0) & (at_row < number) & (at_col >= 0) & (at_col < number) & (cols < side + width)


def paired(source, starts, width, dilation, pairs, last, change):
    lanes = source.shape[2]
    low, high = slice(0, lanes), slice(lanes, 2 * lanes)

    def step(k, _):
        rows, lower = pl.ds(4 * k, 4), pl.ds(4 * k + dilation, 4)
        window = [change(source[rows, at : at + width]).astype(BF16) for at in starts]
        pairs[rows, :, low] = window[0]
        pairs[rows, :, high] = window[1]
        last[lower, :, low] = window[2]
        last[rows, :, high] = window[2]
        return 0

    lax.fori_loop(0, source.shape[0] // 4, step, 0)


def taps_sum(pairs, last, top, rows, dilation, weights):
    width, lanes = pairs.shape[1], pairs.shape[2] // 2
    size = rows * width
    total = None
    for k in range(5):
        if k < 3:
            window = pairs[pl.ds(top + dilation * k, rows)]
        elif k == 3:
            window = last[pl.ds(top + dilation, rows)]
        else:
            window = last[pl.ds(top + 3 * dilation, rows), :, :lanes]
        weight = weights[2 * lanes * k : min(2 * lanes * (k + 1), 9 * lanes)]
        term = dot(window.reshape(size, window.shape[2]), weight)
        total = term if total is None else total + term
    return total


def positive(x):
    return jnp.maximum(x, 0)


def assemble(area, tile, above, below, left, right):
    side = tile.shape[0]
    full, wide, channels = area.shape
    middle = slice(LEAD, LEAD + side)
    area[:, :LEAD] = jnp.zeros((full, LEAD, channels), F32)
    area[:, LEAD + side :] = jnp.zeros((full, wide - LEAD - side, channels), F32)
    area[HALO : HALO + side, middle] = tile
    area[:HALO, middle] = above[:HALO].astype(F32)
    area[HALO + side :, middle] = below[:HALO].astype(F32)
    area[:, LEAD - HALO : LEAD] = left[...].astype(F32)
    area[:, LEAD + side : LEAD + side + HALO] = right[...].astype(F32)


def first_branch(area, pairs, last, weights, bias, proj, store):
    full, wide = pairs.shape[:2]
    start = LEAD - SECOND_DILATION
    starts = [start + FIRST_DILATION * b for b in (-1, 0, 1)]
    paired(area, starts, wide, FIRST_DILATION, pairs, last, positive)

    def rows(step, _):
        top = step * 8
        pre = taps_sum(pairs, last, top, 8, FIRST_DILATION, weights) + bias[...]
        branch = dot(positive(pre).astype(BF16), proj[...])
        inputs = area[pl.ds(top + FIRST_DILATION, 8), start : start + wide]
        branch = rounded(inputs + branch.reshape(inputs.shape))
        store(top, pre.reshape(8, wide, pre.shape[1]), branch)
        return 0

    lax.fori_loop(0, (full - 2 * FIRST_DILATION) // 8, rows, 0)


def own_kernel(
    tile, above, below, left, right, late, weights, bias, proj,
    swapped, gate_first, bottle_first, near_hidden,
    area, pairs, last, pre,
):
    side, first, second, inner = tile.shape[0], FIRST_DILATION, SECOND_DILATION, bias.shape[1]
    near, small = gate_first.shape[:2]
    span = side + 2 * second
    assemble(area, tile[...].astype(F32), above, below, left, right)

    def store(top, pre_act, branch):
        pre[pl.ds(top, 8)] = pre_act
        swapped[pl.ds(top, 8)] = branch[:, :span].astype(BF16)

    first_branch(area, pairs, last, weights, bias, proj, store)
    swapped[span:, :side] = late[...]
    for b in (-1, 0, 1):
        at = LEAD + first * b
        near_hidden[b + 1] = positive(area[HALO - first : HALO + side + first, at : at + small]).astype(BF16)
    edge = second - first
    part = pre[edge : edge + near, edge : edge + small]
    alive = (part > 0) & inside(part.shape, side, first, 0)
    gate_first[:, :, :inner] = jnp.where(alive, 1.0, 0.0).astype(BF16)
    gate_first[:, :, inner:] = jnp.zeros((near, small, gate_first.shape[2] - inner), BF16)
    bottle_first[...] = positive(pre[second : second + side, second : second + small]).astype(BF16)


def middle_kernel(
    kept, other, w_second, b_second, p_second,
    gate_second, hidden_pairs, hidden_last, bottle_second, grad_tile, grad_pre, above, below,
    current, padded, pre_second,
):
    side, channels, span = above.shape[1], kept.shape[2], kept.shape[1]
    first, second, inner = FIRST_DILATION, SECOND_DILATION, bottle_second.shape[2]
    near, small = gate_second.shape[:2]
    turned = jnp.swapaxes(other[:span].astype(F32), 0, 1)
    sym = rounded((kept[:span].astype(F32) + turned) * 0.5)
    current[:, :span] = jnp.where(inside(sym.shape, side, second, 0), sym, 0)
    current[:, span:] = jnp.zeros((span, current.shape[1] - span, channels), F32)
    edge = second - first
    part = current[edge : edge + near, edge : edge + small]
    gate_second[...] = jnp.where(part > 0, 1.0, 0.0).astype(BF16)
    paired(current, [0, second, 2 * second], small, second, hidden_pairs, hidden_last, positive)

    def rows(step, _):
        top = step * 8
        total = taps_sum(hidden_pairs, hidden_last, top, 8, second, w_second) + b_second[...]
        pre_second[pl.ds(top, 8)] = total.reshape(8, small, total.shape[1])
        return 0

    lax.fori_loop(0, side // 8, rows, 0)
    bottle_second[...] = positive(pre_second[:, :, :inner]).astype(BF16)

    turned = jnp.swapaxes(other[span:, :side].astype(F32), 0, 1)
    padded[:, side:] = jnp.zeros((side, small - side, channels), F32)
    padded[:, :side] = rounded((kept[span:, :side].astype(F32) + turned) * 0.5)
    branch = padded[...].astype(BF16)
    grad_tile[...] = branch
    grad = dot(branch.reshape(side * small, channels), p_second[...]).reshape(side, small, 2 * inner)
    grad = jnp.where(pre_second[...] > 0, grad, 0)
    grad_pre[...] = grad.astype(BF16)
    grad, branch = grad[:, :side].astype(BF16), padded[:, :side].astype(BF16)
    above[:HALO], above[HALO:] = grad[:HALO], branch[:first]
    below[:HALO], below[HALO:] = grad[side - HALO :], branch[side - first :]


def weight_sums(rows, ends, grad_pre, hidden, bottle, grad_tile):
    side, small, lanes = grad_pre.shape
    inner = bottle.shape[2]
    size = side * small
    flat = grad_pre.reshape(size, lanes)
    turned = flat.T[:inner].astype(BF16)
    for a in range(3):
        b = 0
        while b < 3:
            window = hidden(a, b)
            grads = dot(turned, window.reshape(size, window.shape[2]))
            for at in range(0, window.shape[2], grad_tile.shape[2]):
                rows[(3 * a + b) * inner : (3 * a + b + 1) * inner] = grads[:, at : at + grad_tile.shape[2]]
                b += 1
    turned = bottle[...].reshape(size, inner).astype(F32).T.astype(BF16)
    rows[9 * inner : 10 * inner] = dot(turned, grad_tile.reshape(size, grad_tile.shape[2]))
    ends[...] = jnp.zeros(ends.shape, F32)
    ends[:, :lanes] = jnp.broadcast_to(jnp.sum(flat, axis=0, keepdims=True), (ends.shape[0], lanes))


def weights_kernel(
    mine, theirs, w_first, w_second, v_second, v_first, p_first, p_second, p_back, b_first, b_second, packed
):
    inner, channels = p_first.shape
    section = lax.axis_index("segment")
    packed[section] = mine[...]
    packed[1 - section] = theirs[...]

    def conv(section, k):
        return packed[section, k * inner : (k + 1) * inner]

    def turned(x):
        return x.astype(F32).T.astype(BF16)

    zero = jnp.zeros((inner, channels), BF16)
    for at, k in enumerate(ORDER):
        here = slice(at * channels, (at + 1) * channels)
        own, other = conv(1, k), conv(1, 3 * (k % 3) + k // 3)
        w_first[here] = turned(conv(0, k))
        w_second[here] = turned(jnp.concatenate([own, other], axis=0))
        v_second[k, :inner, :channels], v_second[k, :inner, channels:] = own, zero
        v_second[k, inner:, :channels], v_second[k, inner:, channels:] = zero, other
        v_first[k, :inner], v_first[k, inner:] = conv(0, k), zero
    p_first[...] = conv(0, 9)
    p_second[...] = turned(jnp.concatenate([conv(1, 9), conv(1, 9)], axis=0))
    p_back[...] = turned(jnp.concatenate([conv(0, 9), zero], axis=0))
    b_first[...] = packed[0, 10 * inner :].astype(F32)[:1, :inner]
    bias = packed[1, 10 * inner :].astype(F32)[:1, :inner]
    b_second[...] = jnp.concatenate([bias, bias], axis=1)


def second_sums_kernel(grad_pre, pairs, last, bottle, grad_tile, rows, ends):
    side = grad_pre.shape[0]
    channels = grad_tile.shape[2]

    def hidden(a, b):
        top = SECOND_DILATION * a
        if b == 0:
            return pairs[top : top + side]
        return last[top + SECOND_DILATION : top + SECOND_DILATION + side, :, :channels]

    weight_sums(rows, ends, grad_pre[...].astype(F32), hidden, bottle, grad_tile[...])


def backward_kernel(
    grad_pre, grad_tile, above, below, left, right, left_branch, right_branch, gate_second, gate_first, near_hidden,
    bottle_first, v_second, p_first, rows_second, ends_second,
    keep, away, windows, grad_first,
    area, shifted, branch, grads, rows, ends,
):
    side, channels = grad_first.shape[0], grad_first.shape[2]
    first, second = FIRST_DILATION, SECOND_DILATION
    full, near = side + 2 * HALO, side + 2 * first
    small = grad_pre.shape[1]
    middle = slice(LEAD, LEAD + side)

    area[:, :LEAD] = jnp.zeros((full, LEAD, channels), F32)
    area[:, LEAD + side :] = jnp.zeros((full, area.shape[1] - LEAD - side, channels), F32)
    area[HALO : HALO + side, LEAD : LEAD + small] = grad_pre[...].astype(F32)
    area[:HALO, middle] = above[:HALO].astype(F32)
    area[HALO + side :, middle] = below[:HALO].astype(F32)
    area[:, LEAD - HALO : LEAD] = left[...].astype(F32)
    area[:, LEAD + side : LEAD + side + HALO] = right[...].astype(F32)
    branch[...] = jnp.zeros(branch.shape, F32)
    branch[first : first + side, first : first + side] = grad_tile[:, :side].astype(F32)
    branch[:first, first : first + side] = above[HALO:].astype(F32)
    branch[first + side :, first : first + side] = below[HALO:].astype(F32)
    branch[:, :first] = left_branch[...].astype(F32)
    branch[:, first + side : near] = right_branch[...].astype(F32)
    for b in (-1, 0, 1):
        at = LEAD - HALO + second * (1 - b)
        shifted[b + 1] = area[:, at : at + small].astype(BF16)
    grads[:, small:] = jnp.zeros((near, grads.shape[1] - small, channels), F32)

    def sections(step, _):
        top = step * 7
        size = 7 * small
        total = jnp.zeros((size, 2 * channels), F32)
        for a, b in TAPS:
            window = shifted[b + 1, pl.ds(top + second * (1 - a), 7)].reshape(size, channels)
            total = total + dot(window, v_second[tap(a, b)])
        here = pl.ds(top, 7)
        grad = branch[here, :small].reshape(size, channels)
        gate = gate_second[here].astype(F32).reshape(size, channels) > 0
        own = rounded(grad + jnp.where(gate, total[:, :channels], 0))
        other = rounded(grad + jnp.where(gate, total[:, channels:], 0))
        grad = ((own + other) * 0.5).astype(BF16)
        branch[here, :small] = grad.astype(F32).reshape(7, small, channels)
        gate = gate_first[here].astype(F32).reshape(size, channels) > 0
        grad = rounded(jnp.where(gate, dot(grad, p_first[...]), 0))
        grads[here, :small] = grad.reshape(7, small, channels)
        return 0

    lax.fori_loop(0, near // 7, sections, 0)
    for b in (-1, 0, 1):
        at = first * (1 - b)
        windows[b + 1] = grads[:, at : at + small].astype(BF16)
    part = branch[first : first + side, first : first + small]
    grad_first[...] = part[:, :side].astype(BF16)
    real = lax.broadcasted_iota(jnp.int32, part.shape, 1) < side
    part = jnp.where(real, part, 0).astype(BF16)
    grad = jnp.where(real, grads[first : first + side, first : first + small], 0)

    def hidden(a, b):
        return near_hidden[b, first * a : first * a + side]

    weight_sums(rows, ends, grad, hidden, bottle_first, part)

    first_core = lax.axis_index("segment") == 0
    count = rows.shape[0]
    for here, one, two in (
        (slice(0, count), rows[...], rows_second[...]),
        (slice(count, count + ends.shape[0]), ends[...], ends_second[...]),
    ):
        keep[here] = jnp.where(first_core, one, two)
        away[here] = jnp.where(first_core, two, one).astype(BF16)


def pair_kernel(keep, other, parts):
    devices, share = parts.shape[0], parts.shape[1] - 8
    total = keep[...] + other[...].astype(F32)
    count = keep.shape[0] - 16
    for j in range(devices):
        low, high = min(j * share, count), min((j + 1) * share, count)
        pieces = [total[low:high]] if low < high else []
        if high - low < share:
            pieces.append(jnp.zeros((share - (high - low), keep.shape[1]), F32))
        parts[j] = jnp.concatenate(pieces + [total[count : count + 8]]).astype(BF16)


def input_kernel(windows, grad_first, tile, v_first, out):
    side, channels = tile.shape[0], tile.shape[2]
    small = windows.shape[2]
    first = FIRST_DILATION

    def rows(step, _):
        top = step * 8
        total = jnp.zeros((8 * small, channels), F32)
        for a, b in TAPS:
            window = windows[b + 1, pl.ds(top + first * (1 - a), 8)].reshape(8 * small, channels)
            total = total + dot(window, v_first[tap(a, b)])
        here = pl.ds(top, 8)
        total = total.reshape(8, small, channels)[:, :side]
        total = jnp.where(tile[here].astype(F32) > 0, total, 0)
        out[here] = (grad_first[here].astype(F32) + total).astype(BF16)
        return 0

    lax.fori_loop(0, side // 8, rows, 0)


def total_kernel(scale, parts, rows, ends):
    share = rows.shape[1]
    total = jnp.sum(parts[...].astype(F32), axis=0) * scale
    rows[...] = jnp.broadcast_to(total[:share].astype(BF16)[None], rows.shape)
    ends[...] = total[share:]


def outputs_kernel(rows, ends, conv_gradient, bias_gradient, out_gradient):
    count, inner = conv_gradient.shape[0], out_gradient.shape[0]
    conv_gradient[...] = rows[:count].astype(F32)
    out_gradient[...] = rows[count : count + inner].astype(F32)
    bias_gradient[...] = ends[:1, :inner]


def call(kernel, name, outs, scratch, flops, *operands):
    outs = [jax.ShapeDtypeStruct(shape, dtype) for shape, dtype in outs]
    moved = sum(x.size * x.dtype.itemsize for x in list(operands) + outs)
    return pl.pallas_call(
        kernel,
        name=name,
        out_shape=outs,
        scratch_shapes=[pltpu.VMEM(shape, dtype) for shape, dtype in scratch],
        cost_estimate=pl.CostEstimate(flops=flops, bytes_accessed=moved, transcendentals=0),
        compiler_params=pltpu.CompilerParams(vmem_limit_bytes=40 * 1024 * 1024),
    )(*operands)


def local(activations, cotangent, conv_weight, conv_bias, out_weight):
    side, channels, inner = activations.shape[1], activations.shape[3], conv_weight.shape[3]
    number = lax.axis_size("row")
    first, second = FIRST_DILATION, SECOND_DILATION
    full, span, near = side + 2 * HALO, side + 2 * second, side + 2 * first
    wide, small = up16(span), up16(near)
    tile = bring(activations[0])

    above = bring(activations[0, side - HALO :], 1)
    below = bring(activations[0, :HALO], -1)

    def columns(low, high):
        strip = jnp.concatenate([above[:, low:high], tile[:, low:high], below[:, low:high]])
        return jnp.swapaxes(strip, 0, 1)

    left = send(columns(side - HALO, side), lambda r, c: (r, c + 1))
    right = send(columns(0, HALO), lambda r, c: (r, c - 1))
    late = bring(cotangent[0])

    _, conv_bias = lax.optimization_barrier((above, conv_bias))
    bias_rows = jnp.pad(conv_bias, ((0, 15), (0, channels - inner)))
    packed = jnp.concatenate(
        [jnp.swapaxes(conv_weight[0], 1, 2).reshape(9 * inner, channels), out_weight[0], bias_rows]
    )
    others = lax.ppermute(packed, "segment", [(0, 1), (1, 0)])
    w_first, w_second, v_second, v_first, p_first, p_second, p_back, b_first, b_second = call(
        weights_kernel,
        "weights",
        [
            ((9 * channels, inner), BF16),
            ((9 * channels, 2 * inner), BF16),
            ((9, 2 * inner, 2 * channels), BF16),
            ((9, 2 * inner, channels), BF16),
            ((inner, channels), BF16),
            ((channels, 2 * inner), BF16),
            ((channels, 2 * inner), BF16),
            ((1, inner), F32),
            ((1, 2 * inner), F32),
        ],
        [((2,) + packed.shape, BF16)],
        packed.size,
        *(packed, others),
    )

    kept, gate_first, bottle_first, near_hidden = call(
        own_kernel,
        "own_branch",
        [
            ((span + side, span, channels), BF16),
            ((near, small, channels), BF16),
            ((side, small, inner), BF16),
            ((3, near, small, channels), BF16),
        ],
        [
            ((full, LEAD + up16(side + LEAD), channels), F32),
            ((full, wide, 2 * channels), BF16),
            ((full + first, wide, 2 * channels), BF16),
            ((span, wide, inner), F32),
        ],
        span * wide * channels * inner * 20,
        *(tile, above, below, jnp.swapaxes(left, 0, 1), jnp.swapaxes(right, 0, 1), late),
        *(w_first, b_first, p_first),
    )
    other = send(kept, lambda r, c: (c, r))
    gate_second, hidden_pairs, hidden_last, bottle_second, grad_tile, grad_pre, strip_above, strip_below = call(
        middle_kernel,
        "middle",
        [
            ((near, small, channels), BF16),
            ((span, small, 2 * channels), BF16),
            ((span + second, small, 2 * channels), BF16),
            ((side, small, inner), BF16),
            ((side, small, channels), BF16),
            ((side, small, 2 * inner), BF16),
            ((HALO + first, side, channels), BF16),
            ((HALO + first, side, channels), BF16),
        ],
        [
            ((span, wide, channels), F32),
            ((side, small, channels), F32),
            ((side, small, 2 * inner), F32),
        ],
        24 * side * small * channels * 2 * inner,
        *(kept, other, w_second, b_second, p_second),
    )

    above = send(strip_below, lambda r, c: (r + 1, c))
    below = send(strip_above, lambda r, c: (r - 1, c))
    rows_second, ends_second = call(
        second_sums_kernel,
        "second_sums",
        [((10 * inner, channels), F32), ((16, channels), F32)],
        [],
        20 * side * small * channels * inner,
        *(grad_pre, hidden_pairs, hidden_last, bottle_second, grad_tile),
    )

    def columns(low, high, low_branch, high_branch):
        grads = jnp.concatenate([above[:HALO, low:high], grad_pre[:, low:high], below[:HALO, low:high]])
        here = slice(low_branch, high_branch)
        branches = jnp.concatenate([above[HALO:, here], grad_tile[:, here], below[HALO:, here]])
        branches = jnp.pad(branches, ((second, second), (0, 0), (0, 0)))
        return jnp.swapaxes(jnp.concatenate([grads, branches], axis=1), 0, 1)

    left = send(columns(side - HALO, side, side - first, side), lambda r, c: (r, c + 1))
    right = send(columns(0, HALO, 0, first), lambda r, c: (r, c - 1))
    left, right = jnp.swapaxes(left, 0, 1), jnp.swapaxes(right, 0, 1)

    devices = number * number
    share = -(-10 * inner // (8 * devices)) * 8
    keep, away, windows, grad_first = call(
        backward_kernel,
        "backward",
        [
            ((10 * inner + 16, channels), F32),
            ((10 * inner + 16, channels), BF16),
            ((3, near, small, channels), BF16),
            ((side, side, channels), BF16),
        ],
        [
            ((full, LEAD + up16(side + HALO + first), channels), F32),
            ((3, full, small, channels), BF16),
            ((near, small + 16, channels), F32),
            ((near, small + 16, channels), F32),
            ((10 * inner, channels), F32),
            ((16, channels), F32),
        ],
        36 * near * small * channels * channels,
        *(grad_pre, grad_tile, above, below, left[:, :HALO], right[:, :HALO]),
        *(left[second : second + near, HALO:], right[second : second + near, HALO:]),
        *(gate_second, gate_first, near_hidden, bottle_first, v_second, p_back, rows_second, ends_second),
    )

    (parts,) = call(
        pair_kernel,
        "pair",
        [((devices, share + 8, channels), BF16)],
        [],
        keep.size,
        *(keep, lax.ppermute(away, "segment", [(0, 1), (1, 0)])),
    )
    parts = lax.all_to_all(parts, GRID, 0, 0, tiled=True)
    (input_gradient,) = call(
        input_kernel,
        "input",
        [((side, side, channels), BF16)],
        [],
        18 * side * small * channels * channels,
        *(windows, grad_first, tile, v_first),
    )
    input_gradient = take_back(input_gradient)
    cells = lax.axis_size("segment") * (side * number) * (side * number)
    rows, ends = call(
        functools.partial(total_kernel, float(cells) ** -0.5),
        "total",
        [((devices, share, channels), BF16), ((8, channels), F32)],
        [],
        parts.size,
        parts,
    )
    rows, _ = lax.optimization_barrier((rows, input_gradient))
    rows = lax.all_to_all(rows, GRID, 0, 0, tiled=True).reshape(devices * share, channels)
    conv_gradient, bias_gradient, out_gradient = call(
        outputs_kernel,
        "outputs",
        [((9 * inner, channels), F32), ((1, inner), F32), ((inner, channels), F32)],
        [],
        rows.size,
        *(rows, ends),
    )
    conv_gradient = jnp.swapaxes(conv_gradient.reshape(1, 9, inner, channels), 2, 3)
    return (input_gradient[None], conv_gradient, bias_gradient, out_gradient[None])


def solution(mesh):
    in_specs = (
        P("segment", "row", "col", None),
        P("segment", "row", "col", None),
        P("segment", None, None, None),
        P("segment", None),
        P("segment", None, None),
    )
    out_specs = (
        P("segment", "row", "col", None),
        P("segment", None, None, None),
        P("segment", None),
        P("segment", None, None),
    )
    return jax.shard_map(local, mesh=mesh, in_specs=in_specs, out_specs=out_specs, check_vma=False)
```

```python
import functools

import jax
import jax.numpy as jnp
from jax import lax
from jax.experimental import pallas as pl
from jax.experimental.pallas import tpu as pltpu
from jax.sharding import PartitionSpec as P

FIRST_DILATION = 2
SECOND_DILATION = 8
HALO = FIRST_DILATION + SECOND_DILATION
GRID = ("row", "col")
ALL = ("segment",) + GRID
ORDER = [0, 1, 3, 4, 6, 7, 2, 5, 8]
TAPS = [(a, b) for a in (-1, 0, 1) for b in (-1, 0, 1)]
LEAD = 16
F32, BF16 = jnp.float32, jnp.bfloat16


def tap(a, b):
    return 3 * (a + 1) + (b + 1)


def dot(x, y):
    return jnp.dot(x, y, preferred_element_type=F32)


def rounded(x):
    return x.astype(BF16).astype(F32)


def up16(n):
    return -(-n // 16) * 16


def home(batch, r, c):
    number = lax.axis_size("row")
    core, row, col = (batch, r, c) if r == c else (int(r > c), r, c)
    if r != c and (r < c) == (batch == 1):
        row, col = c, r
    return (core * number + row) * number + col


def place():
    row, col = lax.axis_index("row"), lax.axis_index("col")
    low, high = jnp.minimum(row, col), jnp.maximum(row, col)
    upper = lax.axis_index("segment") == 0
    return jnp.where(upper, low, high), jnp.where(upper, high, low)


def permute(x, pair):
    number = lax.axis_size("row")
    tiles = [(m, r, c) for m in range(lax.axis_size("segment")) for r in range(number) for c in range(number)]
    pairs = [pair(*tile) for tile in tiles]
    return lax.ppermute(x, ALL, [found for found in pairs if found is not None])


def stored(batch, r, c):
    number = lax.axis_size("row")
    return (batch * number + r) * number + c


def bring(x, down=0):
    number = lax.axis_size("row")

    def pair(batch, r, c):
        if 0 <= r + down < number:
            return stored(batch, r, c), home(batch, r + down, c)

    return permute(x, pair)


def take_back(x):
    return permute(x, lambda m, r, c: (home(m, r, c), stored(m, r, c)))


def send(x, to):
    number = lax.axis_size("row")

    def pair(batch, r, c):
        row, col = to(r, c)
        if 0 <= row < number and 0 <= col < number:
            return home(batch, r, c), home(batch, row, col)

    return permute(x, pair)


def inside(shape, side, width, top):
    number = lax.axis_size("row") * side
    rows = lax.broadcasted_iota(jnp.int32, shape, 0) + top - width
    cols = lax.broadcasted_iota(jnp.int32, shape, 1) - width
    row, col = place()
    at_row = row * side + rows
    at_col = col * side + cols
    return (at_row >= 0) & (at_row < number) & (at_col >= 0) & (at_col < number) & (cols < side + width)


def paired(source, starts, width, dilation, pairs, last, change):
    lanes = source.shape[2]
    low, high = slice(0, lanes), slice(lanes, 2 * lanes)

    def step(k, _):
        rows, lower = pl.ds(4 * k, 4), pl.ds(4 * k + dilation, 4)
        window = [change(source[rows, at : at + width]).astype(BF16) for at in starts]
        pairs[rows, :, low] = window[0]
        pairs[rows, :, high] = window[1]
        last[lower, :, low] = window[2]
        last[rows, :, high] = window[2]
        return 0

    lax.fori_loop(0, source.shape[0] // 4, step, 0)


def taps_sum(pairs, last, top, rows, dilation, weights):
    width, lanes = pairs.shape[1], pairs.shape[2] // 2
    size = rows * width
    total = None
    for k in range(5):
        if k < 3:
            window = pairs[pl.ds(top + dilation * k, rows)]
        elif k == 3:
            window = last[pl.ds(top + dilation, rows)]
        else:
            window = last[pl.ds(top + 3 * dilation, rows), :, :lanes]
        weight = weights[2 * lanes * k : min(2 * lanes * (k + 1), 9 * lanes)]
        term = dot(window.reshape(size, window.shape[2]), weight)
        total = term if total is None else total + term
    return total


def positive(x):
    return jnp.maximum(x, 0)


def assemble(area, tile, above, below, left, right):
    side = tile.shape[0]
    full, wide, channels = area.shape
    middle = slice(LEAD, LEAD + side)
    area[:, :LEAD] = jnp.zeros((full, LEAD, channels), F32)
    area[:, LEAD + side :] = jnp.zeros((full, wide - LEAD - side, channels), F32)
    area[HALO : HALO + side, middle] = tile
    area[:HALO, middle] = above[:HALO].astype(F32)
    area[HALO + side :, middle] = below[:HALO].astype(F32)
    area[:, LEAD - HALO : LEAD] = left[...].astype(F32)
    area[:, LEAD + side : LEAD + side + HALO] = right[...].astype(F32)


def first_branch(area, pairs, last, weights, bias, proj, store):
    full, wide = pairs.shape[:2]
    start = LEAD - SECOND_DILATION
    starts = [start + FIRST_DILATION * b for b in (-1, 0, 1)]
    paired(area, starts, wide, FIRST_DILATION, pairs, last, positive)

    def rows(step, _):
        top = step * 8
        pre = taps_sum(pairs, last, top, 8, FIRST_DILATION, weights) + bias[...]
        branch = dot(positive(pre).astype(BF16), proj[...])
        inputs = area[pl.ds(top + FIRST_DILATION, 8), start : start + wide]
        branch = rounded(inputs + branch.reshape(inputs.shape))
        store(top, pre.reshape(8, wide, pre.shape[1]), branch)
        return 0

    lax.fori_loop(0, (full - 2 * FIRST_DILATION) // 8, rows, 0)


def own_kernel(
    brought, above, below, left, right, weights, bias, proj,
    swapped, gate_first, bottle_first, near_hidden,
    area, pairs, last, pre,
):
    side, first, second, inner = brought.shape[1], FIRST_DILATION, SECOND_DILATION, bias.shape[1]
    near, small = gate_first.shape[:2]
    span = side + 2 * second
    assemble(area, brought[:side].astype(F32), above, below, left, right)

    def store(top, pre_act, branch):
        pre[pl.ds(top, 8)] = pre_act
        swapped[pl.ds(top, 8)] = branch[:, :span].astype(BF16)

    first_branch(area, pairs, last, weights, bias, proj, store)
    swapped[span:, :side] = brought[side:]
    for b in (-1, 0, 1):
        at = LEAD + first * b
        near_hidden[b + 1] = positive(area[HALO - first : HALO + side + first, at : at + small]).astype(BF16)
    edge = second - first
    part = pre[edge : edge + near, edge : edge + small]
    alive = (part > 0) & inside(part.shape, side, first, 0)
    gate_first[:, :, :inner] = jnp.where(alive, 1.0, 0.0).astype(BF16)
    gate_first[:, :, inner:] = jnp.zeros((near, small, gate_first.shape[2] - inner), BF16)
    bottle_first[...] = positive(pre[second : second + side, second : second + small]).astype(BF16)


def middle_kernel(
    kept, other, w_second, b_second, p_second,
    gate_second, hidden_pairs, hidden_last, bottle_second, grad_tile, grad_pre, above, below,
    current, padded, pre_second,
):
    side, channels, span = above.shape[1], kept.shape[2], kept.shape[1]
    first, second, inner = FIRST_DILATION, SECOND_DILATION, bottle_second.shape[2]
    near, small = gate_second.shape[:2]
    turned = jnp.swapaxes(other[:span].astype(F32), 0, 1)
    sym = rounded((kept[:span].astype(F32) + turned) * 0.5)
    current[:, :span] = jnp.where(inside(sym.shape, side, second, 0), sym, 0)
    current[:, span:] = jnp.zeros((span, current.shape[1] - span, channels), F32)
    edge = second - first
    part = current[edge : edge + near, edge : edge + small]
    gate_second[...] = jnp.where(part > 0, 1.0, 0.0).astype(BF16)
    paired(current, [0, second, 2 * second], small, second, hidden_pairs, hidden_last, positive)

    def rows(step, _):
        top = step * 8
        total = taps_sum(hidden_pairs, hidden_last, top, 8, second, w_second) + b_second[...]
        pre_second[pl.ds(top, 8)] = total.reshape(8, small, total.shape[1])
        return 0

    lax.fori_loop(0, side // 8, rows, 0)
    bottle_second[...] = positive(pre_second[:, :, :inner]).astype(BF16)

    turned = jnp.swapaxes(other[span:, :side].astype(F32), 0, 1)
    padded[:, side:] = jnp.zeros((side, small - side, channels), F32)
    padded[:, :side] = rounded((kept[span:, :side].astype(F32) + turned) * 0.5)
    branch = padded[...].astype(BF16)
    grad_tile[...] = branch
    grad = dot(branch.reshape(side * small, channels), p_second[...]).reshape(side, small, 2 * inner)
    grad = jnp.where(pre_second[...] > 0, grad, 0)
    grad_pre[...] = grad.astype(BF16)
    grad, branch = grad[:, :side].astype(BF16), padded[:, :side].astype(BF16)
    above[:HALO], above[HALO:] = grad[:HALO], branch[:first]
    below[:HALO], below[HALO:] = grad[side - HALO :], branch[side - first :]


def weight_sums(rows, ends, grad_pre, hidden, bottle, grad_tile):
    side, small, lanes = grad_pre.shape
    inner = bottle.shape[2]
    size = side * small
    flat = grad_pre.reshape(size, lanes)
    turned = flat.T[:inner].astype(BF16)
    for a in range(3):
        b = 0
        while b < 3:
            window = hidden(a, b)
            grads = dot(turned, window.reshape(size, window.shape[2]))
            for at in range(0, window.shape[2], grad_tile.shape[2]):
                rows[(3 * a + b) * inner : (3 * a + b + 1) * inner] = grads[:, at : at + grad_tile.shape[2]]
                b += 1
    turned = bottle[...].reshape(size, inner).astype(F32).T.astype(BF16)
    rows[9 * inner : 10 * inner] = dot(turned, grad_tile.reshape(size, grad_tile.shape[2]))
    ends[...] = jnp.zeros(ends.shape, F32)
    ends[:, :lanes] = jnp.broadcast_to(jnp.sum(flat, axis=0, keepdims=True), (ends.shape[0], lanes))


def weights_kernel(
    mine, theirs, w_first, w_second, v_second, v_first, p_first, p_second, p_back, b_first, b_second, packed
):
    inner, channels = p_first.shape
    section = lax.axis_index("segment")
    packed[section] = mine[...]
    packed[1 - section] = theirs[...]

    def conv(section, k):
        return packed[section, k * inner : (k + 1) * inner]

    def turned(x):
        return x.astype(F32).T.astype(BF16)

    zero = jnp.zeros((inner, channels), BF16)
    for at, k in enumerate(ORDER):
        here = slice(at * channels, (at + 1) * channels)
        own, other = conv(1, k), conv(1, 3 * (k % 3) + k // 3)
        w_first[here] = turned(conv(0, k))
        w_second[here] = turned(jnp.concatenate([own, other], axis=0))
        v_second[k, :inner, :channels], v_second[k, :inner, channels:] = own, zero
        v_second[k, inner:, :channels], v_second[k, inner:, channels:] = zero, other
        v_first[k, :inner], v_first[k, inner:] = conv(0, k), zero
    p_first[...] = conv(0, 9)
    p_second[...] = turned(jnp.concatenate([conv(1, 9), conv(1, 9)], axis=0))
    p_back[...] = turned(jnp.concatenate([conv(0, 9), zero], axis=0))
    b_first[...] = packed[0, 10 * inner :].astype(F32)[:1, :inner]
    bias = packed[1, 10 * inner :].astype(F32)[:1, :inner]
    b_second[...] = jnp.concatenate([bias, bias], axis=1)


def second_sums_kernel(grad_pre, pairs, last, bottle, grad_tile, rows, ends):
    side = grad_pre.shape[0]
    channels = grad_tile.shape[2]

    def hidden(a, b):
        top = SECOND_DILATION * a
        if b == 0:
            return pairs[top : top + side]
        return last[top + SECOND_DILATION : top + SECOND_DILATION + side, :, :channels]

    weight_sums(rows, ends, grad_pre[...].astype(F32), hidden, bottle, grad_tile[...])


def backward_kernel(
    grad_pre, grad_tile, above, below, left, right, left_branch, right_branch, gate_second, gate_first, near_hidden,
    bottle_first, v_second, p_first, rows_second, ends_second,
    keep, away, windows, grad_first,
    area, shifted, branch, grads, rows, ends,
):
    side, channels = grad_first.shape[0], grad_first.shape[2]
    first, second = FIRST_DILATION, SECOND_DILATION
    full, near = side + 2 * HALO, side + 2 * first
    small = grad_pre.shape[1]
    middle = slice(LEAD, LEAD + side)

    area[:, :LEAD] = jnp.zeros((full, LEAD, channels), F32)
    area[:, LEAD + side :] = jnp.zeros((full, area.shape[1] - LEAD - side, channels), F32)
    area[HALO : HALO + side, LEAD : LEAD + small] = grad_pre[...].astype(F32)
    area[:HALO, middle] = above[:HALO].astype(F32)
    area[HALO + side :, middle] = below[:HALO].astype(F32)
    area[:, LEAD - HALO : LEAD] = left[...].astype(F32)
    area[:, LEAD + side : LEAD + side + HALO] = right[...].astype(F32)
    branch[...] = jnp.zeros(branch.shape, F32)
    branch[first : first + side, first : first + side] = grad_tile[:, :side].astype(F32)
    branch[:first, first : first + side] = above[HALO:].astype(F32)
    branch[first + side :, first : first + side] = below[HALO:].astype(F32)
    branch[:, :first] = left_branch[...].astype(F32)
    branch[:, first + side : near] = right_branch[...].astype(F32)
    for b in (-1, 0, 1):
        at = LEAD - HALO + second * (1 - b)
        shifted[b + 1] = area[:, at : at + small].astype(BF16)
    grads[:, small:] = jnp.zeros((near, grads.shape[1] - small, channels), F32)

    def sections(step, _):
        top = step * 7
        size = 7 * small
        total = jnp.zeros((size, 2 * channels), F32)
        for a, b in TAPS:
            window = shifted[b + 1, pl.ds(top + second * (1 - a), 7)].reshape(size, channels)
            total = total + dot(window, v_second[tap(a, b)])
        here = pl.ds(top, 7)
        grad = branch[here, :small].reshape(size, channels)
        gate = gate_second[here].astype(F32).reshape(size, channels) > 0
        own = rounded(grad + jnp.where(gate, total[:, :channels], 0))
        other = rounded(grad + jnp.where(gate, total[:, channels:], 0))
        grad = ((own + other) * 0.5).astype(BF16)
        branch[here, :small] = grad.astype(F32).reshape(7, small, channels)
        gate = gate_first[here].astype(F32).reshape(size, channels) > 0
        grad = rounded(jnp.where(gate, dot(grad, p_first[...]), 0))
        grads[here, :small] = grad.reshape(7, small, channels)
        return 0

    lax.fori_loop(0, near // 7, sections, 0)
    for b in (-1, 0, 1):
        at = first * (1 - b)
        windows[b + 1] = grads[:, at : at + small].astype(BF16)
    part = branch[first : first + side, first : first + small]
    grad_first[...] = part[:, :side].astype(BF16)
    real = lax.broadcasted_iota(jnp.int32, part.shape, 1) < side
    part = jnp.where(real, part, 0).astype(BF16)
    grad = jnp.where(real, grads[first : first + side, first : first + small], 0)

    def hidden(a, b):
        return near_hidden[b, first * a : first * a + side]

    weight_sums(rows, ends, grad, hidden, bottle_first, part)

    first_core = lax.axis_index("segment") == 0
    count = rows.shape[0]
    for here, one, two in (
        (slice(0, count), rows[...], rows_second[...]),
        (slice(count, count + ends.shape[0]), ends[...], ends_second[...]),
    ):
        keep[here] = jnp.where(first_core, one, two)
        away[here] = jnp.where(first_core, two, one).astype(BF16)


def pair_kernel(keep, other, parts):
    devices, share = parts.shape[0], parts.shape[1] - 8
    total = keep[...] + other[...].astype(F32)
    count = keep.shape[0] - 16
    for j in range(devices):
        low, high = min(j * share, count), min((j + 1) * share, count)
        pieces = [total[low:high]] if low < high else []
        if high - low < share:
            pieces.append(jnp.zeros((share - (high - low), keep.shape[1]), F32))
        parts[j] = jnp.concatenate(pieces + [total[count : count + 8]]).astype(BF16)


def input_kernel(windows, grad_first, brought, v_first, out):
    side, channels = out.shape[0], out.shape[2]
    small = windows.shape[2]
    first = FIRST_DILATION

    def rows(step, _):
        top = step * 8
        total = jnp.zeros((8 * small, channels), F32)
        for a, b in TAPS:
            window = windows[b + 1, pl.ds(top + first * (1 - a), 8)].reshape(8 * small, channels)
            total = total + dot(window, v_first[tap(a, b)])
        here = pl.ds(top, 8)
        total = total.reshape(8, small, channels)[:, :side]
        total = jnp.where(brought[here].astype(F32) > 0, total, 0)
        out[here] = (grad_first[here].astype(F32) + total).astype(BF16)
        return 0

    lax.fori_loop(0, side // 8, rows, 0)


def total_kernel(scale, parts, rows, ends):
    share = rows.shape[1]
    total = jnp.sum(parts[...].astype(F32), axis=0) * scale
    rows[...] = jnp.broadcast_to(total[:share].astype(BF16)[None], rows.shape)
    ends[...] = total[share:]


def outputs_kernel(rows, ends, conv_gradient, bias_gradient, out_gradient):
    count, inner = conv_gradient.shape[0], out_gradient.shape[0]
    conv_gradient[...] = rows[:count].astype(F32)
    out_gradient[...] = rows[count : count + inner].astype(F32)
    bias_gradient[...] = ends[:1, :inner]


def call(kernel, name, outs, scratch, flops, *operands):
    outs = [jax.ShapeDtypeStruct(shape, dtype) for shape, dtype in outs]
    moved = sum(x.size * x.dtype.itemsize for x in list(operands) + outs)
    return pl.pallas_call(
        kernel,
        name=name,
        out_shape=outs,
        scratch_shapes=[pltpu.VMEM(shape, dtype) for shape, dtype in scratch],
        cost_estimate=pl.CostEstimate(flops=flops, bytes_accessed=moved, transcendentals=0),
        compiler_params=pltpu.CompilerParams(vmem_limit_bytes=40 * 1024 * 1024),
    )(*operands)


def local(activations, cotangent, conv_weight, conv_bias, out_weight):
    side, channels, inner = activations.shape[1], activations.shape[3], conv_weight.shape[3]
    number = lax.axis_size("row")
    first, second = FIRST_DILATION, SECOND_DILATION
    full, span, near = side + 2 * HALO, side + 2 * second, side + 2 * first
    wide, small = up16(span), up16(near)

    brought = bring(jnp.concatenate([activations[0], cotangent[0]]))
    tile = brought[:side]
    above = bring(activations[0, side - HALO :], 1)
    below = bring(activations[0, :HALO], -1)

    def columns(low, high):
        strip = jnp.pad(jnp.swapaxes(tile[:, low:high], 0, 1), ((0, 0), (HALO, HALO), (0, 0)))
        strip = lax.optimization_barrier(strip)
        strip = lax.dynamic_update_slice(strip, jnp.swapaxes(above[:, low:high], 0, 1), (0, 0, 0))
        return lax.dynamic_update_slice(strip, jnp.swapaxes(below[:, low:high], 0, 1), (0, HALO + side, 0))

    left = send(columns(side - HALO, side), lambda r, c: (r, c + 1))
    right = send(columns(0, HALO), lambda r, c: (r, c - 1))

    bias_rows = jnp.pad(conv_bias, ((0, 15), (0, channels - inner)))
    packed = jnp.concatenate(
        [jnp.swapaxes(conv_weight[0], 1, 2).reshape(9 * inner, channels), out_weight[0], bias_rows]
    )
    others = lax.ppermute(packed, "segment", [(0, 1), (1, 0)])
    w_first, w_second, v_second, v_first, p_first, p_second, p_back, b_first, b_second = call(
        weights_kernel,
        "weights",
        [
            ((9 * channels, inner), BF16),
            ((9 * channels, 2 * inner), BF16),
            ((9, 2 * inner, 2 * channels), BF16),
            ((9, 2 * inner, channels), BF16),
            ((inner, channels), BF16),
            ((channels, 2 * inner), BF16),
            ((channels, 2 * inner), BF16),
            ((1, inner), F32),
            ((1, 2 * inner), F32),
        ],
        [((2,) + packed.shape, BF16)],
        packed.size,
        *(packed, others),
    )

    kept, gate_first, bottle_first, near_hidden = call(
        own_kernel,
        "own_branch",
        [
            ((span + side, span, channels), BF16),
            ((near, small, channels), BF16),
            ((side, small, inner), BF16),
            ((3, near, small, channels), BF16),
        ],
        [
            ((full, LEAD + up16(side + LEAD), channels), F32),
            ((full, wide, 2 * channels), BF16),
            ((full + first, wide, 2 * channels), BF16),
            ((span, wide, inner), F32),
        ],
        span * wide * channels * inner * 20,
        *(brought, above, below, jnp.swapaxes(left, 0, 1), jnp.swapaxes(right, 0, 1)),
        *(w_first, b_first, p_first),
    )
    other = send(kept, lambda r, c: (c, r))
    gate_second, hidden_pairs, hidden_last, bottle_second, grad_tile, grad_pre, strip_above, strip_below = call(
        middle_kernel,
        "middle",
        [
            ((near, small, channels), BF16),
            ((span, small, 2 * channels), BF16),
            ((span + second, small, 2 * channels), BF16),
            ((side, small, inner), BF16),
            ((side, small, channels), BF16),
            ((side, small, 2 * inner), BF16),
            ((HALO + first, side, channels), BF16),
            ((HALO + first, side, channels), BF16),
        ],
        [
            ((span, wide, channels), F32),
            ((side, small, channels), F32),
            ((side, small, 2 * inner), F32),
        ],
        24 * side * small * channels * 2 * inner,
        *(kept, other, w_second, b_second, p_second),
    )

    above = send(strip_below, lambda r, c: (r + 1, c))
    below = send(strip_above, lambda r, c: (r - 1, c))
    rows_second, ends_second = call(
        second_sums_kernel,
        "second_sums",
        [((10 * inner, channels), F32), ((16, channels), F32)],
        [],
        20 * side * small * channels * inner,
        *(grad_pre, hidden_pairs, hidden_last, bottle_second, grad_tile),
    )

    def columns(low, high, low_branch, high_branch):
        grads = jnp.concatenate([above[:HALO, low:high], grad_pre[:, low:high], below[:HALO, low:high]])
        here = slice(low_branch, high_branch)
        branches = jnp.concatenate([above[HALO:, here], grad_tile[:, here], below[HALO:, here]])
        branches = jnp.pad(branches, ((second, second), (0, 0), (0, 0)))
        return jnp.swapaxes(jnp.concatenate([grads, branches], axis=1), 0, 1)

    left = send(columns(side - HALO, side, side - first, side), lambda r, c: (r, c + 1))
    right = send(columns(0, HALO, 0, first), lambda r, c: (r, c - 1))
    left, right = jnp.swapaxes(left, 0, 1), jnp.swapaxes(right, 0, 1)

    devices = number * number
    share = -(-10 * inner // (8 * devices)) * 8
    keep, away, windows, grad_first = call(
        backward_kernel,
        "backward",
        [
            ((10 * inner + 16, channels), F32),
            ((10 * inner + 16, channels), BF16),
            ((3, near, small, channels), BF16),
            ((side, side, channels), BF16),
        ],
        [
            ((full, LEAD + up16(side + HALO + first), channels), F32),
            ((3, full, small, channels), BF16),
            ((near, small + 16, channels), F32),
            ((near, small + 16, channels), F32),
            ((10 * inner, channels), F32),
            ((16, channels), F32),
        ],
        36 * near * small * channels * channels,
        *(grad_pre, grad_tile, above, below, left[:, :HALO], right[:, :HALO]),
        *(left[second : second + near, HALO:], right[second : second + near, HALO:]),
        *(gate_second, gate_first, near_hidden, bottle_first, v_second, p_back, rows_second, ends_second),
    )

    (input_gradient,) = call(
        input_kernel,
        "input",
        [((side, side, channels), BF16)],
        [],
        18 * side * small * channels * channels,
        *(windows, grad_first, brought, v_first),
    )
    other = lax.ppermute(away, "segment", [(0, 1), (1, 0)])
    other, input_gradient = lax.optimization_barrier((other, input_gradient))
    (parts,) = call(
        pair_kernel,
        "pair",
        [((devices, share + 8, channels), BF16)],
        [],
        keep.size,
        *(keep, other),
    )
    parts = lax.all_to_all(parts, GRID, 0, 0, tiled=True)
    input_gradient = take_back(input_gradient)
    cells = lax.axis_size("segment") * (side * number) * (side * number)
    rows, ends = call(
        functools.partial(total_kernel, float(cells) ** -0.5),
        "total",
        [((devices, share, channels), BF16), ((8, channels), F32)],
        [],
        parts.size,
        parts,
    )
    rows, _ = lax.optimization_barrier((rows, input_gradient))
    rows = lax.all_to_all(rows, GRID, 0, 0, tiled=True).reshape(devices * share, channels)
    conv_gradient, bias_gradient, out_gradient = call(
        outputs_kernel,
        "outputs",
        [((9 * inner, channels), F32), ((1, inner), F32), ((inner, channels), F32)],
        [],
        rows.size,
        *(rows, ends),
    )
    conv_gradient = jnp.swapaxes(conv_gradient.reshape(1, 9, inner, channels), 2, 3)
    return (input_gradient[None], conv_gradient, bias_gradient, out_gradient[None])


def solution(mesh):
    in_specs = (
        P("segment", "row", "col", None),
        P("segment", "row", "col", None),
        P("segment", None, None, None),
        P("segment", None),
        P("segment", None, None),
    )
    out_specs = (
        P("segment", "row", "col", None),
        P("segment", None, None, None),
        P("segment", None),
        P("segment", None, None),
    )
    return jax.shard_map(local, mesh=mesh, in_specs=in_specs, out_specs=out_specs, check_vma=False)
```

```python
import functools

import jax
import jax.numpy as jnp
from jax import lax
from jax.experimental import pallas as pl
from jax.experimental.pallas import tpu as pltpu
from jax.sharding import PartitionSpec as P

FIRST_DILATION = 2
SECOND_DILATION = 8
HALO = FIRST_DILATION + SECOND_DILATION
GRID = ("row", "col")
ALL = ("segment",) + GRID
ORDER = [0, 1, 3, 4, 6, 7, 2, 5, 8]
TAPS = [(a, b) for a in (-1, 0, 1) for b in (-1, 0, 1)]
LEAD = 16
F32, BF16 = jnp.float32, jnp.bfloat16


def tap(a, b):
    return 3 * (a + 1) + (b + 1)


def dot(x, y):
    return jnp.dot(x, y, preferred_element_type=F32)


def rounded(x):
    return x.astype(BF16).astype(F32)


def up16(n):
    return -(-n // 16) * 16


def home(batch, r, c):
    number = lax.axis_size("row")
    core, row, col = (batch, r, c) if r == c else (int(r > c), r, c)
    if r != c and (r < c) == (batch == 1):
        row, col = c, r
    return (core * number + row) * number + col


def place():
    row, col = lax.axis_index("row"), lax.axis_index("col")
    low, high = jnp.minimum(row, col), jnp.maximum(row, col)
    upper = lax.axis_index("segment") == 0
    return jnp.where(upper, low, high), jnp.where(upper, high, low)


def permute(x, pair):
    number = lax.axis_size("row")
    tiles = [(m, r, c) for m in range(lax.axis_size("segment")) for r in range(number) for c in range(number)]
    pairs = [pair(*tile) for tile in tiles]
    return lax.ppermute(x, ALL, [found for found in pairs if found is not None])


def stored(batch, r, c):
    number = lax.axis_size("row")
    return (batch * number + r) * number + c


def bring(x, down=0):
    number = lax.axis_size("row")

    def pair(batch, r, c):
        if 0 <= r + down < number:
            return stored(batch, r, c), home(batch, r + down, c)

    return permute(x, pair)


def take_back(x):
    return permute(x, lambda m, r, c: (home(m, r, c), stored(m, r, c)))


def send(x, to):
    number = lax.axis_size("row")

    def pair(batch, r, c):
        row, col = to(r, c)
        if 0 <= row < number and 0 <= col < number:
            return home(batch, r, c), home(batch, row, col)

    return permute(x, pair)


def inside(shape, side, width, top):
    number = lax.axis_size("row") * side
    rows = lax.broadcasted_iota(jnp.int32, shape, 0) + top - width
    cols = lax.broadcasted_iota(jnp.int32, shape, 1) - width
    row, col = place()
    at_row = row * side + rows
    at_col = col * side + cols
    return (at_row >= 0) & (at_row < number) & (at_col >= 0) & (at_col < number) & (cols < side + width)


def paired(source, starts, width, dilation, pairs, last, change):
    lanes = source.shape[2]
    low, high = slice(0, lanes), slice(lanes, 2 * lanes)

    def step(k, _):
        rows, lower = pl.ds(4 * k, 4), pl.ds(4 * k + dilation, 4)
        window = [change(source[rows, at : at + width]).astype(BF16) for at in starts]
        pairs[rows, :, low] = window[0]
        pairs[rows, :, high] = window[1]
        last[lower, :, low] = window[2]
        last[rows, :, high] = window[2]
        return 0

    lax.fori_loop(0, source.shape[0] // 4, step, 0)


def taps_sum(pairs, last, top, rows, dilation, weights):
    width, lanes = pairs.shape[1], pairs.shape[2] // 2
    size = rows * width
    total = None
    for k in range(5):
        if k < 3:
            window = pairs[pl.ds(top + dilation * k, rows)]
        elif k == 3:
            window = last[pl.ds(top + dilation, rows)]
        else:
            window = last[pl.ds(top + 3 * dilation, rows), :, :lanes]
        weight = weights[2 * lanes * k : min(2 * lanes * (k + 1), 9 * lanes)]
        term = dot(window.reshape(size, window.shape[2]), weight)
        total = term if total is None else total + term
    return total


def positive(x):
    return jnp.maximum(x, 0)


def assemble(area, tile, above, below, left, right):
    side = tile.shape[0]
    full, wide, channels = area.shape
    middle = slice(LEAD, LEAD + side)
    area[:, :LEAD] = jnp.zeros((full, LEAD, channels), F32)
    area[:, LEAD + side :] = jnp.zeros((full, wide - LEAD - side, channels), F32)
    area[HALO : HALO + side, middle] = tile
    area[:HALO, middle] = above[:HALO].astype(F32)
    area[HALO + side :, middle] = below[:HALO].astype(F32)
    area[:, LEAD - HALO : LEAD] = left[...].astype(F32)
    area[:, LEAD + side : LEAD + side + HALO] = right[...].astype(F32)


def first_branch(area, pairs, last, weights, bias, proj, store):
    full, wide = pairs.shape[:2]
    start = LEAD - SECOND_DILATION
    starts = [start + FIRST_DILATION * b for b in (-1, 0, 1)]
    paired(area, starts, wide, FIRST_DILATION, pairs, last, positive)

    def rows(step, _):
        top = step * 8
        pre = taps_sum(pairs, last, top, 8, FIRST_DILATION, weights) + bias[...]
        branch = dot(positive(pre).astype(BF16), proj[...])
        inputs = area[pl.ds(top + FIRST_DILATION, 8), start : start + wide]
        branch = rounded(inputs + branch.reshape(inputs.shape))
        store(top, pre.reshape(8, wide, pre.shape[1]), branch)
        return 0

    lax.fori_loop(0, (full - 2 * FIRST_DILATION) // 8, rows, 0)


def own_kernel(
    tile, above, below, left, right, weights, bias, proj,
    swapped, gate_first, bottle_first, near_hidden,
    area, pairs, last, pre,
):
    side, first, second, inner = tile.shape[0], FIRST_DILATION, SECOND_DILATION, bias.shape[1]
    near, small = gate_first.shape[:2]
    span = side + 2 * second
    assemble(area, tile[...].astype(F32), above, below, left, right)

    def store(top, pre_act, branch):
        pre[pl.ds(top, 8)] = pre_act
        swapped[pl.ds(top, 8)] = branch[:, :span].astype(BF16)

    first_branch(area, pairs, last, weights, bias, proj, store)
    swapped[span:] = jnp.zeros((side, span, swapped.shape[2]), BF16)
    for b in (-1, 0, 1):
        at = LEAD + first * b
        near_hidden[b + 1] = positive(area[HALO - first : HALO + side + first, at : at + small]).astype(BF16)
    edge = second - first
    part = pre[edge : edge + near, edge : edge + small]
    alive = (part > 0) & inside(part.shape, side, first, 0)
    gate_first[:, :, :inner] = jnp.where(alive, 1.0, 0.0).astype(BF16)
    gate_first[:, :, inner:] = jnp.zeros((near, small, gate_first.shape[2] - inner), BF16)
    bottle_first[...] = positive(pre[second : second + side, second : second + small]).astype(BF16)


def middle_kernel(
    kept, other, w_second, b_second, p_second,
    gate_second, hidden_pairs, hidden_last, bottle_second, grad_tile, grad_pre, above, below,
    current, padded, pre_second,
):
    side, channels, span = above.shape[1], kept.shape[2], kept.shape[1]
    first, second, inner = FIRST_DILATION, SECOND_DILATION, bottle_second.shape[2]
    near, small = gate_second.shape[:2]
    turned = jnp.swapaxes(other[:span].astype(F32), 0, 1)
    sym = rounded((kept[:span].astype(F32) + turned) * 0.5)
    current[:, :span] = jnp.where(inside(sym.shape, side, second, 0), sym, 0)
    current[:, span:] = jnp.zeros((span, current.shape[1] - span, channels), F32)
    edge = second - first
    part = current[edge : edge + near, edge : edge + small]
    gate_second[...] = jnp.where(part > 0, 1.0, 0.0).astype(BF16)
    paired(current, [0, second, 2 * second], small, second, hidden_pairs, hidden_last, positive)

    def rows(step, _):
        top = step * 8
        total = taps_sum(hidden_pairs, hidden_last, top, 8, second, w_second) + b_second[...]
        pre_second[pl.ds(top, 8)] = total.reshape(8, small, total.shape[1])
        return 0

    lax.fori_loop(0, side // 8, rows, 0)
    bottle_second[...] = positive(pre_second[:, :, :inner]).astype(BF16)

    turned = jnp.swapaxes(other[span:, :side].astype(F32), 0, 1)
    padded[:, side:] = jnp.zeros((side, small - side, channels), F32)
    padded[:, :side] = rounded((kept[span:, :side].astype(F32) + turned) * 0.5)
    branch = padded[...].astype(BF16)
    grad_tile[...] = branch
    grad = dot(branch.reshape(side * small, channels), p_second[...]).reshape(side, small, 2 * inner)
    grad = jnp.where(pre_second[...] > 0, grad, 0)
    grad_pre[...] = grad.astype(BF16)
    grad, branch = grad[:, :side].astype(BF16), padded[:, :side].astype(BF16)
    above[:HALO], above[HALO:] = grad[:HALO], branch[:first]
    below[:HALO], below[HALO:] = grad[side - HALO :], branch[side - first :]


def weight_sums(rows, ends, grad_pre, hidden, bottle, grad_tile):
    side, small, lanes = grad_pre.shape
    inner = bottle.shape[2]
    size = side * small
    flat = grad_pre.reshape(size, lanes)
    turned = flat.T[:inner].astype(BF16)
    for a in range(3):
        b = 0
        while b < 3:
            window = hidden(a, b)
            grads = dot(turned, window.reshape(size, window.shape[2]))
            for at in range(0, window.shape[2], grad_tile.shape[2]):
                rows[(3 * a + b) * inner : (3 * a + b + 1) * inner] = grads[:, at : at + grad_tile.shape[2]]
                b += 1
    turned = bottle[...].reshape(size, inner).astype(F32).T.astype(BF16)
    rows[9 * inner : 10 * inner] = dot(turned, grad_tile.reshape(size, grad_tile.shape[2]))
    ends[...] = jnp.zeros(ends.shape, F32)
    ends[:, :lanes] = jnp.broadcast_to(jnp.sum(flat, axis=0, keepdims=True), (ends.shape[0], lanes))


def weights_kernel(
    mine, theirs, w_first, w_second, v_second, v_first, p_first, p_second, p_back, b_first, b_second, packed
):
    inner, channels = p_first.shape
    section = lax.axis_index("segment")
    packed[section] = mine[...]
    packed[1 - section] = theirs[...]

    def conv(section, k):
        return packed[section, k * inner : (k + 1) * inner]

    def turned(x):
        return x.astype(F32).T.astype(BF16)

    zero = jnp.zeros((inner, channels), BF16)
    for at, k in enumerate(ORDER):
        here = slice(at * channels, (at + 1) * channels)
        own, other = conv(1, k), conv(1, 3 * (k % 3) + k // 3)
        w_first[here] = turned(conv(0, k))
        w_second[here] = turned(jnp.concatenate([own, other], axis=0))
        v_second[k, :inner, :channels], v_second[k, :inner, channels:] = own, zero
        v_second[k, inner:, :channels], v_second[k, inner:, channels:] = zero, other
        v_first[k, :inner], v_first[k, inner:] = conv(0, k), zero
    p_first[...] = conv(0, 9)
    p_second[...] = turned(jnp.concatenate([conv(1, 9), conv(1, 9)], axis=0))
    p_back[...] = turned(jnp.concatenate([conv(0, 9), zero], axis=0))
    b_first[...] = packed[0, 10 * inner :].astype(F32)[:1, :inner]
    bias = packed[1, 10 * inner :].astype(F32)[:1, :inner]
    b_second[...] = jnp.concatenate([bias, bias], axis=1)


def second_sums_kernel(grad_pre, pairs, last, bottle, grad_tile, rows, ends):
    side = grad_pre.shape[0]
    channels = grad_tile.shape[2]

    def hidden(a, b):
        top = SECOND_DILATION * a
        if b == 0:
            return pairs[top : top + side]
        return last[top + SECOND_DILATION : top + SECOND_DILATION + side, :, :channels]

    weight_sums(rows, ends, grad_pre[...].astype(F32), hidden, bottle, grad_tile[...])


def backward_kernel(
    grad_pre, grad_tile, above, below, left, right, left_branch, right_branch, gate_second, gate_first, near_hidden,
    bottle_first, v_second, p_first, rows_second, ends_second,
    keep, away, windows, grad_first,
    area, shifted, branch, grads, rows, ends,
):
    side, channels = grad_first.shape[0], grad_first.shape[2]
    first, second = FIRST_DILATION, SECOND_DILATION
    full, near = side + 2 * HALO, side + 2 * first
    small = grad_pre.shape[1]
    middle = slice(LEAD, LEAD + side)

    area[:, :LEAD] = jnp.zeros((full, LEAD, channels), F32)
    area[:, LEAD + side :] = jnp.zeros((full, area.shape[1] - LEAD - side, channels), F32)
    area[HALO : HALO + side, LEAD : LEAD + small] = grad_pre[...].astype(F32)
    area[:HALO, middle] = above[:HALO].astype(F32)
    area[HALO + side :, middle] = below[:HALO].astype(F32)
    area[:, LEAD - HALO : LEAD] = left[...].astype(F32)
    area[:, LEAD + side : LEAD + side + HALO] = right[...].astype(F32)
    branch[...] = jnp.zeros(branch.shape, F32)
    branch[first : first + side, first : first + side] = grad_tile[:, :side].astype(F32)
    branch[:first, first : first + side] = above[HALO:].astype(F32)
    branch[first + side :, first : first + side] = below[HALO:].astype(F32)
    branch[:, :first] = left_branch[...].astype(F32)
    branch[:, first + side : near] = right_branch[...].astype(F32)
    for b in (-1, 0, 1):
        at = LEAD - HALO + second * (1 - b)
        shifted[b + 1] = area[:, at : at + small].astype(BF16)
    grads[:, small:] = jnp.zeros((near, grads.shape[1] - small, channels), F32)

    def sections(step, _):
        top = step * 7
        size = 7 * small
        total = jnp.zeros((size, 2 * channels), F32)
        for a, b in TAPS:
            window = shifted[b + 1, pl.ds(top + second * (1 - a), 7)].reshape(size, channels)
            total = total + dot(window, v_second[tap(a, b)])
        here = pl.ds(top, 7)
        grad = branch[here, :small].reshape(size, channels)
        gate = gate_second[here].astype(F32).reshape(size, channels) > 0
        own = rounded(grad + jnp.where(gate, total[:, :channels], 0))
        other = rounded(grad + jnp.where(gate, total[:, channels:], 0))
        grad = ((own + other) * 0.5).astype(BF16)
        branch[here, :small] = grad.astype(F32).reshape(7, small, channels)
        gate = gate_first[here].astype(F32).reshape(size, channels) > 0
        grad = rounded(jnp.where(gate, dot(grad, p_first[...]), 0))
        grads[here, :small] = grad.reshape(7, small, channels)
        return 0

    lax.fori_loop(0, near // 7, sections, 0)
    for b in (-1, 0, 1):
        at = first * (1 - b)
        windows[b + 1] = grads[:, at : at + small].astype(BF16)
    part = branch[first : first + side, first : first + small]
    grad_first[...] = part[:, :side].astype(BF16)
    real = lax.broadcasted_iota(jnp.int32, part.shape, 1) < side
    part = jnp.where(real, part, 0).astype(BF16)
    grad = jnp.where(real, grads[first : first + side, first : first + small], 0)

    def hidden(a, b):
        return near_hidden[b, first * a : first * a + side]

    weight_sums(rows, ends, grad, hidden, bottle_first, part)

    first_core = lax.axis_index("segment") == 0
    count = rows.shape[0]
    for here, one, two in (
        (slice(0, count), rows[...], rows_second[...]),
        (slice(count, count + ends.shape[0]), ends[...], ends_second[...]),
    ):
        keep[here] = jnp.where(first_core, one, two)
        away[here] = jnp.where(first_core, two, one).astype(BF16)


def pair_kernel(keep, other, parts):
    devices, share = parts.shape[0], parts.shape[1] - 8
    total = keep[...] + other[...].astype(F32)
    count = keep.shape[0] - 16
    for j in range(devices):
        low, high = min(j * share, count), min((j + 1) * share, count)
        pieces = [total[low:high]] if low < high else []
        if high - low < share:
            pieces.append(jnp.zeros((share - (high - low), keep.shape[1]), F32))
        parts[j] = jnp.concatenate(pieces + [total[count : count + 8]]).astype(BF16)


def input_kernel(windows, grad_first, tile, v_first, out):
    side, channels = out.shape[0], out.shape[2]
    small = windows.shape[2]
    first = FIRST_DILATION

    def rows(step, _):
        top = step * 8
        total = jnp.zeros((8 * small, channels), F32)
        for a, b in TAPS:
            window = windows[b + 1, pl.ds(top + first * (1 - a), 8)].reshape(8 * small, channels)
            total = total + dot(window, v_first[tap(a, b)])
        here = pl.ds(top, 8)
        total = total.reshape(8, small, channels)[:, :side]
        total = jnp.where(tile[here].astype(F32) > 0, total, 0)
        out[here] = (grad_first[here].astype(F32) + total).astype(BF16)
        return 0

    lax.fori_loop(0, side // 8, rows, 0)


def total_kernel(scale, parts, rows, ends):
    share = rows.shape[1]
    total = jnp.sum(parts[...].astype(F32), axis=0) * scale
    rows[...] = jnp.broadcast_to(total[:share].astype(BF16)[None], rows.shape)
    ends[...] = total[share:]


def outputs_kernel(rows, ends, moved, conv_gradient, bias_gradient, out_gradient, input_gradient):
    count, inner = conv_gradient.shape[0], out_gradient.shape[0]
    conv_gradient[...] = rows[:count].astype(F32)
    out_gradient[...] = rows[count : count + inner].astype(F32)
    bias_gradient[...] = ends[:1, :inner]
    input_gradient[...] = moved[...]


def call(kernel, name, outs, scratch, flops, *operands):
    outs = [jax.ShapeDtypeStruct(shape, dtype) for shape, dtype in outs]
    moved = sum(x.size * x.dtype.itemsize for x in list(operands) + outs)
    return pl.pallas_call(
        kernel,
        name=name,
        out_shape=outs,
        scratch_shapes=[pltpu.VMEM(shape, dtype) for shape, dtype in scratch],
        cost_estimate=pl.CostEstimate(flops=flops, bytes_accessed=moved, transcendentals=0),
        compiler_params=pltpu.CompilerParams(vmem_limit_bytes=40 * 1024 * 1024),
    )(*operands)


def local(activations, cotangent, conv_weight, conv_bias, out_weight):
    side, channels, inner = activations.shape[1], activations.shape[3], conv_weight.shape[3]
    number = lax.axis_size("row")
    first, second = FIRST_DILATION, SECOND_DILATION
    full, span, near = side + 2 * HALO, side + 2 * second, side + 2 * first
    wide, small = up16(span), up16(near)

    tile = bring(activations[0])
    above = bring(activations[0, side - HALO :], 1)
    below = bring(activations[0, :HALO], -1)

    def columns(low, high):
        strip = jnp.pad(jnp.swapaxes(tile[:, low:high], 0, 1), ((0, 0), (HALO, HALO), (0, 0)))
        strip = lax.optimization_barrier(strip)
        strip = lax.dynamic_update_slice(strip, jnp.swapaxes(above[:, low:high], 0, 1), (0, 0, 0))
        return lax.dynamic_update_slice(strip, jnp.swapaxes(below[:, low:high], 0, 1), (0, HALO + side, 0))

    left = send(columns(side - HALO, side), lambda r, c: (r, c + 1))
    right = send(columns(0, HALO), lambda r, c: (r, c - 1))
    late = bring(cotangent[0])

    bias_rows = jnp.pad(conv_bias, ((0, 15), (0, channels - inner)))
    packed = jnp.concatenate(
        [jnp.swapaxes(conv_weight[0], 1, 2).reshape(9 * inner, channels), out_weight[0], bias_rows]
    )
    others = lax.ppermute(packed, "segment", [(0, 1), (1, 0)])
    w_first, w_second, v_second, v_first, p_first, p_second, p_back, b_first, b_second = call(
        weights_kernel,
        "weights",
        [
            ((9 * channels, inner), BF16),
            ((9 * channels, 2 * inner), BF16),
            ((9, 2 * inner, 2 * channels), BF16),
            ((9, 2 * inner, channels), BF16),
            ((inner, channels), BF16),
            ((channels, 2 * inner), BF16),
            ((channels, 2 * inner), BF16),
            ((1, inner), F32),
            ((1, 2 * inner), F32),
        ],
        [((2,) + packed.shape, BF16)],
        packed.size,
        *(packed, others),
    )

    kept, gate_first, bottle_first, near_hidden = call(
        own_kernel,
        "own_branch",
        [
            ((span + side, span, channels), BF16),
            ((near, small, channels), BF16),
            ((side, small, inner), BF16),
            ((3, near, small, channels), BF16),
        ],
        [
            ((full, LEAD + up16(side + LEAD), channels), F32),
            ((full, wide, 2 * channels), BF16),
            ((full + first, wide, 2 * channels), BF16),
            ((span, wide, inner), F32),
        ],
        span * wide * channels * inner * 20,
        *(tile, above, below, jnp.swapaxes(left, 0, 1), jnp.swapaxes(right, 0, 1)),
        *(w_first, b_first, p_first),
    )
    kept = lax.dynamic_update_slice(kept, late, (span, 0, 0))
    other = send(kept, lambda r, c: (c, r))
    gate_second, hidden_pairs, hidden_last, bottle_second, grad_tile, grad_pre, strip_above, strip_below = call(
        middle_kernel,
        "middle",
        [
            ((near, small, channels), BF16),
            ((span, small, 2 * channels), BF16),
            ((span + second, small, 2 * channels), BF16),
            ((side, small, inner), BF16),
            ((side, small, channels), BF16),
            ((side, small, 2 * inner), BF16),
            ((HALO + first, side, channels), BF16),
            ((HALO + first, side, channels), BF16),
        ],
        [
            ((span, wide, channels), F32),
            ((side, small, channels), F32),
            ((side, small, 2 * inner), F32),
        ],
        24 * side * small * channels * 2 * inner,
        *(kept, other, w_second, b_second, p_second),
    )

    above = send(strip_below, lambda r, c: (r + 1, c))
    below = send(strip_above, lambda r, c: (r - 1, c))
    rows_second, ends_second = call(
        second_sums_kernel,
        "second_sums",
        [((10 * inner, channels), F32), ((16, channels), F32)],
        [],
        20 * side * small * channels * inner,
        *(grad_pre, hidden_pairs, hidden_last, bottle_second, grad_tile),
    )

    def columns(low, high, low_branch, high_branch):
        grads = jnp.concatenate([above[:HALO, low:high], grad_pre[:, low:high], below[:HALO, low:high]])
        here = slice(low_branch, high_branch)
        branches = jnp.concatenate([above[HALO:, here], grad_tile[:, here], below[HALO:, here]])
        branches = jnp.pad(branches, ((second, second), (0, 0), (0, 0)))
        return jnp.swapaxes(jnp.concatenate([grads, branches], axis=1), 0, 1)

    left = send(columns(side - HALO, side, side - first, side), lambda r, c: (r, c + 1))
    right = send(columns(0, HALO, 0, first), lambda r, c: (r, c - 1))
    left, right = jnp.swapaxes(left, 0, 1), jnp.swapaxes(right, 0, 1)

    devices = number * number
    share = -(-10 * inner // (8 * devices)) * 8
    keep, away, windows, grad_first = call(
        backward_kernel,
        "backward",
        [
            ((10 * inner + 16, channels), F32),
            ((10 * inner + 16, channels), BF16),
            ((3, near, small, channels), BF16),
            ((side, side, channels), BF16),
        ],
        [
            ((full, LEAD + up16(side + HALO + first), channels), F32),
            ((3, full, small, channels), BF16),
            ((near, small + 16, channels), F32),
            ((near, small + 16, channels), F32),
            ((10 * inner, channels), F32),
            ((16, channels), F32),
        ],
        36 * near * small * channels * channels,
        *(grad_pre, grad_tile, above, below, left[:, :HALO], right[:, :HALO]),
        *(left[second : second + near, HALO:], right[second : second + near, HALO:]),
        *(gate_second, gate_first, near_hidden, bottle_first, v_second, p_back, rows_second, ends_second),
    )

    (input_gradient,) = call(
        input_kernel,
        "input",
        [((side, side, channels), BF16)],
        [],
        18 * side * small * channels * channels,
        *(windows, grad_first, tile, v_first),
    )
    other = lax.ppermute(away, "segment", [(0, 1), (1, 0)])
    other, input_gradient = lax.optimization_barrier((other, input_gradient))
    (parts,) = call(
        pair_kernel,
        "pair",
        [((devices, share + 8, channels), BF16)],
        [],
        keep.size,
        *(keep, other),
    )
    parts = lax.all_to_all(parts, GRID, 0, 0, tiled=True)
    input_gradient = take_back(input_gradient)
    cells = lax.axis_size("segment") * (side * number) * (side * number)
    rows, ends = call(
        functools.partial(total_kernel, float(cells) ** -0.5),
        "total",
        [((devices, share, channels), BF16), ((8, channels), F32)],
        [],
        parts.size,
        parts,
    )
    rows, _ = lax.optimization_barrier((rows, input_gradient))
    rows = lax.all_to_all(rows, GRID, 0, 0, tiled=True).reshape(devices * share, channels)
    conv_gradient, bias_gradient, out_gradient, input_gradient = call(
        outputs_kernel,
        "outputs",
        [
            ((9 * inner, channels), F32),
            ((1, inner), F32),
            ((inner, channels), F32),
            ((side, side, channels), BF16),
        ],
        [],
        rows.size,
        *(rows, ends, input_gradient),
    )
    conv_gradient = jnp.swapaxes(conv_gradient.reshape(1, 9, inner, channels), 2, 3)
    return (input_gradient[None], conv_gradient, bias_gradient, out_gradient[None])


def solution(mesh):
    in_specs = (
        P("segment", "row", "col", None),
        P("segment", "row", "col", None),
        P("segment", None, None, None),
        P("segment", None),
        P("segment", None, None),
    )
    out_specs = (
        P("segment", "row", "col", None),
        P("segment", None, None, None),
        P("segment", None),
        P("segment", None, None),
    )
    return jax.shard_map(local, mesh=mesh, in_specs=in_specs, out_specs=out_specs, check_vma=False)
```

```python
import functools

import jax
import jax.numpy as jnp
from jax import lax
from jax.experimental import pallas as pl
from jax.experimental.pallas import tpu as pltpu
from jax.sharding import PartitionSpec as P

FIRST_DILATION = 2
SECOND_DILATION = 8
HALO = FIRST_DILATION + SECOND_DILATION
GRID = ("row", "col")
ALL = ("segment",) + GRID
ORDER = [0, 1, 3, 4, 6, 7, 2, 5, 8]
TAPS = [(a, b) for a in (-1, 0, 1) for b in (-1, 0, 1)]
LEAD = 16
F32, BF16 = jnp.float32, jnp.bfloat16


def tap(a, b):
    return 3 * (a + 1) + (b + 1)


def dot(x, y):
    return jnp.dot(x, y, preferred_element_type=F32)


def rounded(x):
    return x.astype(BF16).astype(F32)


def up16(n):
    return -(-n // 16) * 16


def home(batch, r, c):
    number = lax.axis_size("row")
    core, row, col = (batch, r, c) if r == c else (int(r > c), r, c)
    if r != c and (r < c) == (batch == 1):
        row, col = c, r
    return (core * number + row) * number + col


def place():
    row, col = lax.axis_index("row"), lax.axis_index("col")
    low, high = jnp.minimum(row, col), jnp.maximum(row, col)
    upper = lax.axis_index("segment") == 0
    return jnp.where(upper, low, high), jnp.where(upper, high, low)


def permute(x, pair):
    number = lax.axis_size("row")
    tiles = [(m, r, c) for m in range(lax.axis_size("segment")) for r in range(number) for c in range(number)]
    pairs = [pair(*tile) for tile in tiles]
    return lax.ppermute(x, ALL, [found for found in pairs if found is not None])


def stored(batch, r, c):
    number = lax.axis_size("row")
    return (batch * number + r) * number + c


def bring(x, down=0):
    number = lax.axis_size("row")

    def pair(batch, r, c):
        if 0 <= r + down < number:
            return stored(batch, r, c), home(batch, r + down, c)

    return permute(x, pair)


def take_back(x):
    return permute(x, lambda m, r, c: (home(m, r, c), stored(m, r, c)))


def send(x, to):
    number = lax.axis_size("row")

    def pair(batch, r, c):
        row, col = to(r, c)
        if 0 <= row < number and 0 <= col < number:
            return home(batch, r, c), home(batch, row, col)

    return permute(x, pair)


def inside(shape, side, width, top):
    number = lax.axis_size("row") * side
    rows = lax.broadcasted_iota(jnp.int32, shape, 0) + top - width
    cols = lax.broadcasted_iota(jnp.int32, shape, 1) - width
    row, col = place()
    at_row = row * side + rows
    at_col = col * side + cols
    return (at_row >= 0) & (at_row < number) & (at_col >= 0) & (at_col < number) & (cols < side + width)


def paired(source, starts, width, dilation, pairs, last, change):
    lanes = source.shape[2]
    low, high = slice(0, lanes), slice(lanes, 2 * lanes)

    def step(k, _):
        rows, lower = pl.ds(4 * k, 4), pl.ds(4 * k + dilation, 4)
        window = [change(source[rows, at : at + width]).astype(BF16) for at in starts]
        pairs[rows, :, low] = window[0]
        pairs[rows, :, high] = window[1]
        last[lower, :, low] = window[2]
        last[rows, :, high] = window[2]
        return 0

    lax.fori_loop(0, source.shape[0] // 4, step, 0)


def taps_sum(pairs, last, top, rows, dilation, weights):
    width, lanes = pairs.shape[1], pairs.shape[2] // 2
    size = rows * width
    total = None
    for k in range(5):
        if k < 3:
            window = pairs[pl.ds(top + dilation * k, rows)]
        elif k == 3:
            window = last[pl.ds(top + dilation, rows)]
        else:
            window = last[pl.ds(top + 3 * dilation, rows), :, :lanes]
        weight = weights[2 * lanes * k : min(2 * lanes * (k + 1), 9 * lanes)]
        term = dot(window.reshape(size, window.shape[2]), weight)
        total = term if total is None else total + term
    return total


def positive(x):
    return jnp.maximum(x, 0)


def assemble(area, tile, above, below, left, right):
    side = tile.shape[0]
    full, wide, channels = area.shape
    middle = slice(LEAD, LEAD + side)
    area[:, :LEAD] = jnp.zeros((full, LEAD, channels), F32)
    area[:, LEAD + side :] = jnp.zeros((full, wide - LEAD - side, channels), F32)
    area[HALO : HALO + side, middle] = tile
    area[:HALO, middle] = above[:HALO].astype(F32)
    area[HALO + side :, middle] = below[:HALO].astype(F32)
    area[:, LEAD - HALO : LEAD] = left[...].astype(F32)
    area[:, LEAD + side : LEAD + side + HALO] = right[...].astype(F32)


def first_branch(area, pairs, last, weights, bias, proj, store):
    full, wide = pairs.shape[:2]
    start = LEAD - SECOND_DILATION
    starts = [start + FIRST_DILATION * b for b in (-1, 0, 1)]
    paired(area, starts, wide, FIRST_DILATION, pairs, last, positive)

    def rows(step, _):
        top = step * 8
        pre = taps_sum(pairs, last, top, 8, FIRST_DILATION, weights) + bias[...]
        branch = dot(positive(pre).astype(BF16), proj[...])
        inputs = area[pl.ds(top + FIRST_DILATION, 8), start : start + wide]
        branch = rounded(inputs + branch.reshape(inputs.shape))
        store(top, pre.reshape(8, wide, pre.shape[1]), branch)
        return 0

    lax.fori_loop(0, (full - 2 * FIRST_DILATION) // 8, rows, 0)


def own_kernel(
    tile, above, below, left, right, weights, bias, proj,
    swapped, gate_first, bottle_first, near_hidden,
    area, pairs, last, pre,
):
    side, first, second, inner = tile.shape[0], FIRST_DILATION, SECOND_DILATION, bias.shape[1]
    near, small = gate_first.shape[:2]
    span = side + 2 * second
    assemble(area, tile[...].astype(F32), above, below, left, right)

    def store(top, pre_act, branch):
        pre[pl.ds(top, 8)] = pre_act
        swapped[pl.ds(top, 8)] = branch[:, :span].astype(BF16)

    first_branch(area, pairs, last, weights, bias, proj, store)
    swapped[span:] = jnp.zeros((side, span, swapped.shape[2]), BF16)
    for b in (-1, 0, 1):
        at = LEAD + first * b
        near_hidden[b + 1] = positive(area[HALO - first : HALO + side + first, at : at + small]).astype(BF16)
    edge = second - first
    part = pre[edge : edge + near, edge : edge + small]
    alive = (part > 0) & inside(part.shape, side, first, 0)
    gate_first[:, :, :inner] = jnp.where(alive, 1.0, 0.0).astype(BF16)
    gate_first[:, :, inner:] = jnp.zeros((near, small, gate_first.shape[2] - inner), BF16)
    bottle_first[...] = positive(pre[second : second + side, second : second + small]).astype(BF16)


def middle_kernel(
    kept, other, w_second, b_second, p_second,
    gate_second, hidden_pairs, hidden_last, bottle_second, grad_tile, grad_pre, above, below,
    current, padded, pre_second,
):
    side, channels, span = above.shape[1], kept.shape[2], kept.shape[1]
    first, second, inner = FIRST_DILATION, SECOND_DILATION, bottle_second.shape[2]
    near, small = gate_second.shape[:2]
    turned = jnp.swapaxes(other[:span].astype(F32), 0, 1)
    sym = rounded((kept[:span].astype(F32) + turned) * 0.5)
    current[:, :span] = jnp.where(inside(sym.shape, side, second, 0), sym, 0)
    current[:, span:] = jnp.zeros((span, current.shape[1] - span, channels), F32)
    edge = second - first
    part = current[edge : edge + near, edge : edge + small]
    gate_second[...] = jnp.where(part > 0, 1.0, 0.0).astype(BF16)
    paired(current, [0, second, 2 * second], small, second, hidden_pairs, hidden_last, positive)

    def rows(step, _):
        top = step * 8
        total = taps_sum(hidden_pairs, hidden_last, top, 8, second, w_second) + b_second[...]
        pre_second[pl.ds(top, 8)] = total.reshape(8, small, total.shape[1])
        return 0

    lax.fori_loop(0, side // 8, rows, 0)
    bottle_second[...] = positive(pre_second[:, :, :inner]).astype(BF16)

    turned = jnp.swapaxes(other[span:, :side].astype(F32), 0, 1)
    padded[:, side:] = jnp.zeros((side, small - side, channels), F32)
    padded[:, :side] = rounded((kept[span:, :side].astype(F32) + turned) * 0.5)
    branch = padded[...].astype(BF16)
    grad_tile[...] = branch
    grad = dot(branch.reshape(side * small, channels), p_second[...]).reshape(side, small, 2 * inner)
    grad = jnp.where(pre_second[...] > 0, grad, 0)
    grad_pre[...] = grad.astype(BF16)
    grad, branch = grad[:, :side].astype(BF16), padded[:, :side].astype(BF16)
    above[:HALO], above[HALO:] = grad[:HALO], branch[:first]
    below[:HALO], below[HALO:] = grad[side - HALO :], branch[side - first :]


def weight_sums(rows, ends, grad_pre, hidden, bottle, grad_tile):
    side, small, lanes = grad_pre.shape
    inner = bottle.shape[2]
    size = side * small
    flat = grad_pre.reshape(size, lanes)
    turned = flat.T[:inner].astype(BF16)
    for a in range(3):
        b = 0
        while b < 3:
            window = hidden(a, b)
            grads = dot(turned, window.reshape(size, window.shape[2]))
            for at in range(0, window.shape[2], grad_tile.shape[2]):
                rows[(3 * a + b) * inner : (3 * a + b + 1) * inner] = grads[:, at : at + grad_tile.shape[2]]
                b += 1
    turned = bottle[...].reshape(size, inner).astype(F32).T.astype(BF16)
    rows[9 * inner : 10 * inner] = dot(turned, grad_tile.reshape(size, grad_tile.shape[2]))
    ends[...] = jnp.zeros(ends.shape, F32)
    ends[:, :lanes] = jnp.broadcast_to(jnp.sum(flat, axis=0, keepdims=True), (ends.shape[0], lanes))


def weights_kernel(
    mine, theirs, w_first, w_second, v_second, v_first, p_first, p_second, p_back, b_first, b_second, packed
):
    inner, channels = p_first.shape
    section = lax.axis_index("segment")
    packed[section] = mine[...]
    packed[1 - section] = theirs[...]

    def conv(section, k):
        return packed[section, k * inner : (k + 1) * inner]

    def turned(x):
        return x.astype(F32).T.astype(BF16)

    zero = jnp.zeros((inner, channels), BF16)
    for at, k in enumerate(ORDER):
        here = slice(at * channels, (at + 1) * channels)
        own, other = conv(1, k), conv(1, 3 * (k % 3) + k // 3)
        w_first[here] = turned(conv(0, k))
        w_second[here] = turned(jnp.concatenate([own, other], axis=0))
        v_second[k, :inner, :channels], v_second[k, :inner, channels:] = own, zero
        v_second[k, inner:, :channels], v_second[k, inner:, channels:] = zero, other
        v_first[k, :inner], v_first[k, inner:] = conv(0, k), zero
    p_first[...] = conv(0, 9)
    p_second[...] = turned(jnp.concatenate([conv(1, 9), conv(1, 9)], axis=0))
    p_back[...] = turned(jnp.concatenate([conv(0, 9), zero], axis=0))
    b_first[...] = packed[0, 10 * inner :].astype(F32)[:1, :inner]
    bias = packed[1, 10 * inner :].astype(F32)[:1, :inner]
    b_second[...] = jnp.concatenate([bias, bias], axis=1)


def second_sums_kernel(grad_pre, pairs, last, bottle, grad_tile, rows, ends):
    side = grad_pre.shape[0]
    channels = grad_tile.shape[2]

    def hidden(a, b):
        top = SECOND_DILATION * a
        if b == 0:
            return pairs[top : top + side]
        return last[top + SECOND_DILATION : top + SECOND_DILATION + side, :, :channels]

    weight_sums(rows, ends, grad_pre[...].astype(F32), hidden, bottle, grad_tile[...])


def backward_kernel(
    grad_pre, grad_tile, above, below, left, right, left_branch, right_branch, gate_second, gate_first, near_hidden,
    bottle_first, v_second, p_first, rows_second, ends_second,
    keep, away, windows, grad_first,
    area, shifted, branch, grads, rows, ends,
):
    side, channels = grad_first.shape[0], grad_first.shape[2]
    first, second = FIRST_DILATION, SECOND_DILATION
    full, near = side + 2 * HALO, side + 2 * first
    small = grad_pre.shape[1]
    middle = slice(LEAD, LEAD + side)

    area[:, :LEAD] = jnp.zeros((full, LEAD, channels), F32)
    area[:, LEAD + side :] = jnp.zeros((full, area.shape[1] - LEAD - side, channels), F32)
    area[HALO : HALO + side, LEAD : LEAD + small] = grad_pre[...].astype(F32)
    area[:HALO, middle] = above[:HALO].astype(F32)
    area[HALO + side :, middle] = below[:HALO].astype(F32)
    area[:, LEAD - HALO : LEAD] = left[...].astype(F32)
    area[:, LEAD + side : LEAD + side + HALO] = right[...].astype(F32)
    branch[...] = jnp.zeros(branch.shape, F32)
    branch[first : first + side, first : first + side] = grad_tile[:, :side].astype(F32)
    branch[:first, first : first + side] = above[HALO:].astype(F32)
    branch[first + side :, first : first + side] = below[HALO:].astype(F32)
    branch[:, :first] = left_branch[...].astype(F32)
    branch[:, first + side : near] = right_branch[...].astype(F32)
    for b in (-1, 0, 1):
        at = LEAD - HALO + second * (1 - b)
        shifted[b + 1] = area[:, at : at + small].astype(BF16)
    grads[:, small:] = jnp.zeros((near, grads.shape[1] - small, channels), F32)

    def sections(step, _):
        top = step * 7
        size = 7 * small
        total = jnp.zeros((size, 2 * channels), F32)
        for a, b in TAPS:
            window = shifted[b + 1, pl.ds(top + second * (1 - a), 7)].reshape(size, channels)
            total = total + dot(window, v_second[tap(a, b)])
        here = pl.ds(top, 7)
        grad = branch[here, :small].reshape(size, channels)
        gate = gate_second[here].astype(F32).reshape(size, channels) > 0
        own = rounded(grad + jnp.where(gate, total[:, :channels], 0))
        other = rounded(grad + jnp.where(gate, total[:, channels:], 0))
        grad = ((own + other) * 0.5).astype(BF16)
        branch[here, :small] = grad.astype(F32).reshape(7, small, channels)
        gate = gate_first[here].astype(F32).reshape(size, channels) > 0
        grad = rounded(jnp.where(gate, dot(grad, p_first[...]), 0))
        grads[here, :small] = grad.reshape(7, small, channels)
        return 0

    lax.fori_loop(0, near // 7, sections, 0)
    for b in (-1, 0, 1):
        at = first * (1 - b)
        windows[b + 1] = grads[:, at : at + small].astype(BF16)
    part = branch[first : first + side, first : first + small]
    grad_first[...] = part[:, :side].astype(BF16)
    real = lax.broadcasted_iota(jnp.int32, part.shape, 1) < side
    part = jnp.where(real, part, 0).astype(BF16)
    grad = jnp.where(real, grads[first : first + side, first : first + small], 0)

    def hidden(a, b):
        return near_hidden[b, first * a : first * a + side]

    weight_sums(rows, ends, grad, hidden, bottle_first, part)

    first_core = lax.axis_index("segment") == 0
    count = rows.shape[0]
    for here, one, two in (
        (slice(0, count), rows[...], rows_second[...]),
        (slice(count, count + ends.shape[0]), ends[...], ends_second[...]),
    ):
        keep[here] = jnp.where(first_core, one, two)
        away[here] = jnp.where(first_core, two, one).astype(BF16)


def pair_kernel(keep, other, parts):
    devices, share = parts.shape[0], parts.shape[1] - 8
    total = keep[...] + other[...].astype(F32)
    count = keep.shape[0] - 16
    for j in range(devices):
        low, high = min(j * share, count), min((j + 1) * share, count)
        pieces = [total[low:high]] if low < high else []
        if high - low < share:
            pieces.append(jnp.zeros((share - (high - low), keep.shape[1]), F32))
        parts[j] = jnp.concatenate(pieces + [total[count : count + 8]]).astype(BF16)


def input_kernel(windows, grad_first, tile, v_first, out):
    side, channels = out.shape[0], out.shape[2]
    small = windows.shape[2]
    first = FIRST_DILATION

    def rows(step, _):
        top = step * 8
        total = jnp.zeros((8 * small, channels), F32)
        for a, b in TAPS:
            window = windows[b + 1, pl.ds(top + first * (1 - a), 8)].reshape(8 * small, channels)
            total = total + dot(window, v_first[tap(a, b)])
        here = pl.ds(top, 8)
        total = total.reshape(8, small, channels)[:, :side]
        total = jnp.where(tile[here].astype(F32) > 0, total, 0)
        out[here] = (grad_first[here].astype(F32) + total).astype(BF16)
        return 0

    lax.fori_loop(0, side // 8, rows, 0)


def total_kernel(scale, parts, rows, ends):
    share = rows.shape[1]
    total = jnp.sum(parts[...].astype(F32), axis=0) * scale
    rows[...] = jnp.broadcast_to(total[:share].astype(BF16)[None], rows.shape)
    ends[...] = total[share:]


def outputs_kernel(rows, ends, moved, conv_gradient, bias_gradient, out_gradient, input_gradient):
    count, inner = conv_gradient.shape[0], out_gradient.shape[0]
    conv_gradient[...] = rows[:count].astype(F32)
    out_gradient[...] = rows[count : count + inner].astype(F32)
    bias_gradient[...] = ends[:1, :inner]
    input_gradient[...] = moved[...]


def call(kernel, name, outs, scratch, flops, *operands):
    outs = [jax.ShapeDtypeStruct(shape, dtype) for shape, dtype in outs]
    moved = sum(x.size * x.dtype.itemsize for x in list(operands) + outs)
    return pl.pallas_call(
        kernel,
        name=name,
        out_shape=outs,
        scratch_shapes=[pltpu.VMEM(shape, dtype) for shape, dtype in scratch],
        cost_estimate=pl.CostEstimate(flops=flops, bytes_accessed=moved, transcendentals=0),
        compiler_params=pltpu.CompilerParams(vmem_limit_bytes=40 * 1024 * 1024),
    )(*operands)


def local(activations, cotangent, conv_weight, conv_bias, out_weight):
    side, channels, inner = activations.shape[1], activations.shape[3], conv_weight.shape[3]
    number = lax.axis_size("row")
    first, second = FIRST_DILATION, SECOND_DILATION
    full, span, near = side + 2 * HALO, side + 2 * second, side + 2 * first
    wide, small = up16(span), up16(near)

    tile = bring(activations[0])
    above = bring(activations[0, side - HALO :], 1)
    below = bring(activations[0, :HALO], -1)

    def columns(low, high):
        strip = jnp.pad(jnp.swapaxes(tile[:, low:high], 0, 1), ((0, 0), (HALO, HALO), (0, 0)))
        strip = lax.optimization_barrier(strip)
        strip = lax.dynamic_update_slice(strip, jnp.swapaxes(above[:, low:high], 0, 1), (0, 0, 0))
        return lax.dynamic_update_slice(strip, jnp.swapaxes(below[:, low:high], 0, 1), (0, HALO + side, 0))

    strips = (columns(side - HALO, side), columns(0, HALO))
    strips, late = lax.optimization_barrier((strips, cotangent[0]))
    left, right = send(strips[0], lambda r, c: (r, c + 1)), send(strips[1], lambda r, c: (r, c - 1))
    late = bring(late)

    bias_rows = jnp.pad(conv_bias, ((0, 15), (0, channels - inner)))
    packed = jnp.concatenate(
        [jnp.swapaxes(conv_weight[0], 1, 2).reshape(9 * inner, channels), out_weight[0], bias_rows]
    )
    others = lax.ppermute(packed, "segment", [(0, 1), (1, 0)])
    w_first, w_second, v_second, v_first, p_first, p_second, p_back, b_first, b_second = call(
        weights_kernel,
        "weights",
        [
            ((9 * channels, inner), BF16),
            ((9 * channels, 2 * inner), BF16),
            ((9, 2 * inner, 2 * channels), BF16),
            ((9, 2 * inner, channels), BF16),
            ((inner, channels), BF16),
            ((channels, 2 * inner), BF16),
            ((channels, 2 * inner), BF16),
            ((1, inner), F32),
            ((1, 2 * inner), F32),
        ],
        [((2,) + packed.shape, BF16)],
        packed.size,
        *(packed, others),
    )

    kept, gate_first, bottle_first, near_hidden = call(
        own_kernel,
        "own_branch",
        [
            ((span + side, span, channels), BF16),
            ((near, small, channels), BF16),
            ((side, small, inner), BF16),
            ((3, near, small, channels), BF16),
        ],
        [
            ((full, LEAD + up16(side + LEAD), channels), F32),
            ((full, wide, 2 * channels), BF16),
            ((full + first, wide, 2 * channels), BF16),
            ((span, wide, inner), F32),
        ],
        span * wide * channels * inner * 400,
        *(tile, above, below, jnp.swapaxes(left, 0, 1), jnp.swapaxes(right, 0, 1)),
        *(w_first, b_first, p_first),
    )
    kept = lax.dynamic_update_slice(kept, late, (span, 0, 0))
    other = send(kept, lambda r, c: (c, r))
    gate_second, hidden_pairs, hidden_last, bottle_second, grad_tile, grad_pre, strip_above, strip_below = call(
        middle_kernel,
        "middle",
        [
            ((near, small, channels), BF16),
            ((span, small, 2 * channels), BF16),
            ((span + second, small, 2 * channels), BF16),
            ((side, small, inner), BF16),
            ((side, small, channels), BF16),
            ((side, small, 2 * inner), BF16),
            ((HALO + first, side, channels), BF16),
            ((HALO + first, side, channels), BF16),
        ],
        [
            ((span, wide, channels), F32),
            ((side, small, channels), F32),
            ((side, small, 2 * inner), F32),
        ],
        24 * side * small * channels * 2 * inner,
        *(kept, other, w_second, b_second, p_second),
    )

    above = send(strip_below, lambda r, c: (r + 1, c))
    below = send(strip_above, lambda r, c: (r - 1, c))
    rows_second, ends_second = call(
        second_sums_kernel,
        "second_sums",
        [((10 * inner, channels), F32), ((16, channels), F32)],
        [],
        20 * side * small * channels * inner,
        *(grad_pre, hidden_pairs, hidden_last, bottle_second, grad_tile),
    )

    def columns(low, high, low_branch, high_branch):
        grads = jnp.concatenate([above[:HALO, low:high], grad_pre[:, low:high], below[:HALO, low:high]])
        here = slice(low_branch, high_branch)
        branches = jnp.concatenate([above[HALO:, here], grad_tile[:, here], below[HALO:, here]])
        branches = jnp.pad(branches, ((second, second), (0, 0), (0, 0)))
        return jnp.swapaxes(jnp.concatenate([grads, branches], axis=1), 0, 1)

    left = send(columns(side - HALO, side, side - first, side), lambda r, c: (r, c + 1))
    right = send(columns(0, HALO, 0, first), lambda r, c: (r, c - 1))
    left, right = jnp.swapaxes(left, 0, 1), jnp.swapaxes(right, 0, 1)

    devices = number * number
    share = -(-10 * inner // (8 * devices)) * 8
    keep, away, windows, grad_first = call(
        backward_kernel,
        "backward",
        [
            ((10 * inner + 16, channels), F32),
            ((10 * inner + 16, channels), BF16),
            ((3, near, small, channels), BF16),
            ((side, side, channels), BF16),
        ],
        [
            ((full, LEAD + up16(side + HALO + first), channels), F32),
            ((3, full, small, channels), BF16),
            ((near, small + 16, channels), F32),
            ((near, small + 16, channels), F32),
            ((10 * inner, channels), F32),
            ((16, channels), F32),
        ],
        36 * near * small * channels * channels,
        *(grad_pre, grad_tile, above, below, left[:, :HALO], right[:, :HALO]),
        *(left[second : second + near, HALO:], right[second : second + near, HALO:]),
        *(gate_second, gate_first, near_hidden, bottle_first, v_second, p_back, rows_second, ends_second),
    )

    (input_gradient,) = call(
        input_kernel,
        "input",
        [((side, side, channels), BF16)],
        [],
        18 * side * small * channels * channels,
        *(windows, grad_first, tile, v_first),
    )
    other = lax.ppermute(away, "segment", [(0, 1), (1, 0)])
    other, input_gradient = lax.optimization_barrier((other, input_gradient))
    (parts,) = call(
        pair_kernel,
        "pair",
        [((devices, share + 8, channels), BF16)],
        [],
        keep.size,
        *(keep, other),
    )
    parts = lax.all_to_all(parts, GRID, 0, 0, tiled=True)
    input_gradient = take_back(input_gradient)
    cells = lax.axis_size("segment") * (side * number) * (side * number)
    rows, ends = call(
        functools.partial(total_kernel, float(cells) ** -0.5),
        "total",
        [((devices, share, channels), BF16), ((8, channels), F32)],
        [],
        parts.size,
        parts,
    )
    rows, _ = lax.optimization_barrier((rows, input_gradient))
    rows = lax.all_to_all(rows, GRID, 0, 0, tiled=True).reshape(devices * share, channels)
    conv_gradient, bias_gradient, out_gradient, input_gradient = call(
        outputs_kernel,
        "outputs",
        [
            ((9 * inner, channels), F32),
            ((1, inner), F32),
            ((inner, channels), F32),
            ((side, side, channels), BF16),
        ],
        [],
        rows.size,
        *(rows, ends, input_gradient),
    )
    conv_gradient = jnp.swapaxes(conv_gradient.reshape(1, 9, inner, channels), 2, 3)
    return (input_gradient[None], conv_gradient, bias_gradient, out_gradient[None])


def solution(mesh):
    in_specs = (
        P("segment", "row", "col", None),
        P("segment", "row", "col", None),
        P("segment", None, None, None),
        P("segment", None),
        P("segment", None, None),
    )
    out_specs = (
        P("segment", "row", "col", None),
        P("segment", None, None, None),
        P("segment", None),
        P("segment", None, None),
    )
    return jax.shard_map(local, mesh=mesh, in_specs=in_specs, out_specs=out_specs, check_vma=False)
```

```python
import functools

import jax
import jax.numpy as jnp
from jax import lax
from jax.experimental import pallas as pl
from jax.experimental.pallas import tpu as pltpu
from jax.sharding import PartitionSpec as P

FIRST_DILATION = 2
SECOND_DILATION = 8
HALO = FIRST_DILATION + SECOND_DILATION
GRID = ("row", "col")
ALL = ("segment",) + GRID
ORDER = [0, 1, 3, 4, 6, 7, 2, 5, 8]
TAPS = [(a, b) for a in (-1, 0, 1) for b in (-1, 0, 1)]
LEAD = 16
F32, BF16 = jnp.float32, jnp.bfloat16


def tap(a, b):
    return 3 * (a + 1) + (b + 1)


def dot(x, y):
    return jnp.dot(x, y, preferred_element_type=F32)


def rounded(x):
    return x.astype(BF16).astype(F32)


def up16(n):
    return -(-n // 16) * 16


def home(batch, r, c):
    number = lax.axis_size("row")
    core, row, col = (batch, r, c) if r == c else (int(r > c), r, c)
    if r != c and (r < c) == (batch == 1):
        row, col = c, r
    return (core * number + row) * number + col


def place():
    row, col = lax.axis_index("row"), lax.axis_index("col")
    low, high = jnp.minimum(row, col), jnp.maximum(row, col)
    upper = lax.axis_index("segment") == 0
    return jnp.where(upper, low, high), jnp.where(upper, high, low)


def permute(x, pair):
    number = lax.axis_size("row")
    tiles = [(m, r, c) for m in range(lax.axis_size("segment")) for r in range(number) for c in range(number)]
    pairs = [pair(*tile) for tile in tiles]
    return lax.ppermute(x, ALL, [found for found in pairs if found is not None])


def stored(batch, r, c):
    number = lax.axis_size("row")
    return (batch * number + r) * number + c


def bring(x, turn=None):
    def pair(batch, r, c):
        row = r if turn is None else partner(r, turn)
        if row is not None:
            return stored(batch, r, c), home(batch, row, c)

    return permute(x, pair)


def take_back(x):
    return permute(x, lambda m, r, c: (home(m, r, c), stored(m, r, c)))


def swap(x):
    return permute(x, lambda m, r, c: (home(m, r, c), home(m, c, r)))


def partner(index, turn):
    other = index + 1 if (index + turn) % 2 == 0 else index - 1
    return other if 0 <= other < lax.axis_size("row") else None


def exchange(x, axis, turn):
    def pair(batch, r, c):
        other = partner(c if axis else r, turn)
        if other is not None:
            return home(batch, r, c), home(batch, r, other) if axis else home(batch, other, c)

    return permute(x, pair)


def sends_last(axis, turn):
    return lax.rem(place()[axis] + turn, 2) == 0


def around(axis, got):
    even = sends_last(axis, 0)
    return jnp.where(even, got[1], got[0]), jnp.where(even, got[0], got[1])


def inside(shape, side, width, top):
    number = lax.axis_size("row") * side
    rows = lax.broadcasted_iota(jnp.int32, shape, 0) + top - width
    cols = lax.broadcasted_iota(jnp.int32, shape, 1) - width
    row, col = place()
    at_row = row * side + rows
    at_col = col * side + cols
    return (at_row >= 0) & (at_row < number) & (at_col >= 0) & (at_col < number) & (cols < side + width)


def paired(source, starts, width, dilation, pairs, last, change):
    lanes = source.shape[2]
    low, high = slice(0, lanes), slice(lanes, 2 * lanes)

    def step(k, _):
        rows, lower = pl.ds(4 * k, 4), pl.ds(4 * k + dilation, 4)
        window = [change(source[rows, at : at + width]).astype(BF16) for at in starts]
        pairs[rows, :, low] = window[0]
        pairs[rows, :, high] = window[1]
        last[lower, :, low] = window[2]
        last[rows, :, high] = window[2]
        return 0

    lax.fori_loop(0, source.shape[0] // 4, step, 0)


def taps_sum(pairs, last, top, rows, dilation, weights):
    width, lanes = pairs.shape[1], pairs.shape[2] // 2
    size = rows * width
    total = None
    for k in range(5):
        if k < 3:
            window = pairs[pl.ds(top + dilation * k, rows)]
        elif k == 3:
            window = last[pl.ds(top + dilation, rows)]
        else:
            window = last[pl.ds(top + 3 * dilation, rows), :, :lanes]
        weight = weights[2 * lanes * k : min(2 * lanes * (k + 1), 9 * lanes)]
        term = dot(window.reshape(size, window.shape[2]), weight)
        total = term if total is None else total + term
    return total


def positive(x):
    return jnp.maximum(x, 0)


def assemble(area, tile, above, below, left, right):
    side = tile.shape[0]
    full, wide, channels = area.shape
    middle = slice(LEAD, LEAD + side)
    area[:, :LEAD] = jnp.zeros((full, LEAD, channels), F32)
    area[:, LEAD + side :] = jnp.zeros((full, wide - LEAD - side, channels), F32)
    area[HALO : HALO + side, middle] = tile
    area[:HALO, middle] = above[:HALO].astype(F32)
    area[HALO + side :, middle] = below[:HALO].astype(F32)
    area[:, LEAD - HALO : LEAD] = left[...].astype(F32)
    area[:, LEAD + side : LEAD + side + HALO] = right[...].astype(F32)


def first_branch(area, pairs, last, weights, bias, proj, store):
    full, wide = pairs.shape[:2]
    start = LEAD - SECOND_DILATION
    starts = [start + FIRST_DILATION * b for b in (-1, 0, 1)]
    paired(area, starts, wide, FIRST_DILATION, pairs, last, positive)

    def rows(step, _):
        top = step * 8
        pre = taps_sum(pairs, last, top, 8, FIRST_DILATION, weights) + bias[...]
        branch = dot(positive(pre).astype(BF16), proj[...])
        inputs = area[pl.ds(top + FIRST_DILATION, 8), start : start + wide]
        branch = rounded(inputs + branch.reshape(inputs.shape))
        store(top, pre.reshape(8, wide, pre.shape[1]), branch)
        return 0

    lax.fori_loop(0, (full - 2 * FIRST_DILATION) // 8, rows, 0)


def own_kernel(
    brought, above, below, left, right, weights, bias, proj,
    swapped, gate_first, bottle_first, near_hidden,
    area, pairs, last, pre,
):
    side, first, second, inner = brought.shape[1], FIRST_DILATION, SECOND_DILATION, bias.shape[1]
    near, small = gate_first.shape[:2]
    span = side + 2 * second
    assemble(area, brought[:side].astype(F32), above, below, left, right)

    def store(top, pre_act, branch):
        pre[pl.ds(top, 8)] = pre_act
        swapped[pl.ds(top, 8)] = branch[:, :span].astype(BF16)

    first_branch(area, pairs, last, weights, bias, proj, store)
    swapped[span:, :side] = brought[side:]
    for b in (-1, 0, 1):
        at = LEAD + first * b
        near_hidden[b + 1] = positive(area[HALO - first : HALO + side + first, at : at + small]).astype(BF16)
    edge = second - first
    part = pre[edge : edge + near, edge : edge + small]
    alive = (part > 0) & inside(part.shape, side, first, 0)
    gate_first[:, :, :inner] = jnp.where(alive, 1.0, 0.0).astype(BF16)
    gate_first[:, :, inner:] = jnp.zeros((near, small, gate_first.shape[2] - inner), BF16)
    bottle_first[...] = positive(pre[second : second + side, second : second + small]).astype(BF16)


def middle_kernel(
    kept, other, w_second, b_second, p_second,
    gate_second, hidden_pairs, hidden_last, bottle_second, grad_tile, grad_pre, first_turn, second_turn,
    current, padded, pre_second,
):
    side, channels, span = first_turn.shape[1], kept.shape[2], kept.shape[1]
    first, second, inner = FIRST_DILATION, SECOND_DILATION, bottle_second.shape[2]
    near, small = gate_second.shape[:2]
    turned = jnp.swapaxes(other[:span].astype(F32), 0, 1)
    sym = rounded((kept[:span].astype(F32) + turned) * 0.5)
    current[:, :span] = jnp.where(inside(sym.shape, side, second, 0), sym, 0)
    current[:, span:] = jnp.zeros((span, current.shape[1] - span, channels), F32)
    edge = second - first
    part = current[edge : edge + near, edge : edge + small]
    gate_second[...] = jnp.where(part > 0, 1.0, 0.0).astype(BF16)
    paired(current, [0, second, 2 * second], small, second, hidden_pairs, hidden_last, positive)

    def rows(step, _):
        top = step * 8
        total = taps_sum(hidden_pairs, hidden_last, top, 8, second, w_second) + b_second[...]
        pre_second[pl.ds(top, 8)] = total.reshape(8, small, total.shape[1])
        return 0

    lax.fori_loop(0, side // 8, rows, 0)
    bottle_second[...] = positive(pre_second[:, :, :inner]).astype(BF16)

    turned = jnp.swapaxes(other[span:, :side].astype(F32), 0, 1)
    padded[:, side:] = jnp.zeros((side, small - side, channels), F32)
    padded[:, :side] = rounded((kept[span:, :side].astype(F32) + turned) * 0.5)
    branch = padded[...].astype(BF16)
    grad_tile[...] = branch
    grad = dot(branch.reshape(side * small, channels), p_second[...]).reshape(side, small, 2 * inner)
    grad = jnp.where(pre_second[...] > 0, grad, 0)
    grad_pre[...] = grad.astype(BF16)
    even = sends_last(0, 0)
    for rows, value, width in ((slice(0, HALO), grad, HALO), (slice(HALO, HALO + first), padded[...], first)):
        head, tail = value[:width, :side], value[side - width :, :side]
        first_turn[rows] = jnp.where(even, tail, head).astype(BF16)
        second_turn[rows] = jnp.where(even, head, tail).astype(BF16)


def weight_sums(rows, ends, grad_pre, hidden, bottle, grad_tile):
    side, small, lanes = grad_pre.shape
    inner = bottle.shape[2]
    size = side * small
    flat = grad_pre.reshape(size, lanes)
    turned = flat.T[:inner].astype(BF16)
    for a in range(3):
        b = 0
        while b < 3:
            window = hidden(a, b)
            grads = dot(turned, window.reshape(size, window.shape[2]))
            for at in range(0, window.shape[2], grad_tile.shape[2]):
                rows[(3 * a + b) * inner : (3 * a + b + 1) * inner] = grads[:, at : at + grad_tile.shape[2]]
                b += 1
    turned = bottle[...].reshape(size, inner).astype(F32).T.astype(BF16)
    rows[9 * inner : 10 * inner] = dot(turned, grad_tile.reshape(size, grad_tile.shape[2]))
    ends[...] = jnp.zeros(ends.shape, F32)
    ends[:, :lanes] = jnp.broadcast_to(jnp.sum(flat, axis=0, keepdims=True), (ends.shape[0], lanes))


def weights_kernel(
    mine, theirs, w_first, w_second, v_second, v_first, p_first, p_second, p_back, b_first, b_second, packed
):
    inner, channels = p_first.shape
    section = lax.axis_index("segment")
    packed[section] = mine[...]
    packed[1 - section] = theirs[...]

    def conv(section, k):
        return packed[section, k * inner : (k + 1) * inner]

    def turned(x):
        return x.astype(F32).T.astype(BF16)

    zero = jnp.zeros((inner, channels), BF16)
    for at, k in enumerate(ORDER):
        here = slice(at * channels, (at + 1) * channels)
        own, other = conv(1, k), conv(1, 3 * (k % 3) + k // 3)
        w_first[here] = turned(conv(0, k))
        w_second[here] = turned(jnp.concatenate([own, other], axis=0))
        v_second[k, :inner, :channels], v_second[k, :inner, channels:] = own, zero
        v_second[k, inner:, :channels], v_second[k, inner:, channels:] = zero, other
        v_first[k, :inner], v_first[k, inner:] = conv(0, k), zero
    p_first[...] = conv(0, 9)
    p_second[...] = turned(jnp.concatenate([conv(1, 9), conv(1, 9)], axis=0))
    p_back[...] = turned(jnp.concatenate([conv(0, 9), zero], axis=0))
    b_first[...] = packed[0, 10 * inner :].astype(F32)[:1, :inner]
    bias = packed[1, 10 * inner :].astype(F32)[:1, :inner]
    b_second[...] = jnp.concatenate([bias, bias], axis=1)


def second_sums_kernel(grad_pre, pairs, last, bottle, grad_tile, rows, ends):
    side = grad_pre.shape[0]
    channels = grad_tile.shape[2]

    def hidden(a, b):
        top = SECOND_DILATION * a
        if b == 0:
            return pairs[top : top + side]
        return last[top + SECOND_DILATION : top + SECOND_DILATION + side, :, :channels]

    weight_sums(rows, ends, grad_pre[...].astype(F32), hidden, bottle, grad_tile[...])


def backward_kernel(
    grad_pre, grad_tile, above, below, left, right, left_branch, right_branch, gate_second, gate_first, near_hidden,
    bottle_first, v_second, p_first, rows_second, ends_second,
    keep, away, windows, grad_first,
    area, shifted, branch, grads, rows, ends,
):
    side, channels = grad_first.shape[0], grad_first.shape[2]
    first, second = FIRST_DILATION, SECOND_DILATION
    full, near = side + 2 * HALO, side + 2 * first
    small = grad_pre.shape[1]
    middle = slice(LEAD, LEAD + side)

    area[:, :LEAD] = jnp.zeros((full, LEAD, channels), F32)
    area[:, LEAD + side :] = jnp.zeros((full, area.shape[1] - LEAD - side, channels), F32)
    area[HALO : HALO + side, LEAD : LEAD + small] = grad_pre[...].astype(F32)
    area[:HALO, middle] = above[:HALO].astype(F32)
    area[HALO + side :, middle] = below[:HALO].astype(F32)
    area[:, LEAD - HALO : LEAD] = left[...].astype(F32)
    area[:, LEAD + side : LEAD + side + HALO] = right[...].astype(F32)
    branch[...] = jnp.zeros(branch.shape, F32)
    branch[first : first + side, first : first + side] = grad_tile[:, :side].astype(F32)
    branch[:first, first : first + side] = above[HALO:].astype(F32)
    branch[first + side :, first : first + side] = below[HALO:].astype(F32)
    branch[:, :first] = left_branch[...].astype(F32)
    branch[:, first + side : near] = right_branch[...].astype(F32)
    for b in (-1, 0, 1):
        at = LEAD - HALO + second * (1 - b)
        shifted[b + 1] = area[:, at : at + small].astype(BF16)
    grads[:, small:] = jnp.zeros((near, grads.shape[1] - small, channels), F32)

    def sections(step, _):
        top = step * 7
        size = 7 * small
        total = jnp.zeros((size, 2 * channels), F32)
        for a, b in TAPS:
            window = shifted[b + 1, pl.ds(top + second * (1 - a), 7)].reshape(size, channels)
            total = total + dot(window, v_second[tap(a, b)])
        here = pl.ds(top, 7)
        grad = branch[here, :small].reshape(size, channels)
        gate = gate_second[here].astype(F32).reshape(size, channels) > 0
        own = rounded(grad + jnp.where(gate, total[:, :channels], 0))
        other = rounded(grad + jnp.where(gate, total[:, channels:], 0))
        grad = ((own + other) * 0.5).astype(BF16)
        branch[here, :small] = grad.astype(F32).reshape(7, small, channels)
        gate = gate_first[here].astype(F32).reshape(size, channels) > 0
        grad = rounded(jnp.where(gate, dot(grad, p_first[...]), 0))
        grads[here, :small] = grad.reshape(7, small, channels)
        return 0

    lax.fori_loop(0, near // 7, sections, 0)
    for b in (-1, 0, 1):
        at = first * (1 - b)
        windows[b + 1] = grads[:, at : at + small].astype(BF16)
    part = branch[first : first + side, first : first + small]
    grad_first[...] = part[:, :side].astype(BF16)
    real = lax.broadcasted_iota(jnp.int32, part.shape, 1) < side
    part = jnp.where(real, part, 0).astype(BF16)
    grad = jnp.where(real, grads[first : first + side, first : first + small], 0)

    def hidden(a, b):
        return near_hidden[b, first * a : first * a + side]

    weight_sums(rows, ends, grad, hidden, bottle_first, part)

    first_core = lax.axis_index("segment") == 0
    count = rows.shape[0]
    for here, one, two in (
        (slice(0, count), rows[...], rows_second[...]),
        (slice(count, count + ends.shape[0]), ends[...], ends_second[...]),
    ):
        keep[here] = jnp.where(first_core, one, two)
        away[here] = jnp.where(first_core, two, one).astype(BF16)


def pair_kernel(keep, other, parts):
    devices, share = parts.shape[0], parts.shape[1] - 8
    total = keep[...] + other[...].astype(F32)
    count = keep.shape[0] - 16
    for j in range(devices):
        low, high = min(j * share, count), min((j + 1) * share, count)
        pieces = [total[low:high]] if low < high else []
        if high - low < share:
            pieces.append(jnp.zeros((share - (high - low), keep.shape[1]), F32))
        parts[j] = jnp.concatenate(pieces + [total[count : count + 8]]).astype(BF16)


def input_kernel(windows, grad_first, brought, v_first, out):
    side, channels = out.shape[0], out.shape[2]
    small = windows.shape[2]
    first = FIRST_DILATION

    def rows(step, _):
        top = step * 8
        total = jnp.zeros((8 * small, channels), F32)
        for a, b in TAPS:
            window = windows[b + 1, pl.ds(top + first * (1 - a), 8)].reshape(8 * small, channels)
            total = total + dot(window, v_first[tap(a, b)])
        here = pl.ds(top, 8)
        total = total.reshape(8, small, channels)[:, :side]
        total = jnp.where(brought[here].astype(F32) > 0, total, 0)
        out[here] = (grad_first[here].astype(F32) + total).astype(BF16)
        return 0

    lax.fori_loop(0, side // 8, rows, 0)


def total_kernel(scale, parts, rows, ends):
    share = rows.shape[1]
    total = jnp.sum(parts[...].astype(F32), axis=0) * scale
    rows[...] = jnp.broadcast_to(total[:share].astype(BF16)[None], rows.shape)
    ends[...] = total[share:]


def outputs_kernel(rows, ends, moved, conv_gradient, bias_gradient, out_gradient, input_gradient):
    count, inner = conv_gradient.shape[0], out_gradient.shape[0]
    conv_gradient[...] = rows[:count].astype(F32)
    out_gradient[...] = rows[count : count + inner].astype(F32)
    bias_gradient[...] = ends[:1, :inner]
    input_gradient[...] = moved[...]


def call(kernel, name, outs, scratch, flops, *operands):
    outs = [jax.ShapeDtypeStruct(shape, dtype) for shape, dtype in outs]
    moved = sum(x.size * x.dtype.itemsize for x in list(operands) + outs)
    return pl.pallas_call(
        kernel,
        name=name,
        out_shape=outs,
        scratch_shapes=[pltpu.VMEM(shape, dtype) for shape, dtype in scratch],
        cost_estimate=pl.CostEstimate(flops=flops, bytes_accessed=moved, transcendentals=0),
        compiler_params=pltpu.CompilerParams(vmem_limit_bytes=40 * 1024 * 1024),
    )(*operands)


def local(activations, cotangent, conv_weight, conv_bias, out_weight):
    side, channels, inner = activations.shape[1], activations.shape[3], conv_weight.shape[3]
    number = lax.axis_size("row")
    first, second = FIRST_DILATION, SECOND_DILATION
    full, span, near = side + 2 * HALO, side + 2 * second, side + 2 * first
    wide, small = up16(span), up16(near)

    brought = bring(jnp.concatenate([activations[0], cotangent[0]]))
    tile = brought[:side]
    stored_even = lax.rem(lax.axis_index("row"), 2) == 0
    ends = (activations[0, side - HALO :], activations[0, :HALO])
    got = [bring(jnp.where(stored_even, *ends), 0), bring(jnp.where(stored_even, *ends[::-1]), 1)]
    above, below = around(0, got)

    def columns(turn):
        def chosen(x):
            return jnp.swapaxes(jnp.where(sends_last(1, turn), x[:, side - HALO :], x[:, :HALO]), 0, 1)

        strip = jnp.pad(chosen(tile), ((0, 0), (HALO, HALO), (0, 0)))
        strip = lax.optimization_barrier(strip)
        for row_turn in (0, 1):
            at = jnp.where(sends_last(0, row_turn), HALO + side, 0)
            strip = lax.dynamic_update_slice(strip, chosen(got[row_turn]), (0, at, 0))
        return strip

    left, right = around(1, [exchange(columns(turn), 1, turn) for turn in (0, 1)])

    bias_rows = jnp.pad(conv_bias, ((0, 15), (0, channels - inner)))
    packed = jnp.concatenate(
        [jnp.swapaxes(conv_weight[0], 1, 2).reshape(9 * inner, channels), out_weight[0], bias_rows]
    )
    others = lax.ppermute(packed, "segment", [(0, 1), (1, 0)])
    w_first, w_second, v_second, v_first, p_first, p_second, p_back, b_first, b_second = call(
        weights_kernel,
        "weights",
        [
            ((9 * channels, inner), BF16),
            ((9 * channels, 2 * inner), BF16),
            ((9, 2 * inner, 2 * channels), BF16),
            ((9, 2 * inner, channels), BF16),
            ((inner, channels), BF16),
            ((channels, 2 * inner), BF16),
            ((channels, 2 * inner), BF16),
            ((1, inner), F32),
            ((1, 2 * inner), F32),
        ],
        [((2,) + packed.shape, BF16)],
        packed.size,
        *(packed, others),
    )

    kept, gate_first, bottle_first, near_hidden = call(
        own_kernel,
        "own_branch",
        [
            ((span + side, span, channels), BF16),
            ((near, small, channels), BF16),
            ((side, small, inner), BF16),
            ((3, near, small, channels), BF16),
        ],
        [
            ((full, LEAD + up16(side + LEAD), channels), F32),
            ((full, wide, 2 * channels), BF16),
            ((full + first, wide, 2 * channels), BF16),
            ((span, wide, inner), F32),
        ],
        span * wide * channels * inner * 20,
        *(brought, above, below, jnp.swapaxes(left, 0, 1), jnp.swapaxes(right, 0, 1)),
        *(w_first, b_first, p_first),
    )
    other = swap(kept)
    gate_second, hidden_pairs, hidden_last, bottle_second, grad_tile, grad_pre, *strips = call(
        middle_kernel,
        "middle",
        [
            ((near, small, channels), BF16),
            ((span, small, 2 * channels), BF16),
            ((span + second, small, 2 * channels), BF16),
            ((side, small, inner), BF16),
            ((side, small, channels), BF16),
            ((side, small, 2 * inner), BF16),
            ((HALO + first, side, channels), BF16),
            ((HALO + first, side, channels), BF16),
        ],
        [
            ((span, wide, channels), F32),
            ((side, small, channels), F32),
            ((side, small, 2 * inner), F32),
        ],
        24 * side * small * channels * 2 * inner,
        *(kept, other, w_second, b_second, p_second),
    )

    above, below = around(0, [exchange(strips[turn], 0, turn) for turn in (0, 1)])
    rows_second, ends_second = call(
        second_sums_kernel,
        "second_sums",
        [((10 * inner, channels), F32), ((16, channels), F32)],
        [],
        20 * side * small * channels * inner,
        *(grad_pre, hidden_pairs, hidden_last, bottle_second, grad_tile),
    )

    def columns(turn):
        def chosen(x, width):
            return jnp.where(sends_last(1, turn), x[:, side - width : side], x[:, :width])

        grads = jnp.concatenate([chosen(x, HALO) for x in (above[:HALO], grad_pre, below[:HALO])])
        branches = jnp.concatenate([chosen(x, first) for x in (above[HALO:], grad_tile, below[HALO:])])
        branches = jnp.pad(branches, ((second, second), (0, 0), (0, 0)))
        return jnp.swapaxes(jnp.concatenate([grads, branches], axis=1), 0, 1)

    left, right = around(1, [exchange(columns(turn), 1, turn) for turn in (0, 1)])
    left, right = jnp.swapaxes(left, 0, 1), jnp.swapaxes(right, 0, 1)

    devices = number * number
    share = -(-10 * inner // (8 * devices)) * 8
    keep, away, windows, grad_first = call(
        backward_kernel,
        "backward",
        [
            ((10 * inner + 16, channels), F32),
            ((10 * inner + 16, channels), BF16),
            ((3, near, small, channels), BF16),
            ((side, side, channels), BF16),
        ],
        [
            ((full, LEAD + up16(side + HALO + first), channels), F32),
            ((3, full, small, channels), BF16),
            ((near, small + 16, channels), F32),
            ((near, small + 16, channels), F32),
            ((10 * inner, channels), F32),
            ((16, channels), F32),
        ],
        36 * near * small * channels * channels,
        *(grad_pre, grad_tile, above, below, left[:, :HALO], right[:, :HALO]),
        *(left[second : second + near, HALO:], right[second : second + near, HALO:]),
        *(gate_second, gate_first, near_hidden, bottle_first, v_second, p_back, rows_second, ends_second),
    )

    (input_gradient,) = call(
        input_kernel,
        "input",
        [((side, side, channels), BF16)],
        [],
        18 * side * small * channels * channels,
        *(windows, grad_first, brought, v_first),
    )
    other = lax.ppermute(away, "segment", [(0, 1), (1, 0)])
    other, input_gradient = lax.optimization_barrier((other, input_gradient))
    (parts,) = call(
        pair_kernel,
        "pair",
        [((devices, share + 8, channels), BF16)],
        [],
        keep.size,
        *(keep, other),
    )
    parts = lax.all_to_all(parts, GRID, 0, 0, tiled=True)
    input_gradient = take_back(input_gradient)
    cells = lax.axis_size("segment") * (side * number) * (side * number)
    rows, ends = call(
        functools.partial(total_kernel, float(cells) ** -0.5),
        "total",
        [((devices, share, channels), BF16), ((8, channels), F32)],
        [],
        parts.size,
        parts,
    )
    rows, _ = lax.optimization_barrier((rows, input_gradient))
    rows = lax.all_to_all(rows, GRID, 0, 0, tiled=True).reshape(devices * share, channels)
    conv_gradient, bias_gradient, out_gradient, input_gradient = call(
        outputs_kernel,
        "outputs",
        [
            ((9 * inner, channels), F32),
            ((1, inner), F32),
            ((inner, channels), F32),
            ((side, side, channels), BF16),
        ],
        [],
        rows.size,
        *(rows, ends, input_gradient),
    )
    conv_gradient = jnp.swapaxes(conv_gradient.reshape(1, 9, inner, channels), 2, 3)
    return (input_gradient[None], conv_gradient, bias_gradient, out_gradient[None])


def solution(mesh):
    in_specs = (
        P("segment", "row", "col", None),
        P("segment", "row", "col", None),
        P("segment", None, None, None),
        P("segment", None),
        P("segment", None, None),
    )
    out_specs = (
        P("segment", "row", "col", None),
        P("segment", None, None, None),
        P("segment", None),
        P("segment", None, None),
    )
    return jax.shard_map(local, mesh=mesh, in_specs=in_specs, out_specs=out_specs, check_vma=False)
```

```python
import functools

import jax
import jax.numpy as jnp
from jax import lax
from jax.experimental import pallas as pl
from jax.experimental.pallas import tpu as pltpu
from jax.sharding import PartitionSpec as P

FIRST_DILATION = 2
SECOND_DILATION = 8
HALO = FIRST_DILATION + SECOND_DILATION
GRID = ("row", "col")
ALL = ("segment",) + GRID
ORDER = [0, 1, 3, 4, 6, 7, 2, 5, 8]
TAPS = [(a, b) for a in (-1, 0, 1) for b in (-1, 0, 1)]
LEAD = 16
F32, BF16 = jnp.float32, jnp.bfloat16


def tap(a, b):
    return 3 * (a + 1) + (b + 1)


def dot(x, y):
    return jnp.dot(x, y, preferred_element_type=F32)


def rounded(x):
    return x.astype(BF16).astype(F32)


def up16(n):
    return -(-n // 16) * 16


def home(batch, r, c):
    number = lax.axis_size("row")
    core, row, col = (batch, r, c) if r == c else (int(r > c), r, c)
    if r != c and (r < c) == (batch == 1):
        row, col = c, r
    return (core * number + row) * number + col


def place():
    row, col = lax.axis_index("row"), lax.axis_index("col")
    low, high = jnp.minimum(row, col), jnp.maximum(row, col)
    upper = lax.axis_index("segment") == 0
    return jnp.where(upper, low, high), jnp.where(upper, high, low)


def permute(x, pair):
    number = lax.axis_size("row")
    tiles = [(m, r, c) for m in range(lax.axis_size("segment")) for r in range(number) for c in range(number)]
    pairs = [pair(*tile) for tile in tiles]
    return lax.ppermute(x, ALL, [found for found in pairs if found is not None])


def stored(batch, r, c):
    number = lax.axis_size("row")
    return (batch * number + r) * number + c


def bring(x, turn=None):
    def pair(batch, r, c):
        row = r if turn is None else partner(r, turn)
        if row is not None:
            return stored(batch, r, c), home(batch, row, c)

    return permute(x, pair)


def take_back(x):
    return permute(x, lambda m, r, c: (home(m, r, c), stored(m, r, c)))


def swap(x):
    return permute(x, lambda m, r, c: (home(m, r, c), home(m, c, r)))


def partner(index, turn):
    other = index + 1 if (index + turn) % 2 == 0 else index - 1
    return other if 0 <= other < lax.axis_size("row") else None


def exchange(x, axis, turn):
    def pair(batch, r, c):
        other = partner(c if axis else r, turn)
        if other is not None:
            return home(batch, r, c), home(batch, r, other) if axis else home(batch, other, c)

    return permute(x, pair)


def sends_last(axis, turn):
    return lax.rem(place()[axis] + turn, 2) == 0


def around(axis, got):
    even = sends_last(axis, 0)
    return jnp.where(even, got[1], got[0]), jnp.where(even, got[0], got[1])


def inside(shape, side, width, top):
    number = lax.axis_size("row") * side
    rows = lax.broadcasted_iota(jnp.int32, shape, 0) + top - width
    cols = lax.broadcasted_iota(jnp.int32, shape, 1) - width
    row, col = place()
    at_row = row * side + rows
    at_col = col * side + cols
    return (at_row >= 0) & (at_row < number) & (at_col >= 0) & (at_col < number) & (cols < side + width)


def paired(source, starts, width, dilation, pairs, last, change):
    lanes = source.shape[2]
    low, high = slice(0, lanes), slice(lanes, 2 * lanes)

    def step(k, _):
        rows, lower = pl.ds(4 * k, 4), pl.ds(4 * k + dilation, 4)
        window = [change(source[rows, at : at + width]).astype(BF16) for at in starts]
        pairs[rows, :, low] = window[0]
        pairs[rows, :, high] = window[1]
        last[lower, :, low] = window[2]
        last[rows, :, high] = window[2]
        return 0

    lax.fori_loop(0, source.shape[0] // 4, step, 0)


def taps_sum(pairs, last, top, rows, dilation, weights):
    width, lanes = pairs.shape[1], pairs.shape[2] // 2
    size = rows * width
    total = None
    for k in range(5):
        if k < 3:
            window = pairs[pl.ds(top + dilation * k, rows)]
        elif k == 3:
            window = last[pl.ds(top + dilation, rows)]
        else:
            window = last[pl.ds(top + 3 * dilation, rows), :, :lanes]
        weight = weights[2 * lanes * k : min(2 * lanes * (k + 1), 9 * lanes)]
        term = dot(window.reshape(size, window.shape[2]), weight)
        total = term if total is None else total + term
    return total


def positive(x):
    return jnp.maximum(x, 0)


def assemble(area, tile, above, below, left, right):
    side = tile.shape[0]
    full, wide, channels = area.shape
    middle = slice(LEAD, LEAD + side)
    area[:, :LEAD] = jnp.zeros((full, LEAD, channels), F32)
    area[:, LEAD + side :] = jnp.zeros((full, wide - LEAD - side, channels), F32)
    area[HALO : HALO + side, middle] = tile
    area[:HALO, middle] = above[:HALO].astype(F32)
    area[HALO + side :, middle] = below[:HALO].astype(F32)
    area[:, LEAD - HALO : LEAD] = left[...].astype(F32)
    area[:, LEAD + side : LEAD + side + HALO] = right[...].astype(F32)


def first_branch(area, pairs, last, weights, bias, proj, store):
    full, wide = pairs.shape[:2]
    start = LEAD - SECOND_DILATION
    starts = [start + FIRST_DILATION * b for b in (-1, 0, 1)]
    paired(area, starts, wide, FIRST_DILATION, pairs, last, positive)

    def rows(step, _):
        top = step * 8
        pre = taps_sum(pairs, last, top, 8, FIRST_DILATION, weights) + bias[...]
        branch = dot(positive(pre).astype(BF16), proj[...])
        inputs = area[pl.ds(top + FIRST_DILATION, 8), start : start + wide]
        branch = rounded(inputs + branch.reshape(inputs.shape))
        store(top, pre.reshape(8, wide, pre.shape[1]), branch)
        return 0

    lax.fori_loop(0, (full - 2 * FIRST_DILATION) // 8, rows, 0)


def own_kernel(
    tile, above, below, left, right, weights, bias, proj,
    swapped, gate_first, bottle_first, near_hidden,
    area, pairs, last, pre,
):
    side, first, second, inner = tile.shape[0], FIRST_DILATION, SECOND_DILATION, bias.shape[1]
    near, small = gate_first.shape[:2]
    span = side + 2 * second
    assemble(area, tile[...].astype(F32), above, below, left, right)

    def store(top, pre_act, branch):
        pre[pl.ds(top, 8)] = pre_act
        swapped[pl.ds(top, 8)] = branch[:, :span].astype(BF16)

    first_branch(area, pairs, last, weights, bias, proj, store)
    swapped[span:] = jnp.zeros((side, span, swapped.shape[2]), BF16)
    for b in (-1, 0, 1):
        at = LEAD + first * b
        near_hidden[b + 1] = positive(area[HALO - first : HALO + side + first, at : at + small]).astype(BF16)
    edge = second - first
    part = pre[edge : edge + near, edge : edge + small]
    alive = (part > 0) & inside(part.shape, side, first, 0)
    gate_first[:, :, :inner] = jnp.where(alive, 1.0, 0.0).astype(BF16)
    gate_first[:, :, inner:] = jnp.zeros((near, small, gate_first.shape[2] - inner), BF16)
    bottle_first[...] = positive(pre[second : second + side, second : second + small]).astype(BF16)


def middle_kernel(
    kept, other, w_second, b_second, p_second,
    gate_second, hidden_pairs, hidden_last, bottle_second, grad_tile, grad_pre, first_turn, second_turn,
    current, padded, pre_second,
):
    side, channels, span = first_turn.shape[1], kept.shape[2], kept.shape[1]
    first, second, inner = FIRST_DILATION, SECOND_DILATION, bottle_second.shape[2]
    near, small = gate_second.shape[:2]
    turned = jnp.swapaxes(other[:span].astype(F32), 0, 1)
    sym = rounded((kept[:span].astype(F32) + turned) * 0.5)
    current[:, :span] = jnp.where(inside(sym.shape, side, second, 0), sym, 0)
    current[:, span:] = jnp.zeros((span, current.shape[1] - span, channels), F32)
    edge = second - first
    part = current[edge : edge + near, edge : edge + small]
    gate_second[...] = jnp.where(part > 0, 1.0, 0.0).astype(BF16)
    paired(current, [0, second, 2 * second], small, second, hidden_pairs, hidden_last, positive)

    def rows(step, _):
        top = step * 8
        total = taps_sum(hidden_pairs, hidden_last, top, 8, second, w_second) + b_second[...]
        pre_second[pl.ds(top, 8)] = total.reshape(8, small, total.shape[1])
        return 0

    lax.fori_loop(0, side // 8, rows, 0)
    bottle_second[...] = positive(pre_second[:, :, :inner]).astype(BF16)

    turned = jnp.swapaxes(other[span:, :side].astype(F32), 0, 1)
    padded[:, side:] = jnp.zeros((side, small - side, channels), F32)
    padded[:, :side] = rounded((kept[span:, :side].astype(F32) + turned) * 0.5)
    branch = padded[...].astype(BF16)
    grad_tile[...] = branch
    grad = dot(branch.reshape(side * small, channels), p_second[...]).reshape(side, small, 2 * inner)
    grad = jnp.where(pre_second[...] > 0, grad, 0)
    grad_pre[...] = grad.astype(BF16)
    even = sends_last(0, 0)
    for rows, value, width in ((slice(0, HALO), grad, HALO), (slice(HALO, HALO + first), padded[...], first)):
        head, tail = value[:width, :side], value[side - width :, :side]
        first_turn[rows] = jnp.where(even, tail, head).astype(BF16)
        second_turn[rows] = jnp.where(even, head, tail).astype(BF16)


def weight_sums(rows, ends, grad_pre, hidden, bottle, grad_tile):
    side, small, lanes = grad_pre.shape
    inner = bottle.shape[2]
    size = side * small
    flat = grad_pre.reshape(size, lanes)
    turned = flat.T[:inner].astype(BF16)
    for a in range(3):
        b = 0
        while b < 3:
            window = hidden(a, b)
            grads = dot(turned, window.reshape(size, window.shape[2]))
            for at in range(0, window.shape[2], grad_tile.shape[2]):
                rows[(3 * a + b) * inner : (3 * a + b + 1) * inner] = grads[:, at : at + grad_tile.shape[2]]
                b += 1
    turned = bottle[...].reshape(size, inner).astype(F32).T.astype(BF16)
    rows[9 * inner : 10 * inner] = dot(turned, grad_tile.reshape(size, grad_tile.shape[2]))
    ends[...] = jnp.zeros(ends.shape, F32)
    ends[:, :lanes] = jnp.broadcast_to(jnp.sum(flat, axis=0, keepdims=True), (ends.shape[0], lanes))


def weights_kernel(
    mine, theirs, w_first, w_second, v_second, v_first, p_first, p_second, p_back, b_first, b_second, packed
):
    inner, channels = p_first.shape
    section = lax.axis_index("segment")
    packed[section] = mine[...]
    packed[1 - section] = theirs[...]

    def conv(section, k):
        return packed[section, k * inner : (k + 1) * inner]

    def turned(x):
        return x.astype(F32).T.astype(BF16)

    zero = jnp.zeros((inner, channels), BF16)
    for at, k in enumerate(ORDER):
        here = slice(at * channels, (at + 1) * channels)
        own, other = conv(1, k), conv(1, 3 * (k % 3) + k // 3)
        w_first[here] = turned(conv(0, k))
        w_second[here] = turned(jnp.concatenate([own, other], axis=0))
        v_second[k, :inner, :channels], v_second[k, :inner, channels:] = own, zero
        v_second[k, inner:, :channels], v_second[k, inner:, channels:] = zero, other
        v_first[k, :inner], v_first[k, inner:] = conv(0, k), zero
    p_first[...] = conv(0, 9)
    p_second[...] = turned(jnp.concatenate([conv(1, 9), conv(1, 9)], axis=0))
    p_back[...] = turned(jnp.concatenate([conv(0, 9), zero], axis=0))
    b_first[...] = packed[0, 10 * inner :].astype(F32)[:1, :inner]
    bias = packed[1, 10 * inner :].astype(F32)[:1, :inner]
    b_second[...] = jnp.concatenate([bias, bias], axis=1)


def second_sums_kernel(grad_pre, pairs, last, bottle, grad_tile, rows, ends):
    side = grad_pre.shape[0]
    channels = grad_tile.shape[2]

    def hidden(a, b):
        top = SECOND_DILATION * a
        if b == 0:
            return pairs[top : top + side]
        return last[top + SECOND_DILATION : top + SECOND_DILATION + side, :, :channels]

    weight_sums(rows, ends, grad_pre[...].astype(F32), hidden, bottle, grad_tile[...])


def backward_kernel(
    grad_pre, grad_tile, above, below, left, right, left_branch, right_branch, gate_second, gate_first, near_hidden,
    bottle_first, v_second, p_first, rows_second, ends_second,
    keep, away, windows, grad_first,
    area, shifted, branch, grads, rows, ends,
):
    side, channels = grad_first.shape[0], grad_first.shape[2]
    first, second = FIRST_DILATION, SECOND_DILATION
    full, near = side + 2 * HALO, side + 2 * first
    small = grad_pre.shape[1]
    middle = slice(LEAD, LEAD + side)

    area[:, :LEAD] = jnp.zeros((full, LEAD, channels), F32)
    area[:, LEAD + side :] = jnp.zeros((full, area.shape[1] - LEAD - side, channels), F32)
    area[HALO : HALO + side, LEAD : LEAD + small] = grad_pre[...].astype(F32)
    area[:HALO, middle] = above[:HALO].astype(F32)
    area[HALO + side :, middle] = below[:HALO].astype(F32)
    area[:, LEAD - HALO : LEAD] = left[...].astype(F32)
    area[:, LEAD + side : LEAD + side + HALO] = right[...].astype(F32)
    branch[...] = jnp.zeros(branch.shape, F32)
    branch[first : first + side, first : first + side] = grad_tile[:, :side].astype(F32)
    branch[:first, first : first + side] = above[HALO:].astype(F32)
    branch[first + side :, first : first + side] = below[HALO:].astype(F32)
    branch[:, :first] = left_branch[...].astype(F32)
    branch[:, first + side : near] = right_branch[...].astype(F32)
    for b in (-1, 0, 1):
        at = LEAD - HALO + second * (1 - b)
        shifted[b + 1] = area[:, at : at + small].astype(BF16)
    grads[:, small:] = jnp.zeros((near, grads.shape[1] - small, channels), F32)

    def sections(step, _):
        top = step * 7
        size = 7 * small
        total = jnp.zeros((size, 2 * channels), F32)
        for a, b in TAPS:
            window = shifted[b + 1, pl.ds(top + second * (1 - a), 7)].reshape(size, channels)
            total = total + dot(window, v_second[tap(a, b)])
        here = pl.ds(top, 7)
        grad = branch[here, :small].reshape(size, channels)
        gate = gate_second[here].astype(F32).reshape(size, channels) > 0
        own = rounded(grad + jnp.where(gate, total[:, :channels], 0))
        other = rounded(grad + jnp.where(gate, total[:, channels:], 0))
        grad = ((own + other) * 0.5).astype(BF16)
        branch[here, :small] = grad.astype(F32).reshape(7, small, channels)
        gate = gate_first[here].astype(F32).reshape(size, channels) > 0
        grad = rounded(jnp.where(gate, dot(grad, p_first[...]), 0))
        grads[here, :small] = grad.reshape(7, small, channels)
        return 0

    lax.fori_loop(0, near // 7, sections, 0)
    for b in (-1, 0, 1):
        at = first * (1 - b)
        windows[b + 1] = grads[:, at : at + small].astype(BF16)
    part = branch[first : first + side, first : first + small]
    grad_first[...] = part[:, :side].astype(BF16)
    real = lax.broadcasted_iota(jnp.int32, part.shape, 1) < side
    part = jnp.where(real, part, 0).astype(BF16)
    grad = jnp.where(real, grads[first : first + side, first : first + small], 0)

    def hidden(a, b):
        return near_hidden[b, first * a : first * a + side]

    weight_sums(rows, ends, grad, hidden, bottle_first, part)

    first_core = lax.axis_index("segment") == 0
    count = rows.shape[0]
    for here, one, two in (
        (slice(0, count), rows[...], rows_second[...]),
        (slice(count, count + ends.shape[0]), ends[...], ends_second[...]),
    ):
        keep[here] = jnp.where(first_core, one, two)
        away[here] = jnp.where(first_core, two, one).astype(BF16)


def pair_kernel(keep, other, parts):
    devices, share = parts.shape[0], parts.shape[1] - 8
    total = keep[...] + other[...].astype(F32)
    count = keep.shape[0] - 16
    for j in range(devices):
        low, high = min(j * share, count), min((j + 1) * share, count)
        pieces = [total[low:high]] if low < high else []
        if high - low < share:
            pieces.append(jnp.zeros((share - (high - low), keep.shape[1]), F32))
        parts[j] = jnp.concatenate(pieces + [total[count : count + 8]]).astype(BF16)


def input_kernel(windows, grad_first, tile, v_first, out):
    side, channels = out.shape[0], out.shape[2]
    small = windows.shape[2]
    first = FIRST_DILATION

    def rows(step, _):
        top = step * 8
        total = jnp.zeros((8 * small, channels), F32)
        for a, b in TAPS:
            window = windows[b + 1, pl.ds(top + first * (1 - a), 8)].reshape(8 * small, channels)
            total = total + dot(window, v_first[tap(a, b)])
        here = pl.ds(top, 8)
        total = total.reshape(8, small, channels)[:, :side]
        total = jnp.where(tile[here].astype(F32) > 0, total, 0)
        out[here] = (grad_first[here].astype(F32) + total).astype(BF16)
        return 0

    lax.fori_loop(0, side // 8, rows, 0)


def total_kernel(scale, parts, rows, ends):
    share = rows.shape[1]
    total = jnp.sum(parts[...].astype(F32), axis=0) * scale
    rows[...] = jnp.broadcast_to(total[:share].astype(BF16)[None], rows.shape)
    ends[...] = total[share:]


def outputs_kernel(rows, ends, moved, conv_gradient, bias_gradient, out_gradient, input_gradient):
    count, inner = conv_gradient.shape[0], out_gradient.shape[0]
    conv_gradient[...] = rows[:count].astype(F32)
    out_gradient[...] = rows[count : count + inner].astype(F32)
    bias_gradient[...] = ends[:1, :inner]
    input_gradient[...] = moved[...]


def call(kernel, name, outs, scratch, flops, *operands):
    outs = [jax.ShapeDtypeStruct(shape, dtype) for shape, dtype in outs]
    moved = sum(x.size * x.dtype.itemsize for x in list(operands) + outs)
    return pl.pallas_call(
        kernel,
        name=name,
        out_shape=outs,
        scratch_shapes=[pltpu.VMEM(shape, dtype) for shape, dtype in scratch],
        cost_estimate=pl.CostEstimate(flops=flops, bytes_accessed=moved, transcendentals=0),
        compiler_params=pltpu.CompilerParams(vmem_limit_bytes=40 * 1024 * 1024),
    )(*operands)


def local(activations, cotangent, conv_weight, conv_bias, out_weight):
    side, channels, inner = activations.shape[1], activations.shape[3], conv_weight.shape[3]
    number = lax.axis_size("row")
    first, second = FIRST_DILATION, SECOND_DILATION
    full, span, near = side + 2 * HALO, side + 2 * second, side + 2 * first
    wide, small = up16(span), up16(near)

    tile = bring(activations[0])
    stored_even = lax.rem(lax.axis_index("row"), 2) == 0
    ends = (activations[0, side - HALO :], activations[0, :HALO])
    got = [bring(jnp.where(stored_even, *ends), 0), bring(jnp.where(stored_even, *ends[::-1]), 1)]
    above, below = around(0, got)

    def columns(turn):
        def chosen(x):
            return jnp.swapaxes(jnp.where(sends_last(1, turn), x[:, side - HALO :], x[:, :HALO]), 0, 1)

        strip = jnp.pad(chosen(tile), ((0, 0), (HALO, HALO), (0, 0)))
        strip = lax.optimization_barrier(strip)
        for row_turn in (0, 1):
            at = jnp.where(sends_last(0, row_turn), HALO + side, 0)
            strip = lax.dynamic_update_slice(strip, chosen(got[row_turn]), (0, at, 0))
        return strip

    strips, late = lax.optimization_barrier(([columns(0), columns(1)], cotangent[0]))
    left, right = around(1, [exchange(strips[turn], 1, turn) for turn in (0, 1)])
    late = bring(late)

    bias_rows = jnp.pad(conv_bias, ((0, 15), (0, channels - inner)))
    packed = jnp.concatenate(
        [jnp.swapaxes(conv_weight[0], 1, 2).reshape(9 * inner, channels), out_weight[0], bias_rows]
    )
    others = lax.ppermute(packed, "segment", [(0, 1), (1, 0)])
    w_first, w_second, v_second, v_first, p_first, p_second, p_back, b_first, b_second = call(
        weights_kernel,
        "weights",
        [
            ((9 * channels, inner), BF16),
            ((9 * channels, 2 * inner), BF16),
            ((9, 2 * inner, 2 * channels), BF16),
            ((9, 2 * inner, channels), BF16),
            ((inner, channels), BF16),
            ((channels, 2 * inner), BF16),
            ((channels, 2 * inner), BF16),
            ((1, inner), F32),
            ((1, 2 * inner), F32),
        ],
        [((2,) + packed.shape, BF16)],
        packed.size,
        *(packed, others),
    )

    kept, gate_first, bottle_first, near_hidden = call(
        own_kernel,
        "own_branch",
        [
            ((span + side, span, channels), BF16),
            ((near, small, channels), BF16),
            ((side, small, inner), BF16),
            ((3, near, small, channels), BF16),
        ],
        [
            ((full, LEAD + up16(side + LEAD), channels), F32),
            ((full, wide, 2 * channels), BF16),
            ((full + first, wide, 2 * channels), BF16),
            ((span, wide, inner), F32),
        ],
        span * wide * channels * inner * 400,
        *(tile, above, below, jnp.swapaxes(left, 0, 1), jnp.swapaxes(right, 0, 1)),
        *(w_first, b_first, p_first),
    )
    kept = lax.dynamic_update_slice(kept, late, (span, 0, 0))
    other = swap(kept)
    gate_second, hidden_pairs, hidden_last, bottle_second, grad_tile, grad_pre, *strips = call(
        middle_kernel,
        "middle",
        [
            ((near, small, channels), BF16),
            ((span, small, 2 * channels), BF16),
            ((span + second, small, 2 * channels), BF16),
            ((side, small, inner), BF16),
            ((side, small, channels), BF16),
            ((side, small, 2 * inner), BF16),
            ((HALO + first, side, channels), BF16),
            ((HALO + first, side, channels), BF16),
        ],
        [
            ((span, wide, channels), F32),
            ((side, small, channels), F32),
            ((side, small, 2 * inner), F32),
        ],
        24 * side * small * channels * 2 * inner,
        *(kept, other, w_second, b_second, p_second),
    )

    above, below = around(0, [exchange(strips[turn], 0, turn) for turn in (0, 1)])
    rows_second, ends_second = call(
        second_sums_kernel,
        "second_sums",
        [((10 * inner, channels), F32), ((16, channels), F32)],
        [],
        20 * side * small * channels * inner,
        *(grad_pre, hidden_pairs, hidden_last, bottle_second, grad_tile),
    )

    def columns(turn):
        def chosen(x, width):
            return jnp.where(sends_last(1, turn), x[:, side - width : side], x[:, :width])

        grads = jnp.concatenate([chosen(x, HALO) for x in (above[:HALO], grad_pre, below[:HALO])])
        branches = jnp.concatenate([chosen(x, first) for x in (above[HALO:], grad_tile, below[HALO:])])
        branches = jnp.pad(branches, ((second, second), (0, 0), (0, 0)))
        return jnp.swapaxes(jnp.concatenate([grads, branches], axis=1), 0, 1)

    left, right = around(1, [exchange(columns(turn), 1, turn) for turn in (0, 1)])
    left, right = jnp.swapaxes(left, 0, 1), jnp.swapaxes(right, 0, 1)

    devices = number * number
    share = -(-10 * inner // (8 * devices)) * 8
    keep, away, windows, grad_first = call(
        backward_kernel,
        "backward",
        [
            ((10 * inner + 16, channels), F32),
            ((10 * inner + 16, channels), BF16),
            ((3, near, small, channels), BF16),
            ((side, side, channels), BF16),
        ],
        [
            ((full, LEAD + up16(side + HALO + first), channels), F32),
            ((3, full, small, channels), BF16),
            ((near, small + 16, channels), F32),
            ((near, small + 16, channels), F32),
            ((10 * inner, channels), F32),
            ((16, channels), F32),
        ],
        36 * near * small * channels * channels,
        *(grad_pre, grad_tile, above, below, left[:, :HALO], right[:, :HALO]),
        *(left[second : second + near, HALO:], right[second : second + near, HALO:]),
        *(gate_second, gate_first, near_hidden, bottle_first, v_second, p_back, rows_second, ends_second),
    )

    (input_gradient,) = call(
        input_kernel,
        "input",
        [((side, side, channels), BF16)],
        [],
        18 * side * small * channels * channels,
        *(windows, grad_first, tile, v_first),
    )
    other = lax.ppermute(away, "segment", [(0, 1), (1, 0)])
    other, input_gradient = lax.optimization_barrier((other, input_gradient))
    (parts,) = call(
        pair_kernel,
        "pair",
        [((devices, share + 8, channels), BF16)],
        [],
        keep.size,
        *(keep, other),
    )
    parts = lax.all_to_all(parts, GRID, 0, 0, tiled=True)
    input_gradient = take_back(input_gradient)
    cells = lax.axis_size("segment") * (side * number) * (side * number)
    rows, ends = call(
        functools.partial(total_kernel, float(cells) ** -0.5),
        "total",
        [((devices, share, channels), BF16), ((8, channels), F32)],
        [],
        parts.size,
        parts,
    )
    rows, _ = lax.optimization_barrier((rows, input_gradient))
    rows = lax.all_to_all(rows, GRID, 0, 0, tiled=True).reshape(devices * share, channels)
    conv_gradient, bias_gradient, out_gradient, input_gradient = call(
        outputs_kernel,
        "outputs",
        [
            ((9 * inner, channels), F32),
            ((1, inner), F32),
            ((inner, channels), F32),
            ((side, side, channels), BF16),
        ],
        [],
        rows.size,
        *(rows, ends, input_gradient),
    )
    conv_gradient = jnp.swapaxes(conv_gradient.reshape(1, 9, inner, channels), 2, 3)
    return (input_gradient[None], conv_gradient, bias_gradient, out_gradient[None])


def solution(mesh):
    in_specs = (
        P("segment", "row", "col", None),
        P("segment", "row", "col", None),
        P("segment", None, None, None),
        P("segment", None),
        P("segment", None, None),
    )
    out_specs = (
        P("segment", "row", "col", None),
        P("segment", None, None, None),
        P("segment", None),
        P("segment", None, None),
    )
    return jax.shard_map(local, mesh=mesh, in_specs=in_specs, out_specs=out_specs, check_vma=False)
```

```python
import functools

import jax
import jax.numpy as jnp
from jax import lax
from jax.experimental import pallas as pl
from jax.experimental.pallas import tpu as pltpu
from jax.sharding import PartitionSpec as P

FIRST_DILATION = 2
SECOND_DILATION = 8
HALO = FIRST_DILATION + SECOND_DILATION
GRID = ("row", "col")
ALL = ("segment",) + GRID
ORDER = [0, 1, 3, 4, 6, 7, 2, 5, 8]
TAPS = [(a, b) for a in (-1, 0, 1) for b in (-1, 0, 1)]
LEAD = 16
F32, BF16 = jnp.float32, jnp.bfloat16


def tap(a, b):
    return 3 * (a + 1) + (b + 1)


def dot(x, y):
    return jnp.dot(x, y, preferred_element_type=F32)


def rounded(x):
    return x.astype(BF16).astype(F32)


def up16(n):
    return -(-n // 16) * 16


def home(batch, r, c):
    number = lax.axis_size("row")
    core, row, col = (batch, r, c) if r == c else (int(r > c), r, c)
    if r != c and (r < c) == (batch == 1):
        row, col = c, r
    return (core * number + row) * number + col


def place():
    row, col = lax.axis_index("row"), lax.axis_index("col")
    low, high = jnp.minimum(row, col), jnp.maximum(row, col)
    upper = lax.axis_index("segment") == 0
    return jnp.where(upper, low, high), jnp.where(upper, high, low)


def permute(x, pair):
    number = lax.axis_size("row")
    tiles = [(m, r, c) for m in range(lax.axis_size("segment")) for r in range(number) for c in range(number)]
    pairs = [pair(*tile) for tile in tiles]
    return lax.ppermute(x, ALL, [found for found in pairs if found is not None])


def stored(batch, r, c):
    number = lax.axis_size("row")
    return (batch * number + r) * number + c


def bring(x, turn=None):
    def pair(batch, r, c):
        row = r if turn is None else partner(r, turn)
        if row is not None:
            return stored(batch, r, c), home(batch, row, c)

    return permute(x, pair)


def take_back(x):
    return permute(x, lambda m, r, c: (home(m, r, c), stored(m, r, c)))


def swap(x):
    return permute(x, lambda m, r, c: (home(m, r, c), home(m, c, r)))


def partner(index, turn):
    other = index + 1 if (index + turn) % 2 == 0 else index - 1
    return other if 0 <= other < lax.axis_size("row") else None


def exchange(x, axis, turn):
    def pair(batch, r, c):
        other = partner(c if axis else r, turn)
        if other is not None:
            return home(batch, r, c), home(batch, r, other) if axis else home(batch, other, c)

    return permute(x, pair)


def sends_last(axis, turn):
    return lax.rem(place()[axis] + turn, 2) == 0


def around(axis, got):
    even = sends_last(axis, 0)
    return jnp.where(even, got[1], got[0]), jnp.where(even, got[0], got[1])


def inside(shape, side, width, top):
    number = lax.axis_size("row") * side
    rows = lax.broadcasted_iota(jnp.int32, shape, 0) + top - width
    cols = lax.broadcasted_iota(jnp.int32, shape, 1) - width
    row, col = place()
    at_row = row * side + rows
    at_col = col * side + cols
    return (at_row >= 0) & (at_row < number) & (at_col >= 0) & (at_col < number) & (cols < side + width)


def paired(source, starts, width, dilation, pairs, last, change):
    lanes = source.shape[2]
    low, high = slice(0, lanes), slice(lanes, 2 * lanes)

    def step(k, _):
        rows, lower = pl.ds(4 * k, 4), pl.ds(4 * k + dilation, 4)
        window = [change(source[rows, at : at + width]).astype(BF16) for at in starts]
        pairs[rows, :, low] = window[0]
        pairs[rows, :, high] = window[1]
        last[lower, :, low] = window[2]
        last[rows, :, high] = window[2]
        return 0

    lax.fori_loop(0, source.shape[0] // 4, step, 0)


def taps_sum(pairs, last, top, rows, dilation, weights):
    width, lanes = pairs.shape[1], pairs.shape[2] // 2
    size = rows * width
    total = None
    for k in range(5):
        if k < 3:
            window = pairs[pl.ds(top + dilation * k, rows)]
        elif k == 3:
            window = last[pl.ds(top + dilation, rows)]
        else:
            window = last[pl.ds(top + 3 * dilation, rows), :, :lanes]
        weight = weights[2 * lanes * k : min(2 * lanes * (k + 1), 9 * lanes)]
        term = dot(window.reshape(size, window.shape[2]), weight)
        total = term if total is None else total + term
    return total


def positive(x):
    return jnp.maximum(x, 0)


def assemble(area, tile, above, below, left, right):
    side = tile.shape[0]
    full, wide, channels = area.shape
    middle = slice(LEAD, LEAD + side)
    area[:, :LEAD] = jnp.zeros((full, LEAD, channels), F32)
    area[:, LEAD + side :] = jnp.zeros((full, wide - LEAD - side, channels), F32)
    area[HALO : HALO + side, middle] = tile
    area[:HALO, middle] = above[:HALO].astype(F32)
    area[HALO + side :, middle] = below[:HALO].astype(F32)
    area[:, LEAD - HALO : LEAD] = left[...].astype(F32)
    area[:, LEAD + side : LEAD + side + HALO] = right[...].astype(F32)


def first_branch(area, pairs, last, weights, bias, proj, store):
    full, wide = pairs.shape[:2]
    start = LEAD - SECOND_DILATION
    starts = [start + FIRST_DILATION * b for b in (-1, 0, 1)]
    paired(area, starts, wide, FIRST_DILATION, pairs, last, positive)

    def rows(step, _):
        top = step * 8
        pre = taps_sum(pairs, last, top, 8, FIRST_DILATION, weights) + bias[...]
        branch = dot(positive(pre).astype(BF16), proj[...])
        inputs = area[pl.ds(top + FIRST_DILATION, 8), start : start + wide]
        branch = rounded(inputs + branch.reshape(inputs.shape))
        store(top, pre.reshape(8, wide, pre.shape[1]), branch)
        return 0

    lax.fori_loop(0, (full - 2 * FIRST_DILATION) // 8, rows, 0)


def own_kernel(
    tile, above, below, left, right, weights, bias, proj,
    swapped, pre,
    area, pairs, last,
):
    side, span = tile.shape[0], pre.shape[0]
    assemble(area, tile[...].astype(F32), above, below, left, right)

    def store(top, pre_act, branch):
        pre[pl.ds(top, 8)] = pre_act
        swapped[pl.ds(top, 8)] = branch[:, :span].astype(BF16)

    first_branch(area, pairs, last, weights, bias, proj, store)
    swapped[span:] = jnp.zeros((side, span, swapped.shape[2]), BF16)


def near_kernel(tile, above, below, left, right, pre, hidden_pairs, hidden_last, gate_first, bottle_first, area):
    side, channels, inner = tile.shape[0], tile.shape[2], pre.shape[2]
    first, second = FIRST_DILATION, SECOND_DILATION
    near, small = gate_first.shape[:2]
    assemble(area, tile[...].astype(F32), above, below, left, right)
    for b in (-1, 0, 1):
        at = LEAD + first * b
        window = positive(area[HALO - first : HALO + side + first, at : at + small]).astype(BF16)
        if b < 1:
            hidden_pairs[:, :, (b + 1) * channels : (b + 2) * channels] = window
        else:
            hidden_last[...] = window
    edge = second - first
    part = pre[edge : edge + near, edge : edge + small]
    alive = (part > 0) & inside(part.shape, side, first, 0)
    gate_first[:, :, :inner] = jnp.where(alive, 1.0, 0.0).astype(BF16)
    gate_first[:, :, inner:] = jnp.zeros((near, small, gate_first.shape[2] - inner), BF16)
    bottle_first[...] = positive(pre[second : second + side, second : second + small]).astype(BF16)


def middle_kernel(
    kept, other, w_second, b_second, p_second,
    gate_second, hidden_pairs, hidden_last, bottle_second, grad_tile, grad_pre, first_turn, second_turn,
    current, padded, pre_second,
):
    side, channels, span = first_turn.shape[1], kept.shape[2], kept.shape[1]
    first, second, inner = FIRST_DILATION, SECOND_DILATION, bottle_second.shape[2]
    near, small = gate_second.shape[:2]
    turned = jnp.swapaxes(other[:span].astype(F32), 0, 1)
    sym = rounded((kept[:span].astype(F32) + turned) * 0.5)
    current[:, :span] = jnp.where(inside(sym.shape, side, second, 0), sym, 0)
    current[:, span:] = jnp.zeros((span, current.shape[1] - span, channels), F32)
    edge = second - first
    part = current[edge : edge + near, edge : edge + small]
    gate_second[...] = jnp.where(part > 0, 1.0, 0.0).astype(BF16)
    paired(current, [0, second, 2 * second], small, second, hidden_pairs, hidden_last, positive)

    def rows(step, _):
        top = step * 8
        total = taps_sum(hidden_pairs, hidden_last, top, 8, second, w_second) + b_second[...]
        pre_second[pl.ds(top, 8)] = total.reshape(8, small, total.shape[1])
        return 0

    lax.fori_loop(0, side // 8, rows, 0)
    bottle_second[...] = positive(pre_second[:, :, :inner]).astype(BF16)

    turned = jnp.swapaxes(other[span:, :side].astype(F32), 0, 1)
    padded[:, side:] = jnp.zeros((side, small - side, channels), F32)
    padded[:, :side] = rounded((kept[span:, :side].astype(F32) + turned) * 0.5)
    branch = padded[...].astype(BF16)
    grad_tile[...] = branch
    grad = dot(branch.reshape(side * small, channels), p_second[...]).reshape(side, small, 2 * inner)
    grad = jnp.where(pre_second[...] > 0, grad, 0)
    grad_pre[...] = grad.astype(BF16)
    even = sends_last(0, 0)
    for rows, value, width in ((slice(0, HALO), grad, HALO), (slice(HALO, HALO + first), padded[...], first)):
        head, tail = value[:width, :side], value[side - width :, :side]
        first_turn[rows] = jnp.where(even, tail, head).astype(BF16)
        second_turn[rows] = jnp.where(even, head, tail).astype(BF16)


def weight_sums(rows, ends, grad_pre, hidden, bottle, grad_tile):
    side, small, lanes = grad_pre.shape
    inner = bottle.shape[2]
    size = side * small
    flat = grad_pre.reshape(size, lanes)
    turned = flat.T[:inner].astype(BF16)
    for a in range(3):
        b = 0
        while b < 3:
            window = hidden(a, b)
            grads = dot(turned, window.reshape(size, window.shape[2]))
            for at in range(0, window.shape[2], grad_tile.shape[2]):
                rows[(3 * a + b) * inner : (3 * a + b + 1) * inner] = grads[:, at : at + grad_tile.shape[2]]
                b += 1
    turned = bottle[...].reshape(size, inner).astype(F32).T.astype(BF16)
    rows[9 * inner : 10 * inner] = dot(turned, grad_tile.reshape(size, grad_tile.shape[2]))
    ends[...] = jnp.zeros(ends.shape, F32)
    ends[:, :lanes] = jnp.broadcast_to(jnp.sum(flat, axis=0, keepdims=True), (ends.shape[0], lanes))


def weights_kernel(
    mine, theirs, w_first, w_second, v_second, v_first, p_first, p_second, p_back, b_first, b_second, packed
):
    inner, channels = p_first.shape
    section = lax.axis_index("segment")
    packed[section] = mine[...]
    packed[1 - section] = theirs[...]

    def conv(section, k):
        return packed[section, k * inner : (k + 1) * inner]

    def turned(x):
        return x.astype(F32).T.astype(BF16)

    zero = jnp.zeros((inner, channels), BF16)
    for at, k in enumerate(ORDER):
        here = slice(at * channels, (at + 1) * channels)
        own, other = conv(1, k), conv(1, 3 * (k % 3) + k // 3)
        w_first[here] = turned(conv(0, k))
        w_second[here] = turned(jnp.concatenate([own, other], axis=0))
        upper, lower = (slice((2 * k + half) * inner, (2 * k + half + 1) * inner) for half in (0, 1))
        v_second[upper, :channels], v_second[upper, channels:] = own, zero
        v_second[lower, :channels], v_second[lower, channels:] = zero, other
        v_first[k, :inner], v_first[k, inner:] = conv(0, k), zero
    p_first[...] = conv(0, 9)
    p_second[...] = turned(jnp.concatenate([conv(1, 9), conv(1, 9)], axis=0))
    p_back[...] = turned(jnp.concatenate([conv(0, 9), zero], axis=0))
    b_first[...] = packed[0, 10 * inner :].astype(F32)[:1, :inner]
    bias = packed[1, 10 * inner :].astype(F32)[:1, :inner]
    b_second[...] = jnp.concatenate([bias, bias], axis=1)


def second_sums_kernel(grad_pre, pairs, last, bottle, grad_tile, rows, ends):
    side = grad_pre.shape[0]
    channels = grad_tile.shape[2]

    def hidden(a, b):
        top = SECOND_DILATION * a
        if b == 0:
            return pairs[top : top + side]
        return last[top + SECOND_DILATION : top + SECOND_DILATION + side, :, :channels]

    weight_sums(rows, ends, grad_pre[...].astype(F32), hidden, bottle, grad_tile[...])


def backward_kernel(
    grad_pre, grad_tile, above, below, left, right, left_branch, right_branch, gate_second, gate_first, near_pairs,
    near_last, bottle_first, v_second, p_first, rows_second, ends_second,
    keep, away, windows, grad_first,
    area, pairs, last, branch, grads, rows, ends,
):
    side, channels = grad_first.shape[0], grad_first.shape[2]
    first, second = FIRST_DILATION, SECOND_DILATION
    full, near = side + 2 * HALO, side + 2 * first
    small = grad_pre.shape[1]
    middle = slice(LEAD, LEAD + side)

    area[:, :LEAD] = jnp.zeros((full, LEAD, channels), F32)
    area[:, LEAD + side :] = jnp.zeros((full, area.shape[1] - LEAD - side, channels), F32)
    area[HALO : HALO + side, LEAD : LEAD + small] = grad_pre[...].astype(F32)
    area[:HALO, middle] = above[:HALO].astype(F32)
    area[HALO + side :, middle] = below[:HALO].astype(F32)
    area[:, LEAD - HALO : LEAD] = left[...].astype(F32)
    area[:, LEAD + side : LEAD + side + HALO] = right[...].astype(F32)
    branch[...] = jnp.zeros(branch.shape, F32)
    branch[first : first + side, first : first + side] = grad_tile[:, :side].astype(F32)
    branch[:first, first : first + side] = above[HALO:].astype(F32)
    branch[first + side :, first : first + side] = below[HALO:].astype(F32)
    branch[:, :first] = left_branch[...].astype(F32)
    branch[:, first + side : near] = right_branch[...].astype(F32)
    for b in (-1, 0, 1):
        at = LEAD - HALO + second * (1 - b)
        window = area[:, at : at + small].astype(BF16)
        if b < 1:
            pairs[:, :, (b + 1) * channels : (b + 2) * channels] = window
        else:
            last[...] = window
    grads[:, small:] = jnp.zeros((near, grads.shape[1] - small, channels), F32)

    def sections(step, _):
        top = step * 7
        size = 7 * small
        total = None
        for a in (-1, 0, 1):
            rows_of = pl.ds(top + second * (1 - a), 7)
            at = 3 * (a + 1) * channels
            term = dot(pairs[rows_of].reshape(size, 2 * channels), v_second[at : at + 2 * channels])
            total = term if total is None else total + term
            total = total + dot(last[rows_of].reshape(size, channels), v_second[at + 2 * channels : at + 3 * channels])
        here = pl.ds(top, 7)
        grad = branch[here, :small].reshape(size, channels)
        gate = gate_second[here].astype(F32).reshape(size, channels) > 0
        own = rounded(grad + jnp.where(gate, total[:, :channels], 0))
        other = rounded(grad + jnp.where(gate, total[:, channels:], 0))
        grad = ((own + other) * 0.5).astype(BF16)
        branch[here, :small] = grad.astype(F32).reshape(7, small, channels)
        gate = gate_first[here].astype(F32).reshape(size, channels) > 0
        grad = rounded(jnp.where(gate, dot(grad, p_first[...]), 0))
        grads[here, :small] = grad.reshape(7, small, channels)
        return 0

    lax.fori_loop(0, near // 7, sections, 0)
    for b in (-1, 0, 1):
        at = first * (1 - b)
        windows[b + 1] = grads[:, at : at + small].astype(BF16)
    part = branch[first : first + side, first : first + small]
    grad_first[...] = part[:, :side].astype(BF16)
    real = lax.broadcasted_iota(jnp.int32, part.shape, 1) < side
    part = jnp.where(real, part, 0).astype(BF16)
    grad = jnp.where(real, grads[first : first + side, first : first + small], 0)

    def hidden(a, b):
        return (near_last if b else near_pairs)[first * a : first * a + side]

    weight_sums(rows, ends, grad, hidden, bottle_first, part)

    first_core = lax.axis_index("segment") == 0
    count = rows.shape[0]
    for here, one, two in (
        (slice(0, count), rows[...], rows_second[...]),
        (slice(count, count + ends.shape[0]), ends[...], ends_second[...]),
    ):
        keep[here] = jnp.where(first_core, one, two)
        away[here] = jnp.where(first_core, two, one).astype(BF16)


def pair_kernel(keep, other, parts):
    devices, share = parts.shape[0], parts.shape[1] - 8
    total = keep[...] + other[...].astype(F32)
    count = keep.shape[0] - 16
    for j in range(devices):
        low, high = min(j * share, count), min((j + 1) * share, count)
        pieces = [total[low:high]] if low < high else []
        if high - low < share:
            pieces.append(jnp.zeros((share - (high - low), keep.shape[1]), F32))
        parts[j] = jnp.concatenate(pieces + [total[count : count + 8]]).astype(BF16)


def input_kernel(windows, grad_first, tile, v_first, out):
    side, channels = out.shape[0], out.shape[2]
    small = windows.shape[2]
    first = FIRST_DILATION

    def rows(step, _):
        top = step * 8
        total = jnp.zeros((8 * small, channels), F32)
        for a, b in TAPS:
            window = windows[b + 1, pl.ds(top + first * (1 - a), 8)].reshape(8 * small, channels)
            total = total + dot(window, v_first[tap(a, b)])
        here = pl.ds(top, 8)
        total = total.reshape(8, small, channels)[:, :side]
        total = jnp.where(tile[here].astype(F32) > 0, total, 0)
        out[here] = (grad_first[here].astype(F32) + total).astype(BF16)
        return 0

    lax.fori_loop(0, side // 8, rows, 0)


def total_kernel(scale, parts, rows, ends):
    share = rows.shape[1]
    total = jnp.sum(parts[...].astype(F32), axis=0) * scale
    rows[...] = jnp.broadcast_to(total[:share].astype(BF16)[None], rows.shape)
    ends[...] = total[share:]


def outputs_kernel(rows, ends, moved, conv_gradient, bias_gradient, out_gradient, input_gradient):
    count, inner = conv_gradient.shape[0], out_gradient.shape[0]
    conv_gradient[...] = rows[:count].astype(F32)
    out_gradient[...] = rows[count : count + inner].astype(F32)
    bias_gradient[...] = ends[:1, :inner]
    input_gradient[...] = moved[...]


def call(kernel, name, outs, scratch, flops, *operands):
    outs = [jax.ShapeDtypeStruct(shape, dtype) for shape, dtype in outs]
    moved = sum(x.size * x.dtype.itemsize for x in list(operands) + outs)
    return pl.pallas_call(
        kernel,
        name=name,
        out_shape=outs,
        scratch_shapes=[pltpu.VMEM(shape, dtype) for shape, dtype in scratch],
        cost_estimate=pl.CostEstimate(flops=flops, bytes_accessed=moved, transcendentals=0),
        compiler_params=pltpu.CompilerParams(vmem_limit_bytes=40 * 1024 * 1024),
    )(*operands)


def local(activations, cotangent, conv_weight, conv_bias, out_weight):
    side, channels, inner = activations.shape[1], activations.shape[3], conv_weight.shape[3]
    number = lax.axis_size("row")
    first, second = FIRST_DILATION, SECOND_DILATION
    full, span, near = side + 2 * HALO, side + 2 * second, side + 2 * first
    wide, small = up16(span), up16(near)

    tile = bring(activations[0])
    stored_even = lax.rem(lax.axis_index("row"), 2) == 0
    ends = (activations[0, side - HALO :], activations[0, :HALO])
    got = [bring(jnp.where(stored_even, *ends), 0), bring(jnp.where(stored_even, *ends[::-1]), 1)]
    above, below = around(0, got)

    def columns(turn):
        def chosen(x):
            return jnp.swapaxes(jnp.where(sends_last(1, turn), x[:, side - HALO :], x[:, :HALO]), 0, 1)

        strip = jnp.pad(chosen(tile), ((0, 0), (HALO, HALO), (0, 0)))
        strip = lax.optimization_barrier(strip)
        for row_turn in (0, 1):
            at = jnp.where(sends_last(0, row_turn), HALO + side, 0)
            strip = lax.dynamic_update_slice(strip, chosen(got[row_turn]), (0, at, 0))
        return strip

    strips, late = lax.optimization_barrier(([columns(0), columns(1)], cotangent[0]))
    left, right = around(1, [exchange(strips[turn], 1, turn) for turn in (0, 1)])
    late = bring(late)

    bias_rows = jnp.pad(conv_bias, ((0, 15), (0, channels - inner)))
    packed = jnp.concatenate(
        [jnp.swapaxes(conv_weight[0], 1, 2).reshape(9 * inner, channels), out_weight[0], bias_rows]
    )
    others = lax.ppermute(packed, "segment", [(0, 1), (1, 0)])
    w_first, w_second, v_second, v_first, p_first, p_second, p_back, b_first, b_second = call(
        weights_kernel,
        "weights",
        [
            ((9 * channels, inner), BF16),
            ((9 * channels, 2 * inner), BF16),
            ((18 * inner, 2 * channels), BF16),
            ((9, 2 * inner, channels), BF16),
            ((inner, channels), BF16),
            ((channels, 2 * inner), BF16),
            ((channels, 2 * inner), BF16),
            ((1, inner), F32),
            ((1, 2 * inner), F32),
        ],
        [((2,) + packed.shape, BF16)],
        packed.size,
        *(packed, others),
    )

    own = (tile, above, below, jnp.swapaxes(left, 0, 1), jnp.swapaxes(right, 0, 1))
    area = ((full, LEAD + up16(side + LEAD), channels), F32)
    kept, pre_first = call(
        own_kernel,
        "own_branch",
        [((span + side, span, channels), BF16), ((span, wide, inner), F32)],
        [area, ((full, wide, 2 * channels), BF16), ((full + first, wide, 2 * channels), BF16)],
        span * wide * channels * inner * 400,
        *own,
        *(w_first, b_first, p_first),
    )
    kept = lax.dynamic_update_slice(kept, late, (span, 0, 0))
    other = swap(kept)
    gate_second, hidden_pairs, hidden_last, bottle_second, grad_tile, grad_pre, *strips = call(
        middle_kernel,
        "middle",
        [
            ((near, small, channels), BF16),
            ((span, small, 2 * channels), BF16),
            ((span + second, small, 2 * channels), BF16),
            ((side, small, inner), BF16),
            ((side, small, channels), BF16),
            ((side, small, 2 * inner), BF16),
            ((HALO + first, side, channels), BF16),
            ((HALO + first, side, channels), BF16),
        ],
        [
            ((span, wide, channels), F32),
            ((side, small, channels), F32),
            ((side, small, 2 * inner), F32),
        ],
        24 * side * small * channels * 2 * inner,
        *(kept, other, w_second, b_second, p_second),
    )

    near_pairs, near_last, gate_first, bottle_first = call(
        near_kernel,
        "near",
        [
            ((near, small, 2 * channels), BF16),
            ((near, small, channels), BF16),
            ((near, small, channels), BF16),
            ((side, small, inner), BF16),
        ],
        [area],
        near * small * channels,
        *own,
        pre_first,
    )

    above, below = around(0, [exchange(strips[turn], 0, turn) for turn in (0, 1)])
    rows_second, ends_second = call(
        second_sums_kernel,
        "second_sums",
        [((10 * inner, channels), F32), ((16, channels), F32)],
        [],
        20 * side * small * channels * inner,
        *(grad_pre, hidden_pairs, hidden_last, bottle_second, grad_tile),
    )

    def columns(turn):
        def chosen(x, width):
            return jnp.where(sends_last(1, turn), x[:, side - width : side], x[:, :width])

        grads = jnp.concatenate([chosen(x, HALO) for x in (above[:HALO], grad_pre, below[:HALO])])
        branches = jnp.concatenate([chosen(x, first) for x in (above[HALO:], grad_tile, below[HALO:])])
        branches = jnp.pad(branches, ((second, second), (0, 0), (0, 0)))
        return jnp.swapaxes(jnp.concatenate([grads, branches], axis=1), 0, 1)

    left, right = around(1, [exchange(columns(turn), 1, turn) for turn in (0, 1)])
    left, right = jnp.swapaxes(left, 0, 1), jnp.swapaxes(right, 0, 1)

    devices = number * number
    share = -(-10 * inner // (8 * devices)) * 8
    keep, away, windows, grad_first = call(
        backward_kernel,
        "backward",
        [
            ((10 * inner + 16, channels), F32),
            ((10 * inner + 16, channels), BF16),
            ((3, near, small, channels), BF16),
            ((side, side, channels), BF16),
        ],
        [
            ((full, LEAD + up16(side + HALO + first), channels), F32),
            ((full, small, 2 * channels), BF16),
            ((full, small, channels), BF16),
            ((near, small + 16, channels), F32),
            ((near, small + 16, channels), F32),
            ((10 * inner, channels), F32),
            ((16, channels), F32),
        ],
        36 * near * small * channels * channels,
        *(grad_pre, grad_tile, above, below, left[:, :HALO], right[:, :HALO]),
        *(left[second : second + near, HALO:], right[second : second + near, HALO:]),
        *(gate_second, gate_first, near_pairs, near_last, bottle_first, v_second, p_back, rows_second, ends_second),
    )

    (input_gradient,) = call(
        input_kernel,
        "input",
        [((side, side, channels), BF16)],
        [],
        18 * side * small * channels * channels,
        *(windows, grad_first, tile, v_first),
    )
    other = lax.ppermute(away, "segment", [(0, 1), (1, 0)])
    other, input_gradient = lax.optimization_barrier((other, input_gradient))
    (parts,) = call(
        pair_kernel,
        "pair",
        [((devices, share + 8, channels), BF16)],
        [],
        keep.size,
        *(keep, other),
    )
    parts = lax.all_to_all(parts, GRID, 0, 0, tiled=True)
    input_gradient = take_back(input_gradient)
    cells = lax.axis_size("segment") * (side * number) * (side * number)
    rows, ends = call(
        functools.partial(total_kernel, float(cells) ** -0.5),
        "total",
        [((devices, share, channels), BF16), ((8, channels), F32)],
        [],
        parts.size,
        parts,
    )
    rows, _ = lax.optimization_barrier((rows, input_gradient))
    rows = lax.all_to_all(rows, GRID, 0, 0, tiled=True).reshape(devices * share, channels)
    conv_gradient, bias_gradient, out_gradient, input_gradient = call(
        outputs_kernel,
        "outputs",
        [
            ((9 * inner, channels), F32),
            ((1, inner), F32),
            ((inner, channels), F32),
            ((side, side, channels), BF16),
        ],
        [],
        rows.size,
        *(rows, ends, input_gradient),
    )
    conv_gradient = jnp.swapaxes(conv_gradient.reshape(1, 9, inner, channels), 2, 3)
    return (input_gradient[None], conv_gradient, bias_gradient, out_gradient[None])


def solution(mesh):
    in_specs = (
        P("segment", "row", "col", None),
        P("segment", "row", "col", None),
        P("segment", None, None, None),
        P("segment", None),
        P("segment", None, None),
    )
    out_specs = (
        P("segment", "row", "col", None),
        P("segment", None, None, None),
        P("segment", None),
        P("segment", None, None),
    )
    return jax.shard_map(local, mesh=mesh, in_specs=in_specs, out_specs=out_specs, check_vma=False)
```

```python
import functools

import jax
import jax.numpy as jnp
from jax import lax
from jax.experimental import pallas as pl
from jax.experimental.pallas import tpu as pltpu
from jax.sharding import PartitionSpec as P

FIRST_DILATION = 2
SECOND_DILATION = 8
HALO = FIRST_DILATION + SECOND_DILATION
GRID = ("row", "col")
ALL = ("segment",) + GRID
ORDER = [0, 1, 3, 4, 6, 7, 2, 5, 8]
TAPS = [(a, b) for a in (-1, 0, 1) for b in (-1, 0, 1)]
LEAD = 16
F32, BF16 = jnp.float32, jnp.bfloat16


def tap(a, b):
    return 3 * (a + 1) + (b + 1)


def dot(x, y):
    return jnp.dot(x, y, preferred_element_type=F32)


def rounded(x):
    return x.astype(BF16).astype(F32)


def up16(n):
    return -(-n // 16) * 16


def home(batch, r, c):
    number = lax.axis_size("row")
    core, row, col = (batch, r, c) if r == c else (int(r > c), r, c)
    if r != c and (r < c) == (batch == 1):
        row, col = c, r
    return (core * number + row) * number + col


def place():
    row, col = lax.axis_index("row"), lax.axis_index("col")
    low, high = jnp.minimum(row, col), jnp.maximum(row, col)
    upper = lax.axis_index("segment") == 0
    return jnp.where(upper, low, high), jnp.where(upper, high, low)


def permute(x, pair):
    number = lax.axis_size("row")
    tiles = [(m, r, c) for m in range(lax.axis_size("segment")) for r in range(number) for c in range(number)]
    pairs = [pair(*tile) for tile in tiles]
    return lax.ppermute(x, ALL, [found for found in pairs if found is not None])


def stored(batch, r, c):
    number = lax.axis_size("row")
    return (batch * number + r) * number + c


def bring(x, turn=None):
    def pair(batch, r, c):
        row = r if turn is None else partner(r, turn)
        if row is not None:
            return stored(batch, r, c), home(batch, row, c)

    return permute(x, pair)


def take_back(x):
    return permute(x, lambda m, r, c: (home(m, r, c), stored(m, r, c)))


def swap(x):
    return permute(x, lambda m, r, c: (home(m, r, c), home(m, c, r)))


def partner(index, turn):
    other = index + 1 if (index + turn) % 2 == 0 else index - 1
    return other if 0 <= other < lax.axis_size("row") else None


def exchange(x, axis, turn):
    def pair(batch, r, c):
        other = partner(c if axis else r, turn)
        if other is not None:
            return home(batch, r, c), home(batch, r, other) if axis else home(batch, other, c)

    return permute(x, pair)


def sends_last(axis, turn):
    return lax.rem(place()[axis] + turn, 2) == 0


def around(axis, got):
    even = sends_last(axis, 0)
    return jnp.where(even, got[1], got[0]), jnp.where(even, got[0], got[1])


def inside(shape, side, width, top):
    number = lax.axis_size("row") * side
    rows = lax.broadcasted_iota(jnp.int32, shape, 0) + top - width
    cols = lax.broadcasted_iota(jnp.int32, shape, 1) - width
    row, col = place()
    at_row = row * side + rows
    at_col = col * side + cols
    return (at_row >= 0) & (at_row < number) & (at_col >= 0) & (at_col < number) & (cols < side + width)


def paired(source, starts, width, dilation, pairs, last, change):
    lanes = source.shape[2]
    low, high = slice(0, lanes), slice(lanes, 2 * lanes)

    def step(k, _):
        rows, lower = pl.ds(4 * k, 4), pl.ds(4 * k + dilation, 4)
        window = [change(source[rows, at : at + width]).astype(BF16) for at in starts]
        pairs[rows, :, low] = window[0]
        pairs[rows, :, high] = window[1]
        last[lower, :, low] = window[2]
        last[rows, :, high] = window[2]
        return 0

    lax.fori_loop(0, source.shape[0] // 4, step, 0, unroll=True)


def taps_sum(pairs, last, top, rows, dilation, weights):
    width, lanes = pairs.shape[1], pairs.shape[2] // 2
    size = rows * width
    total = None
    for k in range(5):
        if k < 3:
            window = pairs[pl.ds(top + dilation * k, rows)]
        elif k == 3:
            window = last[pl.ds(top + dilation, rows)]
        else:
            window = last[pl.ds(top + 3 * dilation, rows), :, :lanes]
        weight = weights[2 * lanes * k : min(2 * lanes * (k + 1), 9 * lanes)]
        term = dot(window.reshape(size, window.shape[2]), weight)
        total = term if total is None else total + term
    return total


def positive(x):
    return jnp.maximum(x, 0)


def assemble(area, tile, above, below, left, right):
    side = tile.shape[0]
    full, wide, channels = area.shape
    middle = slice(LEAD, LEAD + side)
    area[:, :LEAD] = jnp.zeros((full, LEAD, channels), F32)
    area[:, LEAD + side :] = jnp.zeros((full, wide - LEAD - side, channels), F32)
    area[HALO : HALO + side, middle] = tile
    area[:HALO, middle] = above[:HALO].astype(F32)
    area[HALO + side :, middle] = below[:HALO].astype(F32)
    area[:, LEAD - HALO : LEAD] = left[...].astype(F32)
    area[:, LEAD + side : LEAD + side + HALO] = right[...].astype(F32)


def first_branch(area, pairs, last, weights, bias, proj, store):
    full, wide = pairs.shape[:2]
    start = LEAD - SECOND_DILATION
    starts = [start + FIRST_DILATION * b for b in (-1, 0, 1)]
    paired(area, starts, wide, FIRST_DILATION, pairs, last, positive)

    def rows(step, _):
        top = step * 8
        pre = taps_sum(pairs, last, top, 8, FIRST_DILATION, weights) + bias[...]
        branch = dot(positive(pre).astype(BF16), proj[...])
        inputs = area[pl.ds(top + FIRST_DILATION, 8), start : start + wide]
        branch = rounded(inputs + branch.reshape(inputs.shape))
        store(top, pre.reshape(8, wide, pre.shape[1]), branch)
        return 0

    lax.fori_loop(0, (full - 2 * FIRST_DILATION) // 8, rows, 0, unroll=True)


def own_kernel(
    tile, above, below, left, right, weights, bias, proj,
    swapped, pre,
    area, pairs, last,
):
    side, span = tile.shape[0], pre.shape[0]
    assemble(area, tile[...].astype(F32), above, below, left, right)

    def store(top, pre_act, branch):
        pre[pl.ds(top, 8)] = pre_act
        swapped[pl.ds(top, 8)] = branch[:, :span].astype(BF16)

    first_branch(area, pairs, last, weights, bias, proj, store)
    swapped[span:] = jnp.zeros((side, span, swapped.shape[2]), BF16)


def near_kernel(tile, above, below, left, right, pre, hidden_pairs, hidden_last, gate_first, bottle_first, area):
    side, channels, inner = tile.shape[0], tile.shape[2], pre.shape[2]
    first, second = FIRST_DILATION, SECOND_DILATION
    near, small = gate_first.shape[:2]
    assemble(area, tile[...].astype(F32), above, below, left, right)
    for b in (-1, 0, 1):
        at = LEAD + first * b
        window = positive(area[HALO - first : HALO + side + first, at : at + small]).astype(BF16)
        if b < 1:
            hidden_pairs[:, :, (b + 1) * channels : (b + 2) * channels] = window
        else:
            hidden_last[...] = window
    edge = second - first
    part = pre[edge : edge + near, edge : edge + small]
    alive = (part > 0) & inside(part.shape, side, first, 0)
    gate_first[:, :, :inner] = jnp.where(alive, 1.0, 0.0).astype(BF16)
    gate_first[:, :, inner:] = jnp.zeros((near, small, gate_first.shape[2] - inner), BF16)
    bottle_first[...] = positive(pre[second : second + side, second : second + small]).astype(BF16)


def middle_kernel(
    kept, other, w_second, b_second, p_second,
    gate_second, hidden_pairs, hidden_last, bottle_second, grad_tile, grad_pre, first_turn, second_turn,
    current, padded, pre_second,
):
    side, channels, span = first_turn.shape[1], kept.shape[2], kept.shape[1]
    first, second, inner = FIRST_DILATION, SECOND_DILATION, bottle_second.shape[2]
    near, small = gate_second.shape[:2]
    turned = jnp.swapaxes(other[:span].astype(F32), 0, 1)
    sym = rounded((kept[:span].astype(F32) + turned) * 0.5)
    current[:, :span] = jnp.where(inside(sym.shape, side, second, 0), sym, 0)
    current[:, span:] = jnp.zeros((span, current.shape[1] - span, channels), F32)
    edge = second - first
    part = current[edge : edge + near, edge : edge + small]
    gate_second[...] = jnp.where(part > 0, 1.0, 0.0).astype(BF16)
    paired(current, [0, second, 2 * second], small, second, hidden_pairs, hidden_last, positive)

    def rows(step, _):
        top = step * 8
        total = taps_sum(hidden_pairs, hidden_last, top, 8, second, w_second) + b_second[...]
        pre_second[pl.ds(top, 8)] = total.reshape(8, small, total.shape[1])
        return 0

    lax.fori_loop(0, side // 8, rows, 0, unroll=True)
    bottle_second[...] = positive(pre_second[:, :, :inner]).astype(BF16)

    turned = jnp.swapaxes(other[span:, :side].astype(F32), 0, 1)
    padded[:, side:] = jnp.zeros((side, small - side, channels), F32)
    padded[:, :side] = rounded((kept[span:, :side].astype(F32) + turned) * 0.5)
    branch = padded[...].astype(BF16)
    grad_tile[...] = branch
    grad = dot(branch.reshape(side * small, channels), p_second[...]).reshape(side, small, 2 * inner)
    grad = jnp.where(pre_second[...] > 0, grad, 0)
    grad_pre[...] = grad.astype(BF16)
    even = sends_last(0, 0)
    for rows, value, width in ((slice(0, HALO), grad, HALO), (slice(HALO, HALO + first), padded[...], first)):
        head, tail = value[:width, :side], value[side - width :, :side]
        first_turn[rows] = jnp.where(even, tail, head).astype(BF16)
        second_turn[rows] = jnp.where(even, head, tail).astype(BF16)


def weight_sums(rows, ends, grad_pre, hidden, bottle, grad_tile):
    side, small, lanes = grad_pre.shape
    inner = bottle.shape[2]
    size = side * small
    flat = grad_pre.reshape(size, lanes)
    turned = flat.T[:inner].astype(BF16)
    for a in range(3):
        b = 0
        while b < 3:
            window = hidden(a, b)
            grads = dot(turned, window.reshape(size, window.shape[2]))
            for at in range(0, window.shape[2], grad_tile.shape[2]):
                rows[(3 * a + b) * inner : (3 * a + b + 1) * inner] = grads[:, at : at + grad_tile.shape[2]]
                b += 1
    turned = bottle[...].reshape(size, inner).astype(F32).T.astype(BF16)
    rows[9 * inner : 10 * inner] = dot(turned, grad_tile.reshape(size, grad_tile.shape[2]))
    ends[...] = jnp.zeros(ends.shape, F32)
    ends[:, :lanes] = jnp.broadcast_to(jnp.sum(flat, axis=0, keepdims=True), (ends.shape[0], lanes))


def weights_kernel(
    mine, theirs, w_first, w_second, v_second, v_first, p_first, p_second, p_back, b_first, b_second, packed
):
    inner, channels = p_first.shape
    section = lax.axis_index("segment")
    packed[section] = mine[...]
    packed[1 - section] = theirs[...]

    def conv(section, k):
        return packed[section, k * inner : (k + 1) * inner]

    def turned(x):
        return x.astype(F32).T.astype(BF16)

    zero = jnp.zeros((inner, channels), BF16)
    for at, k in enumerate(ORDER):
        here = slice(at * channels, (at + 1) * channels)
        own, other = conv(1, k), conv(1, 3 * (k % 3) + k // 3)
        w_first[here] = turned(conv(0, k))
        w_second[here] = turned(jnp.concatenate([own, other], axis=0))
        upper, lower = (slice((2 * k + half) * inner, (2 * k + half + 1) * inner) for half in (0, 1))
        v_second[upper, :channels], v_second[upper, channels:] = own, zero
        v_second[lower, :channels], v_second[lower, channels:] = zero, other
        v_first[k, :inner], v_first[k, inner:] = conv(0, k), zero
    p_first[...] = conv(0, 9)
    p_second[...] = turned(jnp.concatenate([conv(1, 9), conv(1, 9)], axis=0))
    p_back[...] = turned(jnp.concatenate([conv(0, 9), zero], axis=0))
    b_first[...] = packed[0, 10 * inner :].astype(F32)[:1, :inner]
    bias = packed[1, 10 * inner :].astype(F32)[:1, :inner]
    b_second[...] = jnp.concatenate([bias, bias], axis=1)


def second_sums_kernel(grad_pre, pairs, last, bottle, grad_tile, rows, ends):
    side = grad_pre.shape[0]
    channels = grad_tile.shape[2]

    def hidden(a, b):
        top = SECOND_DILATION * a
        if b == 0:
            return pairs[top : top + side]
        return last[top + SECOND_DILATION : top + SECOND_DILATION + side, :, :channels]

    weight_sums(rows, ends, grad_pre[...].astype(F32), hidden, bottle, grad_tile[...])


def backward_kernel(
    grad_pre, grad_tile, above, below, left, right, left_branch, right_branch, gate_second, gate_first, near_pairs,
    near_last, bottle_first, v_second, p_first, rows_second, ends_second,
    keep, away, windows, grad_first,
    area, pairs, last, branch, grads, rows, ends,
):
    side, channels = grad_first.shape[0], grad_first.shape[2]
    first, second = FIRST_DILATION, SECOND_DILATION
    full, near = side + 2 * HALO, side + 2 * first
    small = grad_pre.shape[1]
    middle = slice(LEAD, LEAD + side)

    area[:, :LEAD] = jnp.zeros((full, LEAD, channels), F32)
    area[:, LEAD + side :] = jnp.zeros((full, area.shape[1] - LEAD - side, channels), F32)
    area[HALO : HALO + side, LEAD : LEAD + small] = grad_pre[...].astype(F32)
    area[:HALO, middle] = above[:HALO].astype(F32)
    area[HALO + side :, middle] = below[:HALO].astype(F32)
    area[:, LEAD - HALO : LEAD] = left[...].astype(F32)
    area[:, LEAD + side : LEAD + side + HALO] = right[...].astype(F32)
    branch[...] = jnp.zeros(branch.shape, F32)
    branch[first : first + side, first : first + side] = grad_tile[:, :side].astype(F32)
    branch[:first, first : first + side] = above[HALO:].astype(F32)
    branch[first + side :, first : first + side] = below[HALO:].astype(F32)
    branch[:, :first] = left_branch[...].astype(F32)
    branch[:, first + side : near] = right_branch[...].astype(F32)
    for b in (-1, 0, 1):
        at = LEAD - HALO + second * (1 - b)
        window = area[:, at : at + small].astype(BF16)
        if b < 1:
            pairs[:, :, (b + 1) * channels : (b + 2) * channels] = window
        else:
            last[...] = window
    grads[:, small:] = jnp.zeros((near, grads.shape[1] - small, channels), F32)

    def sections(step, _):
        top = step * 7
        size = 7 * small
        total = None
        for a in (-1, 0, 1):
            rows_of = pl.ds(top + second * (1 - a), 7)
            at = 3 * (a + 1) * channels
            term = dot(pairs[rows_of].reshape(size, 2 * channels), v_second[at : at + 2 * channels])
            total = term if total is None else total + term
            total = total + dot(last[rows_of].reshape(size, channels), v_second[at + 2 * channels : at + 3 * channels])
        here = pl.ds(top, 7)
        grad = branch[here, :small].reshape(size, channels)
        gate = gate_second[here].astype(F32).reshape(size, channels) > 0
        own = rounded(grad + jnp.where(gate, total[:, :channels], 0))
        other = rounded(grad + jnp.where(gate, total[:, channels:], 0))
        grad = ((own + other) * 0.5).astype(BF16)
        branch[here, :small] = grad.astype(F32).reshape(7, small, channels)
        gate = gate_first[here].astype(F32).reshape(size, channels) > 0
        grad = rounded(jnp.where(gate, dot(grad, p_first[...]), 0))
        grads[here, :small] = grad.reshape(7, small, channels)
        return 0

    lax.fori_loop(0, near // 7, sections, 0, unroll=True)
    for b in (-1, 0, 1):
        at = first * (1 - b)
        windows[b + 1] = grads[:, at : at + small].astype(BF16)
    part = branch[first : first + side, first : first + small]
    grad_first[...] = part[:, :side].astype(BF16)
    real = lax.broadcasted_iota(jnp.int32, part.shape, 1) < side
    part = jnp.where(real, part, 0).astype(BF16)
    grad = jnp.where(real, grads[first : first + side, first : first + small], 0)

    def hidden(a, b):
        return (near_last if b else near_pairs)[first * a : first * a + side]

    weight_sums(rows, ends, grad, hidden, bottle_first, part)

    first_core = lax.axis_index("segment") == 0
    count = rows.shape[0]
    for here, one, two in (
        (slice(0, count), rows[...], rows_second[...]),
        (slice(count, count + ends.shape[0]), ends[...], ends_second[...]),
    ):
        keep[here] = jnp.where(first_core, one, two)
        away[here] = jnp.where(first_core, two, one).astype(BF16)


def pair_kernel(keep, other, parts):
    devices, share = parts.shape[0], parts.shape[1] - 8
    total = keep[...] + other[...].astype(F32)
    count = keep.shape[0] - 16
    for j in range(devices):
        low, high = min(j * share, count), min((j + 1) * share, count)
        pieces = [total[low:high]] if low < high else []
        if high - low < share:
            pieces.append(jnp.zeros((share - (high - low), keep.shape[1]), F32))
        parts[j] = jnp.concatenate(pieces + [total[count : count + 8]]).astype(BF16)


def input_kernel(windows, grad_first, tile, v_first, out):
    side, channels = out.shape[0], out.shape[2]
    small = windows.shape[2]
    first = FIRST_DILATION

    def rows(step, _):
        top = step * 8
        total = jnp.zeros((8 * small, channels), F32)
        for a, b in TAPS:
            window = windows[b + 1, pl.ds(top + first * (1 - a), 8)].reshape(8 * small, channels)
            total = total + dot(window, v_first[tap(a, b)])
        here = pl.ds(top, 8)
        total = total.reshape(8, small, channels)[:, :side]
        total = jnp.where(tile[here].astype(F32) > 0, total, 0)
        out[here] = (grad_first[here].astype(F32) + total).astype(BF16)
        return 0

    lax.fori_loop(0, side // 8, rows, 0, unroll=True)


def total_kernel(scale, parts, rows, ends):
    share = rows.shape[1]
    total = jnp.sum(parts[...].astype(F32), axis=0) * scale
    rows[...] = jnp.broadcast_to(total[:share].astype(BF16)[None], rows.shape)
    ends[...] = total[share:]


def outputs_kernel(rows, ends, moved, conv_gradient, bias_gradient, out_gradient, input_gradient):
    count, inner = conv_gradient.shape[0], out_gradient.shape[0]
    conv_gradient[...] = rows[:count].astype(F32)
    out_gradient[...] = rows[count : count + inner].astype(F32)
    bias_gradient[...] = ends[:1, :inner]
    input_gradient[...] = moved[...]


def call(kernel, name, outs, scratch, flops, *operands):
    outs = [jax.ShapeDtypeStruct(shape, dtype) for shape, dtype in outs]
    moved = sum(x.size * x.dtype.itemsize for x in list(operands) + outs)
    return pl.pallas_call(
        kernel,
        name=name,
        out_shape=outs,
        scratch_shapes=[pltpu.VMEM(shape, dtype) for shape, dtype in scratch],
        cost_estimate=pl.CostEstimate(flops=flops, bytes_accessed=moved, transcendentals=0),
        compiler_params=pltpu.CompilerParams(vmem_limit_bytes=40 * 1024 * 1024),
    )(*operands)


def local(activations, cotangent, conv_weight, conv_bias, out_weight):
    side, channels, inner = activations.shape[1], activations.shape[3], conv_weight.shape[3]
    number = lax.axis_size("row")
    first, second = FIRST_DILATION, SECOND_DILATION
    full, span, near = side + 2 * HALO, side + 2 * second, side + 2 * first
    wide, small = up16(span), up16(near)

    tile = bring(activations[0])
    stored_even = lax.rem(lax.axis_index("row"), 2) == 0
    ends = (activations[0, side - HALO :], activations[0, :HALO])
    got = [bring(jnp.where(stored_even, *ends), 0), bring(jnp.where(stored_even, *ends[::-1]), 1)]
    above, below = around(0, got)

    def columns(turn):
        def chosen(x):
            return jnp.swapaxes(jnp.where(sends_last(1, turn), x[:, side - HALO :], x[:, :HALO]), 0, 1)

        strip = jnp.pad(chosen(tile), ((0, 0), (HALO, HALO), (0, 0)))
        strip = lax.optimization_barrier(strip)
        for row_turn in (0, 1):
            at = jnp.where(sends_last(0, row_turn), HALO + side, 0)
            strip = lax.dynamic_update_slice(strip, chosen(got[row_turn]), (0, at, 0))
        return strip

    strips, late = lax.optimization_barrier(([columns(0), columns(1)], cotangent[0]))
    left, right = around(1, [exchange(strips[turn], 1, turn) for turn in (0, 1)])
    late = bring(late)

    bias_rows = jnp.pad(conv_bias, ((0, 15), (0, channels - inner)))
    packed = jnp.concatenate(
        [jnp.swapaxes(conv_weight[0], 1, 2).reshape(9 * inner, channels), out_weight[0], bias_rows]
    )
    others = lax.ppermute(packed, "segment", [(0, 1), (1, 0)])
    w_first, w_second, v_second, v_first, p_first, p_second, p_back, b_first, b_second = call(
        weights_kernel,
        "weights",
        [
            ((9 * channels, inner), BF16),
            ((9 * channels, 2 * inner), BF16),
            ((18 * inner, 2 * channels), BF16),
            ((9, 2 * inner, channels), BF16),
            ((inner, channels), BF16),
            ((channels, 2 * inner), BF16),
            ((channels, 2 * inner), BF16),
            ((1, inner), F32),
            ((1, 2 * inner), F32),
        ],
        [((2,) + packed.shape, BF16)],
        packed.size,
        *(packed, others),
    )

    own = (tile, above, below, jnp.swapaxes(left, 0, 1), jnp.swapaxes(right, 0, 1))
    area = ((full, LEAD + up16(side + LEAD), channels), F32)
    kept, pre_first = call(
        own_kernel,
        "own_branch",
        [((span + side, span, channels), BF16), ((span, wide, inner), F32)],
        [area, ((full, wide, 2 * channels), BF16), ((full + first, wide, 2 * channels), BF16)],
        span * wide * channels * inner * 400,
        *own,
        *(w_first, b_first, p_first),
    )
    kept = lax.dynamic_update_slice(kept, late, (span, 0, 0))
    other = swap(kept)
    gate_second, hidden_pairs, hidden_last, bottle_second, grad_tile, grad_pre, *strips = call(
        middle_kernel,
        "middle",
        [
            ((near, small, channels), BF16),
            ((span, small, 2 * channels), BF16),
            ((span + second, small, 2 * channels), BF16),
            ((side, small, inner), BF16),
            ((side, small, channels), BF16),
            ((side, small, 2 * inner), BF16),
            ((HALO + first, side, channels), BF16),
            ((HALO + first, side, channels), BF16),
        ],
        [
            ((span, wide, channels), F32),
            ((side, small, channels), F32),
            ((side, small, 2 * inner), F32),
        ],
        24 * side * small * channels * 2 * inner,
        *(kept, other, w_second, b_second, p_second),
    )

    near_pairs, near_last, gate_first, bottle_first = call(
        near_kernel,
        "near",
        [
            ((near, small, 2 * channels), BF16),
            ((near, small, channels), BF16),
            ((near, small, channels), BF16),
            ((side, small, inner), BF16),
        ],
        [area],
        near * small * channels,
        *own,
        pre_first,
    )

    above, below = around(0, [exchange(strips[turn], 0, turn) for turn in (0, 1)])
    rows_second, ends_second = call(
        second_sums_kernel,
        "second_sums",
        [((10 * inner, channels), F32), ((16, channels), F32)],
        [],
        20 * side * small * channels * inner,
        *(grad_pre, hidden_pairs, hidden_last, bottle_second, grad_tile),
    )

    def columns(turn):
        def chosen(x, width):
            return jnp.where(sends_last(1, turn), x[:, side - width : side], x[:, :width])

        grads = jnp.concatenate([chosen(x, HALO) for x in (above[:HALO], grad_pre, below[:HALO])])
        branches = jnp.concatenate([chosen(x, first) for x in (above[HALO:], grad_tile, below[HALO:])])
        branches = jnp.pad(branches, ((second, second), (0, 0), (0, 0)))
        return jnp.swapaxes(jnp.concatenate([grads, branches], axis=1), 0, 1)

    left, right = around(1, [exchange(columns(turn), 1, turn) for turn in (0, 1)])
    left, right = jnp.swapaxes(left, 0, 1), jnp.swapaxes(right, 0, 1)

    devices = number * number
    share = -(-10 * inner // (8 * devices)) * 8
    keep, away, windows, grad_first = call(
        backward_kernel,
        "backward",
        [
            ((10 * inner + 16, channels), F32),
            ((10 * inner + 16, channels), BF16),
            ((3, near, small, channels), BF16),
            ((side, side, channels), BF16),
        ],
        [
            ((full, LEAD + up16(side + HALO + first), channels), F32),
            ((full, small, 2 * channels), BF16),
            ((full, small, channels), BF16),
            ((near, small + 16, channels), F32),
            ((near, small + 16, channels), F32),
            ((10 * inner, channels), F32),
            ((16, channels), F32),
        ],
        36 * near * small * channels * channels,
        *(grad_pre, grad_tile, above, below, left[:, :HALO], right[:, :HALO]),
        *(left[second : second + near, HALO:], right[second : second + near, HALO:]),
        *(gate_second, gate_first, near_pairs, near_last, bottle_first, v_second, p_back, rows_second, ends_second),
    )

    (input_gradient,) = call(
        input_kernel,
        "input",
        [((side, side, channels), BF16)],
        [],
        18 * side * small * channels * channels,
        *(windows, grad_first, tile, v_first),
    )
    other = lax.ppermute(away, "segment", [(0, 1), (1, 0)])
    other, input_gradient = lax.optimization_barrier((other, input_gradient))
    (parts,) = call(
        pair_kernel,
        "pair",
        [((devices, share + 8, channels), BF16)],
        [],
        keep.size,
        *(keep, other),
    )
    parts = lax.all_to_all(parts, GRID, 0, 0, tiled=True)
    input_gradient = take_back(input_gradient)
    cells = lax.axis_size("segment") * (side * number) * (side * number)
    rows, ends = call(
        functools.partial(total_kernel, float(cells) ** -0.5),
        "total",
        [((devices, share, channels), BF16), ((8, channels), F32)],
        [],
        parts.size,
        parts,
    )
    rows, _ = lax.optimization_barrier((rows, input_gradient))
    rows = lax.all_to_all(rows, GRID, 0, 0, tiled=True).reshape(devices * share, channels)
    conv_gradient, bias_gradient, out_gradient, input_gradient = call(
        outputs_kernel,
        "outputs",
        [
            ((9 * inner, channels), F32),
            ((1, inner), F32),
            ((inner, channels), F32),
            ((side, side, channels), BF16),
        ],
        [],
        rows.size,
        *(rows, ends, input_gradient),
    )
    conv_gradient = jnp.swapaxes(conv_gradient.reshape(1, 9, inner, channels), 2, 3)
    return (input_gradient[None], conv_gradient, bias_gradient, out_gradient[None])


def solution(mesh):
    in_specs = (
        P("segment", "row", "col", None),
        P("segment", "row", "col", None),
        P("segment", None, None, None),
        P("segment", None),
        P("segment", None, None),
    )
    out_specs = (
        P("segment", "row", "col", None),
        P("segment", None, None, None),
        P("segment", None),
        P("segment", None, None),
    )
    return jax.shard_map(local, mesh=mesh, in_specs=in_specs, out_specs=out_specs, check_vma=False)
```

```python
import functools

import jax
import jax.numpy as jnp
from jax import lax
from jax.experimental import pallas as pl
from jax.experimental.pallas import tpu as pltpu
from jax.sharding import PartitionSpec as P

FIRST_DILATION = 2
SECOND_DILATION = 8
HALO = FIRST_DILATION + SECOND_DILATION
GRID = ("row", "col")
ALL = ("segment",) + GRID
ORDER = [0, 1, 3, 4, 6, 7, 2, 5, 8]
TAPS = [(a, b) for a in (-1, 0, 1) for b in (-1, 0, 1)]
LEAD = 16
F32, BF16 = jnp.float32, jnp.bfloat16


def tap(a, b):
    return 3 * (a + 1) + (b + 1)


def dot(x, y):
    return jnp.dot(x, y, preferred_element_type=F32)


def rounded(x):
    return x.astype(BF16).astype(F32)


def up16(n):
    return -(-n // 16) * 16


def home(batch, r, c):
    number = lax.axis_size("row")
    core, row, col = (batch, r, c) if r == c else (int(r > c), r, c)
    if r != c and (r < c) == (batch == 1):
        row, col = c, r
    return (core * number + row) * number + col


def place():
    row, col = lax.axis_index("row"), lax.axis_index("col")
    low, high = jnp.minimum(row, col), jnp.maximum(row, col)
    upper = lax.axis_index("segment") == 0
    return jnp.where(upper, low, high), jnp.where(upper, high, low)


def permute(x, pair):
    number = lax.axis_size("row")
    tiles = [(m, r, c) for m in range(lax.axis_size("segment")) for r in range(number) for c in range(number)]
    pairs = [pair(*tile) for tile in tiles]
    return lax.ppermute(x, ALL, [found for found in pairs if found is not None])


def stored(batch, r, c):
    number = lax.axis_size("row")
    return (batch * number + r) * number + c


def bring(x, turn=None):
    def pair(batch, r, c):
        row = r if turn is None else partner(r, turn)
        if row is not None:
            return stored(batch, r, c), home(batch, row, c)

    return permute(x, pair)


def take_back(x):
    return permute(x, lambda m, r, c: (home(m, r, c), stored(m, r, c)))


def swap(x):
    return permute(x, lambda m, r, c: (home(m, r, c), home(m, c, r)))


def partner(index, turn):
    other = index + 1 if (index + turn) % 2 == 0 else index - 1
    return other if 0 <= other < lax.axis_size("row") else None


def exchange(x, axis, turn):
    def pair(batch, r, c):
        other = partner(c if axis else r, turn)
        if other is not None:
            return home(batch, r, c), home(batch, r, other) if axis else home(batch, other, c)

    return permute(x, pair)


def sends_last(axis, turn):
    return lax.rem(place()[axis] + turn, 2) == 0


def around(axis, got):
    even = sends_last(axis, 0)
    return jnp.where(even, got[1], got[0]), jnp.where(even, got[0], got[1])


def inside(shape, side, width, top):
    number = lax.axis_size("row") * side
    rows = lax.broadcasted_iota(jnp.int32, shape, 0) + top - width
    cols = lax.broadcasted_iota(jnp.int32, shape, 1) - width
    row, col = place()
    at_row = row * side + rows
    at_col = col * side + cols
    return (at_row >= 0) & (at_row < number) & (at_col >= 0) & (at_col < number) & (cols < side + width)


def paired(source, starts, width, dilation, pairs, last, change):
    lanes = source.shape[2]
    low, high = slice(0, lanes), slice(lanes, 2 * lanes)

    def step(k, _):
        rows, lower = pl.ds(4 * k, 4), pl.ds(4 * k + dilation, 4)
        window = [change(source[rows, at : at + width]).astype(BF16) for at in starts]
        pairs[rows, :, low] = window[0]
        pairs[rows, :, high] = window[1]
        last[lower, :, low] = window[2]
        last[rows, :, high] = window[2]
        return 0

    lax.fori_loop(0, source.shape[0] // 4, step, 0, unroll=True)


def taps_sum(pairs, last, top, rows, dilation, weights):
    width, lanes = pairs.shape[1], pairs.shape[2] // 2
    size = rows * width
    total = None
    for k in range(5):
        if k < 3:
            window = pairs[pl.ds(top + dilation * k, rows)]
        elif k == 3:
            window = last[pl.ds(top + dilation, rows)]
        else:
            window = last[pl.ds(top + 3 * dilation, rows), :, :lanes]
        weight = weights[2 * lanes * k : min(2 * lanes * (k + 1), 9 * lanes)]
        term = dot(window.reshape(size, window.shape[2]), weight)
        total = term if total is None else total + term
    return total


def positive(x):
    return jnp.maximum(x, 0)


def assemble(area, tile, above, below, left, right):
    side = tile.shape[0]
    full, wide, channels = area.shape
    middle = slice(LEAD, LEAD + side)
    area[:, :LEAD] = jnp.zeros((full, LEAD, channels), F32)
    area[:, LEAD + side :] = jnp.zeros((full, wide - LEAD - side, channels), F32)
    area[HALO : HALO + side, middle] = tile
    area[:HALO, middle] = above[:HALO].astype(F32)
    area[HALO + side :, middle] = below[:HALO].astype(F32)
    area[:, LEAD - HALO : LEAD] = left[...].astype(F32)
    area[:, LEAD + side : LEAD + side + HALO] = right[...].astype(F32)


def first_branch(area, pairs, last, weights, bias, proj, store):
    full, wide = pairs.shape[:2]
    start = LEAD - SECOND_DILATION
    starts = [start + FIRST_DILATION * b for b in (-1, 0, 1)]
    paired(area, starts, wide, FIRST_DILATION, pairs, last, positive)

    def rows(step, _):
        top = step * 8
        pre = taps_sum(pairs, last, top, 8, FIRST_DILATION, weights) + bias[...]
        branch = dot(positive(pre).astype(BF16), proj[...])
        inputs = area[pl.ds(top + FIRST_DILATION, 8), start : start + wide]
        branch = rounded(inputs + branch.reshape(inputs.shape))
        store(top, pre.reshape(8, wide, pre.shape[1]), branch)
        return 0

    lax.fori_loop(0, (full - 2 * FIRST_DILATION) // 8, rows, 0, unroll=True)


def own_kernel(
    tile, above, below, left, right, weights, bias, proj,
    swapped, pre,
    area, pairs, last,
):
    side, span = tile.shape[0], pre.shape[0]
    assemble(area, tile[...].astype(F32), above, below, left, right)

    def store(top, pre_act, branch):
        pre[pl.ds(top, 8)] = pre_act
        swapped[pl.ds(top, 8)] = branch[:, :span].astype(BF16)

    first_branch(area, pairs, last, weights, bias, proj, store)
    swapped[span:] = jnp.zeros((side, span, swapped.shape[2]), BF16)


def near_kernel(tile, above, below, left, right, pre, hidden_pairs, hidden_last, gate_first, bottle_first, area):
    side, channels, inner = tile.shape[0], tile.shape[2], pre.shape[2]
    first, second = FIRST_DILATION, SECOND_DILATION
    near, small = gate_first.shape[:2]
    assemble(area, tile[...].astype(F32), above, below, left, right)
    for b in (-1, 0, 1):
        at = LEAD + first * b
        window = positive(area[HALO - first : HALO + side + first, at : at + small]).astype(BF16)
        if b < 1:
            hidden_pairs[:, :, (b + 1) * channels : (b + 2) * channels] = window
        else:
            hidden_last[...] = window
    edge = second - first
    part = pre[edge : edge + near, edge : edge + small]
    alive = (part > 0) & inside(part.shape, side, first, 0)
    gate_first[:, :, :inner] = jnp.where(alive, 1.0, 0.0).astype(BF16)
    gate_first[:, :, inner:] = jnp.zeros((near, small, gate_first.shape[2] - inner), BF16)
    bottle_first[...] = positive(pre[second : second + side, second : second + small]).astype(BF16)


def middle_kernel(
    kept, other, w_second, b_second, p_second,
    gate_second, hidden_pairs, hidden_last, bottle_second, grad_tile, grad_pre, first_turn, second_turn,
    current, padded, pre_second,
):
    side, channels, span = first_turn.shape[1], kept.shape[2], kept.shape[1]
    first, second, inner = FIRST_DILATION, SECOND_DILATION, bottle_second.shape[2]
    near, small = gate_second.shape[:2]
    turned = jnp.swapaxes(other[:span].astype(F32), 0, 1)
    sym = rounded((kept[:span].astype(F32) + turned) * 0.5)
    current[:, :span] = jnp.where(inside(sym.shape, side, second, 0), sym, 0)
    current[:, span:] = jnp.zeros((span, current.shape[1] - span, channels), F32)
    edge = second - first
    part = current[edge : edge + near, edge : edge + small]
    gate_second[...] = jnp.where(part > 0, 1.0, 0.0).astype(BF16)
    paired(current, [0, second, 2 * second], small, second, hidden_pairs, hidden_last, positive)

    def rows(step, _):
        top = step * 8
        total = taps_sum(hidden_pairs, hidden_last, top, 8, second, w_second) + b_second[...]
        pre_second[pl.ds(top, 8)] = total.reshape(8, small, total.shape[1])
        return 0

    lax.fori_loop(0, side // 8, rows, 0, unroll=True)
    bottle_second[...] = positive(pre_second[:, :, :inner]).astype(BF16)

    turned = jnp.swapaxes(other[span:, :side].astype(F32), 0, 1)
    padded[:, side:] = jnp.zeros((side, small - side, channels), F32)
    padded[:, :side] = rounded((kept[span:, :side].astype(F32) + turned) * 0.5)
    branch = padded[...].astype(BF16)
    grad_tile[...] = branch
    grad = dot(branch.reshape(side * small, channels), p_second[...]).reshape(side, small, 2 * inner)
    grad = jnp.where(pre_second[...] > 0, grad, 0)
    grad_pre[...] = grad.astype(BF16)
    even = sends_last(0, 0)
    for rows, value, width in ((slice(0, HALO), grad, HALO), (slice(HALO, HALO + first), padded[...], first)):
        head, tail = value[:width, :side], value[side - width :, :side]
        first_turn[rows] = jnp.where(even, tail, head).astype(BF16)
        second_turn[rows] = jnp.where(even, head, tail).astype(BF16)


def weight_sums(rows, ends, grad_pre, hidden, bottle, grad_tile):
    side, small, lanes = grad_pre.shape
    inner = bottle.shape[2]
    size = side * small
    flat = grad_pre.reshape(size, lanes)
    turned = flat.T[:inner].astype(BF16)
    for a in range(3):
        b = 0
        while b < 3:
            window = hidden(a, b)
            grads = dot(turned, window.reshape(size, window.shape[2]))
            for at in range(0, window.shape[2], grad_tile.shape[2]):
                rows[(3 * a + b) * inner : (3 * a + b + 1) * inner] = grads[:, at : at + grad_tile.shape[2]]
                b += 1
    turned = bottle[...].reshape(size, inner).astype(F32).T.astype(BF16)
    rows[9 * inner : 10 * inner] = dot(turned, grad_tile.reshape(size, grad_tile.shape[2]))
    ends[...] = jnp.zeros(ends.shape, F32)
    ends[:, :lanes] = jnp.broadcast_to(jnp.sum(flat, axis=0, keepdims=True), (ends.shape[0], lanes))


def weights_kernel(
    mine, theirs, w_first, w_second, v_second, v_first, p_first, p_second, p_back, b_first, b_second, packed
):
    inner, channels = p_first.shape
    section = lax.axis_index("segment")
    packed[section] = mine[...]
    packed[1 - section] = theirs[...]

    def conv(section, k):
        return packed[section, k * inner : (k + 1) * inner]

    def turned(x):
        return x.astype(F32).T.astype(BF16)

    zero = jnp.zeros((inner, channels), BF16)
    for at, k in enumerate(ORDER):
        here = slice(at * channels, (at + 1) * channels)
        own, other = conv(1, k), conv(1, 3 * (k % 3) + k // 3)
        w_first[here] = turned(conv(0, k))
        w_second[here] = turned(jnp.concatenate([own, other], axis=0))
        upper, lower = (slice((2 * k + half) * inner, (2 * k + half + 1) * inner) for half in (0, 1))
        v_second[upper, :channels], v_second[upper, channels:] = own, zero
        v_second[lower, :channels], v_second[lower, channels:] = zero, other
        v_first[k, :inner], v_first[k, inner:] = conv(0, k), zero
    p_first[...] = conv(0, 9)
    p_second[...] = turned(jnp.concatenate([conv(1, 9), conv(1, 9)], axis=0))
    p_back[...] = turned(jnp.concatenate([conv(0, 9), zero], axis=0))
    b_first[...] = packed[0, 10 * inner :].astype(F32)[:1, :inner]
    bias = packed[1, 10 * inner :].astype(F32)[:1, :inner]
    b_second[...] = jnp.concatenate([bias, bias], axis=1)


def second_sums_kernel(grad_pre, pairs, last, bottle, grad_tile, rows, ends):
    side = grad_pre.shape[0]
    channels = grad_tile.shape[2]

    def hidden(a, b):
        top = SECOND_DILATION * a
        if b == 0:
            return pairs[top : top + side]
        return last[top + SECOND_DILATION : top + SECOND_DILATION + side, :, :channels]

    weight_sums(rows, ends, grad_pre[...].astype(F32), hidden, bottle, grad_tile[...])


def backward_kernel(
    grad_pre, grad_tile, above, below, left, right, left_branch, right_branch, gate_second, gate_first, near_pairs,
    near_last, bottle_first, v_second, p_first, rows_second, ends_second,
    keep, away, windows, grad_first,
    area, pairs, last, branch, grads, rows, ends,
):
    side, channels = grad_first.shape[0], grad_first.shape[2]
    first, second = FIRST_DILATION, SECOND_DILATION
    full, near = side + 2 * HALO, side + 2 * first
    small = grad_pre.shape[1]
    middle = slice(LEAD, LEAD + side)

    area[:, :LEAD] = jnp.zeros((full, LEAD, channels), F32)
    area[:, LEAD + side :] = jnp.zeros((full, area.shape[1] - LEAD - side, channels), F32)
    area[HALO : HALO + side, LEAD : LEAD + small] = grad_pre[...].astype(F32)
    area[:HALO, middle] = above[:HALO].astype(F32)
    area[HALO + side :, middle] = below[:HALO].astype(F32)
    area[:, LEAD - HALO : LEAD] = left[...].astype(F32)
    area[:, LEAD + side : LEAD + side + HALO] = right[...].astype(F32)
    branch[...] = jnp.zeros(branch.shape, F32)
    branch[first : first + side, first : first + side] = grad_tile[:, :side].astype(F32)
    branch[:first, first : first + side] = above[HALO:].astype(F32)
    branch[first + side :, first : first + side] = below[HALO:].astype(F32)
    branch[:, :first] = left_branch[...].astype(F32)
    branch[:, first + side : near] = right_branch[...].astype(F32)
    for b in (-1, 0, 1):
        at = LEAD - HALO + second * (1 - b)
        window = area[:, at : at + small].astype(BF16)
        if b < 1:
            pairs[:, :, (b + 1) * channels : (b + 2) * channels] = window
        else:
            last[...] = window
    grads[:, small:] = jnp.zeros((near, grads.shape[1] - small, channels), F32)

    def sections(step, _):
        top = step * 7
        size = 7 * small
        total = None
        for a in (-1, 0, 1):
            rows_of = pl.ds(top + second * (1 - a), 7)
            at = 3 * (a + 1) * channels
            term = dot(pairs[rows_of].reshape(size, 2 * channels), v_second[at : at + 2 * channels])
            total = term if total is None else total + term
            total = total + dot(last[rows_of].reshape(size, channels), v_second[at + 2 * channels : at + 3 * channels])
        here = pl.ds(top, 7)
        grad = branch[here, :small].reshape(size, channels)
        gate = gate_second[here].astype(F32).reshape(size, channels) > 0
        own = rounded(grad + jnp.where(gate, total[:, :channels], 0))
        other = rounded(grad + jnp.where(gate, total[:, channels:], 0))
        grad = ((own + other) * 0.5).astype(BF16)
        branch[here, :small] = grad.astype(F32).reshape(7, small, channels)
        gate = gate_first[here].astype(F32).reshape(size, channels) > 0
        grad = rounded(jnp.where(gate, dot(grad, p_first[...]), 0))
        grads[here, :small] = grad.reshape(7, small, channels)
        return 0

    lax.fori_loop(0, near // 7, sections, 0, unroll=True)
    for b in (-1, 0, 1):
        at = first * (1 - b)
        windows[b + 1] = grads[:, at : at + small].astype(BF16)
    part = branch[first : first + side, first : first + small]
    grad_first[...] = part[:, :side].astype(BF16)
    real = lax.broadcasted_iota(jnp.int32, part.shape, 1) < side
    part = jnp.where(real, part, 0).astype(BF16)
    grad = jnp.where(real, grads[first : first + side, first : first + small], 0)

    def hidden(a, b):
        return (near_last if b else near_pairs)[first * a : first * a + side]

    weight_sums(rows, ends, grad, hidden, bottle_first, part)

    first_core = lax.axis_index("segment") == 0
    count = rows.shape[0]
    for here, one, two in (
        (slice(0, count), rows[...], rows_second[...]),
        (slice(count, count + ends.shape[0]), ends[...], ends_second[...]),
    ):
        keep[here] = jnp.where(first_core, one, two)
        away[here] = jnp.where(first_core, two, one).astype(BF16)


def pair_kernel(keep, other, parts):
    devices, share = parts.shape[0], parts.shape[1] - 8
    total = keep[...] + other[...].astype(F32)
    count = keep.shape[0] - 16
    for j in range(devices):
        low, high = min(j * share, count), min((j + 1) * share, count)
        pieces = [total[low:high]] if low < high else []
        if high - low < share:
            pieces.append(jnp.zeros((share - (high - low), keep.shape[1]), F32))
        parts[j] = jnp.concatenate(pieces + [total[count : count + 8]]).astype(BF16)


def input_kernel(windows, grad_first, tile, v_first, out):
    side, channels = out.shape[0], out.shape[2]
    small = windows.shape[2]
    first = FIRST_DILATION

    def rows(step, _):
        top = step * 8
        total = jnp.zeros((8 * small, channels), F32)
        for a, b in TAPS:
            window = windows[b + 1, pl.ds(top + first * (1 - a), 8)].reshape(8 * small, channels)
            total = total + dot(window, v_first[tap(a, b)])
        here = pl.ds(top, 8)
        total = total.reshape(8, small, channels)[:, :side]
        total = jnp.where(tile[here].astype(F32) > 0, total, 0)
        out[here] = (grad_first[here].astype(F32) + total).astype(BF16)
        return 0

    lax.fori_loop(0, side // 8, rows, 0, unroll=True)


def total_kernel(scale, parts, rows, ends):
    share = rows.shape[1]
    total = jnp.sum(parts[...].astype(F32), axis=0) * scale
    rows[...] = jnp.broadcast_to(total[:share].astype(BF16)[None], rows.shape)
    ends[...] = total[share:]


def outputs_kernel(rows, ends, moved, conv_gradient, bias_gradient, out_gradient, input_gradient):
    count, inner = conv_gradient.shape[0], out_gradient.shape[0]
    conv_gradient[...] = rows[:count].astype(F32)
    out_gradient[...] = rows[count : count + inner].astype(F32)
    bias_gradient[...] = ends[:1, :inner]
    input_gradient[...] = moved[...]


def call(kernel, name, outs, scratch, flops, *operands):
    outs = [jax.ShapeDtypeStruct(shape, dtype) for shape, dtype in outs]
    moved = sum(x.size * x.dtype.itemsize for x in list(operands) + outs)
    return pl.pallas_call(
        kernel,
        name=name,
        out_shape=outs,
        scratch_shapes=[pltpu.VMEM(shape, dtype) for shape, dtype in scratch],
        cost_estimate=pl.CostEstimate(flops=flops, bytes_accessed=moved, transcendentals=0),
        compiler_params=pltpu.CompilerParams(vmem_limit_bytes=40 * 1024 * 1024),
    )(*operands)


def local(activations, cotangent, conv_weight, conv_bias, out_weight):
    side, channels, inner = activations.shape[1], activations.shape[3], conv_weight.shape[3]
    number = lax.axis_size("row")
    first, second = FIRST_DILATION, SECOND_DILATION
    full, span, near = side + 2 * HALO, side + 2 * second, side + 2 * first
    wide, small = up16(span), up16(near)

    tile = bring(activations[0])
    stored_even = lax.rem(lax.axis_index("row"), 2) == 0
    ends = (activations[0, side - HALO :], activations[0, :HALO])
    got = [bring(jnp.where(stored_even, *ends), 0), bring(jnp.where(stored_even, *ends[::-1]), 1)]
    above, below = around(0, got)

    def columns(turn):
        def chosen(x):
            return jnp.swapaxes(jnp.where(sends_last(1, turn), x[:, side - HALO :], x[:, :HALO]), 0, 1)

        strip = jnp.pad(chosen(tile), ((0, 0), (HALO, HALO), (0, 0)))
        strip = lax.optimization_barrier(strip)
        for row_turn in (0, 1):
            at = jnp.where(sends_last(0, row_turn), HALO + side, 0)
            strip = lax.dynamic_update_slice(strip, chosen(got[row_turn]), (0, at, 0))
        return strip

    strips, late = lax.optimization_barrier(([columns(0), columns(1)], cotangent[0]))
    left, right = around(1, [exchange(strips[turn], 1, turn) for turn in (0, 1)])
    late = bring(late)

    bias_rows = jnp.pad(conv_bias, ((0, 15), (0, channels - inner)))
    packed = jnp.concatenate(
        [jnp.swapaxes(conv_weight[0], 1, 2).reshape(9 * inner, channels), out_weight[0], bias_rows]
    )
    others = lax.ppermute(packed, "segment", [(0, 1), (1, 0)])
    w_first, w_second, v_second, v_first, p_first, p_second, p_back, b_first, b_second = call(
        weights_kernel,
        "weights",
        [
            ((9 * channels, inner), BF16),
            ((9 * channels, 2 * inner), BF16),
            ((18 * inner, 2 * channels), BF16),
            ((9, 2 * inner, channels), BF16),
            ((inner, channels), BF16),
            ((channels, 2 * inner), BF16),
            ((channels, 2 * inner), BF16),
            ((1, inner), F32),
            ((1, 2 * inner), F32),
        ],
        [((2,) + packed.shape, BF16)],
        packed.size,
        *(packed, others),
    )

    own = (tile, above, below, jnp.swapaxes(left, 0, 1), jnp.swapaxes(right, 0, 1))
    area = ((full, LEAD + up16(side + LEAD), channels), F32)
    kept, pre_first = call(
        own_kernel,
        "own_branch",
        [((span + side, span, channels), BF16), ((span, wide, inner), F32)],
        [area, ((full, wide, 2 * channels), BF16), ((full + first, wide, 2 * channels), BF16)],
        span * wide * channels * inner * 400,
        *own,
        *(w_first, b_first, p_first),
    )
    kept = lax.dynamic_update_slice(kept, late, (span, 0, 0))
    other = swap(kept)
    gate_second, hidden_pairs, hidden_last, bottle_second, grad_tile, grad_pre, *strips = call(
        middle_kernel,
        "middle",
        [
            ((near, small, channels), BF16),
            ((span, small, 2 * channels), BF16),
            ((span + second, small, 2 * channels), BF16),
            ((side, small, inner), BF16),
            ((side, small, channels), BF16),
            ((side, small, 2 * inner), BF16),
            ((HALO + first, side, channels), BF16),
            ((HALO + first, side, channels), BF16),
        ],
        [
            ((span, wide, channels), F32),
            ((side, small, channels), F32),
            ((side, small, 2 * inner), F32),
        ],
        24 * side * small * channels * 2 * inner,
        *(kept, other, w_second, b_second, p_second),
    )

    near_pairs, near_last, gate_first, bottle_first = call(
        near_kernel,
        "near",
        [
            ((near, small, 2 * channels), BF16),
            ((near, small, channels), BF16),
            ((near, small, channels), BF16),
            ((side, small, inner), BF16),
        ],
        [area],
        near * small * channels,
        *own,
        pre_first,
    )

    above, below = around(0, [exchange(strips[turn], 0, turn) for turn in (0, 1)])
    rows_second, ends_second = call(
        second_sums_kernel,
        "second_sums",
        [((10 * inner, channels), F32), ((16, channels), F32)],
        [],
        20 * side * small * channels * inner,
        *(grad_pre, hidden_pairs, hidden_last, bottle_second, grad_tile),
    )

    def columns(turn):
        def chosen(x, width):
            return jnp.where(sends_last(1, turn), x[:, side - width : side], x[:, :width])

        grads = jnp.concatenate([chosen(x, HALO) for x in (above[:HALO], grad_pre, below[:HALO])])
        branches = jnp.concatenate([chosen(x, first) for x in (above[HALO:], grad_tile, below[HALO:])])
        branches = jnp.pad(branches, ((second, second), (0, 0), (0, 0)))
        return jnp.swapaxes(jnp.concatenate([grads, branches], axis=1), 0, 1)

    left, right = around(1, [exchange(columns(turn), 1, turn) for turn in (0, 1)])
    left, right = jnp.swapaxes(left, 0, 1), jnp.swapaxes(right, 0, 1)

    devices = number * number
    share = -(-10 * inner // (8 * devices)) * 8
    keep, away, windows, grad_first = call(
        backward_kernel,
        "backward",
        [
            ((10 * inner + 16, channels), F32),
            ((10 * inner + 16, channels), BF16),
            ((3, near, small, channels), BF16),
            ((side, side, channels), BF16),
        ],
        [
            ((full, LEAD + up16(side + HALO + first), channels), F32),
            ((full, small, 2 * channels), BF16),
            ((full, small, channels), BF16),
            ((near, small + 16, channels), F32),
            ((near, small + 16, channels), F32),
            ((10 * inner, channels), F32),
            ((16, channels), F32),
        ],
        36 * near * small * channels * channels,
        *(grad_pre, grad_tile, above, below, left[:, :HALO], right[:, :HALO]),
        *(left[second : second + near, HALO:], right[second : second + near, HALO:]),
        *(gate_second, gate_first, near_pairs, near_last, bottle_first, v_second, p_back, rows_second, ends_second),
    )

    (input_gradient,) = call(
        input_kernel,
        "input",
        [((side, side, channels), BF16)],
        [],
        18 * side * small * channels * channels,
        *(windows, grad_first, tile, v_first),
    )
    other = lax.ppermute(away, "segment", [(0, 1), (1, 0)])
    other, input_gradient = lax.optimization_barrier((other, input_gradient))
    (parts,) = call(
        pair_kernel,
        "pair",
        [((devices, share + 8, channels), BF16)],
        [],
        keep.size,
        *(keep, other),
    )
    parts = lax.all_to_all(parts, GRID, 0, 0, tiled=True)
    input_gradient = take_back(input_gradient)
    cells = lax.axis_size("segment") * (side * number) * (side * number)
    rows, ends = call(
        functools.partial(total_kernel, float(cells) ** -0.5),
        "total",
        [((devices, share, channels), BF16), ((8, channels), F32)],
        [],
        parts.size,
        parts,
    )
    rows = lax.all_to_all(rows, GRID, 0, 0, tiled=True).reshape(devices * share, channels)
    conv_gradient, bias_gradient, out_gradient, input_gradient = call(
        outputs_kernel,
        "outputs",
        [
            ((9 * inner, channels), F32),
            ((1, inner), F32),
            ((inner, channels), F32),
            ((side, side, channels), BF16),
        ],
        [],
        rows.size,
        *(rows, ends, input_gradient),
    )
    conv_gradient = jnp.swapaxes(conv_gradient.reshape(1, 9, inner, channels), 2, 3)
    return (input_gradient[None], conv_gradient, bias_gradient, out_gradient[None])


def solution(mesh):
    in_specs = (
        P("segment", "row", "col", None),
        P("segment", "row", "col", None),
        P("segment", None, None, None),
        P("segment", None),
        P("segment", None, None),
    )
    out_specs = (
        P("segment", "row", "col", None),
        P("segment", None, None, None),
        P("segment", None),
        P("segment", None, None),
    )
    return jax.shard_map(local, mesh=mesh, in_specs=in_specs, out_specs=out_specs, check_vma=False)
```

```python
import functools

import jax
import jax.numpy as jnp
from jax import lax
from jax.experimental import pallas as pl
from jax.experimental.pallas import tpu as pltpu
from jax.sharding import PartitionSpec as P

FIRST_DILATION = 2
SECOND_DILATION = 8
HALO = FIRST_DILATION + SECOND_DILATION
GRID = ("row", "col")
ALL = ("segment",) + GRID
ORDER = [0, 1, 3, 4, 6, 7, 2, 5, 8]
TAPS = [(a, b) for a in (-1, 0, 1) for b in (-1, 0, 1)]
LEAD = 16
F32, BF16 = jnp.float32, jnp.bfloat16


def tap(a, b):
    return 3 * (a + 1) + (b + 1)


def dot(x, y):
    return jnp.dot(x, y, preferred_element_type=F32)


def rounded(x):
    return x.astype(BF16).astype(F32)


def up16(n):
    return -(-n // 16) * 16


def home(batch, r, c):
    number = lax.axis_size("row")
    core, row, col = (batch, r, c) if r == c else (int(r > c), r, c)
    if r != c and (r < c) == (batch == 1):
        row, col = c, r
    return (core * number + row) * number + col


def place():
    row, col = lax.axis_index("row"), lax.axis_index("col")
    low, high = jnp.minimum(row, col), jnp.maximum(row, col)
    upper = lax.axis_index("segment") == 0
    return jnp.where(upper, low, high), jnp.where(upper, high, low)


def permute(x, pair):
    number = lax.axis_size("row")
    tiles = [(m, r, c) for m in range(lax.axis_size("segment")) for r in range(number) for c in range(number)]
    pairs = [pair(*tile) for tile in tiles]
    return lax.ppermute(x, ALL, [found for found in pairs if found is not None])


def stored(batch, r, c):
    number = lax.axis_size("row")
    return (batch * number + r) * number + c


def bring(x, turn=None):
    def pair(batch, r, c):
        row = r if turn is None else partner(r, turn)
        if row is not None:
            return stored(batch, r, c), home(batch, row, c)

    return permute(x, pair)


def take_back(x):
    return permute(x, lambda m, r, c: (home(m, r, c), stored(m, r, c)))


def swap(x):
    return permute(x, lambda m, r, c: (home(m, r, c), home(m, c, r)))


def partner(index, turn):
    other = index + 1 if (index + turn) % 2 == 0 else index - 1
    return other if 0 <= other < lax.axis_size("row") else None


def exchange(x, axis, turn):
    def pair(batch, r, c):
        other = partner(c if axis else r, turn)
        if other is not None:
            return home(batch, r, c), home(batch, r, other) if axis else home(batch, other, c)

    return permute(x, pair)


def sends_last(axis, turn):
    return lax.rem(place()[axis] + turn, 2) == 0


def around(axis, got):
    even = sends_last(axis, 0)
    return jnp.where(even, got[1], got[0]), jnp.where(even, got[0], got[1])


def inside(shape, side, width, top):
    number = lax.axis_size("row") * side
    rows = lax.broadcasted_iota(jnp.int32, shape, 0) + top - width
    cols = lax.broadcasted_iota(jnp.int32, shape, 1) - width
    row, col = place()
    at_row = row * side + rows
    at_col = col * side + cols
    return (at_row >= 0) & (at_row < number) & (at_col >= 0) & (at_col < number) & (cols < side + width)


def paired(source, starts, width, dilation, pairs, last, change):
    lanes = source.shape[2]
    low, high = slice(0, lanes), slice(lanes, 2 * lanes)

    def step(k, _):
        rows, lower = pl.ds(4 * k, 4), pl.ds(4 * k + dilation, 4)
        window = [change(source[rows, at : at + width]).astype(BF16) for at in starts]
        pairs[rows, :, low] = window[0]
        pairs[rows, :, high] = window[1]
        last[lower, :, low] = window[2]
        last[rows, :, high] = window[2]
        return 0

    lax.fori_loop(0, source.shape[0] // 4, step, 0, unroll=True)


def taps_sum(pairs, last, top, rows, dilation, weights):
    width, lanes = pairs.shape[1], pairs.shape[2] // 2
    size = rows * width
    total = None
    for k in range(5):
        if k < 3:
            window = pairs[pl.ds(top + dilation * k, rows)]
        elif k == 3:
            window = last[pl.ds(top + dilation, rows)]
        else:
            window = last[pl.ds(top + 3 * dilation, rows), :, :lanes]
        weight = weights[2 * lanes * k : min(2 * lanes * (k + 1), 9 * lanes)]
        term = dot(window.reshape(size, window.shape[2]), weight)
        total = term if total is None else total + term
    return total


def positive(x):
    return jnp.maximum(x, 0)


def assemble(area, tile, above, below, left, right):
    side = tile.shape[0]
    full, wide, channels = area.shape
    middle = slice(LEAD, LEAD + side)
    area[:, :LEAD] = jnp.zeros((full, LEAD, channels), F32)
    area[:, LEAD + side :] = jnp.zeros((full, wide - LEAD - side, channels), F32)
    area[HALO : HALO + side, middle] = tile
    area[:HALO, middle] = above[:HALO].astype(F32)
    area[HALO + side :, middle] = below[:HALO].astype(F32)
    area[:, LEAD - HALO : LEAD] = left[...].astype(F32)
    area[:, LEAD + side : LEAD + side + HALO] = right[...].astype(F32)


def first_branch(area, pairs, last, weights, bias, proj, store):
    full, wide = pairs.shape[:2]
    start = LEAD - SECOND_DILATION
    starts = [start + FIRST_DILATION * b for b in (-1, 0, 1)]
    paired(area, starts, wide, FIRST_DILATION, pairs, last, positive)

    def rows(step, _):
        top = step * 8
        pre = taps_sum(pairs, last, top, 8, FIRST_DILATION, weights) + bias[...]
        branch = dot(positive(pre).astype(BF16), proj[...])
        inputs = area[pl.ds(top + FIRST_DILATION, 8), start : start + wide]
        branch = rounded(inputs + branch.reshape(inputs.shape))
        store(top, pre.reshape(8, wide, pre.shape[1]), branch)
        return 0

    lax.fori_loop(0, (full - 2 * FIRST_DILATION) // 8, rows, 0, unroll=True)


def own_kernel(
    tile, above, below, left, right, weights, bias, proj,
    swapped, pre,
    area, pairs, last,
):
    side, span = tile.shape[0], pre.shape[0]
    assemble(area, tile[...].astype(F32), above, below, left, right)

    def store(top, pre_act, branch):
        pre[pl.ds(top, 8)] = pre_act
        swapped[pl.ds(top, 8)] = branch[:, :span].astype(BF16)

    first_branch(area, pairs, last, weights, bias, proj, store)
    swapped[span:] = jnp.zeros((side, span, swapped.shape[2]), BF16)


def near_kernel(tile, above, below, left, right, pre, hidden_pairs, hidden_last, gate_first, bottle_first, area):
    side, channels, inner = tile.shape[0], tile.shape[2], pre.shape[2]
    first, second = FIRST_DILATION, SECOND_DILATION
    near, small = gate_first.shape[:2]
    assemble(area, tile[...].astype(F32), above, below, left, right)
    for b in (-1, 0, 1):
        at = LEAD + first * b
        window = positive(area[HALO - first : HALO + side + first, at : at + small]).astype(BF16)
        if b < 1:
            hidden_pairs[:, :, (b + 1) * channels : (b + 2) * channels] = window
        else:
            hidden_last[...] = window
    edge = second - first
    part = pre[edge : edge + near, edge : edge + small]
    alive = (part > 0) & inside(part.shape, side, first, 0)
    gate_first[:, :, :inner] = jnp.where(alive, 1.0, 0.0).astype(BF16)
    gate_first[:, :, inner:] = jnp.zeros((near, small, gate_first.shape[2] - inner), BF16)
    bottle_first[...] = positive(pre[second : second + side, second : second + small]).astype(BF16)


def middle_kernel(
    kept, other, w_second, b_second, p_second,
    gate_second, hidden_pairs, hidden_last, bottle_second, grad_tile, grad_pre, first_turn, second_turn,
    current, padded, pre_second,
):
    side, channels, span = first_turn.shape[1], kept.shape[2], kept.shape[1]
    first, second, inner = FIRST_DILATION, SECOND_DILATION, bottle_second.shape[2]
    near, small = gate_second.shape[:2]
    turned = jnp.swapaxes(other[:span].astype(F32), 0, 1)
    sym = rounded((kept[:span].astype(F32) + turned) * 0.5)
    current[:, :span] = jnp.where(inside(sym.shape, side, second, 0), sym, 0)
    current[:, span:] = jnp.zeros((span, current.shape[1] - span, channels), F32)
    edge = second - first
    part = current[edge : edge + near, edge : edge + small]
    gate_second[...] = jnp.where(part > 0, 1.0, 0.0).astype(BF16)
    paired(current, [0, second, 2 * second], small, second, hidden_pairs, hidden_last, positive)

    def rows(step, _):
        top = step * 8
        total = taps_sum(hidden_pairs, hidden_last, top, 8, second, w_second) + b_second[...]
        pre_second[pl.ds(top, 8)] = total.reshape(8, small, total.shape[1])
        return 0

    lax.fori_loop(0, side // 8, rows, 0, unroll=True)
    bottle_second[...] = positive(pre_second[:, :, :inner]).astype(BF16)

    turned = jnp.swapaxes(other[span:, :side].astype(F32), 0, 1)
    padded[:, side:] = jnp.zeros((side, small - side, channels), F32)
    padded[:, :side] = rounded((kept[span:, :side].astype(F32) + turned) * 0.5)
    branch = padded[...].astype(BF16)
    grad_tile[...] = branch
    grad = dot(branch.reshape(side * small, channels), p_second[...]).reshape(side, small, 2 * inner)
    grad = jnp.where(pre_second[...] > 0, grad, 0)
    grad_pre[...] = grad.astype(BF16)
    even = sends_last(0, 0)
    for rows, value, width in ((slice(0, HALO), grad, HALO), (slice(HALO, HALO + first), padded[...], first)):
        head, tail = value[:width, :side], value[side - width :, :side]
        first_turn[rows] = jnp.where(even, tail, head).astype(BF16)
        second_turn[rows] = jnp.where(even, head, tail).astype(BF16)


def weight_sums(rows, ends, grad_pre, hidden, bottle, grad_tile):
    side, small, lanes = grad_pre.shape
    inner = bottle.shape[2]
    size = side * small
    flat = grad_pre.reshape(size, lanes)
    turned = flat.T[:inner].astype(BF16)
    for a in range(3):
        b = 0
        while b < 3:
            window = hidden(a, b)
            grads = dot(turned, window.reshape(size, window.shape[2]))
            for at in range(0, window.shape[2], grad_tile.shape[2]):
                rows[(3 * a + b) * inner : (3 * a + b + 1) * inner] = grads[:, at : at + grad_tile.shape[2]]
                b += 1
    turned = bottle[...].reshape(size, inner).astype(F32).T.astype(BF16)
    rows[9 * inner : 10 * inner] = dot(turned, grad_tile.reshape(size, grad_tile.shape[2]))
    ends[...] = jnp.zeros(ends.shape, F32)
    ends[:, :lanes] = jnp.broadcast_to(jnp.sum(flat, axis=0, keepdims=True), (ends.shape[0], lanes))


def weights_kernel(
    mine, theirs, w_first, w_second, v_second, v_first, p_first, p_second, p_back, b_first, b_second, packed
):
    inner, channels = p_first.shape
    section = lax.axis_index("segment")
    packed[section] = mine[...]
    packed[1 - section] = theirs[...]

    def conv(section, k):
        return packed[section, k * inner : (k + 1) * inner]

    def turned(x):
        return x.astype(F32).T.astype(BF16)

    zero = jnp.zeros((inner, channels), BF16)
    for at, k in enumerate(ORDER):
        here = slice(at * channels, (at + 1) * channels)
        own, other = conv(1, k), conv(1, 3 * (k % 3) + k // 3)
        w_first[here] = turned(conv(0, k))
        w_second[here] = turned(jnp.concatenate([own, other], axis=0))
        upper, lower = (slice((2 * k + half) * inner, (2 * k + half + 1) * inner) for half in (0, 1))
        v_second[upper, :channels], v_second[upper, channels:] = own, zero
        v_second[lower, :channels], v_second[lower, channels:] = zero, other
        v_first[k, :inner], v_first[k, inner:] = conv(0, k), zero
    p_first[...] = conv(0, 9)
    p_second[...] = turned(jnp.concatenate([conv(1, 9), conv(1, 9)], axis=0))
    p_back[...] = turned(jnp.concatenate([conv(0, 9), zero], axis=0))
    b_first[...] = packed[0, 10 * inner :].astype(F32)[:1, :inner]
    bias = packed[1, 10 * inner :].astype(F32)[:1, :inner]
    b_second[...] = jnp.concatenate([bias, bias], axis=1)


def second_sums_kernel(grad_pre, pairs, last, bottle, grad_tile, rows, ends):
    side = grad_pre.shape[0]
    channels = grad_tile.shape[2]

    def hidden(a, b):
        top = SECOND_DILATION * a
        if b == 0:
            return pairs[top : top + side]
        return last[top + SECOND_DILATION : top + SECOND_DILATION + side, :, :channels]

    weight_sums(rows, ends, grad_pre[...].astype(F32), hidden, bottle, grad_tile[...])


def backward_kernel(
    grad_pre, grad_tile, above, below, left, right, left_branch, right_branch, gate_second, gate_first, near_pairs,
    near_last, bottle_first, v_second, p_first, rows_second, ends_second,
    keep, away, windows, grad_first,
    area, pairs, last, branch, grads, rows, ends,
):
    side, channels = grad_first.shape[0], grad_first.shape[2]
    first, second = FIRST_DILATION, SECOND_DILATION
    full, near = side + 2 * HALO, side + 2 * first
    small = grad_pre.shape[1]
    middle = slice(LEAD, LEAD + side)

    area[:, :LEAD] = jnp.zeros((full, LEAD, channels), F32)
    area[:, LEAD + side :] = jnp.zeros((full, area.shape[1] - LEAD - side, channels), F32)
    area[HALO : HALO + side, LEAD : LEAD + small] = grad_pre[...].astype(F32)
    area[:HALO, middle] = above[:HALO].astype(F32)
    area[HALO + side :, middle] = below[:HALO].astype(F32)
    area[:, LEAD - HALO : LEAD] = left[...].astype(F32)
    area[:, LEAD + side : LEAD + side + HALO] = right[...].astype(F32)
    branch[...] = jnp.zeros(branch.shape, F32)
    branch[first : first + side, first : first + side] = grad_tile[:, :side].astype(F32)
    branch[:first, first : first + side] = above[HALO:].astype(F32)
    branch[first + side :, first : first + side] = below[HALO:].astype(F32)
    branch[:, :first] = left_branch[...].astype(F32)
    branch[:, first + side : near] = right_branch[...].astype(F32)
    for b in (-1, 0, 1):
        at = LEAD - HALO + second * (1 - b)
        window = area[:, at : at + small].astype(BF16)
        if b < 1:
            pairs[:, :, (b + 1) * channels : (b + 2) * channels] = window
        else:
            last[...] = window
    grads[:, small:] = jnp.zeros((near, grads.shape[1] - small, channels), F32)

    def sections(step, _):
        top = step * 7
        size = 7 * small
        total = None
        for a in (-1, 0, 1):
            rows_of = pl.ds(top + second * (1 - a), 7)
            at = 3 * (a + 1) * channels
            term = dot(pairs[rows_of].reshape(size, 2 * channels), v_second[at : at + 2 * channels])
            total = term if total is None else total + term
            total = total + dot(last[rows_of].reshape(size, channels), v_second[at + 2 * channels : at + 3 * channels])
        here = pl.ds(top, 7)
        grad = branch[here, :small].reshape(size, channels)
        gate = gate_second[here].astype(F32).reshape(size, channels) > 0
        own = rounded(grad + jnp.where(gate, total[:, :channels], 0))
        other = rounded(grad + jnp.where(gate, total[:, channels:], 0))
        grad = ((own + other) * 0.5).astype(BF16)
        branch[here, :small] = grad.astype(F32).reshape(7, small, channels)
        gate = gate_first[here].astype(F32).reshape(size, channels) > 0
        grad = rounded(jnp.where(gate, dot(grad, p_first[...]), 0))
        grads[here, :small] = grad.reshape(7, small, channels)
        return 0

    lax.fori_loop(0, near // 7, sections, 0, unroll=True)
    for b in (-1, 0, 1):
        at = first * (1 - b)
        windows[b + 1] = grads[:, at : at + small].astype(BF16)
    part = branch[first : first + side, first : first + small]
    grad_first[...] = part[:, :side].astype(BF16)
    real = lax.broadcasted_iota(jnp.int32, part.shape, 1) < side
    part = jnp.where(real, part, 0).astype(BF16)
    grad = jnp.where(real, grads[first : first + side, first : first + small], 0)

    def hidden(a, b):
        return (near_last if b else near_pairs)[first * a : first * a + side]

    weight_sums(rows, ends, grad, hidden, bottle_first, part)

    first_core = lax.axis_index("segment") == 0
    count = rows.shape[0]
    for here, one, two in (
        (slice(0, count), rows[...], rows_second[...]),
        (slice(count, count + ends.shape[0]), ends[...], ends_second[...]),
    ):
        keep[here] = jnp.where(first_core, one, two)
        away[here] = jnp.where(first_core, two, one).astype(BF16)


def pair_kernel(keep, other, parts):
    devices, share = parts.shape[0], parts.shape[1] - 8
    total = keep[...] + other[...].astype(F32)
    count = keep.shape[0] - 16
    for j in range(devices):
        low, high = min(j * share, count), min((j + 1) * share, count)
        pieces = [total[low:high]] if low < high else []
        if high - low < share:
            pieces.append(jnp.zeros((share - (high - low), keep.shape[1]), F32))
        parts[j] = jnp.concatenate(pieces + [total[count : count + 8]]).astype(BF16)


def input_kernel(windows, grad_first, tile, v_first, out):
    side, channels = out.shape[0], out.shape[2]
    small = windows.shape[2]
    first = FIRST_DILATION

    def rows(step, _):
        top = step * 8
        total = jnp.zeros((8 * small, channels), F32)
        for a, b in TAPS:
            window = windows[b + 1, pl.ds(top + first * (1 - a), 8)].reshape(8 * small, channels)
            total = total + dot(window, v_first[tap(a, b)])
        here = pl.ds(top, 8)
        total = total.reshape(8, small, channels)[:, :side]
        total = jnp.where(tile[here].astype(F32) > 0, total, 0)
        out[here] = (grad_first[here].astype(F32) + total).astype(BF16)
        return 0

    lax.fori_loop(0, side // 8, rows, 0, unroll=True)


def total_kernel(scale, parts, rows, ends):
    share = rows.shape[1]
    total = jnp.sum(parts[...].astype(F32), axis=0) * scale
    rows[...] = jnp.broadcast_to(total[:share].astype(BF16)[None], rows.shape)
    ends[...] = total[share:]


def landed_kernel(moved, input_gradient):
    input_gradient[...] = moved[...]


def outputs_kernel(rows, ends, conv_gradient, bias_gradient, out_gradient):
    count, inner = conv_gradient.shape[0], out_gradient.shape[0]
    conv_gradient[...] = rows[:count].astype(F32)
    out_gradient[...] = rows[count : count + inner].astype(F32)
    bias_gradient[...] = ends[:1, :inner]


def call(kernel, name, outs, scratch, flops, *operands):
    outs = [jax.ShapeDtypeStruct(shape, dtype) for shape, dtype in outs]
    moved = sum(x.size * x.dtype.itemsize for x in list(operands) + outs)
    return pl.pallas_call(
        kernel,
        name=name,
        out_shape=outs,
        scratch_shapes=[pltpu.VMEM(shape, dtype) for shape, dtype in scratch],
        cost_estimate=pl.CostEstimate(flops=flops, bytes_accessed=moved, transcendentals=0),
        compiler_params=pltpu.CompilerParams(vmem_limit_bytes=40 * 1024 * 1024),
    )(*operands)


def local(activations, cotangent, conv_weight, conv_bias, out_weight):
    side, channels, inner = activations.shape[1], activations.shape[3], conv_weight.shape[3]
    number = lax.axis_size("row")
    first, second = FIRST_DILATION, SECOND_DILATION
    full, span, near = side + 2 * HALO, side + 2 * second, side + 2 * first
    wide, small = up16(span), up16(near)

    tile = bring(activations[0])
    stored_even = lax.rem(lax.axis_index("row"), 2) == 0
    ends = (activations[0, side - HALO :], activations[0, :HALO])
    got = [bring(jnp.where(stored_even, *ends), 0), bring(jnp.where(stored_even, *ends[::-1]), 1)]
    above, below = around(0, got)

    def columns(turn):
        def chosen(x):
            return jnp.swapaxes(jnp.where(sends_last(1, turn), x[:, side - HALO :], x[:, :HALO]), 0, 1)

        strip = jnp.pad(chosen(tile), ((0, 0), (HALO, HALO), (0, 0)))
        strip = lax.optimization_barrier(strip)
        for row_turn in (0, 1):
            at = jnp.where(sends_last(0, row_turn), HALO + side, 0)
            strip = lax.dynamic_update_slice(strip, chosen(got[row_turn]), (0, at, 0))
        return strip

    strips, late = lax.optimization_barrier(([columns(0), columns(1)], cotangent[0]))
    left, right = around(1, [exchange(strips[turn], 1, turn) for turn in (0, 1)])
    late = bring(late)

    bias_rows = jnp.pad(conv_bias, ((0, 15), (0, channels - inner)))
    packed = jnp.concatenate(
        [jnp.swapaxes(conv_weight[0], 1, 2).reshape(9 * inner, channels), out_weight[0], bias_rows]
    )
    others = lax.ppermute(packed, "segment", [(0, 1), (1, 0)])
    w_first, w_second, v_second, v_first, p_first, p_second, p_back, b_first, b_second = call(
        weights_kernel,
        "weights",
        [
            ((9 * channels, inner), BF16),
            ((9 * channels, 2 * inner), BF16),
            ((18 * inner, 2 * channels), BF16),
            ((9, 2 * inner, channels), BF16),
            ((inner, channels), BF16),
            ((channels, 2 * inner), BF16),
            ((channels, 2 * inner), BF16),
            ((1, inner), F32),
            ((1, 2 * inner), F32),
        ],
        [((2,) + packed.shape, BF16)],
        packed.size,
        *(packed, others),
    )

    own = (tile, above, below, jnp.swapaxes(left, 0, 1), jnp.swapaxes(right, 0, 1))
    area = ((full, LEAD + up16(side + LEAD), channels), F32)
    kept, pre_first = call(
        own_kernel,
        "own_branch",
        [((span + side, span, channels), BF16), ((span, wide, inner), F32)],
        [area, ((full, wide, 2 * channels), BF16), ((full + first, wide, 2 * channels), BF16)],
        span * wide * channels * inner * 400,
        *own,
        *(w_first, b_first, p_first),
    )
    kept = lax.dynamic_update_slice(kept, late, (span, 0, 0))
    other = swap(kept)
    gate_second, hidden_pairs, hidden_last, bottle_second, grad_tile, grad_pre, *strips = call(
        middle_kernel,
        "middle",
        [
            ((near, small, channels), BF16),
            ((span, small, 2 * channels), BF16),
            ((span + second, small, 2 * channels), BF16),
            ((side, small, inner), BF16),
            ((side, small, channels), BF16),
            ((side, small, 2 * inner), BF16),
            ((HALO + first, side, channels), BF16),
            ((HALO + first, side, channels), BF16),
        ],
        [
            ((span, wide, channels), F32),
            ((side, small, channels), F32),
            ((side, small, 2 * inner), F32),
        ],
        24 * side * small * channels * 2 * inner,
        *(kept, other, w_second, b_second, p_second),
    )

    near_pairs, near_last, gate_first, bottle_first = call(
        near_kernel,
        "near",
        [
            ((near, small, 2 * channels), BF16),
            ((near, small, channels), BF16),
            ((near, small, channels), BF16),
            ((side, small, inner), BF16),
        ],
        [area],
        near * small * channels,
        *own,
        pre_first,
    )

    above, below = around(0, [exchange(strips[turn], 0, turn) for turn in (0, 1)])
    rows_second, ends_second = call(
        second_sums_kernel,
        "second_sums",
        [((10 * inner, channels), F32), ((16, channels), F32)],
        [],
        20 * side * small * channels * inner,
        *(grad_pre, hidden_pairs, hidden_last, bottle_second, grad_tile),
    )

    def columns(turn):
        def chosen(x, width):
            return jnp.where(sends_last(1, turn), x[:, side - width : side], x[:, :width])

        grads = jnp.concatenate([chosen(x, HALO) for x in (above[:HALO], grad_pre, below[:HALO])])
        branches = jnp.concatenate([chosen(x, first) for x in (above[HALO:], grad_tile, below[HALO:])])
        branches = jnp.pad(branches, ((second, second), (0, 0), (0, 0)))
        return jnp.swapaxes(jnp.concatenate([grads, branches], axis=1), 0, 1)

    left, right = around(1, [exchange(columns(turn), 1, turn) for turn in (0, 1)])
    left, right = jnp.swapaxes(left, 0, 1), jnp.swapaxes(right, 0, 1)

    devices = number * number
    share = -(-10 * inner // (8 * devices)) * 8
    keep, away, windows, grad_first = call(
        backward_kernel,
        "backward",
        [
            ((10 * inner + 16, channels), F32),
            ((10 * inner + 16, channels), BF16),
            ((3, near, small, channels), BF16),
            ((side, side, channels), BF16),
        ],
        [
            ((full, LEAD + up16(side + HALO + first), channels), F32),
            ((full, small, 2 * channels), BF16),
            ((full, small, channels), BF16),
            ((near, small + 16, channels), F32),
            ((near, small + 16, channels), F32),
            ((10 * inner, channels), F32),
            ((16, channels), F32),
        ],
        36 * near * small * channels * channels,
        *(grad_pre, grad_tile, above, below, left[:, :HALO], right[:, :HALO]),
        *(left[second : second + near, HALO:], right[second : second + near, HALO:]),
        *(gate_second, gate_first, near_pairs, near_last, bottle_first, v_second, p_back, rows_second, ends_second),
    )

    (input_gradient,) = call(
        input_kernel,
        "input",
        [((side, side, channels), BF16)],
        [],
        18 * side * small * channels * channels,
        *(windows, grad_first, tile, v_first),
    )
    other = lax.ppermute(away, "segment", [(0, 1), (1, 0)])
    other, input_gradient = lax.optimization_barrier((other, input_gradient))
    (parts,) = call(
        pair_kernel,
        "pair",
        [((devices, share + 8, channels), BF16)],
        [],
        keep.size,
        *(keep, other),
    )
    parts = lax.all_to_all(parts, GRID, 0, 0, tiled=True)
    input_gradient = take_back(input_gradient)
    cells = lax.axis_size("segment") * (side * number) * (side * number)
    rows, ends = call(
        functools.partial(total_kernel, float(cells) ** -0.5),
        "total",
        [((devices, share, channels), BF16), ((8, channels), F32)],
        [],
        parts.size,
        parts,
    )
    rows = lax.all_to_all(rows, GRID, 0, 0, tiled=True).reshape(devices * share, channels)
    (input_gradient,) = call(
        landed_kernel, "landed", [((side, side, channels), BF16)], [], side**2 * channels * 400000, input_gradient
    )
    rows, input_gradient = lax.optimization_barrier((rows, input_gradient))
    conv_gradient, bias_gradient, out_gradient = call(
        outputs_kernel,
        "outputs",
        [((9 * inner, channels), F32), ((1, inner), F32), ((inner, channels), F32)],
        [],
        rows.size,
        *(rows, ends),
    )
    conv_gradient = jnp.swapaxes(conv_gradient.reshape(1, 9, inner, channels), 2, 3)
    return (input_gradient[None], conv_gradient, bias_gradient, out_gradient[None])


def solution(mesh):
    in_specs = (
        P("segment", "row", "col", None),
        P("segment", "row", "col", None),
        P("segment", None, None, None),
        P("segment", None),
        P("segment", None, None),
    )
    out_specs = (
        P("segment", "row", "col", None),
        P("segment", None, None, None),
        P("segment", None),
        P("segment", None, None),
    )
    return jax.shard_map(local, mesh=mesh, in_specs=in_specs, out_specs=out_specs, check_vma=False)
```

```python
import functools

import jax
import jax.numpy as jnp
from jax import lax
from jax.experimental import pallas as pl
from jax.experimental.pallas import tpu as pltpu
from jax.sharding import PartitionSpec as P

FIRST_DILATION = 2
SECOND_DILATION = 8
HALO = FIRST_DILATION + SECOND_DILATION
GRID = ("row", "col")
ALL = ("segment",) + GRID
ORDER = [0, 1, 3, 4, 6, 7, 2, 5, 8]
TAPS = [(a, b) for a in (-1, 0, 1) for b in (-1, 0, 1)]
LEAD = 16
F32, BF16 = jnp.float32, jnp.bfloat16


def tap(a, b):
    return 3 * (a + 1) + (b + 1)


def dot(x, y):
    return jnp.dot(x, y, preferred_element_type=F32)


def rounded(x):
    return x.astype(BF16).astype(F32)


def up16(n):
    return -(-n // 16) * 16


def home(batch, r, c):
    number = lax.axis_size("row")
    core, row, col = (batch, r, c) if r == c else (int(r > c), r, c)
    if r != c and (r < c) == (batch == 1):
        row, col = c, r
    return (core * number + row) * number + col


def place():
    row, col = lax.axis_index("row"), lax.axis_index("col")
    low, high = jnp.minimum(row, col), jnp.maximum(row, col)
    upper = lax.axis_index("segment") == 0
    return jnp.where(upper, low, high), jnp.where(upper, high, low)


def permute(x, pair):
    number = lax.axis_size("row")
    tiles = [(m, r, c) for m in range(lax.axis_size("segment")) for r in range(number) for c in range(number)]
    pairs = [pair(*tile) for tile in tiles]
    return lax.ppermute(x, ALL, [found for found in pairs if found is not None])


def stored(batch, r, c):
    number = lax.axis_size("row")
    return (batch * number + r) * number + c


def bring(x, turn=None):
    def pair(batch, r, c):
        row = r if turn is None else partner(r, turn)
        if row is not None:
            return stored(batch, r, c), home(batch, row, c)

    return permute(x, pair)


def take_back(x):
    return permute(x, lambda m, r, c: (home(m, r, c), stored(m, r, c)))


def swap(x):
    return permute(x, lambda m, r, c: (home(m, r, c), home(m, c, r)))


def partner(index, turn):
    other = index + 1 if (index + turn) % 2 == 0 else index - 1
    return other if 0 <= other < lax.axis_size("row") else None


def exchange(x, axis, turn):
    def pair(batch, r, c):
        other = partner(c if axis else r, turn)
        if other is not None:
            return home(batch, r, c), home(batch, r, other) if axis else home(batch, other, c)

    return permute(x, pair)


def sends_last(axis, turn):
    return lax.rem(place()[axis] + turn, 2) == 0


def around(axis, got):
    even = sends_last(axis, 0)
    return jnp.where(even, got[1], got[0]), jnp.where(even, got[0], got[1])


def inside(shape, side, width, top):
    number = lax.axis_size("row") * side
    rows = lax.broadcasted_iota(jnp.int32, shape, 0) + top - width
    cols = lax.broadcasted_iota(jnp.int32, shape, 1) - width
    row, col = place()
    at_row = row * side + rows
    at_col = col * side + cols
    return (at_row >= 0) & (at_row < number) & (at_col >= 0) & (at_col < number) & (cols < side + width)


def paired(source, starts, width, dilation, pairs, last, change):
    lanes = source.shape[2]
    low, high = slice(0, lanes), slice(lanes, 2 * lanes)

    def step(k, _):
        rows, lower = pl.ds(4 * k, 4), pl.ds(4 * k + dilation, 4)
        window = [change(source[rows, at : at + width]).astype(BF16) for at in starts]
        pairs[rows, :, low] = window[0]
        pairs[rows, :, high] = window[1]
        last[lower, :, low] = window[2]
        last[rows, :, high] = window[2]
        return 0

    lax.fori_loop(0, source.shape[0] // 4, step, 0, unroll=True)


def taps_sum(pairs, last, top, rows, dilation, weights):
    width, lanes = pairs.shape[1], pairs.shape[2] // 2
    size = rows * width
    total = None
    for k in range(5):
        if k < 3:
            window = pairs[pl.ds(top + dilation * k, rows)]
        elif k == 3:
            window = last[pl.ds(top + dilation, rows)]
        else:
            window = last[pl.ds(top + 3 * dilation, rows), :, :lanes]
        weight = weights[2 * lanes * k : min(2 * lanes * (k + 1), 9 * lanes)]
        term = dot(window.reshape(size, window.shape[2]), weight)
        total = term if total is None else total + term
    return total


def positive(x):
    return jnp.maximum(x, 0)


def assemble(area, tile, above, below, left, right):
    side = tile.shape[0]
    full, wide, channels = area.shape
    middle = slice(LEAD, LEAD + side)
    area[:, :LEAD] = jnp.zeros((full, LEAD, channels), F32)
    area[:, LEAD + side :] = jnp.zeros((full, wide - LEAD - side, channels), F32)
    area[HALO : HALO + side, middle] = tile
    area[:HALO, middle] = above[:HALO].astype(F32)
    area[HALO + side :, middle] = below[:HALO].astype(F32)
    area[:, LEAD - HALO : LEAD] = left[...].astype(F32)
    area[:, LEAD + side : LEAD + side + HALO] = right[...].astype(F32)


def first_branch(area, pairs, last, weights, bias, proj, store):
    full, wide = pairs.shape[:2]
    start = LEAD - SECOND_DILATION
    starts = [start + FIRST_DILATION * b for b in (-1, 0, 1)]
    paired(area, starts, wide, FIRST_DILATION, pairs, last, positive)

    def rows(step, _):
        top = step * 8
        pre = taps_sum(pairs, last, top, 8, FIRST_DILATION, weights) + bias[...]
        branch = dot(positive(pre).astype(BF16), proj[...])
        inputs = area[pl.ds(top + FIRST_DILATION, 8), start : start + wide]
        branch = rounded(inputs + branch.reshape(inputs.shape))
        store(top, pre.reshape(8, wide, pre.shape[1]), branch)
        return 0

    lax.fori_loop(0, (full - 2 * FIRST_DILATION) // 8, rows, 0, unroll=True)


def own_kernel(
    tile, above, below, left, right, weights, bias, proj,
    swapped, pre,
    area, pairs, last,
):
    side, span = tile.shape[0], pre.shape[0]
    assemble(area, tile[...].astype(F32), above, below, left, right)

    def store(top, pre_act, branch):
        pre[pl.ds(top, 8)] = pre_act
        swapped[pl.ds(top, 8)] = branch[:, :span].astype(BF16)

    first_branch(area, pairs, last, weights, bias, proj, store)
    swapped[span:] = jnp.zeros((side, span, swapped.shape[2]), BF16)


def near_kernel(tile, above, below, left, right, pre, hidden_pairs, hidden_last, gate_first, bottle_first, area):
    side, channels, inner = tile.shape[0], tile.shape[2], pre.shape[2]
    first, second = FIRST_DILATION, SECOND_DILATION
    near, small = gate_first.shape[:2]
    assemble(area, tile[...].astype(F32), above, below, left, right)
    for b in (-1, 0, 1):
        at = LEAD + first * b
        window = positive(area[HALO - first : HALO + side + first, at : at + small]).astype(BF16)
        if b < 1:
            hidden_pairs[:, :, (b + 1) * channels : (b + 2) * channels] = window
        else:
            hidden_last[...] = window
    edge = second - first
    part = pre[edge : edge + near, edge : edge + small]
    alive = (part > 0) & inside(part.shape, side, first, 0)
    gate_first[:, :, :inner] = jnp.where(alive, 1.0, 0.0).astype(BF16)
    gate_first[:, :, inner:] = jnp.zeros((near, small, gate_first.shape[2] - inner), BF16)
    bottle_first[...] = positive(pre[second : second + side, second : second + small]).astype(BF16)


def middle_kernel(
    kept, other, w_second, b_second, p_second,
    gate_second, hidden_pairs, hidden_last, bottle_second, grad_tile, grad_pre, first_turn, second_turn,
    current, padded, pre_second,
):
    side, channels, span = first_turn.shape[1], kept.shape[2], kept.shape[1]
    first, second, inner = FIRST_DILATION, SECOND_DILATION, bottle_second.shape[2]
    near, small = gate_second.shape[:2]
    turned = jnp.swapaxes(other[:span].astype(F32), 0, 1)
    sym = rounded((kept[:span].astype(F32) + turned) * 0.5)
    current[:, :span] = jnp.where(inside(sym.shape, side, second, 0), sym, 0)
    current[:, span:] = jnp.zeros((span, current.shape[1] - span, channels), F32)
    edge = second - first
    part = current[edge : edge + near, edge : edge + small]
    gate_second[...] = jnp.where(part > 0, 1.0, 0.0).astype(BF16)
    paired(current, [0, second, 2 * second], small, second, hidden_pairs, hidden_last, positive)

    def rows(step, _):
        top = step * 8
        total = taps_sum(hidden_pairs, hidden_last, top, 8, second, w_second) + b_second[...]
        pre_second[pl.ds(top, 8)] = total.reshape(8, small, total.shape[1])
        return 0

    lax.fori_loop(0, side // 8, rows, 0, unroll=True)
    bottle_second[...] = positive(pre_second[:, :, :inner]).astype(BF16)

    turned = jnp.swapaxes(other[span:, :side].astype(F32), 0, 1)
    padded[:, side:] = jnp.zeros((side, small - side, channels), F32)
    padded[:, :side] = rounded((kept[span:, :side].astype(F32) + turned) * 0.5)
    branch = padded[...].astype(BF16)
    grad_tile[...] = branch
    grad = dot(branch.reshape(side * small, channels), p_second[...]).reshape(side, small, 2 * inner)
    grad = jnp.where(pre_second[...] > 0, grad, 0)
    grad_pre[...] = grad.astype(BF16)
    even = sends_last(0, 0)
    for rows, value, width in ((slice(0, HALO), grad, HALO), (slice(HALO, HALO + first), padded[...], first)):
        head, tail = value[:width, :side], value[side - width :, :side]
        first_turn[rows] = jnp.where(even, tail, head).astype(BF16)
        second_turn[rows] = jnp.where(even, head, tail).astype(BF16)


def weight_sums(rows, ends, grad_pre, hidden, bottle, grad_tile):
    side, small, lanes = grad_pre.shape
    inner = bottle.shape[2]
    size = side * small
    flat = grad_pre.reshape(size, lanes)
    turned = flat.T[:inner].astype(BF16)
    for a in range(3):
        b = 0
        while b < 3:
            window = hidden(a, b)
            grads = dot(turned, window.reshape(size, window.shape[2]))
            for at in range(0, window.shape[2], grad_tile.shape[2]):
                rows[(3 * a + b) * inner : (3 * a + b + 1) * inner] = grads[:, at : at + grad_tile.shape[2]]
                b += 1
    turned = bottle[...].reshape(size, inner).astype(F32).T.astype(BF16)
    rows[9 * inner : 10 * inner] = dot(turned, grad_tile.reshape(size, grad_tile.shape[2]))
    ends[...] = jnp.zeros(ends.shape, F32)
    ends[:, :lanes] = jnp.broadcast_to(jnp.sum(flat, axis=0, keepdims=True), (ends.shape[0], lanes))


def weights_kernel(
    mine, theirs, w_first, w_second, v_second, v_first, p_first, p_second, p_back, b_first, b_second, packed
):
    inner, channels = p_first.shape
    section = lax.axis_index("segment")
    packed[section] = mine[...]
    packed[1 - section] = theirs[...]

    def conv(section, k):
        return packed[section, k * inner : (k + 1) * inner]

    def turned(x):
        return x.astype(F32).T.astype(BF16)

    zero = jnp.zeros((inner, channels), BF16)
    for at, k in enumerate(ORDER):
        here = slice(at * channels, (at + 1) * channels)
        own, other = conv(1, k), conv(1, 3 * (k % 3) + k // 3)
        w_first[here] = turned(conv(0, k))
        w_second[here] = turned(jnp.concatenate([own, other], axis=0))
        upper, lower = (slice((2 * k + half) * inner, (2 * k + half + 1) * inner) for half in (0, 1))
        v_second[upper, :channels], v_second[upper, channels:] = own, zero
        v_second[lower, :channels], v_second[lower, channels:] = zero, other
        v_first[k, :inner], v_first[k, inner:] = conv(0, k), zero
    p_first[...] = conv(0, 9)
    p_second[...] = turned(jnp.concatenate([conv(1, 9), conv(1, 9)], axis=0))
    p_back[...] = turned(jnp.concatenate([conv(0, 9), zero], axis=0))
    b_first[...] = packed[0, 10 * inner :].astype(F32)[:1, :inner]
    bias = packed[1, 10 * inner :].astype(F32)[:1, :inner]
    b_second[...] = jnp.concatenate([bias, bias], axis=1)


def second_sums_kernel(grad_pre, pairs, last, bottle, grad_tile, rows, ends):
    side = grad_pre.shape[0]
    channels = grad_tile.shape[2]

    def hidden(a, b):
        top = SECOND_DILATION * a
        if b == 0:
            return pairs[top : top + side]
        return last[top + SECOND_DILATION : top + SECOND_DILATION + side, :, :channels]

    weight_sums(rows, ends, grad_pre[...].astype(F32), hidden, bottle, grad_tile[...])


def backward_kernel(
    grad_pre, grad_tile, above, below, left, right, left_branch, right_branch, gate_second, gate_first, near_pairs,
    near_last, bottle_first, v_second, p_first, rows_second, ends_second,
    keep, away, grads, grad_first,
    area, pairs, last, branch, rows, ends,
):
    side, channels = grad_first.shape[0], grad_first.shape[2]
    first, second = FIRST_DILATION, SECOND_DILATION
    full, near = side + 2 * HALO, side + 2 * first
    small = grad_pre.shape[1]
    middle = slice(LEAD, LEAD + side)

    area[:, :LEAD] = jnp.zeros((full, LEAD, channels), F32)
    area[:, LEAD + side :] = jnp.zeros((full, area.shape[1] - LEAD - side, channels), F32)
    area[HALO : HALO + side, LEAD : LEAD + small] = grad_pre[...].astype(F32)
    area[:HALO, middle] = above[:HALO].astype(F32)
    area[HALO + side :, middle] = below[:HALO].astype(F32)
    area[:, LEAD - HALO : LEAD] = left[...].astype(F32)
    area[:, LEAD + side : LEAD + side + HALO] = right[...].astype(F32)
    branch[...] = jnp.zeros(branch.shape, F32)
    branch[first : first + side, first : first + side] = grad_tile[:, :side].astype(F32)
    branch[:first, first : first + side] = above[HALO:].astype(F32)
    branch[first + side :, first : first + side] = below[HALO:].astype(F32)
    branch[:, :first] = left_branch[...].astype(F32)
    branch[:, first + side : near] = right_branch[...].astype(F32)
    for b in (-1, 0, 1):
        at = LEAD - HALO + second * (1 - b)
        window = area[:, at : at + small].astype(BF16)
        if b < 1:
            pairs[:, :, (b + 1) * channels : (b + 2) * channels] = window
        else:
            last[...] = window
    grads[:, small:] = jnp.zeros((near, grads.shape[1] - small, channels), F32)

    def sections(step, _):
        top = step * 7
        size = 7 * small
        total = None
        for a in (-1, 0, 1):
            rows_of = pl.ds(top + second * (1 - a), 7)
            at = 3 * (a + 1) * channels
            term = dot(pairs[rows_of].reshape(size, 2 * channels), v_second[at : at + 2 * channels])
            total = term if total is None else total + term
            total = total + dot(last[rows_of].reshape(size, channels), v_second[at + 2 * channels : at + 3 * channels])
        here = pl.ds(top, 7)
        grad = branch[here, :small].reshape(size, channels)
        gate = gate_second[here].astype(F32).reshape(size, channels) > 0
        own = rounded(grad + jnp.where(gate, total[:, :channels], 0))
        other = rounded(grad + jnp.where(gate, total[:, channels:], 0))
        grad = ((own + other) * 0.5).astype(BF16)
        branch[here, :small] = grad.astype(F32).reshape(7, small, channels)
        gate = gate_first[here].astype(F32).reshape(size, channels) > 0
        grad = rounded(jnp.where(gate, dot(grad, p_first[...]), 0))
        grads[here, :small] = grad.reshape(7, small, channels)
        return 0

    lax.fori_loop(0, near // 7, sections, 0, unroll=True)
    part = branch[first : first + side, first : first + small]
    grad_first[...] = part[:, :side].astype(BF16)
    real = lax.broadcasted_iota(jnp.int32, part.shape, 1) < side
    part = jnp.where(real, part, 0).astype(BF16)
    grad = jnp.where(real, grads[first : first + side, first : first + small], 0)

    def hidden(a, b):
        return (near_last if b else near_pairs)[first * a : first * a + side]

    weight_sums(rows, ends, grad, hidden, bottle_first, part)

    first_core = lax.axis_index("segment") == 0
    count = rows.shape[0]
    for here, one, two in (
        (slice(0, count), rows[...], rows_second[...]),
        (slice(count, count + ends.shape[0]), ends[...], ends_second[...]),
    ):
        keep[here] = jnp.where(first_core, one, two)
        away[here] = jnp.where(first_core, two, one).astype(BF16)


def pair_kernel(keep, other, parts):
    devices, share = parts.shape[0], parts.shape[1] - 8
    total = keep[...] + other[...].astype(F32)
    count = keep.shape[0] - 16
    for j in range(devices):
        low, high = min(j * share, count), min((j + 1) * share, count)
        pieces = [total[low:high]] if low < high else []
        if high - low < share:
            pieces.append(jnp.zeros((share - (high - low), keep.shape[1]), F32))
        parts[j] = jnp.concatenate(pieces + [total[count : count + 8]]).astype(BF16)


def input_kernel(grads, grad_first, tile, v_first, out, windows):
    side, channels = out.shape[0], out.shape[2]
    small = windows.shape[2]
    first = FIRST_DILATION
    for b in (-1, 0, 1):
        at = first * (1 - b)
        windows[b + 1] = grads[:, at : at + small].astype(BF16)

    def rows(step, _):
        top = step * 8
        total = jnp.zeros((8 * small, channels), F32)
        for a, b in TAPS:
            window = windows[b + 1, pl.ds(top + first * (1 - a), 8)].reshape(8 * small, channels)
            total = total + dot(window, v_first[tap(a, b)])
        here = pl.ds(top, 8)
        total = total.reshape(8, small, channels)[:, :side]
        total = jnp.where(tile[here].astype(F32) > 0, total, 0)
        out[here] = (grad_first[here].astype(F32) + total).astype(BF16)
        return 0

    lax.fori_loop(0, side // 8, rows, 0, unroll=True)


def total_kernel(scale, parts, rows, ends):
    share = rows.shape[1]
    total = jnp.sum(parts[...].astype(F32), axis=0) * scale
    rows[...] = jnp.broadcast_to(total[:share].astype(BF16)[None], rows.shape)
    ends[...] = total[share:]


def landed_kernel(moved, input_gradient):
    input_gradient[...] = moved[...]


def outputs_kernel(rows, ends, conv_gradient, bias_gradient, out_gradient):
    count, inner = conv_gradient.shape[0], out_gradient.shape[0]
    conv_gradient[...] = rows[:count].astype(F32)
    out_gradient[...] = rows[count : count + inner].astype(F32)
    bias_gradient[...] = ends[:1, :inner]


def call(kernel, name, outs, scratch, flops, *operands):
    outs = [jax.ShapeDtypeStruct(shape, dtype) for shape, dtype in outs]
    moved = sum(x.size * x.dtype.itemsize for x in list(operands) + outs)
    return pl.pallas_call(
        kernel,
        name=name,
        out_shape=outs,
        scratch_shapes=[pltpu.VMEM(shape, dtype) for shape, dtype in scratch],
        cost_estimate=pl.CostEstimate(flops=flops, bytes_accessed=moved, transcendentals=0),
        compiler_params=pltpu.CompilerParams(vmem_limit_bytes=40 * 1024 * 1024),
    )(*operands)


def local(activations, cotangent, conv_weight, conv_bias, out_weight):
    side, channels, inner = activations.shape[1], activations.shape[3], conv_weight.shape[3]
    number = lax.axis_size("row")
    first, second = FIRST_DILATION, SECOND_DILATION
    full, span, near = side + 2 * HALO, side + 2 * second, side + 2 * first
    wide, small = up16(span), up16(near)

    tile = bring(activations[0])
    stored_even = lax.rem(lax.axis_index("row"), 2) == 0
    ends = (activations[0, side - HALO :], activations[0, :HALO])
    got = [bring(jnp.where(stored_even, *ends), 0), bring(jnp.where(stored_even, *ends[::-1]), 1)]
    above, below = around(0, got)

    def columns(turn):
        def chosen(x):
            return jnp.swapaxes(jnp.where(sends_last(1, turn), x[:, side - HALO :], x[:, :HALO]), 0, 1)

        strip = jnp.pad(chosen(tile), ((0, 0), (HALO, HALO), (0, 0)))
        strip = lax.optimization_barrier(strip)
        for row_turn in (0, 1):
            at = jnp.where(sends_last(0, row_turn), HALO + side, 0)
            strip = lax.dynamic_update_slice(strip, chosen(got[row_turn]), (0, at, 0))
        return strip

    strips, late = lax.optimization_barrier(([columns(0), columns(1)], cotangent[0]))
    left, right = around(1, [exchange(strips[turn], 1, turn) for turn in (0, 1)])
    late = bring(late)

    bias_rows = jnp.pad(conv_bias, ((0, 15), (0, channels - inner)))
    packed = jnp.concatenate(
        [jnp.swapaxes(conv_weight[0], 1, 2).reshape(9 * inner, channels), out_weight[0], bias_rows]
    )
    others = lax.ppermute(packed, "segment", [(0, 1), (1, 0)])
    w_first, w_second, v_second, v_first, p_first, p_second, p_back, b_first, b_second = call(
        weights_kernel,
        "weights",
        [
            ((9 * channels, inner), BF16),
            ((9 * channels, 2 * inner), BF16),
            ((18 * inner, 2 * channels), BF16),
            ((9, 2 * inner, channels), BF16),
            ((inner, channels), BF16),
            ((channels, 2 * inner), BF16),
            ((channels, 2 * inner), BF16),
            ((1, inner), F32),
            ((1, 2 * inner), F32),
        ],
        [((2,) + packed.shape, BF16)],
        packed.size,
        *(packed, others),
    )

    own = (tile, above, below, jnp.swapaxes(left, 0, 1), jnp.swapaxes(right, 0, 1))
    area = ((full, LEAD + up16(side + LEAD), channels), F32)
    kept, pre_first = call(
        own_kernel,
        "own_branch",
        [((span + side, span, channels), BF16), ((span, wide, inner), F32)],
        [area, ((full, wide, 2 * channels), BF16), ((full + first, wide, 2 * channels), BF16)],
        span * wide * channels * inner * 400,
        *own,
        *(w_first, b_first, p_first),
    )
    kept = lax.dynamic_update_slice(kept, late, (span, 0, 0))
    other = swap(kept)
    gate_second, hidden_pairs, hidden_last, bottle_second, grad_tile, grad_pre, *strips = call(
        middle_kernel,
        "middle",
        [
            ((near, small, channels), BF16),
            ((span, small, 2 * channels), BF16),
            ((span + second, small, 2 * channels), BF16),
            ((side, small, inner), BF16),
            ((side, small, channels), BF16),
            ((side, small, 2 * inner), BF16),
            ((HALO + first, side, channels), BF16),
            ((HALO + first, side, channels), BF16),
        ],
        [
            ((span, wide, channels), F32),
            ((side, small, channels), F32),
            ((side, small, 2 * inner), F32),
        ],
        24 * side * small * channels * 2 * inner,
        *(kept, other, w_second, b_second, p_second),
    )

    near_pairs, near_last, gate_first, bottle_first = call(
        near_kernel,
        "near",
        [
            ((near, small, 2 * channels), BF16),
            ((near, small, channels), BF16),
            ((near, small, channels), BF16),
            ((side, small, inner), BF16),
        ],
        [area],
        near * small * channels,
        *own,
        pre_first,
    )

    above, below = around(0, [exchange(strips[turn], 0, turn) for turn in (0, 1)])
    rows_second, ends_second = call(
        second_sums_kernel,
        "second_sums",
        [((10 * inner, channels), F32), ((16, channels), F32)],
        [],
        20 * side * small * channels * inner,
        *(grad_pre, hidden_pairs, hidden_last, bottle_second, grad_tile),
    )

    def columns(turn):
        def chosen(x, width):
            return jnp.where(sends_last(1, turn), x[:, side - width : side], x[:, :width])

        grads = jnp.concatenate([chosen(x, HALO) for x in (above[:HALO], grad_pre, below[:HALO])])
        branches = jnp.concatenate([chosen(x, first) for x in (above[HALO:], grad_tile, below[HALO:])])
        branches = jnp.pad(branches, ((second, second), (0, 0), (0, 0)))
        return jnp.swapaxes(jnp.concatenate([grads, branches], axis=1), 0, 1)

    left, right = around(1, [exchange(columns(turn), 1, turn) for turn in (0, 1)])
    left, right = jnp.swapaxes(left, 0, 1), jnp.swapaxes(right, 0, 1)

    devices = number * number
    share = -(-10 * inner // (8 * devices)) * 8
    keep, away, grads, grad_first = call(
        backward_kernel,
        "backward",
        [
            ((10 * inner + 16, channels), F32),
            ((10 * inner + 16, channels), BF16),
            ((near, small + 16, channels), F32),
            ((side, side, channels), BF16),
        ],
        [
            ((full, LEAD + up16(side + HALO + first), channels), F32),
            ((full, small, 2 * channels), BF16),
            ((full, small, channels), BF16),
            ((near, small + 16, channels), F32),
            ((10 * inner, channels), F32),
            ((16, channels), F32),
        ],
        36 * near * small * channels * channels,
        *(grad_pre, grad_tile, above, below, left[:, :HALO], right[:, :HALO]),
        *(left[second : second + near, HALO:], right[second : second + near, HALO:]),
        *(gate_second, gate_first, near_pairs, near_last, bottle_first, v_second, p_back, rows_second, ends_second),
    )

    (input_gradient,) = call(
        input_kernel,
        "input",
        [((side, side, channels), BF16)],
        [((3, near, small, channels), BF16)],
        18 * side * small * channels * channels,
        *(grads, grad_first, tile, v_first),
    )
    other = lax.ppermute(away, "segment", [(0, 1), (1, 0)])
    other, input_gradient = lax.optimization_barrier((other, input_gradient))
    (parts,) = call(
        pair_kernel,
        "pair",
        [((devices, share + 8, channels), BF16)],
        [],
        keep.size,
        *(keep, other),
    )
    parts = lax.all_to_all(parts, GRID, 0, 0, tiled=True)
    input_gradient = take_back(input_gradient)
    cells = lax.axis_size("segment") * (side * number) * (side * number)
    rows, ends = call(
        functools.partial(total_kernel, float(cells) ** -0.5),
        "total",
        [((devices, share, channels), BF16), ((8, channels), F32)],
        [],
        parts.size,
        parts,
    )
    rows = lax.all_to_all(rows, GRID, 0, 0, tiled=True).reshape(devices * share, channels)
    (input_gradient,) = call(
        landed_kernel, "landed", [((side, side, channels), BF16)], [], side**2 * channels * 400000, input_gradient
    )
    rows, input_gradient = lax.optimization_barrier((rows, input_gradient))
    conv_gradient, bias_gradient, out_gradient = call(
        outputs_kernel,
        "outputs",
        [((9 * inner, channels), F32), ((1, inner), F32), ((inner, channels), F32)],
        [],
        rows.size,
        *(rows, ends),
    )
    conv_gradient = jnp.swapaxes(conv_gradient.reshape(1, 9, inner, channels), 2, 3)
    return (input_gradient[None], conv_gradient, bias_gradient, out_gradient[None])


def solution(mesh):
    in_specs = (
        P("segment", "row", "col", None),
        P("segment", "row", "col", None),
        P("segment", None, None, None),
        P("segment", None),
        P("segment", None, None),
    )
    out_specs = (
        P("segment", "row", "col", None),
        P("segment", None, None, None),
        P("segment", None),
        P("segment", None, None),
    )
    return jax.shard_map(local, mesh=mesh, in_specs=in_specs, out_specs=out_specs, check_vma=False)
```
